32 devices in a mesh: row: 4 (over z), wide: 8 (over y, x, core).
Axes of the slice: x: 2, y: 2, z: 4, core: 2. Of those that a mesh axis runs over, the one named last changes fastest.
Arguments:
- eigvec_t: float32 [2048, 32768], P(('row', 'wide')), may hold values from -6 to 6
- householder: float32 [16, 32, 32768], P('row', None, 'wide'), may hold values from -0.0625 to 0.0625
- wy_factor: float32 [6, 32, 32], replicated, may hold values from -0.5 to 0.5, as said below
- block_place: int32 [6], replicated, may hold values from 0 to 15, as said below
- offsets: int32 [6], replicated, may hold values from 0 to 16383, as said below
Outputs:
- vectors: float32 [2048, 32768], P('row', 'wide')
The draws below stay inside these ranges and needn't reach their ends.
Inputs may be any that keep to these rules, and one draw needn't show every extreme that they name: wy_factor[s] is upper triangular. `offsets`: some step has offset 0 and some step has offset 32768 // 2 - 1. `block_place`: no stack position appears twice; positions 0 and 15 both appear.
All inputs are finite; a program needn't handle non-finite values.
Results may differ from the reference program's by a relative error of at most 0.0003.
Values sent between devices are 32-bit elements; how exact they have to be, the bound alone decides.
No kernel may reach another device: no remote copies, remote signals or barrier semaphores. Data moves between devices by JAX's collectives and lax.ppermute only.
A program may use at most 64 MiB of HBM per device.

```python
import jax
import jax.numpy as jnp
from jax import lax

N = 32768
BW = 32
K = 2048
STACK = 16
STEPS = 6


def draw_wy_factor(key, part):
    key_diag, key_off = jax.random.split(jax.random.fold_in(key, 7))
    diag = jax.random.uniform(key_diag, (STEPS, BW), jnp.float32, 0.15, 0.35)
    upper = jnp.clip(0.06 * jax.random.normal(key_off, (STEPS, BW, BW), jnp.float32), -0.3, 0.3)
    upper = jnp.triu(upper, 1)
    return upper + diag[:, :, None] * jnp.eye(BW, dtype=jnp.float32)[None, :, :]


def draw_block_place(key, part):
    key_pick, key_order = jax.random.split(jax.random.fold_in(key, 13))
    inner = 1 + jax.random.permutation(key_pick, jnp.arange(STACK - 2, dtype=jnp.int32))
    chosen = jnp.concatenate([jnp.array([0, STACK - 1], dtype=jnp.int32), inner.astype(jnp.int32)])[:STEPS]
    return jax.random.permutation(key_order, chosen).astype(jnp.int32)


def draw_offsets(key, part):
    key_vals, key_perm = jax.random.split(jax.random.fold_in(key, 11))
    values = jax.random.randint(key_vals, (STEPS,), 0, N // 2, jnp.int32)
    order = jax.random.permutation(key_perm, STEPS)
    values = values.at[order[0]].set(0)
    values = values.at[order[1]].set(N // 2 - 1)
    return values.astype(jnp.int32)


def levels(rng, extent, pieces, smallest, top_value):
    loudness, own = 1.0, jax.random.fold_in(rng, 6)
    for dim, parts in pieces:
        draws = jnp.exp(jax.random.uniform(jax.random.fold_in(own, dim), (parts,), jnp.float32, smallest / len(pieces), top_value / len(pieces)))
        loudness = loudness * jnp.repeat(draws, extent[dim] // parts).reshape([-1 if axis == dim else 1 for axis in range(len(extent))])
    return loudness


def gaussian(own_key, dims, width, limit, shards=(), held_as=jnp.bfloat16):
    level = levels(own_key, dims, shards, -0.22, 0.18) if shards else 1.0
    drawn = jax.random.normal(own_key, dims, jnp.float32) * width * level
    return jnp.minimum(jnp.maximum(drawn, -limit), limit).astype(held_as)


def setup_inputs(seed: int = 0) -> dict:
    key_of = jax.random.split(jax.random.key(seed), 6)
    return {
        "eigvec_t": gaussian(key_of[0], (K, N), 1.0, 6.0, ((0, 32),), jnp.float32),
        "householder": gaussian(key_of[1], (STACK, BW, N), (N // 4) ** -0.5, 0.0625, ((0, 4), (2, 8)), jnp.float32),
        "wy_factor": draw_wy_factor(jax.random.fold_in(key_of[5], 71), 0),
        "block_place": draw_block_place(jax.random.fold_in(key_of[5], 71), 0),
        "offsets": draw_offsets(jax.random.fold_in(key_of[5], 71), 0),
    }


def reference(eigvec_t, householder, wy_factor, block_place, offsets):
    highest = lax.Precision.HIGHEST
    columns = jnp.arange(N, dtype=jnp.int32)

    def apply_step(current, s):
        place = block_place[s].astype(jnp.int32)
        vecs = lax.dynamic_index_in_dim(householder, place, 0, keepdims=False)
        vecs = jnp.where(columns[None, :] >= offsets[s], vecs, jnp.zeros_like(vecs))
        factor = lax.dynamic_index_in_dim(wy_factor, s, 0, keepdims=False)
        inner = jnp.dot(current, vecs.T, precision=highest)
        scaled = jnp.dot(inner, factor.T, precision=highest)
        return current - jnp.dot(scaled, vecs, precision=highest), None

    result, unused = lax.scan(apply_step, eigvec_t, jnp.arange(STEPS, dtype=jnp.int32))
    return result
```

```python
import functools

import jax
import jax.numpy as jnp
from jax import lax
from jax.experimental import pallas as pl
from jax.experimental.pallas import tpu as pltpu
from jax.sharding import PartitionSpec as P

HIGHEST = lax.Precision.HIGHEST
VMEM_LIMIT = 48 * 1024 * 1024
GROUPS = (2, 2, 2, 1, 1)


def dot_t(a, b):
    return lax.dot_general(a, b, (((1,), (1,)), ((), ())), precision=HIGHEST, preferred_element_type=jnp.float32)


def dot(a, b):
    return lax.dot_general(a, b, (((1,), (0,)), ((), ())), precision=HIGHEST, preferred_element_type=jnp.float32)


def params(dims):
    return pltpu.CompilerParams(dimension_semantics=("arbitrary",) * dims, vmem_limit_bytes=VMEM_LIMIT)


def cost(flops, nbytes):
    return pl.CostEstimate(flops=flops, bytes_accessed=nbytes, transcendentals=0)


def own_blocks(householder, block_place, offsets):
    slots, width, ncols = householder.shape
    steps = block_place.shape[0]
    where = jnp.stack([lax.axis_index("row"), lax.axis_index("wide") * ncols]).astype(jnp.int32)

    def kernel(place_ref, offset_ref, where_ref, stack_ref, out_ref):
        s = pl.program_id(0)
        mine = (place_ref[s] // slots) == where_ref[0]
        columns = where_ref[1] + lax.broadcasted_iota(jnp.int32, (1, width, ncols), 2)
        keep = (columns >= offset_ref[s]) & mine
        out_ref[...] = jnp.where(keep, stack_ref[...], 0.0)

    return pl.pallas_call(
        kernel,
        out_shape=jax.ShapeDtypeStruct((steps, width, ncols), jnp.float32),
        grid_spec=pltpu.PrefetchScalarGridSpec(
            num_scalar_prefetch=3,
            grid=(steps,),
            in_specs=[pl.BlockSpec((1, width, ncols), lambda s, place, off, where: (place[s] % slots, 0, 0))],
            out_specs=pl.BlockSpec((1, width, ncols), lambda s, place, off, where: (s, 0, 0)),
        ),
        compiler_params=params(1),
        cost_estimate=cost(0, 8 * steps * width * ncols),
        name="own_blocks",
    )(block_place, offsets, where, householder)


def gram(vecs):
    height, ncols = vecs.shape

    def kernel(v_ref, out_ref):
        v = v_ref[...]
        out_ref[...] = dot_t(v, v)

    return pl.pallas_call(
        kernel,
        out_shape=jax.ShapeDtypeStruct((height, height), jnp.float32),
        compiler_params=pltpu.CompilerParams(vmem_limit_bytes=VMEM_LIMIT),
        cost_estimate=cost(12 * height * height * ncols, 4 * height * ncols),
        name="gram",
    )(vecs)


def merge(cross, factors):
    steps, width, _ = factors.shape
    height = steps * width

    def kernel(cross_ref, factor_ref, out_ref):
        out_ref[...] = jnp.zeros_like(out_ref)
        for k in range(steps):
            rows = pl.ds(k * width, width)
            own = lax.broadcasted_iota(jnp.int32, (width, height), 0) + k * width
            unit = (own == lax.broadcasted_iota(jnp.int32, (width, height), 1)).astype(jnp.float32)
            rest = unit - dot(cross_ref[rows, :], out_ref[...]) if k else unit
            out_ref[rows, :] = dot(factor_ref[k], rest)

    return pl.pallas_call(
        kernel,
        out_shape=jax.ShapeDtypeStruct((height, height), jnp.float32),
        compiler_params=pltpu.CompilerParams(vmem_limit_bytes=VMEM_LIMIT),
        cost_estimate=cost(12 * height * height * height, 8 * height * height),
        name="merge",
    )(cross, factors)


def column_block(ncols):
    return 1024 if ncols % 1024 == 0 else ncols


def inner_products(x, vecs):
    lead, tiles, tile, ncols = x.shape
    height = vecs.shape[0]
    cols = column_block(ncols)

    def kernel(x_ref, v_ref, out_ref):
        part = dot_t(x_ref[...].reshape(lead * tile, cols), v_ref[...]).reshape(lead, 1, tile, height)

        @pl.when(pl.program_id(1) == 0)
        def _():
            out_ref[...] = part

        @pl.when(pl.program_id(1) > 0)
        def _():
            out_ref[...] += part

    return pl.pallas_call(
        kernel,
        out_shape=jax.ShapeDtypeStruct((lead, tiles, tile, height), jnp.float32),
        grid=(tiles, ncols // cols),
        in_specs=[
            pl.BlockSpec((lead, 1, tile, cols), lambda t, c: (0, t, 0, c)),
            pl.BlockSpec((height, cols), lambda t, c: (0, c)),
        ],
        out_specs=pl.BlockSpec((lead, 1, tile, height), lambda t, c: (0, t, 0, 0)),
        compiler_params=params(2),
        cost_estimate=cost(12 * lead * tiles * tile * ncols * height, 4 * lead * tiles * tile * ncols),
        name="inner_products",
    )(x, vecs)


def update(x, sums, merged, vecs, out, first, total):
    lead, tiles, tile, ncols = x.shape
    height = vecs.shape[0]
    cols = column_block(ncols)
    n_sums = len(sums)

    def kernel(*refs):
        sum_refs, (x_ref, m_ref, v_ref) = refs[:n_sums], refs[n_sums:n_sums + 3]
        out_ref, u_ref = refs[-2:]

        @pl.when(pl.program_id(1) == 0)
        def _():
            w = sum_refs[0][...]
            for ref in sum_refs[1:]:
                w = w + ref[...]
            u_ref[...] = dot_t(w.reshape(lead * tile, height), m_ref[...])

        change = dot(u_ref[...], v_ref[...]).reshape(lead, 1, tile, cols)
        out_ref[...] = x_ref[...] - change

    operands = list(sums) + [x, merged, vecs]
    in_specs = [pl.BlockSpec((lead, 1, tile, height), lambda t, c: (0, t, 0, 0))] * n_sums + [
        pl.BlockSpec((lead, 1, tile, cols), lambda t, c: (0, t, 0, c)),
        pl.BlockSpec((height, height), lambda t, c: (0, 0)),
        pl.BlockSpec((height, cols), lambda t, c: (0, c)),
    ]
    aliases = {}
    if out is not None:
        aliases = {len(operands): 0}
        operands.append(out)
        in_specs.append(pl.BlockSpec(memory_space=pl.ANY))
    return pl.pallas_call(
        kernel,
        out_shape=jax.ShapeDtypeStruct((lead, total, tile, ncols), jnp.float32),
        grid=(tiles, ncols // cols),
        in_specs=in_specs,
        out_specs=pl.BlockSpec((lead, 1, tile, cols), lambda t, c: (0, first + t, 0, c)),
        scratch_shapes=[pltpu.VMEM((lead * tile, height), jnp.float32)],
        input_output_aliases=aliases,
        compiler_params=params(2),
        cost_estimate=cost(12 * lead * tiles * tile * ncols * height, 8 * lead * tiles * tile * ncols),
        name="update",
    )(*operands)


def partial_sums(part, axis, size):
    pair = part + lax.ppermute(part, axis, [(i, i ^ 1) for i in range(size)])
    return [pair] + [lax.ppermute(pair, axis, [(i, i ^ k) for i in range(size)]) for k in range(2, size, 2)]


def body(n_wide, eigvec_t, householder, wy_factor, block_place, offsets):
    rows, order = eigvec_t.shape
    steps, width, _ = wy_factor.shape
    ncols = order // n_wide
    height = steps * width
    tile = 8 if rows % 8 == 0 else rows
    tiles = rows // tile
    groups = GROUPS if sum(GROUPS) == tiles else (tiles,)

    parts = []
    first = 0
    for size in groups:
        part = eigvec_t[first * tile:(first + size) * tile].reshape(size, tile, n_wide, ncols)
        parts.append((first, size, lax.all_to_all(part, "wide", split_axis=2, concat_axis=0)))
        first += size

    vecs = lax.psum(own_blocks(householder, block_place, offsets), "row").reshape(height, ncols)
    cross = functools.reduce(jnp.add, partial_sums(gram(vecs), "wide", n_wide))
    merged = merge(cross, wy_factor)

    out = None
    for first, size, x in parts:
        if tile % 8:
            x = x.reshape(1, 1, n_wide * rows, ncols)
        sums = partial_sums(inner_products(x, vecs), "wide", n_wide)
        out = update(x, sums, merged, vecs, out, first, tiles)
    return out.reshape(n_wide * rows, ncols)


def solution(mesh):
    return jax.shard_map(
        functools.partial(body, mesh.shape["wide"]),
        mesh=mesh,
        in_specs=(P(("row", "wide"), None), P("row", None, "wide"), P(), P(), P()),
        out_specs=P("row", "wide"),
        check_vma=False,
    )
```

```python
import functools

import jax
import jax.numpy as jnp
from jax import lax
from jax.experimental import pallas as pl
from jax.experimental.pallas import tpu as pltpu
from jax.sharding import PartitionSpec as P

HIGHEST = lax.Precision.HIGHEST
VMEM_LIMIT = 56 * 1024 * 1024
GROUPS = (2, 2, 2, 1, 1)
SPLITS = 2


def dot_t(a, b):
    return lax.dot_general(a, b, (((1,), (1,)), ((), ())), precision=HIGHEST, preferred_element_type=jnp.float32)


def dot(a, b):
    return lax.dot_general(a, b, (((1,), (0,)), ((), ())), precision=HIGHEST, preferred_element_type=jnp.float32)


def halves(x):
    high = x.astype(jnp.bfloat16)
    return high, (x - high.astype(jnp.float32)).astype(jnp.bfloat16)


def dot3(a, b, dims):
    def one(x, y):
        return lax.dot_general(x, y, (dims, ((), ())), preferred_element_type=jnp.float32)
    return one(a[0], b[0]) + (one(a[0], b[1]) + one(a[1], b[0]))


def params(dims=0):
    semantics = ("arbitrary",) * dims if dims else None
    return pltpu.CompilerParams(dimension_semantics=semantics, vmem_limit_bytes=VMEM_LIMIT)


def cost(flops, nbytes):
    return pl.CostEstimate(flops=flops, bytes_accessed=nbytes, transcendentals=0)


SMEM = pl.BlockSpec(memory_space=pltpu.SMEM)
ANY = pl.BlockSpec(memory_space=pl.ANY)
VMEM = pl.BlockSpec(memory_space=pltpu.VMEM)


def pack(here, x, first, rows, n_wide):
    ncols = x.shape[1] // n_wide

    def kernel(here_ref, x_ref, *refs):
        outs, sems = refs[:-1], refs[-1]
        copies = []
        for k, out in enumerate(outs):
            start = pl.multiple_of((here_ref[1] ^ k) * ncols, ncols)
            source = x_ref.at[pl.ds(first, rows), pl.ds(start, ncols)]
            copies.append(pltpu.make_async_copy(source, out, sems.at[k]))
        for copy in copies:
            copy.start()
        for copy in copies:
            copy.wait()

    return pl.pallas_call(
        kernel,
        out_shape=[jax.ShapeDtypeStruct((rows, ncols), jnp.float32)] * n_wide,
        in_specs=[SMEM, ANY],
        out_specs=[ANY] * n_wide,
        scratch_shapes=[pltpu.SemaphoreType.DMA((n_wide,))],
        compiler_params=params(),
        cost_estimate=cost(0, 8 * rows * x.shape[1]),
        name="pack",
    )(here, x)


def plan(place_ref, slots, n_rows):
    places = [place_ref[s] for s in range(place_ref.shape[0])]
    roots = [lax.div(p, slots) for p in places]
    slot = [lax.rem(p, slots) for p in places]
    ranks = [sum([(roots[i] == roots[s]).astype(jnp.int32) for i in range(s)], jnp.int32(0)) for s in range(len(places))]
    counts = [sum([(r == i).astype(jnp.int32) for r in roots], jnp.int32(0)) for i in range(n_rows)]
    return roots, slot, ranks, counts


def feed(here, place, stack, ups, downs, n_rows, part, cols):
    slots, width, _ = stack.shape
    turn = len(ups)

    def kernel(here_ref, place_ref, stack_ref, *refs):
        arrived, (out_up, out_down, sems) = refs[:-3], refs[-3:]
        roots, slot, ranks, _ = plan(place_ref, slots, n_rows)
        me = here_ref[0]
        mine = [r == me for r in roots]
        count = sum([m.astype(jnp.int32) for m in mine], jnp.int32(0))
        own = sum([jnp.where(m & (k == turn), s, 0) for m, k, s in zip(mine, ranks, slot)], jnp.int32(0))
        older = turn - jnp.maximum(count, 1)
        stored = stack_ref.at[own, :, pl.ds(part * cols, cols)]
        for side, out in ((0, out_up), (1, out_down)):
            @pl.when((older < 0) | (count > turn))
            def _():
                pltpu.make_async_copy(stored, out, sems.at[side]).start()

            for i in range(turn):
                @pl.when((older == i) & (count <= turn))
                def _():
                    pltpu.make_async_copy(arrived[side * turn + i], out, sems.at[side]).start()
        for side, out in ((0, out_up), (1, out_down)):
            pltpu.make_async_copy(stored, out, sems.at[side]).wait()

    return pl.pallas_call(
        kernel,
        out_shape=[jax.ShapeDtypeStruct((width, cols), jnp.float32)] * 2,
        in_specs=[SMEM, SMEM, ANY] + [ANY] * (2 * turn),
        out_specs=[ANY] * 2,
        scratch_shapes=[pltpu.SemaphoreType.DMA((2,))],
        compiler_params=params(),
        cost_estimate=cost(0, 16 * width * cols),
        name="feed",
    )(here, place, stack, *ups, *downs)


def assemble(here, place, offsets, stack, ups, downs, n_rows):
    slots, width, ncols = stack.shape
    steps = place.shape[0]
    height = steps * width
    turns, splits = len(ups), len(ups[0])
    cols = ncols // splits

    def kernel(here_ref, place_ref, offset_ref, stack_ref, *refs):
        arrived, (high_ref, low_ref, gram_ref, held, sems) = refs[:-5], refs[-5:]
        up, down = arrived[:turns * splits], arrived[turns * splits:]
        roots, slot, ranks, counts = plan(place_ref, slots, n_rows)
        me = here_ref[0]
        for s in range(steps):
            root = roots[s]
            low, high = jnp.minimum(root, me), jnp.maximum(root, me)
            between = [jnp.where((i > low) & (i < high), jnp.maximum(counts[i], 1), 0) for i in range(n_rows)]
            turn = sum(between, ranks[s])
            target = held.at[pl.ds(s * width, width)]

            @pl.when(root == me)
            def _():
                pltpu.make_async_copy(stack_ref.at[slot[s]], target, sems.at[s]).start()

            for side, came in ((root < me, up), (root > me, down)):
                for i in range(turns):
                    @pl.when(side & (turn == i))
                    def _():
                        for p in range(splits):
                            piece = held.at[pl.ds(s * width, width), pl.ds(p * cols, cols)]
                            pltpu.make_async_copy(came[i * splits + p], piece, sems.at[s]).start()
        columns = here_ref[1] * ncols + lax.broadcasted_iota(jnp.int32, (width, ncols), 1)
        for s in range(steps):
            rows = pl.ds(s * width, width)
            pltpu.make_async_copy(stack_ref.at[0], held.at[rows], sems.at[s]).wait()
            masked = jnp.where(columns >= offset_ref[s], held[rows, :], 0.0)
            held[rows, :] = masked
            high, low = halves(masked)
            high_ref[rows, :] = high
            low_ref[rows, :] = low
        gram_ref[...] = dot_t(held[...], held[...])

    return pl.pallas_call(
        kernel,
        out_shape=[
            jax.ShapeDtypeStruct((height, ncols), jnp.bfloat16),
            jax.ShapeDtypeStruct((height, ncols), jnp.bfloat16),
            jax.ShapeDtypeStruct((height, height), jnp.float32),
        ],
        in_specs=[SMEM, SMEM, SMEM, ANY] + [ANY] * (2 * turns * splits),
        out_specs=[VMEM] * 3,
        scratch_shapes=[pltpu.VMEM((height, ncols), jnp.float32), pltpu.SemaphoreType.DMA((steps,))],
        compiler_params=params(),
        cost_estimate=cost(12 * height * height * ncols, 8 * height * ncols),
        name="assemble",
    )(here, place, offsets, stack, *[p for turn in ups for p in turn], *[p for turn in downs for p in turn])


def merge(cross, factors):
    steps, width, _ = factors.shape
    height = steps * width

    def kernel(*refs):
        cross_refs, (factor_ref, out_ref, total) = refs[:-3], refs[-3:]
        total[...] = sum([ref[...] for ref in cross_refs[1:]], cross_refs[0][...])
        out_ref[...] = jnp.zeros_like(out_ref)
        for k in range(steps):
            rows = pl.ds(k * width, width)
            own = lax.broadcasted_iota(jnp.int32, (width, height), 0) + k * width
            unit = (own == lax.broadcasted_iota(jnp.int32, (width, height), 1)).astype(jnp.float32)
            rest = unit - dot(total[rows, :], out_ref[...]) if k else unit
            out_ref[rows, :] = dot(factor_ref[k], rest)

    return pl.pallas_call(
        kernel,
        out_shape=jax.ShapeDtypeStruct((height, height), jnp.float32),
        scratch_shapes=[pltpu.VMEM((height, height), jnp.float32)],
        compiler_params=params(),
        cost_estimate=cost(12 * height * height * height, 8 * height * height),
        name="merge",
    )(*cross, factors)


def column_block(ncols):
    return 1024 if ncols % 1024 == 0 else ncols


def inner_products(pieces, vecs):
    n = len(pieces)
    rows, ncols = pieces[0].shape
    height = vecs[0].shape[0]
    cols = column_block(ncols)

    def kernel(*refs):
        x_refs, (high_ref, low_ref, out_ref) = refs[:n], refs[n:]
        x = jnp.concatenate([ref[...] for ref in x_refs], axis=0)
        part = dot3(halves(x), (high_ref[...], low_ref[...]), ((1,), (1,))).reshape(n, rows, height)

        @pl.when(pl.program_id(0) == 0)
        def _():
            out_ref[...] = part

        @pl.when(pl.program_id(0) > 0)
        def _():
            out_ref[...] += part

    return pl.pallas_call(
        kernel,
        out_shape=jax.ShapeDtypeStruct((n, rows, height), jnp.float32),
        grid=(ncols // cols,),
        in_specs=[pl.BlockSpec((rows, cols), lambda c: (0, c))] * n + [pl.BlockSpec((height, cols), lambda c: (0, c))] * 2,
        out_specs=pl.BlockSpec((n, rows, height), lambda c: (0, 0, 0)),
        compiler_params=params(1),
        cost_estimate=cost(6 * n * rows * ncols * height, 4 * n * rows * ncols),
        name="inner_products",
    )(*pieces, *vecs)


def update(here, pieces, sums, merged, vecs, out, first, total, tile):
    n, n_sums = len(pieces), len(sums)
    rows, ncols = pieces[0].shape
    tiles = rows // tile
    height = vecs[0].shape[0]
    cols = column_block(ncols)

    def kernel(here_ref, *refs):
        x_refs, sum_refs, (m_ref, high_ref, low_ref) = refs[:n], refs[n:n + n_sums], refs[n + n_sums:n + n_sums + 3]
        out_ref, u_high, u_low = refs[-3:]

        @pl.when(pl.program_id(0) == 0)
        def _():
            w = [sum([ref[k ^ m] for (m, _), ref in zip(sums[1:], sum_refs[1:])], sum_refs[0][k ^ sums[0][0]]) for k in range(n)]
            u_high[...], u_low[...] = halves(dot_t(jnp.concatenate(w, axis=0), m_ref[...]))

        change = dot3((u_high[...], u_low[...]), (high_ref[...], low_ref[...]), ((1,), (0,)))
        for k in range(n):
            value = x_refs[k][...] - change[k * rows:(k + 1) * rows]
            source = here_ref[1] ^ k if n > 1 else 0
            out_ref[pl.ds(source, 1)] = value.reshape(1, tiles, tile, cols)

    operands = [here] + list(pieces) + [array for _, array in sums] + [merged, *vecs]
    in_specs = (
        [SMEM]
        + [pl.BlockSpec((rows, cols), lambda c: (0, c))] * n
        + [pl.BlockSpec((n, rows, height), lambda c: (0, 0, 0))] * n_sums
        + [pl.BlockSpec((height, height), lambda c: (0, 0))]
        + [pl.BlockSpec((height, cols), lambda c: (0, c))] * 2
    )
    aliases = {}
    if out is not None:
        aliases = {len(operands): 0}
        operands.append(out)
        in_specs.append(ANY)
    return pl.pallas_call(
        kernel,
        out_shape=jax.ShapeDtypeStruct((n, total, tile, ncols), jnp.float32),
        grid=(ncols // cols,),
        in_specs=in_specs,
        out_specs=pl.BlockSpec((n, tiles, tile, cols), lambda c: (0, first // tiles, 0, c)),
        scratch_shapes=[pltpu.VMEM((n * rows, height), jnp.bfloat16)] * 2,
        input_output_aliases=aliases,
        compiler_params=params(1),
        cost_estimate=cost(6 * n * rows * ncols * height, 8 * n * rows * ncols),
        name="update",
    )(*operands)


def partial_sums(part, size, by_piece):
    def swap(array, k):
        return lax.ppermute(array, "wide", [(i, i ^ k) for i in range(size)])

    other = swap(part, 1)
    if by_piece:
        other = other.reshape(size // 2, 2, *part.shape[1:])[:, ::-1].reshape(part.shape)
    pair = part + other
    return [(0, pair)] + [(k if by_piece else 0, swap(pair, k)) for k in range(2, size, 2)]


def body(n_row, n_wide, eigvec_t, householder, wy_factor, block_place, offsets):
    rows, order = eigvec_t.shape
    steps, width, _ = wy_factor.shape
    slots = householder.shape[0]
    ncols = order // n_wide
    here = jnp.stack([lax.axis_index("row"), lax.axis_index("wide")]).astype(jnp.int32)

    turns = max(z + min(steps - 1, slots * (n_row - 1 - z)) for z in range(n_row - 1))
    cols = ncols // SPLITS
    streams = [([], []) for _ in range(SPLITS)]
    upward = [(i, i + 1) for i in range(n_row - 1)]
    downward = [(i + 1, i) for i in range(n_row - 1)]

    def turn_of(part):
        ups, downs = streams[part]
        to_up, to_down = feed(here, block_place, householder, ups, downs, n_row, part, cols)
        streams[part] = (ups + [lax.ppermute(to_up, "row", upward)], downs + [lax.ppermute(to_down, "row", downward)])

    by_piece = rows % 8 == 0
    tile = 8 if by_piece else rows * n_wide
    total = rows // tile if by_piece else 1
    groups = GROUPS if sum(GROUPS) == total else (total,)
    parts = []
    first = 0
    for size in groups:
        if by_piece:
            pieces = pack(here, eigvec_t, first * tile, size * tile, n_wide)
            pieces = [pieces[0]] + [
                lax.ppermute(pieces[k], "wide", [(i, i ^ k) for i in range(n_wide)]) for k in range(1, n_wide)
            ]
        else:
            pieces = [lax.all_to_all(eigvec_t, "wide", split_axis=1, concat_axis=0, tiled=True)]
        parts.append((first, pieces))
        first += size

    for _ in range(turns):
        for part in range(SPLITS):
            turn_of(part)
    ups = list(zip(*[stream[0] for stream in streams]))
    downs = list(zip(*[stream[1] for stream in streams]))
    high, low, gram = assemble(here, block_place, offsets, householder, ups, downs, n_row)
    merged = merge([array for _, array in partial_sums(gram, n_wide, False)], wy_factor)

    out = None
    for first, pieces in parts:
        sums = partial_sums(inner_products(pieces, (high, low)), n_wide, by_piece)
        out = update(here, pieces, sums, merged, (high, low), out, first, total, tile)
    return out.reshape(n_wide * rows, ncols)


def solution(mesh):
    return jax.shard_map(
        functools.partial(body, mesh.shape["row"], mesh.shape["wide"]),
        mesh=mesh,
        in_specs=(P(("row", "wide"), None), P("row", None, "wide"), P(), P(), P()),
        out_specs=P("row", "wide"),
        check_vma=False,
    )
```

```python
import functools

import jax
import jax.numpy as jnp
from jax import lax
from jax.experimental import pallas as pl
from jax.experimental.pallas import tpu as pltpu
from jax.sharding import PartitionSpec as P

HIGHEST = lax.Precision.HIGHEST
VMEM_LIMIT = 32 * 1024 * 1024
GROUPS = (4, 3, 1)
SPLITS = 2


def dot_t(a, b):
    return lax.dot_general(a, b, (((1,), (1,)), ((), ())), precision=HIGHEST, preferred_element_type=jnp.float32)


def dot(a, b):
    return lax.dot_general(a, b, (((1,), (0,)), ((), ())), precision=HIGHEST, preferred_element_type=jnp.float32)


def halves(x):
    high = x.astype(jnp.bfloat16)
    return high, (x - high.astype(jnp.float32)).astype(jnp.bfloat16)


def dot3(a, b, dims):
    def one(x, y):
        return lax.dot_general(x, y, (dims, ((), ())), preferred_element_type=jnp.float32)
    return one(a[0], b[0]) + (one(a[0], b[1]) + one(a[1], b[0]))


def params(dims=0):
    semantics = ("arbitrary",) * dims if dims else None
    return pltpu.CompilerParams(dimension_semantics=semantics, vmem_limit_bytes=VMEM_LIMIT)


def cost(flops, nbytes):
    return pl.CostEstimate(flops=flops, bytes_accessed=nbytes, transcendentals=0)


SMEM = pl.BlockSpec(memory_space=pltpu.SMEM)
ANY = pl.BlockSpec(memory_space=pl.ANY)
VMEM = pl.BlockSpec(memory_space=pltpu.VMEM)


def pack(x, first, rows, n_wide):
    ncols = x.shape[1] // n_wide

    def kernel(x_ref, out_ref, sems):
        copies = []
        for k in range(n_wide):
            source = x_ref.at[pl.ds(first, rows), pl.ds(k * ncols, ncols)]
            copies.append(pltpu.make_async_copy(source, out_ref.at[k], sems.at[k]))
        for copy in copies:
            copy.start()
        for copy in copies:
            copy.wait()

    return pl.pallas_call(
        kernel,
        out_shape=jax.ShapeDtypeStruct((n_wide, rows, ncols), jnp.float32),
        in_specs=[ANY],
        out_specs=VMEM,
        scratch_shapes=[pltpu.SemaphoreType.DMA((n_wide,))],
        compiler_params=params(),
        cost_estimate=cost(0, 8 * rows * x.shape[1]),
        name="pack",
    )(x)


def plan(place_ref, slots, n_rows):
    places = [place_ref[s] for s in range(place_ref.shape[0])]
    roots = [lax.div(p, slots) for p in places]
    slot = [lax.rem(p, slots) for p in places]
    ranks = [sum([(roots[i] == roots[s]).astype(jnp.int32) for i in range(s)], jnp.int32(0)) for s in range(len(places))]
    counts = [sum([(r == i).astype(jnp.int32) for r in roots], jnp.int32(0)) for i in range(n_rows)]
    return roots, slot, ranks, counts


def feed(here, place, stack, ups, downs, n_rows, part, cols):
    slots, width, _ = stack.shape
    turn = len(ups)

    def kernel(here_ref, place_ref, stack_ref, *refs):
        arrived, (out_up, out_down, sems) = refs[:-3], refs[-3:]
        roots, slot, ranks, _ = plan(place_ref, slots, n_rows)
        me = here_ref[0]
        mine = [r == me for r in roots]
        count = sum([m.astype(jnp.int32) for m in mine], jnp.int32(0))
        own = sum([jnp.where(m & (k == turn), s, 0) for m, k, s in zip(mine, ranks, slot)], jnp.int32(0))
        older = turn - jnp.maximum(count, 1)
        stored = stack_ref.at[own, :, pl.ds(part * cols, cols)]
        for side, out in ((0, out_up), (1, out_down)):
            @pl.when((older < 0) | (count > turn))
            def _():
                pltpu.make_async_copy(stored, out, sems.at[side]).start()

            for i in range(turn):
                @pl.when((older == i) & (count <= turn))
                def _():
                    pltpu.make_async_copy(arrived[side * turn + i], out, sems.at[side]).start()
        for side, out in ((0, out_up), (1, out_down)):
            pltpu.make_async_copy(stored, out, sems.at[side]).wait()

    return pl.pallas_call(
        kernel,
        out_shape=[jax.ShapeDtypeStruct((width, cols), jnp.float32)] * 2,
        in_specs=[SMEM, SMEM, ANY] + [ANY] * (2 * turn),
        out_specs=[VMEM] * 2,
        scratch_shapes=[pltpu.SemaphoreType.DMA((2,))],
        compiler_params=params(),
        cost_estimate=cost(0, 16 * width * cols),
        name="feed",
    )(here, place, stack, *ups, *downs)


def assemble(here, place, offsets, stack, ups, downs, n_rows):
    slots, width, ncols = stack.shape
    steps = place.shape[0]
    height = steps * width
    turns, splits = len(ups), len(ups[0])
    cols = ncols // splits

    def kernel(here_ref, place_ref, offset_ref, stack_ref, *refs):
        arrived, (high_ref, low_ref, gram_ref, held, sems) = refs[:-5], refs[-5:]
        up, down = arrived[:turns * splits], arrived[turns * splits:]
        roots, slot, ranks, counts = plan(place_ref, slots, n_rows)
        me = here_ref[0]
        for s in range(steps):
            root = roots[s]
            low, high = jnp.minimum(root, me), jnp.maximum(root, me)
            between = [jnp.where((i > low) & (i < high), jnp.maximum(counts[i], 1), 0) for i in range(n_rows)]
            turn = sum(between, ranks[s])
            target = held.at[pl.ds(s * width, width)]

            @pl.when(root == me)
            def _():
                pltpu.make_async_copy(stack_ref.at[slot[s]], target, sems.at[s]).start()

            for side, came in ((root < me, up), (root > me, down)):
                for i in range(turns):
                    @pl.when(side & (turn == i))
                    def _():
                        for p in range(splits):
                            piece = held.at[pl.ds(s * width, width), pl.ds(p * cols, cols)]
                            pltpu.make_async_copy(came[i * splits + p], piece, sems.at[s]).start()
        columns = here_ref[1] * ncols + lax.broadcasted_iota(jnp.int32, (width, ncols), 1)
        for s in range(steps):
            rows = pl.ds(s * width, width)
            pltpu.make_async_copy(stack_ref.at[0], held.at[rows], sems.at[s]).wait()
            masked = jnp.where(columns >= offset_ref[s], held[rows, :], 0.0)
            held[rows, :] = masked
            high, low = halves(masked)
            high_ref[rows, :] = high
            low_ref[rows, :] = low
        gram_ref[...] = dot_t(held[...], held[...])

    return pl.pallas_call(
        kernel,
        out_shape=[
            jax.ShapeDtypeStruct((height, ncols), jnp.bfloat16),
            jax.ShapeDtypeStruct((height, ncols), jnp.bfloat16),
            jax.ShapeDtypeStruct((height, height), jnp.float32),
        ],
        in_specs=[SMEM, SMEM, SMEM, ANY] + [ANY] * (2 * turns * splits),
        out_specs=[VMEM] * 3,
        scratch_shapes=[pltpu.VMEM((height, ncols), jnp.float32), pltpu.SemaphoreType.DMA((steps,))],
        compiler_params=params(),
        cost_estimate=cost(12 * height * height * ncols, 8 * height * ncols),
        name="assemble",
    )(here, place, offsets, stack, *[p for turn in ups for p in turn], *[p for turn in downs for p in turn])


def merge(cross, factors):
    steps, width, _ = factors.shape
    height = steps * width

    def kernel(*refs):
        cross_refs, (factor_ref, out_ref, total) = refs[:-3], refs[-3:]
        total[...] = sum([ref[...] for ref in cross_refs[1:]], cross_refs[0][...])
        out_ref[...] = jnp.zeros_like(out_ref)
        for k in range(steps):
            rows = pl.ds(k * width, width)
            own = lax.broadcasted_iota(jnp.int32, (width, height), 0) + k * width
            unit = (own == lax.broadcasted_iota(jnp.int32, (width, height), 1)).astype(jnp.float32)
            rest = unit - dot(total[rows, :], out_ref[...]) if k else unit
            out_ref[rows, :] = dot(factor_ref[k], rest)

    return pl.pallas_call(
        kernel,
        out_shape=jax.ShapeDtypeStruct((height, height), jnp.float32),
        scratch_shapes=[pltpu.VMEM((height, height), jnp.float32)],
        compiler_params=params(),
        cost_estimate=cost(12 * height * height * height, 8 * height * height),
        name="merge",
    )(*cross, factors)


def column_block(ncols):
    return 1024 if ncols % 1024 == 0 else ncols


def inner_products(x, vecs):
    lead, rows, ncols = x.shape
    height = vecs[0].shape[0]
    cols = column_block(ncols)

    def kernel(x_ref, high_ref, low_ref, out_ref):
        block = x_ref[...].reshape(lead * rows, cols)
        part = dot3(halves(block), (high_ref[...], low_ref[...]), ((1,), (1,))).reshape(lead, rows, height)

        @pl.when(pl.program_id(0) == 0)
        def _():
            out_ref[...] = part

        @pl.when(pl.program_id(0) > 0)
        def _():
            out_ref[...] += part

    return pl.pallas_call(
        kernel,
        out_shape=jax.ShapeDtypeStruct((lead, rows, height), jnp.float32),
        grid=(ncols // cols,),
        in_specs=[pl.BlockSpec((lead, rows, cols), lambda c: (0, 0, c))] + [pl.BlockSpec((height, cols), lambda c: (0, c))] * 2,
        out_specs=pl.BlockSpec((lead, rows, height), lambda c: (0, 0, 0)),
        compiler_params=params(1),
        cost_estimate=cost(6 * lead * rows * ncols * height, 4 * lead * rows * ncols),
        name="inner_products",
    )(x, *vecs)


def update(x, sums, merged, vecs, out, first, total):
    lead, rows, ncols = x.shape
    n_sums = len(sums)
    height = vecs[0].shape[0]
    cols = column_block(ncols)

    def kernel(*refs):
        sum_refs, (x_ref, m_ref, high_ref, low_ref) = refs[:n_sums], refs[n_sums:n_sums + 4]
        out_ref, u_high, u_low = refs[-3:]

        @pl.when(pl.program_id(0) == 0)
        def _():
            w = sum([ref[...] for ref in sum_refs[1:]], sum_refs[0][...]).reshape(lead * rows, height)
            u_high[...], u_low[...] = halves(dot_t(w, m_ref[...]))

        change = dot3((u_high[...], u_low[...]), (high_ref[...], low_ref[...]), ((1,), (0,)))
        out_ref[...] = (x_ref[...].reshape(lead * rows, cols) - change).reshape(lead, rows, cols)

    operands = list(sums) + [x, merged, *vecs]
    in_specs = (
        [pl.BlockSpec((lead, rows, height), lambda c: (0, 0, 0))] * n_sums
        + [pl.BlockSpec((lead, rows, cols), lambda c: (0, 0, c))]
        + [pl.BlockSpec((height, height), lambda c: (0, 0))]
        + [pl.BlockSpec((height, cols), lambda c: (0, c))] * 2
    )
    aliases = {}
    if out is not None:
        aliases = {len(operands): 0}
        operands.append(out)
        in_specs.append(ANY)
    return pl.pallas_call(
        kernel,
        out_shape=jax.ShapeDtypeStruct((lead, total, ncols), jnp.float32),
        grid=(ncols // cols,),
        in_specs=in_specs,
        out_specs=pl.BlockSpec((pl.Element(lead), pl.Element(rows), pl.Element(cols)), lambda c: (0, first, c * cols)),
        scratch_shapes=[pltpu.VMEM((lead * rows, height), jnp.bfloat16)] * 2,
        input_output_aliases=aliases,
        compiler_params=params(1),
        cost_estimate=cost(6 * lead * rows * ncols * height, 8 * lead * rows * ncols),
        name="update",
    )(*operands)


def partial_sums(part, size):
    def swap(array, k):
        return lax.ppermute(array, "wide", [(i, i ^ k) for i in range(size)])

    pair = part + swap(part, 1)
    return [pair] + [swap(pair, k) for k in range(2, size, 2)]


def body(n_row, n_wide, eigvec_t, householder, wy_factor, block_place, offsets):
    rows, order = eigvec_t.shape
    steps, width, _ = wy_factor.shape
    slots = householder.shape[0]
    ncols = order // n_wide
    here = jnp.stack([lax.axis_index("row"), lax.axis_index("wide")]).astype(jnp.int32)

    turns = max(z + min(steps - 1, slots * (n_row - 1 - z)) for z in range(n_row - 1))
    cols = ncols // SPLITS
    streams = [([], []) for _ in range(SPLITS)]
    upward = [(i, i + 1) for i in range(n_row - 1)]
    downward = [(i + 1, i) for i in range(n_row - 1)]

    def turn_of(part):
        ups, downs = streams[part]
        to_up, to_down = feed(here, block_place, householder, ups, downs, n_row, part, cols)
        streams[part] = (ups + [lax.ppermute(to_up, "row", upward)], downs + [lax.ppermute(to_down, "row", downward)])

    whole = rows % 8 == 0
    groups = [8 * size for size in GROUPS] if 8 * sum(GROUPS) == rows else [rows]
    parts = []
    first = 0
    for size in groups:
        if whole:
            x = lax.all_to_all(pack(eigvec_t, first, size, n_wide), "wide", split_axis=0, concat_axis=0, tiled=True)
        else:
            x = lax.all_to_all(eigvec_t, "wide", split_axis=1, concat_axis=0, tiled=True)[None]
        parts.append((first, x))
        first += size

    for _ in range(turns):
        for part in range(SPLITS):
            turn_of(part)
    ups = list(zip(*[stream[0] for stream in streams]))
    downs = list(zip(*[stream[1] for stream in streams]))
    high, low, gram = assemble(here, block_place, offsets, householder, ups, downs, n_row)
    merged = merge(partial_sums(gram, n_wide), wy_factor)

    out = None
    total = rows if whole else rows * n_wide
    for first, x in parts:
        sums = partial_sums(inner_products(x, (high, low)), n_wide)
        out = update(x, sums, merged, (high, low), out, first, total)
    return out.reshape(n_wide * rows, ncols)


def solution(mesh):
    return jax.shard_map(
        functools.partial(body, mesh.shape["row"], mesh.shape["wide"]),
        mesh=mesh,
        in_specs=(P(("row", "wide"), None), P("row", None, "wide"), P(), P(), P()),
        out_specs=P("row", "wide"),
        check_vma=False,
    )
```

```python
import functools

import jax
import jax.numpy as jnp
from jax import lax
from jax.experimental import pallas as pl
from jax.experimental.pallas import tpu as pltpu
from jax.sharding import PartitionSpec as P

HIGHEST = lax.Precision.HIGHEST
VMEM_LIMIT = 24 * 1024 * 1024
PACK_LIMIT = 56 * 1024 * 1024
GROUPS = (4, 3, 1)
SEND_AFTER = (0, 3)
SPLITS = 2


def dot_t(a, b):
    return lax.dot_general(a, b, (((1,), (1,)), ((), ())), precision=HIGHEST, preferred_element_type=jnp.float32)


def dot(a, b):
    return lax.dot_general(a, b, (((1,), (0,)), ((), ())), precision=HIGHEST, preferred_element_type=jnp.float32)


def halves(x):
    high = x.astype(jnp.bfloat16)
    return high, (x - high.astype(jnp.float32)).astype(jnp.bfloat16)


def dot3(a, b, dims):
    rows = a[0].shape[0]
    both = lax.dot_general(jnp.concatenate(a, axis=0), b[0], (dims, ((), ())), preferred_element_type=jnp.float32)
    last = lax.dot_general(a[0], b[1], (dims, ((), ())), preferred_element_type=jnp.float32)
    return both[:rows] + (both[rows:] + last)


def after(x, *tokens):
    return lax.optimization_barrier((x, *tokens))[0]


def params(dims=0, limit=VMEM_LIMIT):
    semantics = ("arbitrary",) * dims if dims else None
    return pltpu.CompilerParams(dimension_semantics=semantics, vmem_limit_bytes=limit)


def cost(flops, nbytes):
    return pl.CostEstimate(flops=flops, bytes_accessed=nbytes, transcendentals=0)


SMEM = pl.BlockSpec(memory_space=pltpu.SMEM)
ANY = pl.BlockSpec(memory_space=pl.ANY)
VMEM = pl.BlockSpec(memory_space=pltpu.VMEM)


def pack(x, first, rows, n_wide):
    ncols = x.shape[1] // n_wide

    def kernel(x_ref, out_ref, sems):
        copies = []
        for k in range(n_wide):
            source = x_ref.at[pl.ds(first, rows), pl.ds(k * ncols, ncols)]
            copies.append(pltpu.make_async_copy(source, out_ref.at[k], sems.at[k]))
        for copy in copies:
            copy.start()
        for copy in copies:
            copy.wait()

    return pl.pallas_call(
        kernel,
        out_shape=jax.ShapeDtypeStruct((n_wide, rows, ncols), jnp.float32),
        in_specs=[ANY],
        out_specs=VMEM,
        scratch_shapes=[pltpu.SemaphoreType.DMA((n_wide,))],
        compiler_params=params(limit=PACK_LIMIT),
        cost_estimate=cost(0, 8 * rows * x.shape[1]),
        name="pack",
    )(x)


def plan(place_ref, slots, n_rows):
    places = [place_ref[s] for s in range(place_ref.shape[0])]
    roots = [lax.div(p, slots) for p in places]
    slot = [lax.rem(p, slots) for p in places]
    ranks = [sum([(roots[i] == roots[s]).astype(jnp.int32) for i in range(s)], jnp.int32(0)) for s in range(len(places))]
    counts = [sum([(r == i).astype(jnp.int32) for r in roots], jnp.int32(0)) for i in range(n_rows)]
    return roots, slot, ranks, counts


def feed(here, place, stack, evens, odds, n_rows, part, cols):
    slots, width, _ = stack.shape
    turn = len(evens)

    def kernel(here_ref, place_ref, stack_ref, *refs):
        arrived, (out_even, out_odd, sems) = refs[:-3], refs[-3:]
        roots, slot, ranks, _ = plan(place_ref, slots, n_rows)
        me = here_ref[0]
        mine = [r == me for r in roots]
        count = sum([m.astype(jnp.int32) for m in mine], jnp.int32(0))
        own = sum([jnp.where(m & (k == turn), s, 0) for m, k, s in zip(mine, ranks, slot)], jnp.int32(0))
        older = turn - jnp.maximum(count, 1)
        stored = stack_ref.at[own, :, pl.ds(part * cols, cols)]
        for side, out in ((0, out_even), (1, out_odd)):
            @pl.when((older < 0) | (count > turn))
            def _():
                pltpu.make_async_copy(stored, out, sems.at[side]).start()

            for i in range(turn):
                @pl.when((older == i) & (count <= turn))
                def _():
                    pltpu.make_async_copy(arrived[(1 - side) * turn + i], out, sems.at[side]).start()
        for side, out in ((0, out_even), (1, out_odd)):
            pltpu.make_async_copy(stored, out, sems.at[side]).wait()

    return pl.pallas_call(
        kernel,
        out_shape=[jax.ShapeDtypeStruct((width, cols), jnp.float32)] * 2,
        in_specs=[SMEM, SMEM, ANY] + [ANY] * (2 * turn),
        out_specs=[VMEM] * 2,
        scratch_shapes=[pltpu.SemaphoreType.DMA((2,))],
        compiler_params=params(),
        cost_estimate=cost(0, 16 * width * cols),
        name="feed",
    )(here, place, stack, *evens, *odds)


def packed_width(steps, width):
    return -(-(width * steps * (steps - 1) // 2) // 128) * 128


def assemble(here, place, offsets, stack, evens, odds, n_rows):
    slots, width, ncols = stack.shape
    steps = place.shape[0]
    height = steps * width
    turns, splits = len(evens), len(evens[0])
    cols = ncols // splits

    def kernel(here_ref, place_ref, offset_ref, stack_ref, *refs):
        arrived, (high_ref, low_ref, gram_ref, held, sems) = refs[:-5], refs[-5:]
        even, odd = arrived[:turns * splits], arrived[turns * splits:]
        roots, slot, ranks, counts = plan(place_ref, slots, n_rows)
        me = here_ref[0]
        me_odd = lax.rem(me, 2) == 1
        for s in range(steps):
            root = roots[s]
            low, high = jnp.minimum(root, me), jnp.maximum(root, me)
            between = [jnp.where((i > low) & (i < high), jnp.maximum(counts[i], 1), 0) for i in range(n_rows)]
            turn = sum(between, ranks[s])
            target = held.at[pl.ds(s * width, width)]
            below, above = root < me, root > me

            @pl.when(root == me)
            def _():
                pltpu.make_async_copy(stack_ref.at[slot[s]], target, sems.at[s]).start()

            for side, came in (((below & me_odd) | (above & ~me_odd), even), ((below & ~me_odd) | (above & me_odd), odd)):
                for i in range(turns):
                    @pl.when(side & (turn == i))
                    def _():
                        for p in range(splits):
                            piece = held.at[pl.ds(s * width, width), pl.ds(p * cols, cols)]
                            pltpu.make_async_copy(came[i * splits + p], piece, sems.at[s]).start()
        columns = here_ref[1] * ncols + lax.broadcasted_iota(jnp.int32, (width, ncols), 1)
        for s in range(steps):
            rows = pl.ds(s * width, width)
            pltpu.make_async_copy(stack_ref.at[0], held.at[rows], sems.at[s]).wait()
            masked = jnp.where(columns >= offset_ref[s], held[rows, :], 0.0)
            held[rows, :] = masked
            high, low = halves(masked)
            high_ref[rows, :] = high
            low_ref[rows, :] = low
        gram = dot_t(held[...], held[...])
        gram_ref[...] = jnp.zeros_like(gram_ref)
        first = 0
        for s in range(1, steps):
            gram_ref[:, first:first + s * width] = gram[s * width:(s + 1) * width, :s * width]
            first += s * width

    return pl.pallas_call(
        kernel,
        out_shape=[
            jax.ShapeDtypeStruct((height, ncols), jnp.bfloat16),
            jax.ShapeDtypeStruct((height, ncols), jnp.bfloat16),
            jax.ShapeDtypeStruct((width, packed_width(steps, width)), jnp.float32),
        ],
        in_specs=[SMEM, SMEM, SMEM, ANY] + [ANY] * (2 * turns * splits),
        out_specs=[VMEM] * 3,
        scratch_shapes=[pltpu.VMEM((height, ncols), jnp.float32), pltpu.SemaphoreType.DMA((steps,))],
        compiler_params=params(),
        cost_estimate=cost(12 * height * height * ncols, 8 * height * ncols),
        name="assemble",
    )(here, place, offsets, stack, *[p for turn in evens for p in turn], *[p for turn in odds for p in turn])


def merge(cross, factors, vecs):
    steps, width, _ = factors.shape
    height, ncols = vecs[0].shape

    def kernel(*refs):
        cross_refs, (factor_ref, v_high, v_low, p_high, p_low, total, m_ref) = refs[:-7], refs[-7:]
        total[...] = sum([ref[...] for ref in cross_refs[1:]], cross_refs[0][...])
        first = 0
        for k in range(steps):
            own = lax.broadcasted_iota(jnp.int32, (width, height), 0) + k * width
            rest = (own == lax.broadcasted_iota(jnp.int32, (width, height), 1)).astype(jnp.float32)
            if k:
                rest = rest - dot(total[:, first:first + k * width], m_ref[:k * width, :])
                first += k * width
            m_ref[k * width:(k + 1) * width, :] = dot(factor_ref[k], rest)
        product = dot3(halves(m_ref[...].T), (v_high[...], v_low[...]), ((1,), (0,)))
        p_high[...], p_low[...] = halves(product)

    return pl.pallas_call(
        kernel,
        out_shape=[jax.ShapeDtypeStruct((height, ncols), jnp.bfloat16)] * 2,
        out_specs=[VMEM] * 2,
        in_specs=[VMEM] * (len(cross) + 3),
        scratch_shapes=[pltpu.VMEM(cross[0].shape, jnp.float32), pltpu.VMEM((height, height), jnp.float32)],
        compiler_params=params(),
        cost_estimate=cost(6 * height * height * ncols, 8 * height * ncols),
        name="merge",
    )(*cross, factors, *vecs)


def column_block(rows, ncols):
    return 1024 if rows > 128 and ncols % 1024 == 0 else ncols


def fold(w):
    half = w.shape[0] // 2
    return jnp.concatenate([w[:half], w[half:]], axis=1)


def unfold(w):
    height = w.shape[1] // 2
    return jnp.concatenate([w[:, :height], w[:, height:]], axis=0)


def inner_products(here, x, vecs, split):
    lead, rows, ncols = x.shape
    height = vecs[0].shape[0]
    cols = column_block(lead * rows, ncols)
    blocks = ncols // cols
    parts = 2 if split else 1
    half = lead * rows // parts

    def kernel(here_ref, x_ref, high_ref, low_ref, *refs):
        outs, total = refs[:-1], refs[-1]
        block = pl.program_id(0)
        here_cols = pl.ds(pl.multiple_of(block * cols, cols), cols) if blocks > 1 else slice(None)
        part = dot3(
            halves(x_ref[...].reshape(lead * rows, cols)), (high_ref[:, here_cols], low_ref[:, here_cols]), ((1,), (1,))
        )

        @pl.when(block == 0)
        def _():
            total[...] = part

        @pl.when(block > 0)
        def _():
            total[...] += part

        @pl.when(block == blocks - 1)
        def _():
            core = lax.rem(here_ref[1], 2)
            for i, out in enumerate(outs):
                start = pl.multiple_of((core ^ i) * half, 8) if split else 0
                out[...] = fold(total[pl.ds(start, half), :])

    return pl.pallas_call(
        kernel,
        out_shape=[jax.ShapeDtypeStruct((half // 2, 2 * height), jnp.float32)] * parts,
        grid=(blocks,),
        in_specs=[SMEM, pl.BlockSpec((lead, rows, cols), lambda c: (0, 0, c)), VMEM, VMEM],
        out_specs=[pl.BlockSpec((half // 2, 2 * height), lambda c: (0, 0))] * parts,
        scratch_shapes=[pltpu.VMEM((lead * rows, height), jnp.float32)],
        compiler_params=params(1),
        cost_estimate=cost(6 * lead * rows * ncols * height, 4 * lead * rows * ncols),
        name="inner_products",
    )(here, x, *vecs)


def update(here, x, sums, other, changes, out, first, total):
    lead, rows, ncols = x.shape
    n_sums = len(sums)
    height = changes[0].shape[0]
    cols = column_block(lead * rows, ncols)
    blocks = ncols // cols
    half = lead * rows // 2

    def kernel(here_ref, *refs):
        sum_refs, (x_ref, high_ref, low_ref) = refs[:n_sums], refs[n_sums:n_sums + 3]
        out_ref, w_high, w_low = refs[-3:]
        block = pl.program_id(0)

        @pl.when(block == 0)
        def _():
            w = unfold(sum([ref[...] for ref in sum_refs[1:]], sum_refs[0][...]))
            if other is None:
                w_high[...], w_low[...] = halves(w)
            else:
                core = lax.rem(here_ref[1], 2)
                mine = pl.ds(pl.multiple_of(core * half, 16), half)
                w_high[mine, :], w_low[mine, :] = halves(w)
                theirs = pl.ds(pl.multiple_of((1 - core) * half, 16), half)
                w_high[theirs, :], w_low[theirs, :] = halves(unfold(refs[n_sums + 3][...]))

        here_cols = pl.ds(pl.multiple_of(block * cols, cols), cols) if blocks > 1 else slice(None)
        change = dot3((w_high[...], w_low[...]), (high_ref[:, here_cols], low_ref[:, here_cols]), ((1,), (0,)))
        out_ref[...] = (x_ref[...].reshape(lead * rows, cols) - change).reshape(lead, rows, cols)

    operands = [here] + list(sums) + [x, *changes]
    in_specs = [SMEM] + [VMEM] * n_sums + [pl.BlockSpec((lead, rows, cols), lambda c: (0, 0, c)), VMEM, VMEM]
    if other is not None:
        operands.append(other)
        in_specs.append(VMEM)
    aliases = {}
    if out is not None:
        aliases = {len(operands): 0}
        operands.append(out)
        in_specs.append(ANY)
    return pl.pallas_call(
        kernel,
        out_shape=jax.ShapeDtypeStruct((lead, total, ncols), jnp.float32),
        grid=(blocks,),
        in_specs=in_specs,
        out_specs=pl.BlockSpec((pl.Element(lead), pl.Element(rows), pl.Element(cols)), lambda c: (0, first, c * cols)),
        scratch_shapes=[pltpu.VMEM((lead * rows, height), jnp.bfloat16)] * 2,
        input_output_aliases=aliases,
        compiler_params=params(1),
        cost_estimate=cost(6 * lead * rows * ncols * height, 8 * lead * rows * ncols),
        name="update",
    )(*operands)


def swap(array, k, size):
    return lax.ppermute(array, "wide", [(i, i ^ k) for i in range(size)])


def spread(pair, size):
    return [pair] + [swap(pair, k, size) for k in range(2, size, 2)]


def body(n_row, n_wide, eigvec_t, householder, wy_factor, block_place, offsets):
    rows, order = eigvec_t.shape
    steps, width, _ = wy_factor.shape
    slots = householder.shape[0]
    ncols = order // n_wide
    here = jnp.stack([lax.axis_index("row"), lax.axis_index("wide")]).astype(jnp.int32)

    turns = max(z + min(steps - 1, slots * (n_row - 1 - z)) for z in range(n_row - 1))
    cols = ncols // SPLITS
    streams = [([], []) for _ in range(SPLITS)]

    def exchange(array, odd):
        pairs = []
        for z in range(n_row):
            mate = ((z + odd) ^ 1) - odd
            for w in range(n_wide):
                target = mate * n_wide + w if 0 <= mate < n_row else z * n_wide + (w ^ 1)
                pairs.append((z * n_wide + w, target))
        return lax.ppermute(array, ("row", "wide"), pairs)

    whole = rows % 8 == 0
    groups = [8 * size for size in GROUPS] if 8 * sum(GROUPS) == rows else [rows]
    starts = [sum(groups[:i]) for i in range(len(groups))]
    parts = []

    def send(token):
        if len(parts) < len(groups):
            i = len(parts)
            if whole:
                piece = pack(after(eigvec_t, token), starts[i], groups[i], n_wide)
                x = lax.all_to_all(piece, "wide", split_axis=0, concat_axis=0, tiled=True)
            else:
                piece = after(eigvec_t, token)
                x = lax.all_to_all(piece, "wide", split_axis=1, concat_axis=0, tiled=True)[None]
            parts.append(x)
            return piece
        return token

    token = here
    for turn in range(turns):
        for part in range(SPLITS):
            evens, odds = streams[part]
            to_even, to_odd = feed(after(here, token), block_place, householder, evens, odds, n_row, part, cols)
            token = to_odd
            streams[part] = (evens + [exchange(to_even, 0)], odds + [exchange(to_odd, 1)])
        if turn in SEND_AFTER:
            token = send(token)
    evens = list(zip(*[stream[0] for stream in streams]))
    odds = list(zip(*[stream[1] for stream in streams]))
    high, low, gram = assemble(here, block_place, offsets, householder, evens, odds, n_row)
    while len(parts) < len(groups):
        send(gram)
    changes = merge(spread(gram + swap(gram, 1, n_wide), n_wide), wy_factor, (high, low))

    out = None
    total = rows if whole else rows * n_wide
    for i, x in enumerate(parts):
        if i < len(parts) - 1:
            mine, theirs = inner_products(here, x, (high, low), True)
            sums = spread(mine + swap(theirs, 1, n_wide), n_wide)
            mine = functools.reduce(jnp.add, sums)
            sums, other = [mine], swap(mine, 1, n_wide)
        else:
            mine, = inner_products(here, x, (high, low), False)
            sums, other = spread(mine + swap(mine, 1, n_wide), n_wide), None
        out = update(here, x, sums, other, changes, out, starts[i], total)
    return out.reshape(n_wide * rows, ncols)


def solution(mesh):
    return jax.shard_map(
        functools.partial(body, mesh.shape["row"], mesh.shape["wide"]),
        mesh=mesh,
        in_specs=(P(("row", "wide"), None), P("row", None, "wide"), P(), P(), P()),
        out_specs=P("row", "wide"),
        check_vma=False,
    )
```

```python
import functools

import jax
import jax.numpy as jnp
from jax import lax
from jax.experimental import pallas as pl
from jax.experimental.pallas import tpu as pltpu
from jax.sharding import PartitionSpec as P

HIGHEST = lax.Precision.HIGHEST
VMEM_LIMIT = 24 * 1024 * 1024
PACK_LIMIT = 56 * 1024 * 1024
GROUPS = (4, 3, 1)
ARRIVED = (3, 1)
SPLITS = 2


def dot_t(a, b):
    return lax.dot_general(a, b, (((1,), (1,)), ((), ())), precision=HIGHEST, preferred_element_type=jnp.float32)


def dot(a, b):
    return lax.dot_general(a, b, (((1,), (0,)), ((), ())), precision=HIGHEST, preferred_element_type=jnp.float32)


def halves(x):
    high = x.astype(jnp.bfloat16)
    return high, (x - high.astype(jnp.float32)).astype(jnp.bfloat16)


def dot3(a, b, dims):
    rows = a[0].shape[0]
    both = lax.dot_general(jnp.concatenate(a, axis=0), b[0], (dims, ((), ())), preferred_element_type=jnp.float32)
    last = lax.dot_general(a[0], b[1], (dims, ((), ())), preferred_element_type=jnp.float32)
    return both[:rows] + (both[rows:] + last)


def after(x, *tokens):
    return lax.optimization_barrier((x, *tokens))[0]


def params(dims=0, limit=VMEM_LIMIT):
    semantics = ("arbitrary",) * dims if dims else None
    return pltpu.CompilerParams(dimension_semantics=semantics, vmem_limit_bytes=limit)


def cost(flops, nbytes):
    return pl.CostEstimate(flops=flops, bytes_accessed=nbytes, transcendentals=0)


SMEM = pl.BlockSpec(memory_space=pltpu.SMEM)
ANY = pl.BlockSpec(memory_space=pl.ANY)
VMEM = pl.BlockSpec(memory_space=pltpu.VMEM)


def pack(x, first, rows, n_wide):
    ncols = x.shape[1] // n_wide

    def kernel(x_ref, out_ref, sems):
        copies = []
        for k in range(n_wide):
            source = x_ref.at[pl.ds(first, rows), pl.ds(k * ncols, ncols)]
            copies.append(pltpu.make_async_copy(source, out_ref.at[k], sems.at[k]))
        for copy in copies:
            copy.start()
        for copy in copies:
            copy.wait()

    return pl.pallas_call(
        kernel,
        out_shape=jax.ShapeDtypeStruct((n_wide, rows, ncols), jnp.float32),
        in_specs=[ANY],
        out_specs=VMEM,
        scratch_shapes=[pltpu.SemaphoreType.DMA((n_wide,))],
        compiler_params=params(limit=PACK_LIMIT),
        cost_estimate=cost(0, 8 * rows * x.shape[1]),
        name="pack",
    )(x)


def plan(place_ref, slots, n_rows):
    places = [place_ref[s] for s in range(place_ref.shape[0])]
    roots = [lax.div(p, slots) for p in places]
    slot = [lax.rem(p, slots) for p in places]
    ranks = [sum([(roots[i] == roots[s]).astype(jnp.int32) for i in range(s)], jnp.int32(0)) for s in range(len(places))]
    counts = [sum([(r == i).astype(jnp.int32) for r in roots], jnp.int32(0)) for i in range(n_rows)]
    return roots, slot, ranks, counts


def feed(here, place, stack, evens, odds, n_rows, part, cols):
    slots, width, _ = stack.shape
    turn = len(evens)

    def kernel(here_ref, place_ref, stack_ref, *refs):
        arrived, (out_even, out_odd, sems) = refs[:-3], refs[-3:]
        roots, slot, ranks, _ = plan(place_ref, slots, n_rows)
        me = here_ref[0]
        mine = [r == me for r in roots]
        count = sum([m.astype(jnp.int32) for m in mine], jnp.int32(0))
        own = sum([jnp.where(m & (k == turn), s, 0) for m, k, s in zip(mine, ranks, slot)], jnp.int32(0))
        older = turn - jnp.maximum(count, 1)
        stored = stack_ref.at[own, :, pl.ds(part * cols, cols)]
        for side, out in ((0, out_even), (1, out_odd)):
            @pl.when((older < 0) | (count > turn))
            def _():
                pltpu.make_async_copy(stored, out, sems.at[side]).start()

            for i in range(turn):
                @pl.when((older == i) & (count <= turn))
                def _():
                    pltpu.make_async_copy(arrived[(1 - side) * turn + i], out, sems.at[side]).start()
        for side, out in ((0, out_even), (1, out_odd)):
            pltpu.make_async_copy(stored, out, sems.at[side]).wait()

    return pl.pallas_call(
        kernel,
        out_shape=[jax.ShapeDtypeStruct((width, cols), jnp.float32)] * 2,
        in_specs=[SMEM, SMEM, ANY] + [ANY] * (2 * turn),
        out_specs=[VMEM] * 2,
        scratch_shapes=[pltpu.SemaphoreType.DMA((2,))],
        compiler_params=params(),
        cost_estimate=cost(0, 16 * width * cols),
        name="feed",
    )(here, place, stack, *evens, *odds)


def packed_width(steps, width):
    return -(-(width * steps * (steps - 1) // 2) // 128) * 128


def assemble(here, place, offsets, stack, evens, odds, n_rows):
    slots, width, ncols = stack.shape
    steps = place.shape[0]
    height = steps * width
    turns, splits = len(evens), len(evens[0])
    cols = ncols // splits

    def kernel(here_ref, place_ref, offset_ref, stack_ref, *refs):
        arrived, (high_ref, low_ref, gram_ref, held, sems) = refs[:-5], refs[-5:]
        even, odd = arrived[:turns * splits], arrived[turns * splits:]
        roots, slot, ranks, counts = plan(place_ref, slots, n_rows)
        me = here_ref[0]
        me_odd = lax.rem(me, 2) == 1
        for s in range(steps):
            root = roots[s]
            low, high = jnp.minimum(root, me), jnp.maximum(root, me)
            between = [jnp.where((i > low) & (i < high), jnp.maximum(counts[i], 1), 0) for i in range(n_rows)]
            turn = sum(between, ranks[s])
            target = held.at[pl.ds(s * width, width)]
            below, above = root < me, root > me

            @pl.when(root == me)
            def _():
                pltpu.make_async_copy(stack_ref.at[slot[s]], target, sems.at[s]).start()

            for side, came in (((below & me_odd) | (above & ~me_odd), even), ((below & ~me_odd) | (above & me_odd), odd)):
                for i in range(turns):
                    @pl.when(side & (turn == i))
                    def _():
                        for p in range(splits):
                            piece = held.at[pl.ds(s * width, width), pl.ds(p * cols, cols)]
                            pltpu.make_async_copy(came[i * splits + p], piece, sems.at[s]).start()
        columns = here_ref[1] * ncols + lax.broadcasted_iota(jnp.int32, (width, ncols), 1)
        for s in range(steps):
            rows = pl.ds(s * width, width)
            pltpu.make_async_copy(stack_ref.at[0], held.at[rows], sems.at[s]).wait()
            masked = jnp.where(columns >= offset_ref[s], held[rows, :], 0.0)
            held[rows, :] = masked
            high, low = halves(masked)
            high_ref[rows, :] = high
            low_ref[rows, :] = low
        gram = dot_t(held[...], held[...])
        gram_ref[...] = jnp.zeros_like(gram_ref)
        first = 0
        for s in range(1, steps):
            gram_ref[:, first:first + s * width] = gram[s * width:(s + 1) * width, :s * width]
            first += s * width

    return pl.pallas_call(
        kernel,
        out_shape=[
            jax.ShapeDtypeStruct((height, ncols), jnp.bfloat16),
            jax.ShapeDtypeStruct((height, ncols), jnp.bfloat16),
            jax.ShapeDtypeStruct((width, packed_width(steps, width)), jnp.float32),
        ],
        in_specs=[SMEM, SMEM, SMEM, ANY] + [ANY] * (2 * turns * splits),
        out_specs=[VMEM] * 3,
        scratch_shapes=[pltpu.VMEM((height, ncols), jnp.float32), pltpu.SemaphoreType.DMA((steps,))],
        compiler_params=params(),
        cost_estimate=cost(12 * height * height * ncols, 8 * height * ncols),
        name="assemble",
    )(here, place, offsets, stack, *[p for turn in evens for p in turn], *[p for turn in odds for p in turn])


def merge(cross, factors, vecs):
    steps, width, _ = factors.shape
    height, ncols = vecs[0].shape

    def kernel(*refs):
        cross_refs, (factor_ref, v_high, v_low, p_high, p_low, total, m_ref) = refs[:-7], refs[-7:]
        total[...] = sum([ref[...] for ref in cross_refs[1:]], cross_refs[0][...])
        first = 0
        for k in range(steps):
            own = lax.broadcasted_iota(jnp.int32, (width, height), 0) + k * width
            rest = (own == lax.broadcasted_iota(jnp.int32, (width, height), 1)).astype(jnp.float32)
            if k:
                rest = rest - dot(total[:, first:first + k * width], m_ref[:k * width, :])
                first += k * width
            m_ref[k * width:(k + 1) * width, :] = dot(factor_ref[k], rest)
        product = dot3(halves(m_ref[...].T), (v_high[...], v_low[...]), ((1,), (0,)))
        p_high[...], p_low[...] = halves(product)

    return pl.pallas_call(
        kernel,
        out_shape=[jax.ShapeDtypeStruct((height, ncols), jnp.bfloat16)] * 2,
        out_specs=[VMEM] * 2,
        in_specs=[VMEM] * (len(cross) + 3),
        scratch_shapes=[pltpu.VMEM(cross[0].shape, jnp.float32), pltpu.VMEM((height, height), jnp.float32)],
        compiler_params=params(),
        cost_estimate=cost(6 * height * height * ncols, 8 * height * ncols),
        name="merge",
    )(*cross, factors, *vecs)


def column_block(rows, ncols):
    return 1024 if rows > 128 and ncols % 1024 == 0 else ncols


def fold(w):
    half = w.shape[0] // 2
    return jnp.concatenate([w[:half], w[half:]], axis=1)


def unfold(w):
    height = w.shape[1] // 2
    return jnp.concatenate([w[:, :height], w[:, height:]], axis=0)


def inner_products(here, x, vecs, split):
    lead, rows, ncols = x.shape
    height = vecs[0].shape[0]
    cols = column_block(lead * rows, ncols)
    blocks = ncols // cols
    parts = 2 if split else 1
    half = lead * rows // parts

    def kernel(here_ref, x_ref, high_ref, low_ref, *refs):
        outs, total = refs[:-1], refs[-1]
        block = pl.program_id(0)
        here_cols = pl.ds(pl.multiple_of(block * cols, cols), cols) if blocks > 1 else slice(None)
        part = dot3(
            halves(x_ref[...].reshape(lead * rows, cols)), (high_ref[:, here_cols], low_ref[:, here_cols]), ((1,), (1,))
        )

        @pl.when(block == 0)
        def _():
            total[...] = part

        @pl.when(block > 0)
        def _():
            total[...] += part

        @pl.when(block == blocks - 1)
        def _():
            core = lax.rem(here_ref[1], 2)
            for i, out in enumerate(outs):
                start = pl.multiple_of((core ^ i) * half, 8) if split else 0
                out[...] = fold(total[pl.ds(start, half), :])

    return pl.pallas_call(
        kernel,
        out_shape=[jax.ShapeDtypeStruct((half // 2, 2 * height), jnp.float32)] * parts,
        grid=(blocks,),
        in_specs=[SMEM, pl.BlockSpec((lead, rows, cols), lambda c: (0, 0, c)), VMEM, VMEM],
        out_specs=[pl.BlockSpec((half // 2, 2 * height), lambda c: (0, 0))] * parts,
        scratch_shapes=[pltpu.VMEM((lead * rows, height), jnp.float32)],
        compiler_params=params(1),
        cost_estimate=cost(6 * lead * rows * ncols * height, 4 * lead * rows * ncols),
        name="inner_products",
    )(here, x, *vecs)


def update(here, x, sums, other, changes, out, first, total):
    lead, rows, ncols = x.shape
    n_sums = len(sums)
    height = changes[0].shape[0]
    cols = column_block(lead * rows, ncols)
    blocks = ncols // cols
    half = lead * rows // 2

    def kernel(here_ref, *refs):
        sum_refs, (x_ref, high_ref, low_ref) = refs[:n_sums], refs[n_sums:n_sums + 3]
        out_ref, w_high, w_low = refs[-3:]
        block = pl.program_id(0)

        @pl.when(block == 0)
        def _():
            w = unfold(sum([ref[...] for ref in sum_refs[1:]], sum_refs[0][...]))
            if other is None:
                w_high[...], w_low[...] = halves(w)
            else:
                core = lax.rem(here_ref[1], 2)
                mine = pl.ds(pl.multiple_of(core * half, 16), half)
                w_high[mine, :], w_low[mine, :] = halves(w)
                theirs = pl.ds(pl.multiple_of((1 - core) * half, 16), half)
                w_high[theirs, :], w_low[theirs, :] = halves(unfold(refs[n_sums + 3][...]))

        here_cols = pl.ds(pl.multiple_of(block * cols, cols), cols) if blocks > 1 else slice(None)
        change = dot3((w_high[...], w_low[...]), (high_ref[:, here_cols], low_ref[:, here_cols]), ((1,), (0,)))
        out_ref[...] = (x_ref[...].reshape(lead * rows, cols) - change).reshape(lead, rows, cols)

    operands = [here] + list(sums) + [x, *changes]
    in_specs = [SMEM] + [VMEM] * n_sums + [pl.BlockSpec((lead, rows, cols), lambda c: (0, 0, c)), VMEM, VMEM]
    if other is not None:
        operands.append(other)
        in_specs.append(VMEM)
    aliases = {}
    if out is not None:
        aliases = {len(operands): 0}
        operands.append(out)
        in_specs.append(ANY)
    return pl.pallas_call(
        kernel,
        out_shape=jax.ShapeDtypeStruct((lead, total, ncols), jnp.float32),
        grid=(blocks,),
        in_specs=in_specs,
        out_specs=pl.BlockSpec((pl.Element(lead), pl.Element(rows), pl.Element(cols)), lambda c: (0, first, c * cols)),
        scratch_shapes=[pltpu.VMEM((lead * rows, height), jnp.bfloat16)] * 2,
        input_output_aliases=aliases,
        compiler_params=params(1),
        cost_estimate=cost(6 * lead * rows * ncols * height, 8 * lead * rows * ncols),
        name="update",
    )(*operands)


def swap(array, k, size):
    return lax.ppermute(array, "wide", [(i, i ^ k) for i in range(size)])


def spread(pair, size):
    return [pair] + [swap(pair, k, size) for k in range(2, size, 2)]


def body(n_row, n_wide, eigvec_t, householder, wy_factor, block_place, offsets):
    rows, order = eigvec_t.shape
    steps, width, _ = wy_factor.shape
    slots = householder.shape[0]
    ncols = order // n_wide
    here = jnp.stack([lax.axis_index("row"), lax.axis_index("wide")]).astype(jnp.int32)

    turns = max(z + min(steps - 1, slots * (n_row - 1 - z)) for z in range(n_row - 1))
    cols = ncols // SPLITS
    streams = [([], []) for _ in range(SPLITS)]

    def exchange(array, odd):
        pairs = []
        for z in range(n_row):
            mate = ((z + odd) ^ 1) - odd
            for w in range(n_wide):
                target = mate * n_wide + w if 0 <= mate < n_row else z * n_wide + (w ^ 1)
                pairs.append((z * n_wide + w, target))
        return lax.ppermute(array, ("row", "wide"), pairs)

    whole = rows % 8 == 0
    groups = [8 * size for size in GROUPS] if 8 * sum(GROUPS) == rows else [rows]
    starts = [sum(groups[:i]) for i in range(len(groups))]
    parts = []

    def send(*tokens):
        i = len(parts)
        if whole:
            piece = pack(after(eigvec_t, *tokens), starts[i], groups[i], n_wide)
            parts.append(lax.all_to_all(piece, "wide", split_axis=0, concat_axis=0, tiled=True))
        else:
            piece = after(eigvec_t, *tokens)
            parts.append(lax.all_to_all(piece, "wide", split_axis=1, concat_axis=0, tiled=True)[None])
        return piece

    tokens = [send(here)]
    for turn in range(turns):
        for part in range(SPLITS):
            evens, odds = streams[part]
            to_even, to_odd = feed(after(here, *tokens), block_place, householder, evens, odds, n_row, part, cols)
            tokens = [to_odd]
            streams[part] = (evens + [exchange(to_even, 0)], odds + [exchange(to_odd, 1)])
            if (turn, part) == ARRIVED and len(groups) > 1:
                tokens += [parts[0], send(parts[0])]
    evens = list(zip(*[stream[0] for stream in streams]))
    odds = list(zip(*[stream[1] for stream in streams]))
    high, low, gram = assemble(here, block_place, offsets, householder, evens, odds, n_row)
    cross = spread(gram + swap(gram, 1, n_wide), n_wide)
    while len(parts) < len(groups):
        cross[0] = after(cross[0], parts[-1], send(parts[-1]))
    changes = merge(cross, wy_factor, (high, low))

    out = None
    total = rows if whole else rows * n_wide
    for i, x in enumerate(parts):
        if i < len(parts) - 1:
            mine, theirs = inner_products(here, x, (high, low), True)
            sums = spread(mine + swap(theirs, 1, n_wide), n_wide)
            mine = functools.reduce(jnp.add, sums)
            sums, other = [mine], swap(mine, 1, n_wide)
        else:
            mine, = inner_products(here, x, (high, low), False)
            sums, other = spread(mine + swap(mine, 1, n_wide), n_wide), None
        out = update(here, x, sums, other, changes, out, starts[i], total)
    return out.reshape(n_wide * rows, ncols)


def solution(mesh):
    return jax.shard_map(
        functools.partial(body, mesh.shape["row"], mesh.shape["wide"]),
        mesh=mesh,
        in_specs=(P(("row", "wide"), None), P("row", None, "wide"), P(), P(), P()),
        out_specs=P("row", "wide"),
        check_vma=False,
    )
```

```python
import functools

import jax
import jax.numpy as jnp
from jax import lax
from jax.experimental import pallas as pl
from jax.experimental.pallas import tpu as pltpu
from jax.sharding import PartitionSpec as P

HIGHEST = lax.Precision.HIGHEST
VMEM_LIMIT = 24 * 1024 * 1024
LARGE_LIMIT = 56 * 1024 * 1024
GROUPS = (4, 3, 1)
ARRIVED = (3, 1)
SPLITS = 2


def dot_t(a, b):
    return lax.dot_general(a, b, (((1,), (1,)), ((), ())), precision=HIGHEST, preferred_element_type=jnp.float32)


def dot(a, b):
    return lax.dot_general(a, b, (((1,), (0,)), ((), ())), precision=HIGHEST, preferred_element_type=jnp.float32)


def halves(x):
    high = x.astype(jnp.bfloat16)
    return high, (x - high.astype(jnp.float32)).astype(jnp.bfloat16)


def dot3(a, b, dims):
    rows = a[0].shape[0]
    both = lax.dot_general(jnp.concatenate(a, axis=0), b[0], (dims, ((), ())), preferred_element_type=jnp.float32)
    last = lax.dot_general(a[0], b[1], (dims, ((), ())), preferred_element_type=jnp.float32)
    return both[:rows] + (both[rows:] + last)


def after(x, *tokens):
    return lax.optimization_barrier((x, *tokens))[0]


def params(dims=0, limit=VMEM_LIMIT):
    semantics = ("arbitrary",) * dims if dims else None
    return pltpu.CompilerParams(dimension_semantics=semantics, vmem_limit_bytes=limit)


def cost(flops, nbytes):
    return pl.CostEstimate(flops=flops, bytes_accessed=nbytes, transcendentals=0)


SMEM = pl.BlockSpec(memory_space=pltpu.SMEM)
ANY = pl.BlockSpec(memory_space=pl.ANY)
VMEM = pl.BlockSpec(memory_space=pltpu.VMEM)


def pack(x, first, rows, n_wide):
    ncols = x.shape[1] // n_wide

    def kernel(x_ref, out_ref, sems):
        copies = []
        for k in range(n_wide):
            source = x_ref.at[pl.ds(first, rows), pl.ds(k * ncols, ncols)]
            copies.append(pltpu.make_async_copy(source, out_ref.at[k], sems.at[k]))
        for copy in copies:
            copy.start()
        for copy in copies:
            copy.wait()

    return pl.pallas_call(
        kernel,
        out_shape=jax.ShapeDtypeStruct((n_wide, rows, ncols), jnp.float32),
        in_specs=[ANY],
        out_specs=VMEM,
        scratch_shapes=[pltpu.SemaphoreType.DMA((n_wide,))],
        compiler_params=params(limit=LARGE_LIMIT),
        cost_estimate=cost(0, 8 * rows * x.shape[1]),
        name="pack",
    )(x)


def plan(place_ref, slots, n_rows):
    places = [place_ref[s] for s in range(place_ref.shape[0])]
    roots = [lax.div(p, slots) for p in places]
    slot = [lax.rem(p, slots) for p in places]
    ranks = [sum([(roots[i] == roots[s]).astype(jnp.int32) for i in range(s)], jnp.int32(0)) for s in range(len(places))]
    counts = [sum([(r == i).astype(jnp.int32) for r in roots], jnp.int32(0)) for i in range(n_rows)]
    return roots, slot, ranks, counts


def feed(here, place, stack, evens, odds, n_rows, part, cols):
    slots, width, _ = stack.shape
    turn = len(evens)

    def kernel(here_ref, place_ref, stack_ref, *refs):
        arrived, (out_even, out_odd, sems) = refs[:-3], refs[-3:]
        roots, slot, ranks, _ = plan(place_ref, slots, n_rows)
        me = here_ref[0]
        mine = [r == me for r in roots]
        count = sum([m.astype(jnp.int32) for m in mine], jnp.int32(0))
        own = sum([jnp.where(m & (k == turn), s, 0) for m, k, s in zip(mine, ranks, slot)], jnp.int32(0))
        older = turn - jnp.maximum(count, 1)
        stored = stack_ref.at[own, :, pl.ds(part * cols, cols)]
        for side, out in ((0, out_even), (1, out_odd)):
            @pl.when((older < 0) | (count > turn))
            def _():
                pltpu.make_async_copy(stored, out, sems.at[side]).start()

            for i in range(turn):
                @pl.when((older == i) & (count <= turn))
                def _():
                    pltpu.make_async_copy(arrived[(1 - side) * turn + i], out, sems.at[side]).start()
        for side, out in ((0, out_even), (1, out_odd)):
            pltpu.make_async_copy(stored, out, sems.at[side]).wait()

    return pl.pallas_call(
        kernel,
        out_shape=[jax.ShapeDtypeStruct((width, cols), jnp.float32)] * 2,
        in_specs=[SMEM, SMEM, ANY] + [ANY] * (2 * turn),
        out_specs=[VMEM] * 2,
        scratch_shapes=[pltpu.SemaphoreType.DMA((2,))],
        compiler_params=params(),
        cost_estimate=cost(0, 16 * width * cols),
        name="feed",
    )(here, place, stack, *evens, *odds)


def packed_width(steps, width):
    return -(-(width * steps * (steps - 1) // 2) // 128) * 128


def assemble(here, place, offsets, stack, evens, odds, n_rows):
    slots, width, ncols = stack.shape
    steps = place.shape[0]
    height = steps * width
    turns, splits = len(evens), len(evens[0])
    cols = ncols // splits

    def kernel(here_ref, place_ref, offset_ref, stack_ref, *refs):
        arrived, (high_ref, low_ref, gram_ref, held, sems) = refs[:-5], refs[-5:]
        even, odd = arrived[:turns * splits], arrived[turns * splits:]
        roots, slot, ranks, counts = plan(place_ref, slots, n_rows)
        me = here_ref[0]
        me_odd = lax.rem(me, 2) == 1
        for s in range(steps):
            root = roots[s]
            low, high = jnp.minimum(root, me), jnp.maximum(root, me)
            between = [jnp.where((i > low) & (i < high), jnp.maximum(counts[i], 1), 0) for i in range(n_rows)]
            turn = sum(between, ranks[s])
            target = held.at[pl.ds(s * width, width)]
            below, above = root < me, root > me

            @pl.when(root == me)
            def _():
                pltpu.make_async_copy(stack_ref.at[slot[s]], target, sems.at[s]).start()

            for side, came in (((below & me_odd) | (above & ~me_odd), even), ((below & ~me_odd) | (above & me_odd), odd)):
                for i in range(turns):
                    @pl.when(side & (turn == i))
                    def _():
                        for p in range(splits):
                            piece = held.at[pl.ds(s * width, width), pl.ds(p * cols, cols)]
                            pltpu.make_async_copy(came[i * splits + p], piece, sems.at[s]).start()
        columns = here_ref[1] * ncols + lax.broadcasted_iota(jnp.int32, (width, ncols), 1)
        for s in range(steps):
            rows = pl.ds(s * width, width)
            pltpu.make_async_copy(stack_ref.at[0], held.at[rows], sems.at[s]).wait()
            masked = jnp.where(columns >= offset_ref[s], held[rows, :], 0.0)
            held[rows, :] = masked
            high, low = halves(masked)
            high_ref[rows, :] = high
            low_ref[rows, :] = low
        gram = dot_t(held[...], held[...])
        gram_ref[...] = jnp.zeros_like(gram_ref)
        first = 0
        for s in range(1, steps):
            gram_ref[:, first:first + s * width] = gram[s * width:(s + 1) * width, :s * width]
            first += s * width

    return pl.pallas_call(
        kernel,
        out_shape=[
            jax.ShapeDtypeStruct((height, ncols), jnp.bfloat16),
            jax.ShapeDtypeStruct((height, ncols), jnp.bfloat16),
            jax.ShapeDtypeStruct((width, packed_width(steps, width)), jnp.float32),
        ],
        in_specs=[SMEM, SMEM, SMEM, ANY] + [ANY] * (2 * turns * splits),
        out_specs=[VMEM] * 3,
        scratch_shapes=[pltpu.VMEM((height, ncols), jnp.float32), pltpu.SemaphoreType.DMA((steps,))],
        compiler_params=params(limit=LARGE_LIMIT),
        cost_estimate=cost(12 * height * height * ncols, 8 * height * ncols),
        name="assemble",
    )(here, place, offsets, stack, *[p for turn in evens for p in turn], *[p for turn in odds for p in turn])


def merge(cross, factors, vecs):
    steps, width, _ = factors.shape
    height, ncols = vecs[0].shape

    def kernel(*refs):
        cross_refs, (factor_ref, v_high, v_low, p_high, p_low, total, m_ref) = refs[:-7], refs[-7:]
        total[...] = sum([ref[...] for ref in cross_refs[1:]], cross_refs[0][...])
        first = 0
        for k in range(steps):
            own = lax.broadcasted_iota(jnp.int32, (width, height), 0) + k * width
            rest = (own == lax.broadcasted_iota(jnp.int32, (width, height), 1)).astype(jnp.float32)
            if k:
                rest = rest - dot(total[:, first:first + k * width], m_ref[:k * width, :])
                first += k * width
            m_ref[k * width:(k + 1) * width, :] = dot(factor_ref[k], rest)
        product = dot3(halves(m_ref[...].T), (v_high[...], v_low[...]), ((1,), (0,)))
        p_high[...], p_low[...] = halves(product)

    return pl.pallas_call(
        kernel,
        out_shape=[jax.ShapeDtypeStruct((height, ncols), jnp.bfloat16)] * 2,
        out_specs=[VMEM] * 2,
        in_specs=[VMEM] * (len(cross) + 3),
        scratch_shapes=[pltpu.VMEM(cross[0].shape, jnp.float32), pltpu.VMEM((height, height), jnp.float32)],
        compiler_params=params(),
        cost_estimate=cost(6 * height * height * ncols, 8 * height * ncols),
        name="merge",
    )(*cross, factors, *vecs)


def column_block(rows, ncols):
    return 1024 if rows > 128 and ncols % 1024 == 0 else ncols


def fold(w):
    half = w.shape[0] // 2
    return jnp.concatenate([w[:half], w[half:]], axis=1)


def unfold(w):
    height = w.shape[1] // 2
    return jnp.concatenate([w[:, :height], w[:, height:]], axis=0)


def inner_products(here, x, vecs, split):
    lead, rows, ncols = x.shape
    height = vecs[0].shape[0]
    cols = column_block(lead * rows, ncols)
    blocks = ncols // cols
    parts = 2 if split else 1
    half = lead * rows // parts

    def kernel(here_ref, x_ref, high_ref, low_ref, *refs):
        outs, total = refs[:-1], refs[-1]
        block = pl.program_id(0)
        here_cols = pl.ds(pl.multiple_of(block * cols, cols), cols) if blocks > 1 else slice(None)
        part = dot3(
            halves(x_ref[...].reshape(lead * rows, cols)), (high_ref[:, here_cols], low_ref[:, here_cols]), ((1,), (1,))
        )

        @pl.when(block == 0)
        def _():
            total[...] = part

        @pl.when(block > 0)
        def _():
            total[...] += part

        @pl.when(block == blocks - 1)
        def _():
            core = lax.rem(here_ref[1], 2)
            for i, out in enumerate(outs):
                start = pl.multiple_of((core ^ i) * half, 8) if split else 0
                out[...] = fold(total[pl.ds(start, half), :])

    return pl.pallas_call(
        kernel,
        out_shape=[jax.ShapeDtypeStruct((half // 2, 2 * height), jnp.float32)] * parts,
        grid=(blocks,),
        in_specs=[SMEM, pl.BlockSpec((lead, rows, cols), lambda c: (0, 0, c)), VMEM, VMEM],
        out_specs=[pl.BlockSpec((half // 2, 2 * height), lambda c: (0, 0))] * parts,
        scratch_shapes=[pltpu.VMEM((lead * rows, height), jnp.float32)],
        compiler_params=params(1),
        cost_estimate=cost(6 * lead * rows * ncols * height, 4 * lead * rows * ncols),
        name="inner_products",
    )(here, x, *vecs)


def update(here, x, sums, other, changes, out, first, total):
    lead, rows, ncols = x.shape
    n_sums = len(sums)
    height = changes[0].shape[0]
    cols = column_block(lead * rows, ncols)
    blocks = ncols // cols
    half = lead * rows // 2

    def kernel(here_ref, *refs):
        sum_refs, (x_ref, high_ref, low_ref) = refs[:n_sums], refs[n_sums:n_sums + 3]
        out_ref, w_high, w_low = refs[-3:]
        block = pl.program_id(0)

        @pl.when(block == 0)
        def _():
            w = unfold(sum([ref[...] for ref in sum_refs[1:]], sum_refs[0][...]))
            if other is None:
                w_high[...], w_low[...] = halves(w)
            else:
                core = lax.rem(here_ref[1], 2)
                mine = pl.ds(pl.multiple_of(core * half, 16), half)
                w_high[mine, :], w_low[mine, :] = halves(w)
                theirs = pl.ds(pl.multiple_of((1 - core) * half, 16), half)
                w_high[theirs, :], w_low[theirs, :] = halves(unfold(refs[n_sums + 3][...]))

        here_cols = pl.ds(pl.multiple_of(block * cols, cols), cols) if blocks > 1 else slice(None)
        change = dot3((w_high[...], w_low[...]), (high_ref[:, here_cols], low_ref[:, here_cols]), ((1,), (0,)))
        out_ref[...] = (x_ref[...].reshape(lead * rows, cols) - change).reshape(lead, rows, cols)

    operands = [here] + list(sums) + [x, *changes]
    in_specs = [SMEM] + [VMEM] * n_sums + [pl.BlockSpec((lead, rows, cols), lambda c: (0, 0, c)), VMEM, VMEM]
    if other is not None:
        operands.append(other)
        in_specs.append(VMEM)
    aliases = {}
    if out is not None:
        aliases = {len(operands): 0}
        operands.append(out)
        in_specs.append(ANY)
    return pl.pallas_call(
        kernel,
        out_shape=jax.ShapeDtypeStruct((lead, total, ncols), jnp.float32),
        grid=(blocks,),
        in_specs=in_specs,
        out_specs=pl.BlockSpec((pl.Element(lead), pl.Element(rows), pl.Element(cols)), lambda c: (0, first, c * cols)),
        scratch_shapes=[pltpu.VMEM((lead * rows, height), jnp.bfloat16)] * 2,
        input_output_aliases=aliases,
        compiler_params=params(1),
        cost_estimate=cost(6 * lead * rows * ncols * height, 8 * lead * rows * ncols),
        name="update",
    )(*operands)


def swap(array, k, size):
    return lax.ppermute(array, "wide", [(i, i ^ k) for i in range(size)])


def spread(pair, size):
    return [pair] + [swap(pair, k, size) for k in range(2, size, 2)]


def body(n_row, n_wide, eigvec_t, householder, wy_factor, block_place, offsets):
    rows, order = eigvec_t.shape
    steps, width, _ = wy_factor.shape
    slots = householder.shape[0]
    ncols = order // n_wide
    here = jnp.stack([lax.axis_index("row"), lax.axis_index("wide")]).astype(jnp.int32)

    turns = max(z + min(steps - 1, slots * (n_row - 1 - z)) for z in range(n_row - 1))
    cols = ncols // SPLITS
    streams = [([], []) for _ in range(SPLITS)]

    def exchange(array, odd):
        pairs = []
        for z in range(n_row):
            mate = ((z + odd) ^ 1) - odd
            for w in range(n_wide):
                target = mate * n_wide + w if 0 <= mate < n_row else z * n_wide + (w ^ 1)
                pairs.append((z * n_wide + w, target))
        return lax.ppermute(array, ("row", "wide"), pairs)

    whole = rows % 8 == 0
    groups = [8 * size for size in GROUPS] if 8 * sum(GROUPS) == rows else [rows]
    starts = [sum(groups[:i]) for i in range(len(groups))]
    parts = []

    def send(*tokens):
        i = len(parts)
        if whole:
            piece = pack(after(eigvec_t, *tokens), starts[i], groups[i], n_wide)
            parts.append(lax.all_to_all(piece, "wide", split_axis=0, concat_axis=0, tiled=True))
        else:
            piece = after(eigvec_t, *tokens)
            parts.append(lax.all_to_all(piece, "wide", split_axis=1, concat_axis=0, tiled=True)[None])
        return piece

    tokens = [send(here)]
    for turn in range(turns):
        for part in range(SPLITS):
            evens, odds = streams[part]
            to_even, to_odd = feed(after(here, *tokens), block_place, householder, evens, odds, n_row, part, cols)
            tokens = [to_odd]
            streams[part] = (evens + [exchange(to_even, 0)], odds + [exchange(to_odd, 1)])
            if (turn, part) == ARRIVED and len(groups) > 1:
                tokens += [parts[0], send(parts[0], to_odd)]
    evens = list(zip(*[stream[0] for stream in streams]))
    odds = list(zip(*[stream[1] for stream in streams]))
    high, low, gram = assemble(here, block_place, offsets, householder, evens, odds, n_row)
    cross = spread(gram + swap(gram, 1, n_wide), n_wide)
    inner = [inner_products(here, parts[0], (high, low), len(groups) > 1)]
    while len(parts) < len(groups):
        piece = send(parts[-1], inner[-1][0])
        inner.append(inner_products(here, parts[len(inner)], (high, low), len(inner) < len(groups) - 1))
        cross[0] = after(cross[0], piece)
    while len(inner) < len(groups):
        inner.append(inner_products(here, parts[len(inner)], (high, low), len(inner) < len(groups) - 1))
    changes = merge(cross, wy_factor, (high, low))

    out = None
    total = rows if whole else rows * n_wide
    for i, x in enumerate(parts):
        if i < len(parts) - 1:
            mine, theirs = inner[i]
            sums = spread(mine + swap(theirs, 1, n_wide), n_wide)
            mine = functools.reduce(jnp.add, sums)
            sums, other = [mine], swap(mine, 1, n_wide)
        else:
            mine, = inner[i]
            sums, other = spread(mine + swap(mine, 1, n_wide), n_wide), None
        out = update(here, x, sums, other, changes, out, starts[i], total)
    return out.reshape(n_wide * rows, ncols)


def solution(mesh):
    return jax.shard_map(
        functools.partial(body, mesh.shape["row"], mesh.shape["wide"]),
        mesh=mesh,
        in_specs=(P(("row", "wide"), None), P("row", None, "wide"), P(), P(), P()),
        out_specs=P("row", "wide"),
        check_vma=False,
    )
```

```python
import functools

import jax
import jax.numpy as jnp
from jax import lax
from jax.experimental import pallas as pl
from jax.experimental.pallas import tpu as pltpu
from jax.sharding import PartitionSpec as P

HIGHEST = lax.Precision.HIGHEST
VMEM_LIMIT = 24 * 1024 * 1024
LARGE_LIMIT = 56 * 1024 * 1024
GROUPS = (4, 3, 1)
ARRIVED = (4, 0)
SPLITS = 2


def dot_t(a, b):
    return lax.dot_general(a, b, (((1,), (1,)), ((), ())), precision=HIGHEST, preferred_element_type=jnp.float32)


def dot(a, b):
    return lax.dot_general(a, b, (((1,), (0,)), ((), ())), precision=HIGHEST, preferred_element_type=jnp.float32)


def halves(x):
    high = x.astype(jnp.bfloat16)
    return high, (x - high.astype(jnp.float32)).astype(jnp.bfloat16)


def dot3(a, b, dims):
    rows = a[0].shape[0]
    both = lax.dot_general(jnp.concatenate(a, axis=0), b[0], (dims, ((), ())), preferred_element_type=jnp.float32)
    last = lax.dot_general(a[0], b[1], (dims, ((), ())), preferred_element_type=jnp.float32)
    return both[:rows] + (both[rows:] + last)


def after(x, *tokens):
    return lax.optimization_barrier((x, *tokens))[0]


def params(dims=0, limit=VMEM_LIMIT):
    semantics = ("arbitrary",) * dims if dims else None
    return pltpu.CompilerParams(dimension_semantics=semantics, vmem_limit_bytes=limit)


def cost(flops, nbytes):
    return pl.CostEstimate(flops=flops, bytes_accessed=nbytes, transcendentals=0)


SMEM = pl.BlockSpec(memory_space=pltpu.SMEM)
ANY = pl.BlockSpec(memory_space=pl.ANY)
VMEM = pl.BlockSpec(memory_space=pltpu.VMEM)


def pack(x, first, rows, n_wide):
    ncols = x.shape[1] // n_wide

    def kernel(x_ref, out_ref, sems):
        copies = []
        for k in range(n_wide):
            source = x_ref.at[pl.ds(first, rows), pl.ds(k * ncols, ncols)]
            copies.append(pltpu.make_async_copy(source, out_ref.at[k], sems.at[k]))
        for copy in copies:
            copy.start()
        for copy in copies:
            copy.wait()

    return pl.pallas_call(
        kernel,
        out_shape=jax.ShapeDtypeStruct((n_wide, rows, ncols), jnp.float32),
        in_specs=[ANY],
        out_specs=VMEM,
        scratch_shapes=[pltpu.SemaphoreType.DMA((n_wide,))],
        compiler_params=params(limit=LARGE_LIMIT),
        cost_estimate=cost(0, 8 * rows * x.shape[1]),
        name="pack",
    )(x)


def plan(place_ref, slots, n_rows):
    places = [place_ref[s] for s in range(place_ref.shape[0])]
    roots = [lax.div(p, slots) for p in places]
    slot = [lax.rem(p, slots) for p in places]
    ranks = [sum([(roots[i] == roots[s]).astype(jnp.int32) for i in range(s)], jnp.int32(0)) for s in range(len(places))]
    counts = [sum([(r == i).astype(jnp.int32) for r in roots], jnp.int32(0)) for i in range(n_rows)]
    return roots, slot, ranks, counts


def feed(here, place, stack, evens, odds, n_rows, part, cols):
    slots, width, _ = stack.shape
    turn = len(evens)

    def kernel(here_ref, place_ref, stack_ref, *refs):
        arrived, (out_even, out_odd, sems) = refs[:-3], refs[-3:]
        roots, slot, ranks, _ = plan(place_ref, slots, n_rows)
        me = here_ref[0]
        mine = [r == me for r in roots]
        count = sum([m.astype(jnp.int32) for m in mine], jnp.int32(0))
        own = sum([jnp.where(m & (k == turn), s, 0) for m, k, s in zip(mine, ranks, slot)], jnp.int32(0))
        older = turn - jnp.maximum(count, 1)
        stored = stack_ref.at[own, :, pl.ds(part * cols, cols)]
        for side, out in ((0, out_even), (1, out_odd)):
            @pl.when((older < 0) | (count > turn))
            def _():
                pltpu.make_async_copy(stored, out, sems.at[side]).start()

            for i in range(turn):
                @pl.when((older == i) & (count <= turn))
                def _():
                    pltpu.make_async_copy(arrived[(1 - side) * turn + i], out, sems.at[side]).start()
        for side, out in ((0, out_even), (1, out_odd)):
            pltpu.make_async_copy(stored, out, sems.at[side]).wait()

    return pl.pallas_call(
        kernel,
        out_shape=[jax.ShapeDtypeStruct((width, cols), jnp.float32)] * 2,
        in_specs=[SMEM, SMEM, ANY] + [ANY] * (2 * turn),
        out_specs=[VMEM] * 2,
        scratch_shapes=[pltpu.SemaphoreType.DMA((2,))],
        compiler_params=params(limit=LARGE_LIMIT),
        cost_estimate=cost(0, 16 * width * cols),
        name="feed",
    )(here, place, stack, *evens, *odds)


def packed_width(steps, width):
    return -(-(width * steps * (steps - 1) // 2) // 128) * 128


def assemble(here, place, offsets, stack, evens, odds, n_rows):
    slots, width, ncols = stack.shape
    steps = place.shape[0]
    height = steps * width
    turns, splits = len(evens), len(evens[0])
    cols = ncols // splits

    def kernel(here_ref, place_ref, offset_ref, stack_ref, *refs):
        arrived, (high_ref, low_ref, gram_ref, held, sems) = refs[:-5], refs[-5:]
        even, odd = arrived[:turns * splits], arrived[turns * splits:]
        roots, slot, ranks, counts = plan(place_ref, slots, n_rows)
        me = here_ref[0]
        me_odd = lax.rem(me, 2) == 1
        for s in range(steps):
            root = roots[s]
            low, high = jnp.minimum(root, me), jnp.maximum(root, me)
            between = [jnp.where((i > low) & (i < high), jnp.maximum(counts[i], 1), 0) for i in range(n_rows)]
            turn = sum(between, ranks[s])
            target = held.at[pl.ds(s * width, width)]
            below, above = root < me, root > me

            @pl.when(root == me)
            def _():
                pltpu.make_async_copy(stack_ref.at[slot[s]], target, sems.at[s]).start()

            for side, came in (((below & me_odd) | (above & ~me_odd), even), ((below & ~me_odd) | (above & me_odd), odd)):
                for i in range(turns):
                    @pl.when(side & (turn == i))
                    def _():
                        for p in range(splits):
                            piece = held.at[pl.ds(s * width, width), pl.ds(p * cols, cols)]
                            pltpu.make_async_copy(came[i * splits + p], piece, sems.at[s]).start()
        columns = here_ref[1] * ncols + lax.broadcasted_iota(jnp.int32, (width, ncols), 1)
        for s in range(steps):
            rows = pl.ds(s * width, width)
            pltpu.make_async_copy(stack_ref.at[0], held.at[rows], sems.at[s]).wait()
            masked = jnp.where(columns >= offset_ref[s], held[rows, :], 0.0)
            held[rows, :] = masked
            high, low = halves(masked)
            high_ref[rows, :] = high
            low_ref[rows, :] = low
        gram = dot_t(held[...], held[...])
        gram_ref[...] = jnp.zeros_like(gram_ref)
        first = 0
        for s in range(1, steps):
            gram_ref[:, first:first + s * width] = gram[s * width:(s + 1) * width, :s * width]
            first += s * width

    return pl.pallas_call(
        kernel,
        out_shape=[
            jax.ShapeDtypeStruct((height, ncols), jnp.bfloat16),
            jax.ShapeDtypeStruct((height, ncols), jnp.bfloat16),
            jax.ShapeDtypeStruct((width, packed_width(steps, width)), jnp.float32),
        ],
        in_specs=[SMEM, SMEM, SMEM, ANY] + [ANY] * (2 * turns * splits),
        out_specs=[VMEM] * 3,
        scratch_shapes=[pltpu.VMEM((height, ncols), jnp.float32), pltpu.SemaphoreType.DMA((steps,))],
        compiler_params=params(limit=LARGE_LIMIT),
        cost_estimate=cost(12 * height * height * ncols, 8 * height * ncols),
        name="assemble",
    )(here, place, offsets, stack, *[p for turn in evens for p in turn], *[p for turn in odds for p in turn])


def merge(cross, factors, vecs):
    steps, width, _ = factors.shape
    height, ncols = vecs[0].shape

    def kernel(*refs):
        cross_refs, (factor_ref, v_high, v_low, p_high, p_low, total, m_ref) = refs[:-7], refs[-7:]
        total[...] = sum([ref[...] for ref in cross_refs[1:]], cross_refs[0][...])
        first = 0
        for k in range(steps):
            own = lax.broadcasted_iota(jnp.int32, (width, height), 0) + k * width
            rest = (own == lax.broadcasted_iota(jnp.int32, (width, height), 1)).astype(jnp.float32)
            if k:
                rest = rest - dot(total[:, first:first + k * width], m_ref[:k * width, :])
                first += k * width
            m_ref[k * width:(k + 1) * width, :] = dot(factor_ref[k], rest)
        product = dot3(halves(m_ref[...].T), (v_high[...], v_low[...]), ((1,), (0,)))
        p_high[...], p_low[...] = halves(product)

    return pl.pallas_call(
        kernel,
        out_shape=[jax.ShapeDtypeStruct((height, ncols), jnp.bfloat16)] * 2,
        out_specs=[VMEM] * 2,
        in_specs=[VMEM] * (len(cross) + 3),
        scratch_shapes=[pltpu.VMEM(cross[0].shape, jnp.float32), pltpu.VMEM((height, height), jnp.float32)],
        compiler_params=params(),
        cost_estimate=cost(6 * height * height * ncols, 8 * height * ncols),
        name="merge",
    )(*cross, factors, *vecs)


def column_block(rows, ncols):
    return 1024 if rows > 128 and ncols % 1024 == 0 else ncols


def fold(w):
    half = w.shape[0] // 2
    return jnp.concatenate([w[:half], w[half:]], axis=1)


def unfold(w):
    height = w.shape[1] // 2
    return jnp.concatenate([w[:, :height], w[:, height:]], axis=0)


def inner_products(here, x, vecs, split):
    lead, rows, ncols = x.shape
    height = vecs[0].shape[0]
    cols = column_block(lead * rows, ncols)
    blocks = ncols // cols
    parts = 2 if split else 1
    half = lead * rows // parts

    def kernel(here_ref, x_ref, high_ref, low_ref, *refs):
        outs, total = refs[:-1], refs[-1]
        block = pl.program_id(0)
        here_cols = pl.ds(pl.multiple_of(block * cols, cols), cols) if blocks > 1 else slice(None)
        part = dot3(
            halves(x_ref[...].reshape(lead * rows, cols)), (high_ref[:, here_cols], low_ref[:, here_cols]), ((1,), (1,))
        )

        @pl.when(block == 0)
        def _():
            total[...] = part

        @pl.when(block > 0)
        def _():
            total[...] += part

        @pl.when(block == blocks - 1)
        def _():
            core = lax.rem(here_ref[1], 2)
            for i, out in enumerate(outs):
                start = pl.multiple_of((core ^ i) * half, 8) if split else 0
                out[...] = fold(total[pl.ds(start, half), :])

    return pl.pallas_call(
        kernel,
        out_shape=[jax.ShapeDtypeStruct((half // 2, 2 * height), jnp.float32)] * parts,
        grid=(blocks,),
        in_specs=[SMEM, pl.BlockSpec((lead, rows, cols), lambda c: (0, 0, c)), VMEM, VMEM],
        out_specs=[pl.BlockSpec((half // 2, 2 * height), lambda c: (0, 0))] * parts,
        scratch_shapes=[pltpu.VMEM((lead * rows, height), jnp.float32)],
        compiler_params=params(1),
        cost_estimate=cost(6 * lead * rows * ncols * height, 4 * lead * rows * ncols),
        name="inner_products",
    )(here, x, *vecs)


def update(here, x, sums, other, changes, out, first, total):
    lead, rows, ncols = x.shape
    n_sums = len(sums)
    height = changes[0].shape[0]
    cols = column_block(lead * rows, ncols)
    blocks = ncols // cols
    half = lead * rows // 2

    def kernel(here_ref, *refs):
        sum_refs, (x_ref, high_ref, low_ref) = refs[:n_sums], refs[n_sums:n_sums + 3]
        out_ref, w_high, w_low = refs[-3:]
        block = pl.program_id(0)

        @pl.when(block == 0)
        def _():
            w = unfold(sum([ref[...] for ref in sum_refs[1:]], sum_refs[0][...]))
            if other is None:
                w_high[...], w_low[...] = halves(w)
            else:
                core = lax.rem(here_ref[1], 2)
                mine = pl.ds(pl.multiple_of(core * half, 16), half)
                w_high[mine, :], w_low[mine, :] = halves(w)
                theirs = pl.ds(pl.multiple_of((1 - core) * half, 16), half)
                w_high[theirs, :], w_low[theirs, :] = halves(unfold(refs[n_sums + 3][...]))

        here_cols = pl.ds(pl.multiple_of(block * cols, cols), cols) if blocks > 1 else slice(None)
        change = dot3((w_high[...], w_low[...]), (high_ref[:, here_cols], low_ref[:, here_cols]), ((1,), (0,)))
        out_ref[...] = (x_ref[...].reshape(lead * rows, cols) - change).reshape(lead, rows, cols)

    operands = [here] + list(sums) + [x, *changes]
    in_specs = [SMEM] + [VMEM] * n_sums + [pl.BlockSpec((lead, rows, cols), lambda c: (0, 0, c)), VMEM, VMEM]
    if other is not None:
        operands.append(other)
        in_specs.append(VMEM)
    aliases = {}
    if out is not None:
        aliases = {len(operands): 0}
        operands.append(out)
        in_specs.append(ANY)
    return pl.pallas_call(
        kernel,
        out_shape=jax.ShapeDtypeStruct((lead, total, ncols), jnp.float32),
        grid=(blocks,),
        in_specs=in_specs,
        out_specs=pl.BlockSpec((pl.Element(lead), pl.Element(rows), pl.Element(cols)), lambda c: (0, first, c * cols)),
        scratch_shapes=[pltpu.VMEM((lead * rows, height), jnp.bfloat16)] * 2,
        input_output_aliases=aliases,
        compiler_params=params(1),
        cost_estimate=cost(6 * lead * rows * ncols * height, 8 * lead * rows * ncols),
        name="update",
    )(*operands)


def swap(array, k, size):
    return lax.ppermute(array, "wide", [(i, i ^ k) for i in range(size)])


def spread(pair, size):
    return [pair] + [swap(pair, k, size) for k in range(2, size, 2)]


def body(n_row, n_wide, eigvec_t, householder, wy_factor, block_place, offsets):
    rows, order = eigvec_t.shape
    steps, width, _ = wy_factor.shape
    slots = householder.shape[0]
    ncols = order // n_wide
    here = jnp.stack([lax.axis_index("row"), lax.axis_index("wide")]).astype(jnp.int32)

    turns = max(z + min(steps - 1, slots * (n_row - 1 - z)) for z in range(n_row - 1))
    cols = ncols // SPLITS
    streams = [([], []) for _ in range(SPLITS)]

    def exchange(array, odd):
        pairs = []
        for z in range(n_row):
            mate = ((z + odd) ^ 1) - odd
            for w in range(n_wide):
                target = mate * n_wide + w if 0 <= mate < n_row else z * n_wide + (w ^ 1)
                pairs.append((z * n_wide + w, target))
        return lax.ppermute(array, ("row", "wide"), pairs)

    whole = rows % 8 == 0
    groups = [8 * size for size in GROUPS] if 8 * sum(GROUPS) == rows else [rows]
    starts = [sum(groups[:i]) for i in range(len(groups))]
    parts = []
    if whole:
        pieces = [pack(eigvec_t, start, size, n_wide) for start, size in zip(starts, groups)]
    else:
        pieces = [eigvec_t]

    def send(*tokens):
        piece = after(pieces[len(parts)], *tokens)
        if whole:
            parts.append(lax.all_to_all(piece, "wide", split_axis=0, concat_axis=0, tiled=True))
        else:
            parts.append(lax.all_to_all(piece, "wide", split_axis=1, concat_axis=0, tiled=True)[None])
        return piece

    tokens = [send(here)]
    for turn in range(turns):
        for part in range(SPLITS):
            evens, odds = streams[part]
            to_even, to_odd = feed(after(here, *tokens), block_place, householder, evens, odds, n_row, part, cols)
            tokens = [to_odd]
            streams[part] = (evens + [exchange(to_even, 0)], odds + [exchange(to_odd, 1)])
            if (turn, part) == (0, 0):
                tokens += pieces[1:]
            if (turn, part) == ARRIVED and len(groups) > 1:
                tokens += [parts[0], send(parts[0], to_odd)]
    evens = list(zip(*[stream[0] for stream in streams]))
    odds = list(zip(*[stream[1] for stream in streams]))
    high, low, gram = assemble(here, block_place, offsets, householder, evens, odds, n_row)
    cross = spread(gram + swap(gram, 1, n_wide), n_wide)
    inner = [inner_products(here, parts[0], (high, low), len(groups) > 1)]
    while len(parts) < len(groups):
        piece = send(parts[-1], inner[-1][0])
        inner.append(inner_products(here, parts[len(inner)], (high, low), len(inner) < len(groups) - 1))
        cross[0] = after(cross[0], piece)
    while len(inner) < len(groups):
        inner.append(inner_products(here, parts[len(inner)], (high, low), len(inner) < len(groups) - 1))
    changes = merge(cross, wy_factor, (high, low))

    out = None
    total = rows if whole else rows * n_wide
    for i, x in enumerate(parts):
        if i < len(parts) - 1:
            mine, theirs = inner[i]
            sums = spread(mine + swap(theirs, 1, n_wide), n_wide)
            mine = functools.reduce(jnp.add, sums)
            sums, other = [mine], swap(mine, 1, n_wide)
        else:
            mine, = inner[i]
            sums, other = spread(mine + swap(mine, 1, n_wide), n_wide), None
        out = update(here, x, sums, other, changes, out, starts[i], total)
    return out.reshape(n_wide * rows, ncols)


def solution(mesh):
    return jax.shard_map(
        functools.partial(body, mesh.shape["row"], mesh.shape["wide"]),
        mesh=mesh,
        in_specs=(P(("row", "wide"), None), P("row", None, "wide"), P(), P(), P()),
        out_specs=P("row", "wide"),
        check_vma=False,
    )
```

```python
import functools

import jax
import jax.numpy as jnp
from jax import lax
from jax.experimental import pallas as pl
from jax.experimental.pallas import tpu as pltpu
from jax.sharding import PartitionSpec as P

HIGHEST = lax.Precision.HIGHEST
SMALL_LIMIT = 44 * 1024 * 1024
VMEM_LIMIT = 52 * 1024 * 1024
LARGE_LIMIT = 58 * 1024 * 1024
TAIL = 16
TAIL_TURN = (4, 1)
SPLITS = 2


def dot_t(a, b):
    return lax.dot_general(a, b, (((1,), (1,)), ((), ())), precision=HIGHEST, preferred_element_type=jnp.float32)


def dot(a, b):
    return lax.dot_general(a, b, (((1,), (0,)), ((), ())), precision=HIGHEST, preferred_element_type=jnp.float32)


def halves(x):
    high = x.astype(jnp.bfloat16)
    return high, (x - high.astype(jnp.float32)).astype(jnp.bfloat16)


def dot3(a, b, dims):
    rows = a[0].shape[0]
    both = lax.dot_general(jnp.concatenate(a, axis=0), b[0], (dims, ((), ())), preferred_element_type=jnp.float32)
    last = lax.dot_general(a[0], b[1], (dims, ((), ())), preferred_element_type=jnp.float32)
    return both[:rows] + (both[rows:] + last)


def after(x, *tokens):
    return lax.optimization_barrier((x, *tokens))[0]


def params(dims=0, limit=VMEM_LIMIT):
    semantics = ("arbitrary",) * dims if dims else None
    return pltpu.CompilerParams(dimension_semantics=semantics, vmem_limit_bytes=limit)


def cost(flops, nbytes):
    return pl.CostEstimate(flops=flops, bytes_accessed=nbytes, transcendentals=0)


SMEM = pl.BlockSpec(memory_space=pltpu.SMEM)
ANY = pl.BlockSpec(memory_space=pl.ANY)
VMEM = pl.BlockSpec(memory_space=pltpu.VMEM)


def pack(here, x, first, rows, n_wide, apart):
    ncols = x.shape[1] // n_wide

    def kernel(here_ref, x_ref, *refs):
        outs, (held, in_sems, out_sems) = refs[:-3], refs[-3:]
        into, out_of = [], []
        for k in range(n_wide):
            start = pl.multiple_of((here_ref[1] ^ k) * ncols, ncols) if apart else k * ncols
            source = x_ref.at[pl.ds(first, rows), pl.ds(start, ncols)]
            into.append(pltpu.make_async_copy(source, held.at[k], in_sems.at[k]))
            out_of.append(pltpu.make_async_copy(held.at[k], outs[k] if apart else outs[0].at[k], out_sems.at[k]))
        for copy in into:
            copy.start()
        for k in range(n_wide):
            into[k].wait()
            out_of[k].start()
        for copy in out_of:
            copy.wait()

    shapes = [(rows, ncols)] * n_wide if apart else [(n_wide, rows, ncols)]
    return pl.pallas_call(
        kernel,
        out_shape=[jax.ShapeDtypeStruct(shape, jnp.float32) for shape in shapes],
        in_specs=[SMEM, ANY],
        out_specs=[ANY] * len(shapes),
        scratch_shapes=[
            pltpu.VMEM((n_wide, rows, ncols), jnp.float32),
            pltpu.SemaphoreType.DMA((n_wide,)),
            pltpu.SemaphoreType.DMA((n_wide,)),
        ],
        compiler_params=params(limit=LARGE_LIMIT),
        cost_estimate=cost(0, 8 * rows * x.shape[1]),
        name="pack",
    )(here, x)


def plan(place_ref, slots, n_rows):
    places = [place_ref[s] for s in range(place_ref.shape[0])]
    roots = [lax.div(p, slots) for p in places]
    slot = [lax.rem(p, slots) for p in places]
    ranks = [sum([(roots[i] == roots[s]).astype(jnp.int32) for i in range(s)], jnp.int32(0)) for s in range(len(places))]
    counts = [sum([(r == i).astype(jnp.int32) for r in roots], jnp.int32(0)) for i in range(n_rows)]
    return roots, slot, ranks, counts


def feed(here, place, stack, evens, odds, n_rows, part, cols):
    slots, width, _ = stack.shape
    turn = len(evens)

    def kernel(here_ref, place_ref, stack_ref, *refs):
        arrived, (out_even, out_odd, sems) = refs[:-3], refs[-3:]
        roots, slot, ranks, _ = plan(place_ref, slots, n_rows)
        me = here_ref[0]
        mine = [r == me for r in roots]
        count = sum([m.astype(jnp.int32) for m in mine], jnp.int32(0))
        own = sum([jnp.where(m & (k == turn), s, 0) for m, k, s in zip(mine, ranks, slot)], jnp.int32(0))
        older = turn - jnp.maximum(count, 1)
        stored = stack_ref.at[own, :, pl.ds(part * cols, cols)]
        for side, out in ((0, out_even), (1, out_odd)):
            @pl.when((older < 0) | (count > turn))
            def _():
                pltpu.make_async_copy(stored, out, sems.at[side]).start()

            for i in range(turn):
                @pl.when((older == i) & (count <= turn))
                def _():
                    pltpu.make_async_copy(arrived[(1 - side) * turn + i], out, sems.at[side]).start()
        for side, out in ((0, out_even), (1, out_odd)):
            pltpu.make_async_copy(stored, out, sems.at[side]).wait()

    return pl.pallas_call(
        kernel,
        out_shape=[jax.ShapeDtypeStruct((width, cols), jnp.float32)] * 2,
        in_specs=[SMEM, SMEM, ANY] + [ANY] * (2 * turn),
        out_specs=[VMEM] * 2,
        scratch_shapes=[pltpu.SemaphoreType.DMA((2,))],
        compiler_params=params(limit=SMALL_LIMIT),
        cost_estimate=cost(0, 16 * width * cols),
        name="feed",
    )(here, place, stack, *evens, *odds)


def packed_width(steps, width):
    return -(-(width * steps * (steps - 1) // 2) // 128) * 128


def assemble(here, place, offsets, stack, evens, odds, n_rows):
    slots, width, ncols = stack.shape
    steps = place.shape[0]
    height = steps * width
    turns, splits = len(evens), len(evens[0])
    cols = ncols // splits

    def kernel(here_ref, place_ref, offset_ref, stack_ref, *refs):
        arrived, (high_ref, low_ref, gram_ref, held, sems) = refs[:-5], refs[-5:]
        even, odd = arrived[:turns * splits], arrived[turns * splits:]
        roots, slot, ranks, counts = plan(place_ref, slots, n_rows)
        me = here_ref[0]
        me_odd = lax.rem(me, 2) == 1
        for s in range(steps):
            root = roots[s]
            low, high = jnp.minimum(root, me), jnp.maximum(root, me)
            between = [jnp.where((i > low) & (i < high), jnp.maximum(counts[i], 1), 0) for i in range(n_rows)]
            turn = sum(between, ranks[s])
            target = held.at[pl.ds(s * width, width)]
            below, above = root < me, root > me

            @pl.when(root == me)
            def _():
                pltpu.make_async_copy(stack_ref.at[slot[s]], target, sems.at[s]).start()

            for side, came in (((below & me_odd) | (above & ~me_odd), even), ((below & ~me_odd) | (above & me_odd), odd)):
                for i in range(turns):
                    @pl.when(side & (turn == i))
                    def _():
                        for p in range(splits):
                            piece = held.at[pl.ds(s * width, width), pl.ds(p * cols, cols)]
                            pltpu.make_async_copy(came[i * splits + p], piece, sems.at[s]).start()
        columns = here_ref[1] * ncols + lax.broadcasted_iota(jnp.int32, (width, ncols), 1)
        for s in range(steps):
            rows = pl.ds(s * width, width)
            pltpu.make_async_copy(stack_ref.at[0], held.at[rows], sems.at[s]).wait()
            masked = jnp.where(columns >= offset_ref[s], held[rows, :], 0.0)
            held[rows, :] = masked
            high, low = halves(masked)
            high_ref[rows, :] = high
            low_ref[rows, :] = low
        gram = dot_t(held[...], held[...])
        gram_ref[...] = jnp.zeros_like(gram_ref)
        first = 0
        for s in range(1, steps):
            gram_ref[:, first:first + s * width] = gram[s * width:(s + 1) * width, :s * width]
            first += s * width

    return pl.pallas_call(
        kernel,
        out_shape=[
            jax.ShapeDtypeStruct((height, ncols), jnp.bfloat16),
            jax.ShapeDtypeStruct((height, ncols), jnp.bfloat16),
            jax.ShapeDtypeStruct((width, packed_width(steps, width)), jnp.float32),
        ],
        in_specs=[SMEM, SMEM, SMEM, ANY] + [ANY] * (2 * turns * splits),
        out_specs=[VMEM] * 3,
        scratch_shapes=[pltpu.VMEM((height, ncols), jnp.float32), pltpu.SemaphoreType.DMA((steps,))],
        compiler_params=params(limit=SMALL_LIMIT),
        cost_estimate=cost(12 * height * height * ncols, 8 * height * ncols),
        name="assemble",
    )(here, place, offsets, stack, *[p for turn in evens for p in turn], *[p for turn in odds for p in turn])


def merge(cross, factors, vecs):
    steps, width, _ = factors.shape
    height, ncols = vecs[0].shape

    def kernel(*refs):
        cross_refs, (factor_ref, v_high, v_low, p_high, p_low, total, m_ref) = refs[:-7], refs[-7:]
        total[...] = sum([ref[...] for ref in cross_refs[1:]], cross_refs[0][...])
        first = 0
        for k in range(steps):
            own = lax.broadcasted_iota(jnp.int32, (width, height), 0) + k * width
            rest = (own == lax.broadcasted_iota(jnp.int32, (width, height), 1)).astype(jnp.float32)
            if k:
                rest = rest - dot(total[:, first:first + k * width], m_ref[:k * width, :])
                first += k * width
            m_ref[k * width:(k + 1) * width, :] = dot(factor_ref[k], rest)
        product = dot3(halves(m_ref[...].T), (v_high[...], v_low[...]), ((1,), (0,)))
        p_high[...], p_low[...] = halves(product)

    return pl.pallas_call(
        kernel,
        out_shape=[jax.ShapeDtypeStruct((height, ncols), jnp.bfloat16)] * 2,
        out_specs=[VMEM] * 2,
        in_specs=[VMEM] * (len(cross) + 3),
        scratch_shapes=[pltpu.VMEM(cross[0].shape, jnp.float32), pltpu.VMEM((height, height), jnp.float32)],
        compiler_params=params(),
        cost_estimate=cost(6 * height * height * ncols, 8 * height * ncols),
        name="merge",
    )(*cross, factors, *vecs)


def column_block(rows, ncols):
    return 1024 if rows > 128 and ncols % 1024 == 0 else ncols


def fold(w):
    half = w.shape[0] // 2
    return jnp.concatenate([w[:half], w[half:]], axis=1)


def unfold(w):
    height = w.shape[1] // 2
    return jnp.concatenate([w[:, :height], w[:, height:]], axis=0)


def inner_products(here, x, vecs, split):
    apart = isinstance(x, list)
    pieces = x if apart else [x]
    lead = len(pieces) if apart else x.shape[0]
    rows, ncols = pieces[0].shape[-2:]
    height = vecs[0].shape[0]
    cols = column_block(lead * rows, ncols)
    blocks = ncols // cols
    parts = 2 if split else 1
    half = lead * rows // parts

    def kernel(here_ref, *refs):
        x_refs, (high_ref, low_ref), outs, total = refs[:len(pieces)], refs[len(pieces):len(pieces) + 2], refs[-1 - parts:-1], refs[-1]
        block = pl.program_id(0)
        here_cols = pl.ds(pl.multiple_of(block * cols, cols), cols) if blocks > 1 else slice(None)
        values = jnp.concatenate([ref[...] for ref in x_refs], axis=0).reshape(lead * rows, cols)
        part = dot3(halves(values), (high_ref[:, here_cols], low_ref[:, here_cols]), ((1,), (1,)))

        @pl.when(block == 0)
        def _():
            total[...] = part

        @pl.when(block > 0)
        def _():
            total[...] += part

        @pl.when(block == blocks - 1)
        def _():
            if apart:
                value = total[...]
                for k in range(lead):
                    total[pl.ds(pl.multiple_of((here_ref[1] ^ k) * rows, 8), rows), :] = value[k * rows:(k + 1) * rows]
            core = lax.rem(here_ref[1], 2)
            for i, out in enumerate(outs):
                start = pl.multiple_of((core ^ i) * half, 8) if split else 0
                out[...] = fold(total[pl.ds(start, half), :])

    block_shape, index = ((rows, cols), lambda c: (0, c)) if apart else ((lead, rows, cols), lambda c: (0, 0, c))
    return pl.pallas_call(
        kernel,
        out_shape=[jax.ShapeDtypeStruct((half // 2, 2 * height), jnp.float32)] * parts,
        grid=(blocks,),
        in_specs=[SMEM] + [pl.BlockSpec(block_shape, index)] * len(pieces) + [VMEM, VMEM],
        out_specs=[pl.BlockSpec((half // 2, 2 * height), lambda c: (0, 0))] * parts,
        scratch_shapes=[pltpu.VMEM((lead * rows, height), jnp.float32)],
        compiler_params=params(1),
        cost_estimate=cost(6 * lead * rows * ncols * height, 4 * lead * rows * ncols),
        name="inner_products",
    )(here, *pieces, *vecs)


def update(here, x, sums, other, changes, out, first, total):
    apart = isinstance(x, list)
    pieces = x if apart else [x]
    lead = len(pieces) if apart else x.shape[0]
    rows, ncols = pieces[0].shape[-2:]
    n_sums = len(sums)
    height = changes[0].shape[0]
    cols = column_block(lead * rows, ncols)
    blocks = ncols // cols
    half = lead * rows // 2

    def kernel(here_ref, *refs):
        sum_refs, x_refs = refs[:n_sums], refs[n_sums:n_sums + len(pieces)]
        high_ref, low_ref, *more = refs[n_sums + len(pieces):-4]
        out_ref, w_ref, w_high, w_low = refs[-4:]
        block = pl.program_id(0)

        @pl.when(block == 0)
        def _():
            w = unfold(sum([ref[...] for ref in sum_refs[1:]], sum_refs[0][...]))
            if other is not None:
                core = lax.rem(here_ref[1], 2)
                w_ref[pl.ds(pl.multiple_of(core * half, 8), half), :] = w
                w_ref[pl.ds(pl.multiple_of((1 - core) * half, 8), half), :] = unfold(more[0][...])
                w = w_ref[...]
            if apart:
                w_ref[...] = w
                w = jnp.concatenate(
                    [w_ref[pl.ds(pl.multiple_of((here_ref[1] ^ k) * rows, 8), rows), :] for k in range(lead)], axis=0
                )
            w_high[...], w_low[...] = halves(w)

        here_cols = pl.ds(pl.multiple_of(block * cols, cols), cols) if blocks > 1 else slice(None)
        change = dot3((w_high[...], w_low[...]), (high_ref[:, here_cols], low_ref[:, here_cols]), ((1,), (0,)))
        if apart:
            for k in range(lead):
                out_ref[pl.ds(here_ref[1] ^ k, 1)] = (x_refs[k][...] - change[k * rows:(k + 1) * rows])[None]
        else:
            out_ref[...] = (x_refs[0][...].reshape(lead * rows, cols) - change).reshape(lead, rows, cols)

    block_shape, index = ((rows, cols), lambda c: (0, c)) if apart else ((lead, rows, cols), lambda c: (0, 0, c))
    operands = [here] + list(sums) + pieces + list(changes)
    in_specs = [SMEM] + [VMEM] * n_sums + [pl.BlockSpec(block_shape, index)] * len(pieces) + [VMEM, VMEM]
    if other is not None:
        operands.append(other)
        in_specs.append(VMEM)
    aliases = {}
    if out is not None:
        aliases = {len(operands): 0}
        operands.append(out)
        in_specs.append(ANY)
    return pl.pallas_call(
        kernel,
        out_shape=jax.ShapeDtypeStruct((lead, total, ncols), jnp.float32),
        grid=(blocks,),
        in_specs=in_specs,
        out_specs=pl.BlockSpec((pl.Element(lead), pl.Element(rows), pl.Element(cols)), lambda c: (0, first, c * cols)),
        scratch_shapes=[pltpu.VMEM((lead * rows, height), jnp.float32)]
        + [pltpu.VMEM((lead * rows, height), jnp.bfloat16)] * 2,
        input_output_aliases=aliases,
        compiler_params=params(1),
        cost_estimate=cost(6 * lead * rows * ncols * height, 8 * lead * rows * ncols),
        name="update",
    )(*operands)


def swap(array, k, size):
    return lax.ppermute(array, "wide", [(i, i ^ k) for i in range(size)])


def spread(pair, size):
    return [pair] + [swap(pair, k, size) for k in range(2, size, 2)]


def body(n_row, n_wide, eigvec_t, householder, wy_factor, block_place, offsets):
    rows, order = eigvec_t.shape
    steps, width, _ = wy_factor.shape
    slots = householder.shape[0]
    ncols = order // n_wide
    here = jnp.stack([lax.axis_index("row"), lax.axis_index("wide")]).astype(jnp.int32)

    turns = max(z + min(steps - 1, slots * (n_row - 1 - z)) for z in range(n_row - 1))
    cols = ncols // SPLITS
    streams = [([], []) for _ in range(SPLITS)]

    def exchange(array, odd):
        pairs = []
        for z in range(n_row):
            mate = ((z + odd) ^ 1) - odd
            for w in range(n_wide):
                target = mate * n_wide + w if 0 <= mate < n_row else z * n_wide + (w ^ 1)
                pairs.append((z * n_wide + w, target))
        return lax.ppermute(array, ("row", "wide"), pairs)

    tail = TAIL if rows % 8 == 0 and rows > TAIL else 0
    bulk = rows - tail
    if tail:
        piece, = pack(here, eigvec_t, 0, bulk, n_wide, False)
        early = lax.all_to_all(piece, "wide", split_axis=0, concat_axis=0, tiled=True)
        pieces = pack(here, after(eigvec_t, piece), bulk, tail, n_wide, True)
    else:
        piece = here
        early = lax.all_to_all(eigvec_t, "wide", split_axis=1, concat_axis=0, tiled=True)[None]
        pieces = []

    tokens = [piece]
    for turn in range(turns):
        for part in range(SPLITS):
            evens, odds = streams[part]
            to_even, to_odd = feed(after(here, *tokens), block_place, householder, evens, odds, n_row, part, cols)
            tokens = [to_odd]
            streams[part] = (evens + [exchange(to_even, 0)], odds + [exchange(to_odd, 1)])
            if (turn, part) == (0, 1):
                tokens += pieces
            if (turn, part) == TAIL_TURN and tail:
                late = [pieces[0]] + [swap(after(pieces[k], to_odd), k, n_wide) for k in range(1, n_wide)]
    evens = list(zip(*[stream[0] for stream in streams]))
    odds = list(zip(*[stream[1] for stream in streams]))
    high, low, gram = assemble(here, block_place, offsets, householder, evens, odds, n_row)
    cross = spread(gram + swap(gram, 1, n_wide), n_wide)
    changes = merge(cross, wy_factor, (high, low))

    mine, theirs = inner_products(here, early, (high, low), True)
    mine = functools.reduce(jnp.add, spread(mine + swap(theirs, 1, n_wide), n_wide))
    total = rows if tail else rows * n_wide
    out = update(here, early, [mine], swap(mine, 1, n_wide), changes, None, 0, total)
    if tail:
        part, = inner_products(here, late, (high, low), False)
        out = update(here, late, spread(part + swap(part, 1, n_wide), n_wide), None, changes, out, bulk, total)
    return out.reshape(n_wide * rows, ncols)


def solution(mesh):
    return jax.shard_map(
        functools.partial(body, mesh.shape["row"], mesh.shape["wide"]),
        mesh=mesh,
        in_specs=(P(("row", "wide"), None), P("row", None, "wide"), P(), P(), P()),
        out_specs=P("row", "wide"),
        check_vma=False,
    )
```

```python
import functools

import jax
import jax.numpy as jnp
from jax import lax
from jax.experimental import pallas as pl
from jax.experimental.pallas import tpu as pltpu
from jax.sharding import PartitionSpec as P

HIGHEST = lax.Precision.HIGHEST
SMALL_LIMIT = 44 * 1024 * 1024
VMEM_LIMIT = 52 * 1024 * 1024
LARGE_LIMIT = 58 * 1024 * 1024
TAIL = 16
SPLITS = 2


def dot_t(a, b):
    return lax.dot_general(a, b, (((1,), (1,)), ((), ())), precision=HIGHEST, preferred_element_type=jnp.float32)


def dot(a, b):
    return lax.dot_general(a, b, (((1,), (0,)), ((), ())), precision=HIGHEST, preferred_element_type=jnp.float32)


def halves(x):
    high = x.astype(jnp.bfloat16)
    return high, (x - high.astype(jnp.float32)).astype(jnp.bfloat16)


def dot3(a, b, dims):
    rows = a[0].shape[0]
    both = lax.dot_general(jnp.concatenate(a, axis=0), b[0], (dims, ((), ())), preferred_element_type=jnp.float32)
    last = lax.dot_general(a[0], b[1], (dims, ((), ())), preferred_element_type=jnp.float32)
    return both[:rows] + (both[rows:] + last)


def after(x, *tokens):
    return lax.optimization_barrier((x, *tokens))[0]


def params(dims=0, limit=VMEM_LIMIT):
    semantics = ("arbitrary",) * dims if dims else None
    return pltpu.CompilerParams(dimension_semantics=semantics, vmem_limit_bytes=limit)


def cost(flops, nbytes):
    return pl.CostEstimate(flops=flops, bytes_accessed=nbytes, transcendentals=0)


SMEM = pl.BlockSpec(memory_space=pltpu.SMEM)
ANY = pl.BlockSpec(memory_space=pl.ANY)
VMEM = pl.BlockSpec(memory_space=pltpu.VMEM)


def pack(here, x, first, rows, n_wide, apart):
    ncols = x.shape[1] // n_wide

    def kernel(here_ref, x_ref, *refs):
        outs, (held, in_sems, out_sems) = refs[:-3], refs[-3:]
        into, out_of = [], []
        for k in range(n_wide):
            start = pl.multiple_of((here_ref[1] ^ k) * ncols, ncols) if apart else k * ncols
            source = x_ref.at[pl.ds(first, rows), pl.ds(start, ncols)]
            into.append(pltpu.make_async_copy(source, held.at[k], in_sems.at[k]))
            out_of.append(pltpu.make_async_copy(held.at[k], outs[k] if apart else outs[0].at[k], out_sems.at[k]))
        for copy in into:
            copy.start()
        for k in range(n_wide):
            into[k].wait()
            out_of[k].start()
        for copy in out_of:
            copy.wait()

    shapes = [(rows, ncols)] * n_wide if apart else [(n_wide, rows, ncols)]
    return pl.pallas_call(
        kernel,
        out_shape=[jax.ShapeDtypeStruct(shape, jnp.float32) for shape in shapes],
        in_specs=[SMEM, ANY],
        out_specs=[ANY] * len(shapes),
        scratch_shapes=[
            pltpu.VMEM((n_wide, rows, ncols), jnp.float32),
            pltpu.SemaphoreType.DMA((n_wide,)),
            pltpu.SemaphoreType.DMA((n_wide,)),
        ],
        compiler_params=params(limit=LARGE_LIMIT),
        cost_estimate=cost(0, 8 * rows * x.shape[1]),
        name="pack",
    )(here, x)


def plan(place_ref, slots, n_rows):
    places = [place_ref[s] for s in range(place_ref.shape[0])]
    roots = [lax.div(p, slots) for p in places]
    slot = [lax.rem(p, slots) for p in places]
    ranks = [sum([(roots[i] == roots[s]).astype(jnp.int32) for i in range(s)], jnp.int32(0)) for s in range(len(places))]
    counts = [sum([(r == i).astype(jnp.int32) for r in roots], jnp.int32(0)) for i in range(n_rows)]
    return roots, slot, ranks, counts


def feed(here, place, stack, evens, odds, n_rows, part, cols):
    slots, width, _ = stack.shape
    turn = len(evens)

    def kernel(here_ref, place_ref, stack_ref, *refs):
        arrived, (out_even, out_odd, sems) = refs[:-3], refs[-3:]
        roots, slot, ranks, _ = plan(place_ref, slots, n_rows)
        me = here_ref[0]
        mine = [r == me for r in roots]
        count = sum([m.astype(jnp.int32) for m in mine], jnp.int32(0))
        own = sum([jnp.where(m & (k == turn), s, 0) for m, k, s in zip(mine, ranks, slot)], jnp.int32(0))
        older = turn - jnp.maximum(count, 1)
        stored = stack_ref.at[own, :, pl.ds(part * cols, cols)]
        for side, out in ((0, out_even), (1, out_odd)):
            @pl.when((older < 0) | (count > turn))
            def _():
                pltpu.make_async_copy(stored, out, sems.at[side]).start()

            for i in range(turn):
                @pl.when((older == i) & (count <= turn))
                def _():
                    pltpu.make_async_copy(arrived[(1 - side) * turn + i], out, sems.at[side]).start()
        for side, out in ((0, out_even), (1, out_odd)):
            pltpu.make_async_copy(stored, out, sems.at[side]).wait()

    return pl.pallas_call(
        kernel,
        out_shape=[jax.ShapeDtypeStruct((width, cols), jnp.float32)] * 2,
        in_specs=[SMEM, SMEM, ANY] + [ANY] * (2 * turn),
        out_specs=[VMEM] * 2,
        scratch_shapes=[pltpu.SemaphoreType.DMA((2,))],
        compiler_params=params(limit=SMALL_LIMIT),
        cost_estimate=cost(0, 16 * width * cols),
        name="feed",
    )(here, place, stack, *evens, *odds)


def packed_width(steps, width):
    return -(-(width * steps * (steps - 1) // 2) // 128) * 128


def assemble(here, place, offsets, stack, evens, odds, n_rows):
    slots, width, ncols = stack.shape
    steps = place.shape[0]
    height = steps * width
    turns, splits = len(evens), len(evens[0])
    cols = ncols // splits

    def kernel(here_ref, place_ref, offset_ref, stack_ref, *refs):
        arrived, (high_ref, low_ref, gram_ref, held, sems) = refs[:-5], refs[-5:]
        even, odd = arrived[:turns * splits], arrived[turns * splits:]
        roots, slot, ranks, counts = plan(place_ref, slots, n_rows)
        me = here_ref[0]
        me_odd = lax.rem(me, 2) == 1
        for s in range(steps):
            root = roots[s]
            low, high = jnp.minimum(root, me), jnp.maximum(root, me)
            between = [jnp.where((i > low) & (i < high), jnp.maximum(counts[i], 1), 0) for i in range(n_rows)]
            turn = sum(between, ranks[s])
            target = held.at[pl.ds(s * width, width)]
            below, above = root < me, root > me

            @pl.when(root == me)
            def _():
                pltpu.make_async_copy(stack_ref.at[slot[s]], target, sems.at[s]).start()

            for side, came in (((below & me_odd) | (above & ~me_odd), even), ((below & ~me_odd) | (above & me_odd), odd)):
                for i in range(turns):
                    @pl.when(side & (turn == i))
                    def _():
                        for p in range(splits):
                            piece = held.at[pl.ds(s * width, width), pl.ds(p * cols, cols)]
                            pltpu.make_async_copy(came[i * splits + p], piece, sems.at[s]).start()
        columns = here_ref[1] * ncols + lax.broadcasted_iota(jnp.int32, (width, ncols), 1)
        for s in range(steps):
            rows = pl.ds(s * width, width)
            pltpu.make_async_copy(stack_ref.at[0], held.at[rows], sems.at[s]).wait()
            masked = jnp.where(columns >= offset_ref[s], held[rows, :], 0.0)
            held[rows, :] = masked
            high, low = halves(masked)
            high_ref[rows, :] = high
            low_ref[rows, :] = low
        gram = dot_t(held[...], held[...])
        gram_ref[...] = jnp.zeros_like(gram_ref)
        first = 0
        for s in range(1, steps):
            gram_ref[:, first:first + s * width] = gram[s * width:(s + 1) * width, :s * width]
            first += s * width

    return pl.pallas_call(
        kernel,
        out_shape=[
            jax.ShapeDtypeStruct((height, ncols), jnp.bfloat16),
            jax.ShapeDtypeStruct((height, ncols), jnp.bfloat16),
            jax.ShapeDtypeStruct((width, packed_width(steps, width)), jnp.float32),
        ],
        in_specs=[SMEM, SMEM, SMEM, ANY] + [ANY] * (2 * turns * splits),
        out_specs=[VMEM] * 3,
        scratch_shapes=[pltpu.VMEM((height, ncols), jnp.float32), pltpu.SemaphoreType.DMA((steps,))],
        compiler_params=params(limit=SMALL_LIMIT),
        cost_estimate=cost(12 * height * height * ncols, 8 * height * ncols),
        name="assemble",
    )(here, place, offsets, stack, *[p for turn in evens for p in turn], *[p for turn in odds for p in turn])


def merge(cross, factors, vecs):
    steps, width, _ = factors.shape
    height, ncols = vecs[0].shape

    def kernel(*refs):
        cross_refs, (factor_ref, v_high, v_low, p_high, p_low, total, m_ref) = refs[:-7], refs[-7:]
        total[...] = sum([ref[...] for ref in cross_refs[1:]], cross_refs[0][...])
        first = 0
        for k in range(steps):
            own = lax.broadcasted_iota(jnp.int32, (width, height), 0) + k * width
            rest = (own == lax.broadcasted_iota(jnp.int32, (width, height), 1)).astype(jnp.float32)
            if k:
                rest = rest - dot(total[:, first:first + k * width], m_ref[:k * width, :])
                first += k * width
            m_ref[k * width:(k + 1) * width, :] = dot(factor_ref[k], rest)
        product = dot3(halves(m_ref[...].T), (v_high[...], v_low[...]), ((1,), (0,)))
        p_high[...], p_low[...] = halves(product)

    return pl.pallas_call(
        kernel,
        out_shape=[jax.ShapeDtypeStruct((height, ncols), jnp.bfloat16)] * 2,
        out_specs=[VMEM] * 2,
        in_specs=[VMEM] * (len(cross) + 3),
        scratch_shapes=[pltpu.VMEM(cross[0].shape, jnp.float32), pltpu.VMEM((height, height), jnp.float32)],
        compiler_params=params(),
        cost_estimate=cost(6 * height * height * ncols, 8 * height * ncols),
        name="merge",
    )(*cross, factors, *vecs)


def column_block(rows, ncols, cols):
    return cols if rows > 128 and ncols % cols == 0 else ncols


def fold(w):
    half = w.shape[0] // 2
    return jnp.concatenate([w[:half], w[half:]], axis=1)


def unfold(w):
    height = w.shape[1] // 2
    return jnp.concatenate([w[:, :height], w[:, height:]], axis=0)


def inner_products(here, x, vecs, split):
    apart = isinstance(x, list)
    pieces = x if apart else [x]
    lead = len(pieces) if apart else x.shape[0]
    rows, ncols = pieces[0].shape[-2:]
    height = vecs[0].shape[0]
    cols = column_block(lead * rows, ncols, 1024)
    blocks = ncols // cols
    parts = 2 if split else 1
    half = lead * rows // parts

    def kernel(here_ref, *refs):
        x_refs, (high_ref, low_ref), outs, total = refs[:len(pieces)], refs[len(pieces):len(pieces) + 2], refs[-1 - parts:-1], refs[-1]
        block = pl.program_id(0)
        here_cols = pl.ds(pl.multiple_of(block * cols, cols), cols) if blocks > 1 else slice(None)
        values = jnp.concatenate([ref[...] for ref in x_refs], axis=0).reshape(lead * rows, cols)
        part = dot3(halves(values), (high_ref[:, here_cols], low_ref[:, here_cols]), ((1,), (1,)))

        @pl.when(block == 0)
        def _():
            total[...] = part

        @pl.when(block > 0)
        def _():
            total[...] += part

        @pl.when(block == blocks - 1)
        def _():
            if apart:
                value = total[...]
                for k in range(lead):
                    total[pl.ds(pl.multiple_of((here_ref[1] ^ k) * rows, 8), rows), :] = value[k * rows:(k + 1) * rows]
            core = lax.rem(here_ref[1], 2)
            for i, out in enumerate(outs):
                start = pl.multiple_of((core ^ i) * half, 8) if split else 0
                out[...] = fold(total[pl.ds(start, half), :])

    block_shape, index = ((rows, cols), lambda c: (0, c)) if apart else ((lead, rows, cols), lambda c: (0, 0, c))
    return pl.pallas_call(
        kernel,
        out_shape=[jax.ShapeDtypeStruct((half // 2, 2 * height), jnp.float32)] * parts,
        grid=(blocks,),
        in_specs=[SMEM] + [pl.BlockSpec(block_shape, index)] * len(pieces) + [VMEM, VMEM],
        out_specs=[pl.BlockSpec((half // 2, 2 * height), lambda c: (0, 0))] * parts,
        scratch_shapes=[pltpu.VMEM((lead * rows, height), jnp.float32)],
        compiler_params=params(1),
        cost_estimate=cost(6 * lead * rows * ncols * height, 4 * lead * rows * ncols),
        name="inner_products",
    )(here, *pieces, *vecs)


def update(here, x, sums, other, changes, out, first, total):
    apart = isinstance(x, list)
    pieces = x if apart else [x]
    lead = len(pieces) if apart else x.shape[0]
    rows, ncols = pieces[0].shape[-2:]
    n_sums = len(sums)
    height = changes[0].shape[0]
    cols = column_block(lead * rows, ncols, 512)
    blocks = ncols // cols
    half = lead * rows // 2

    def kernel(here_ref, *refs):
        sum_refs, x_refs = refs[:n_sums], refs[n_sums:n_sums + len(pieces)]
        high_ref, low_ref, *more = refs[n_sums + len(pieces):-4]
        out_ref, w_ref, w_high, w_low = refs[-4:]
        block = pl.program_id(0)

        @pl.when(block == 0)
        def _():
            w = unfold(sum([ref[...] for ref in sum_refs[1:]], sum_refs[0][...]))
            if other is not None:
                core = lax.rem(here_ref[1], 2)
                w_ref[pl.ds(pl.multiple_of(core * half, 8), half), :] = w
                w_ref[pl.ds(pl.multiple_of((1 - core) * half, 8), half), :] = unfold(more[0][...])
                w = w_ref[...]
            if apart:
                w_ref[...] = w
                w = jnp.concatenate(
                    [w_ref[pl.ds(pl.multiple_of((here_ref[1] ^ k) * rows, 8), rows), :] for k in range(lead)], axis=0
                )
            w_high[...], w_low[...] = halves(w)

        here_cols = pl.ds(pl.multiple_of(block * cols, cols), cols) if blocks > 1 else slice(None)
        change = dot3((w_high[...], w_low[...]), (high_ref[:, here_cols], low_ref[:, here_cols]), ((1,), (0,)))
        if apart:
            for k in range(lead):
                out_ref[pl.ds(here_ref[1] ^ k, 1)] = (x_refs[k][...] - change[k * rows:(k + 1) * rows])[None]
        else:
            out_ref[...] = (x_refs[0][...].reshape(lead * rows, cols) - change).reshape(lead, rows, cols)

    block_shape, index = ((rows, cols), lambda c: (0, c)) if apart else ((lead, rows, cols), lambda c: (0, 0, c))
    operands = [here] + list(sums) + pieces + list(changes)
    in_specs = [SMEM] + [VMEM] * n_sums + [pl.BlockSpec(block_shape, index)] * len(pieces) + [VMEM, VMEM]
    if other is not None:
        operands.append(other)
        in_specs.append(VMEM)
    aliases = {}
    if out is not None:
        aliases = {len(operands): 0}
        operands.append(out)
        in_specs.append(ANY)
    return pl.pallas_call(
        kernel,
        out_shape=jax.ShapeDtypeStruct((lead, total, ncols), jnp.float32),
        grid=(blocks,),
        in_specs=in_specs,
        out_specs=pl.BlockSpec((pl.Element(lead), pl.Element(rows), pl.Element(cols)), lambda c: (0, first, c * cols)),
        scratch_shapes=[pltpu.VMEM((lead * rows, height), jnp.float32)]
        + [pltpu.VMEM((lead * rows, height), jnp.bfloat16)] * 2,
        input_output_aliases=aliases,
        compiler_params=params(1),
        cost_estimate=cost(6 * lead * rows * ncols * height, 8 * lead * rows * ncols),
        name="update",
    )(*operands)


def swap(array, k, size):
    return lax.ppermute(array, "wide", [(i, i ^ k) for i in range(size)])


def spread(pair, size):
    return [pair] + [swap(pair, k, size) for k in range(2, size, 2)]


def body(n_row, n_wide, eigvec_t, householder, wy_factor, block_place, offsets):
    rows, order = eigvec_t.shape
    steps, width, _ = wy_factor.shape
    slots = householder.shape[0]
    ncols = order // n_wide
    here = jnp.stack([lax.axis_index("row"), lax.axis_index("wide")]).astype(jnp.int32)

    turns = max(z + min(steps - 1, slots * (n_row - 1 - z)) for z in range(n_row - 1))
    cols = ncols // SPLITS
    streams = [([], []) for _ in range(SPLITS)]

    def exchange(array, odd):
        pairs = []
        for z in range(n_row):
            mate = ((z + odd) ^ 1) - odd
            for w in range(n_wide):
                target = mate * n_wide + w if 0 <= mate < n_row else z * n_wide + (w ^ 1)
                pairs.append((z * n_wide + w, target))
        return lax.ppermute(array, ("row", "wide"), pairs)

    tail = TAIL if rows % 8 == 0 and rows > TAIL else 0
    bulk = rows - tail
    if not tail:
        early = lax.all_to_all(eigvec_t, "wide", split_axis=1, concat_axis=0, tiled=True)[None]

    tokens = []
    for turn in range(turns):
        for part in range(SPLITS):
            evens, odds = streams[part]
            to_even, to_odd = feed(after(here, *tokens), block_place, householder, evens, odds, n_row, part, cols)
            tokens = [to_odd]
            streams[part] = (evens + [exchange(to_even, 0)], odds + [exchange(to_odd, 1)])
            if (turn, part) == (0, 0) and tail:
                piece, = pack(here, after(eigvec_t, to_odd), 0, bulk, n_wide, False)
                early = lax.all_to_all(piece, "wide", split_axis=0, concat_axis=0, tiled=True)
                tokens = [piece]
            if (turn, part) == (1, 0) and tail:
                piece, = pack(here, after(eigvec_t, to_odd), bulk, tail, n_wide, False)
                tokens = [piece]
    evens = list(zip(*[stream[0] for stream in streams]))
    odds = list(zip(*[stream[1] for stream in streams]))
    high, low, gram = assemble(here, block_place, offsets, householder, evens, odds, n_row)
    if tail:
        late = lax.all_to_all(after(piece, gram), "wide", split_axis=0, concat_axis=0, tiled=True)
    cross = spread(gram + swap(gram, 1, n_wide), n_wide)
    changes = merge(cross, wy_factor, (high, low))

    mine, theirs = inner_products(here, early, (high, low), True)
    mine = functools.reduce(jnp.add, spread(mine + swap(theirs, 1, n_wide), n_wide))
    total = rows if tail else rows * n_wide
    out = update(here, early, [mine], swap(mine, 1, n_wide), changes, None, 0, total)
    if tail:
        part, = inner_products(here, late, (high, low), False)
        out = update(here, late, spread(part + swap(part, 1, n_wide), n_wide), None, changes, out, bulk, total)
    return out.reshape(n_wide * rows, ncols)


def solution(mesh):
    return jax.shard_map(
        functools.partial(body, mesh.shape["row"], mesh.shape["wide"]),
        mesh=mesh,
        in_specs=(P(("row", "wide"), None), P("row", None, "wide"), P(), P(), P()),
        out_specs=P("row", "wide"),
        check_vma=False,
    )
```

```python
import functools

import jax
import jax.numpy as jnp
from jax import lax
from jax.experimental import pallas as pl
from jax.experimental.pallas import tpu as pltpu
from jax.sharding import PartitionSpec as P

HIGHEST = lax.Precision.HIGHEST
SMALL_LIMIT = 44 * 1024 * 1024
VMEM_LIMIT = 40 * 1024 * 1024
LARGE_LIMIT = 58 * 1024 * 1024
COLUMNS = 512
SPLITS = 2


def dot_t(a, b):
    return lax.dot_general(a, b, (((1,), (1,)), ((), ())), precision=HIGHEST, preferred_element_type=jnp.float32)


def dot(a, b):
    return lax.dot_general(a, b, (((1,), (0,)), ((), ())), precision=HIGHEST, preferred_element_type=jnp.float32)


def halves(x):
    high = x.astype(jnp.bfloat16)
    return high, (x - high.astype(jnp.float32)).astype(jnp.bfloat16)


def dot3(a, b, dims):
    rows = a[0].shape[0]
    both = lax.dot_general(jnp.concatenate(a, axis=0), b[0], (dims, ((), ())), preferred_element_type=jnp.float32)
    last = lax.dot_general(a[0], b[1], (dims, ((), ())), preferred_element_type=jnp.float32)
    return both[:rows] + (both[rows:] + last)


def after(x, *tokens):
    return lax.optimization_barrier((x, *tokens))[0]


def params(limit=VMEM_LIMIT):
    return pltpu.CompilerParams(vmem_limit_bytes=limit)


def cost(flops, nbytes):
    return pl.CostEstimate(flops=flops, bytes_accessed=nbytes, transcendentals=0)


SMEM = pl.BlockSpec(memory_space=pltpu.SMEM)
ANY = pl.BlockSpec(memory_space=pl.ANY)
VMEM = pl.BlockSpec(memory_space=pltpu.VMEM)


def in_hbm(x):
    return pltpu.with_memory_space_constraint(x, pltpu.HBM)


def pack(x, n_wide):
    rows, order = x.shape
    ncols = order // n_wide

    def kernel(x_ref, out_ref, held, in_sems, out_sems):
        into = [
            pltpu.make_async_copy(x_ref.at[:, pl.ds(k * ncols, ncols)], held.at[k], in_sems.at[k]) for k in range(n_wide)
        ]
        out_of = [pltpu.make_async_copy(held.at[k], out_ref.at[k], out_sems.at[k]) for k in range(n_wide)]
        for copy in into:
            copy.start()
        for k in range(n_wide):
            into[k].wait()
            out_of[k].start()
        for copy in out_of:
            copy.wait()

    return pl.pallas_call(
        kernel,
        out_shape=jax.ShapeDtypeStruct((n_wide, rows, ncols), jnp.float32),
        in_specs=[ANY],
        out_specs=ANY,
        scratch_shapes=[
            pltpu.VMEM((n_wide, rows, ncols), jnp.float32),
            pltpu.SemaphoreType.DMA((n_wide,)),
            pltpu.SemaphoreType.DMA((n_wide,)),
        ],
        compiler_params=params(limit=LARGE_LIMIT),
        cost_estimate=cost(0, 8 * rows * order),
        name="pack",
    )(in_hbm(x))


def plan(place_ref, slots, n_rows):
    places = [place_ref[s] for s in range(place_ref.shape[0])]
    roots = [lax.div(p, slots) for p in places]
    slot = [lax.rem(p, slots) for p in places]
    ranks = [sum([(roots[i] == roots[s]).astype(jnp.int32) for i in range(s)], jnp.int32(0)) for s in range(len(places))]
    counts = [sum([(r == i).astype(jnp.int32) for r in roots], jnp.int32(0)) for i in range(n_rows)]
    return roots, slot, ranks, counts


def feed(here, place, stack, evens, odds, n_rows, part, cols):
    slots, width, _ = stack.shape
    turn = len(evens)

    def kernel(here_ref, place_ref, stack_ref, *refs):
        arrived, (out_even, out_odd, sems) = refs[:-3], refs[-3:]
        roots, slot, ranks, _ = plan(place_ref, slots, n_rows)
        me = here_ref[0]
        mine = [r == me for r in roots]
        count = sum([m.astype(jnp.int32) for m in mine], jnp.int32(0))
        own = sum([jnp.where(m & (k == turn), s, 0) for m, k, s in zip(mine, ranks, slot)], jnp.int32(0))
        older = turn - jnp.maximum(count, 1)
        stored = stack_ref.at[own, :, pl.ds(part * cols, cols)]
        for side, out in ((0, out_even), (1, out_odd)):
            @pl.when((older < 0) | (count > turn))
            def _():
                pltpu.make_async_copy(stored, out, sems.at[side]).start()

            for i in range(turn):
                @pl.when((older == i) & (count <= turn))
                def _():
                    pltpu.make_async_copy(arrived[(1 - side) * turn + i], out, sems.at[side]).start()
        for side, out in ((0, out_even), (1, out_odd)):
            pltpu.make_async_copy(stored, out, sems.at[side]).wait()

    return pl.pallas_call(
        kernel,
        out_shape=[jax.ShapeDtypeStruct((width, cols), jnp.float32)] * 2,
        in_specs=[SMEM, SMEM, ANY] + [ANY] * (2 * turn),
        out_specs=[VMEM] * 2,
        scratch_shapes=[pltpu.SemaphoreType.DMA((2,))],
        compiler_params=params(limit=SMALL_LIMIT),
        cost_estimate=cost(0, 16 * width * cols),
        name="feed",
    )(here, place, stack, *evens, *odds)


def packed_width(steps, width):
    return -(-(width * steps * (steps - 1) // 2) // 128) * 128


def assemble(here, place, offsets, stack, evens, odds, n_rows):
    slots, width, ncols = stack.shape
    steps = place.shape[0]
    height = steps * width
    turns, splits = len(evens), len(evens[0])
    cols = ncols // splits

    def kernel(here_ref, place_ref, offset_ref, stack_ref, *refs):
        arrived, (high_ref, low_ref, gram_ref, held, sems) = refs[:-5], refs[-5:]
        even, odd = arrived[:turns * splits], arrived[turns * splits:]
        roots, slot, ranks, counts = plan(place_ref, slots, n_rows)
        me = here_ref[0]
        me_odd = lax.rem(me, 2) == 1
        for s in range(steps):
            root = roots[s]
            low, high = jnp.minimum(root, me), jnp.maximum(root, me)
            between = [jnp.where((i > low) & (i < high), jnp.maximum(counts[i], 1), 0) for i in range(n_rows)]
            turn = sum(between, ranks[s])
            target = held.at[pl.ds(s * width, width)]
            below, above = root < me, root > me

            @pl.when(root == me)
            def _():
                pltpu.make_async_copy(stack_ref.at[slot[s]], target, sems.at[s]).start()

            for side, came in (((below & me_odd) | (above & ~me_odd), even), ((below & ~me_odd) | (above & me_odd), odd)):
                for i in range(turns):
                    @pl.when(side & (turn == i))
                    def _():
                        for p in range(splits):
                            piece = held.at[pl.ds(s * width, width), pl.ds(p * cols, cols)]
                            pltpu.make_async_copy(came[i * splits + p], piece, sems.at[s]).start()
        columns = here_ref[1] * ncols + lax.broadcasted_iota(jnp.int32, (width, ncols), 1)
        for s in range(steps):
            rows = pl.ds(s * width, width)
            pltpu.make_async_copy(stack_ref.at[0], held.at[rows], sems.at[s]).wait()
            masked = jnp.where(columns >= offset_ref[s], held[rows, :], 0.0)
            held[rows, :] = masked
            high, low = halves(masked)
            high_ref[rows, :] = high
            low_ref[rows, :] = low
        gram = dot_t(held[...], held[...])
        gram_ref[...] = jnp.zeros_like(gram_ref)
        first = 0
        for s in range(1, steps):
            gram_ref[:, first:first + s * width] = gram[s * width:(s + 1) * width, :s * width]
            first += s * width

    return pl.pallas_call(
        kernel,
        out_shape=[
            jax.ShapeDtypeStruct((height, ncols), jnp.bfloat16),
            jax.ShapeDtypeStruct((height, ncols), jnp.bfloat16),
            jax.ShapeDtypeStruct((width, packed_width(steps, width)), jnp.float32),
        ],
        in_specs=[SMEM, SMEM, SMEM, ANY] + [ANY] * (2 * turns * splits),
        out_specs=[VMEM] * 3,
        scratch_shapes=[pltpu.VMEM((height, ncols), jnp.float32), pltpu.SemaphoreType.DMA((steps,))],
        compiler_params=params(limit=SMALL_LIMIT),
        cost_estimate=cost(12 * height * height * ncols, 8 * height * ncols),
        name="assemble",
    )(here, place, offsets, stack, *[p for turn in evens for p in turn], *[p for turn in odds for p in turn])


def merge(cross, factors, vecs):
    steps, width, _ = factors.shape
    height, ncols = vecs[0].shape

    def kernel(*refs):
        cross_refs, (factor_ref, v_high, v_low, p_high, p_low, total, m_ref) = refs[:-7], refs[-7:]
        total[...] = sum([ref[...] for ref in cross_refs[1:]], cross_refs[0][...])
        first = 0
        for k in range(steps):
            own = lax.broadcasted_iota(jnp.int32, (width, height), 0) + k * width
            rest = (own == lax.broadcasted_iota(jnp.int32, (width, height), 1)).astype(jnp.float32)
            if k:
                rest = rest - dot(total[:, first:first + k * width], m_ref[:k * width, :])
                first += k * width
            m_ref[k * width:(k + 1) * width, :] = dot(factor_ref[k], rest)
        product = dot3(halves(m_ref[...].T), (v_high[...], v_low[...]), ((1,), (0,)))
        p_high[...], p_low[...] = halves(product)

    return pl.pallas_call(
        kernel,
        out_shape=[jax.ShapeDtypeStruct((height, ncols), jnp.bfloat16)] * 2,
        out_specs=[VMEM] * 2,
        in_specs=[VMEM] * (len(cross) + 3),
        scratch_shapes=[pltpu.VMEM(cross[0].shape, jnp.float32), pltpu.VMEM((height, height), jnp.float32)],
        compiler_params=params(),
        cost_estimate=cost(6 * height * height * ncols, 8 * height * ncols),
        name="merge",
    )(*cross, factors, *vecs)


def fold(w):
    half = w.shape[0] // 2
    return jnp.concatenate([w[:half], w[half:]], axis=1)


def unfold(w):
    height = w.shape[1] // 2
    return jnp.concatenate([w[:, :height], w[:, height:]], axis=0)


def column_blocks(ncols):
    cols = COLUMNS if ncols % COLUMNS == 0 else ncols
    return [pl.ds(start, cols) for start in range(0, ncols, cols)]


def inner_products(here, x, vecs):
    lead, rows, ncols = x.shape
    height = vecs[0].shape[0]
    half = lead * rows // 2
    blocks = column_blocks(ncols)

    def kernel(here_ref, x_ref, high_ref, low_ref, mine_ref, theirs_ref, held, total, sems):
        copies = [pltpu.make_async_copy(x_ref.at[:, :, at], held.at[:, :, at], sems.at[i]) for i, at in enumerate(blocks)]
        for copy in copies:
            copy.start()
        for i, at in enumerate(blocks):
            copies[i].wait()
            block = held[:, :, at].reshape(lead * rows, at.size)
            part = dot3(halves(block), (high_ref[:, at], low_ref[:, at]), ((1,), (1,)))
            total[...] = part if i == 0 else total[...] + part
        core = lax.rem(here_ref[1], 2)
        mine_ref[...] = fold(total[pl.ds(pl.multiple_of(core * half, 8), half), :])
        theirs_ref[...] = fold(total[pl.ds(pl.multiple_of((1 - core) * half, 8), half), :])

    return pl.pallas_call(
        kernel,
        out_shape=[jax.ShapeDtypeStruct((half // 2, 2 * height), jnp.float32)] * 2 + [pltpu.VMEM(x.shape, jnp.float32)],
        in_specs=[SMEM, ANY, VMEM, VMEM],
        out_specs=[VMEM] * 3,
        scratch_shapes=[pltpu.VMEM((lead * rows, height), jnp.float32), pltpu.SemaphoreType.DMA((len(blocks),))],
        compiler_params=params(),
        cost_estimate=cost(6 * lead * rows * ncols * height, 4 * lead * rows * ncols),
        name="inner_products",
    )(here, in_hbm(x), *vecs)


def update(here, x, mine, theirs, changes):
    lead, rows, ncols = x.shape
    height = changes[0].shape[0]
    half = lead * rows // 2
    blocks = column_blocks(ncols)
    depth = min(2, len(blocks))

    def kernel(here_ref, mine_ref, theirs_ref, x_ref, high_ref, low_ref, out_ref, w_ref, held, sems):
        core = lax.rem(here_ref[1], 2)
        w_ref[pl.ds(pl.multiple_of(core * half, 8), half), :] = unfold(mine_ref[...])
        w_ref[pl.ds(pl.multiple_of((1 - core) * half, 8), half), :] = unfold(theirs_ref[...])
        w = halves(w_ref[...])
        copies = [pltpu.make_async_copy(held.at[i % depth], out_ref.at[:, :, at], sems.at[i]) for i, at in enumerate(blocks)]
        for i, at in enumerate(blocks):
            change = dot3(w, (high_ref[:, at], low_ref[:, at]), ((1,), (0,)))
            if i >= depth:
                copies[i - depth].wait()
            held[i % depth] = x_ref[:, :, at] - change.reshape(lead, rows, at.size)
            copies[i].start()
        for copy in copies[-depth:]:
            copy.wait()

    return pl.pallas_call(
        kernel,
        out_shape=jax.ShapeDtypeStruct(x.shape, jnp.float32),
        in_specs=[SMEM] + [VMEM] * 5,
        out_specs=ANY,
        scratch_shapes=[
            pltpu.VMEM((lead * rows, height), jnp.float32),
            pltpu.VMEM((depth, lead, rows, blocks[0].size), jnp.float32),
            pltpu.SemaphoreType.DMA((len(blocks),)),
        ],
        compiler_params=params(),
        cost_estimate=cost(6 * lead * rows * ncols * height, 8 * lead * rows * ncols),
        name="update",
    )(here, mine, theirs, x, *changes)


def swap(array, k, size):
    return lax.ppermute(array, "wide", [(i, i ^ k) for i in range(size)])


def spread(pair, size):
    return [pair] + [swap(pair, k, size) for k in range(2, size, 2)]


def body(n_row, n_wide, eigvec_t, householder, wy_factor, block_place, offsets):
    rows, order = eigvec_t.shape
    steps, width, _ = wy_factor.shape
    slots = householder.shape[0]
    ncols = order // n_wide
    here = jnp.stack([lax.axis_index("row"), lax.axis_index("wide")]).astype(jnp.int32)

    turns = max(z + min(steps - 1, slots * (n_row - 1 - z)) for z in range(n_row - 1))
    cols = ncols // SPLITS
    streams = [([], []) for _ in range(SPLITS)]

    def exchange(array, odd):
        pairs = []
        for z in range(n_row):
            mate = ((z + odd) ^ 1) - odd
            for w in range(n_wide):
                target = mate * n_wide + w if 0 <= mate < n_row else z * n_wide + (w ^ 1)
                pairs.append((z * n_wide + w, target))
        return lax.ppermute(array, ("row", "wide"), pairs)

    whole = rows % 8 == 0
    if whole:
        piece = pack(eigvec_t, n_wide)
        x = lax.all_to_all(piece, "wide", split_axis=0, concat_axis=0, tiled=True)
        tokens = [piece]
    else:
        x = lax.all_to_all(eigvec_t, "wide", split_axis=1, concat_axis=0, tiled=True)[None]
        tokens = []
    for turn in range(turns):
        for part in range(SPLITS):
            evens, odds = streams[part]
            to_even, to_odd = feed(after(here, *tokens), block_place, householder, evens, odds, n_row, part, cols)
            tokens = [to_odd]
            streams[part] = (evens + [exchange(to_even, 0)], odds + [exchange(to_odd, 1)])
    evens = list(zip(*[stream[0] for stream in streams]))
    odds = list(zip(*[stream[1] for stream in streams]))
    high, low, gram = assemble(here, block_place, offsets, householder, evens, odds, n_row)
    cross = spread(gram + swap(gram, 1, n_wide), n_wide)
    changes = merge(cross, wy_factor, (high, low))

    mine, theirs, x = inner_products(here, x, (high, low))
    mine = functools.reduce(jnp.add, spread(mine + swap(theirs, 1, n_wide), n_wide))
    return update(here, x, mine, swap(mine, 1, n_wide), changes).reshape(n_wide * rows, ncols)


def solution(mesh):
    return jax.shard_map(
        functools.partial(body, mesh.shape["row"], mesh.shape["wide"]),
        mesh=mesh,
        in_specs=(P(("row", "wide"), None), P("row", None, "wide"), P(), P(), P()),
        out_specs=P("row", "wide"),
        check_vma=False,
    )
```

```python
import functools

import jax
import jax.numpy as jnp
from jax import lax
from jax.experimental import pallas as pl
from jax.experimental.pallas import tpu as pltpu
from jax.sharding import PartitionSpec as P

HIGHEST = lax.Precision.HIGHEST
SMALL_LIMIT = 44 * 1024 * 1024
VMEM_LIMIT = 40 * 1024 * 1024
LARGE_LIMIT = 58 * 1024 * 1024
COLUMNS = 512
SPLITS = 2


def dot_t(a, b):
    return lax.dot_general(a, b, (((1,), (1,)), ((), ())), precision=HIGHEST, preferred_element_type=jnp.float32)


def dot(a, b):
    return lax.dot_general(a, b, (((1,), (0,)), ((), ())), precision=HIGHEST, preferred_element_type=jnp.float32)


def halves(x):
    high = x.astype(jnp.bfloat16)
    return high, (x - high.astype(jnp.float32)).astype(jnp.bfloat16)


def dot3(a, b, dims):
    rows = a[0].shape[0]
    both = lax.dot_general(jnp.concatenate(a, axis=0), b[0], (dims, ((), ())), preferred_element_type=jnp.float32)
    last = lax.dot_general(a[0], b[1], (dims, ((), ())), preferred_element_type=jnp.float32)
    return both[:rows] + (both[rows:] + last)


def after(x, *tokens):
    return lax.optimization_barrier((x, *tokens))[0]


def params(limit=VMEM_LIMIT):
    return pltpu.CompilerParams(vmem_limit_bytes=limit)


def cost(flops, nbytes):
    return pl.CostEstimate(flops=flops, bytes_accessed=nbytes, transcendentals=0)


SMEM = pl.BlockSpec(memory_space=pltpu.SMEM)
ANY = pl.BlockSpec(memory_space=pl.ANY)
VMEM = pl.BlockSpec(memory_space=pltpu.VMEM)


def in_hbm(x):
    return pltpu.with_memory_space_constraint(x, pltpu.HBM)


def pack(x, n_wide):
    rows, order = x.shape
    ncols = order // n_wide
    step = 16 if rows % 16 == 0 else rows
    n_copies = n_wide * rows // step

    def kernel(x_ref, out_ref, held, in_sems, out_sems):
        into, out_of = [], []
        for first in range(0, rows, step):
            for k in range(n_wide):
                i, at = len(into), pl.ds(first, step)
                source = x_ref.at[at, pl.ds(k * ncols, ncols)]
                into.append(pltpu.make_async_copy(source, held.at[k, at], in_sems.at[i]))
                out_of.append(pltpu.make_async_copy(held.at[k, at], out_ref.at[k, at], out_sems.at[i]))
        for copy in into:
            copy.start()
        for came, goes in zip(into, out_of):
            came.wait()
            goes.start()
        for copy in out_of:
            copy.wait()

    return pl.pallas_call(
        kernel,
        out_shape=jax.ShapeDtypeStruct((n_wide, rows, ncols), jnp.float32),
        in_specs=[ANY],
        out_specs=ANY,
        scratch_shapes=[
            pltpu.VMEM((n_wide, rows, ncols), jnp.float32),
            pltpu.SemaphoreType.DMA((n_copies,)),
            pltpu.SemaphoreType.DMA((n_copies,)),
        ],
        compiler_params=params(limit=LARGE_LIMIT),
        cost_estimate=cost(0, 8 * rows * order),
        name="pack",
    )(in_hbm(x))


def plan(place_ref, slots, n_rows):
    places = [place_ref[s] for s in range(place_ref.shape[0])]
    roots = [lax.div(p, slots) for p in places]
    slot = [lax.rem(p, slots) for p in places]
    ranks = [sum([(roots[i] == roots[s]).astype(jnp.int32) for i in range(s)], jnp.int32(0)) for s in range(len(places))]
    counts = [sum([(r == i).astype(jnp.int32) for r in roots], jnp.int32(0)) for i in range(n_rows)]
    return roots, slot, ranks, counts


def feed(here, place, stack, evens, odds, n_rows, part, cols):
    slots, width, _ = stack.shape
    turn = len(evens)

    def kernel(here_ref, place_ref, stack_ref, *refs):
        arrived, (out_even, out_odd, sems) = refs[:-3], refs[-3:]
        roots, slot, ranks, _ = plan(place_ref, slots, n_rows)
        me = here_ref[0]
        mine = [r == me for r in roots]
        count = sum([m.astype(jnp.int32) for m in mine], jnp.int32(0))
        own = sum([jnp.where(m & (k == turn), s, 0) for m, k, s in zip(mine, ranks, slot)], jnp.int32(0))
        older = turn - jnp.maximum(count, 1)
        stored = stack_ref.at[own, :, pl.ds(part * cols, cols)]
        for side, out in ((0, out_even), (1, out_odd)):
            @pl.when((older < 0) | (count > turn))
            def _():
                pltpu.make_async_copy(stored, out, sems.at[side]).start()

            for i in range(turn):
                @pl.when((older == i) & (count <= turn))
                def _():
                    pltpu.make_async_copy(arrived[(1 - side) * turn + i], out, sems.at[side]).start()
        for side, out in ((0, out_even), (1, out_odd)):
            pltpu.make_async_copy(stored, out, sems.at[side]).wait()

    return pl.pallas_call(
        kernel,
        out_shape=[jax.ShapeDtypeStruct((width, cols), jnp.float32)] * 2,
        in_specs=[SMEM, SMEM, ANY] + [ANY] * (2 * turn),
        out_specs=[VMEM] * 2,
        scratch_shapes=[pltpu.SemaphoreType.DMA((2,))],
        compiler_params=params(limit=SMALL_LIMIT),
        cost_estimate=cost(0, 16 * width * cols),
        name="feed",
    )(here, place, stack, *evens, *odds)


def packed_width(steps, width):
    return -(-(width * steps * (steps - 1) // 2) // 128) * 128


def assemble(here, place, offsets, stack, evens, odds, n_rows):
    slots, width, ncols = stack.shape
    steps = place.shape[0]
    height = steps * width
    turns, splits = len(evens), len(evens[0])
    cols = ncols // splits

    def kernel(here_ref, place_ref, offset_ref, stack_ref, *refs):
        arrived, (high_ref, low_ref, high_t_ref, low_t_ref, gram_ref, held, sems) = refs[:-7], refs[-7:]
        even, odd = arrived[:turns * splits], arrived[turns * splits:]
        roots, slot, ranks, counts = plan(place_ref, slots, n_rows)
        me = here_ref[0]
        me_odd = lax.rem(me, 2) == 1
        for s in range(steps):
            root = roots[s]
            low, high = jnp.minimum(root, me), jnp.maximum(root, me)
            between = [jnp.where((i > low) & (i < high), jnp.maximum(counts[i], 1), 0) for i in range(n_rows)]
            turn = sum(between, ranks[s])
            target = held.at[pl.ds(s * width, width)]
            below, above = root < me, root > me

            @pl.when(root == me)
            def _():
                pltpu.make_async_copy(stack_ref.at[slot[s]], target, sems.at[s]).start()

            for side, came in (((below & me_odd) | (above & ~me_odd), even), ((below & ~me_odd) | (above & me_odd), odd)):
                for i in range(turns):
                    @pl.when(side & (turn == i))
                    def _():
                        for p in range(splits):
                            piece = held.at[pl.ds(s * width, width), pl.ds(p * cols, cols)]
                            pltpu.make_async_copy(came[i * splits + p], piece, sems.at[s]).start()
        columns = here_ref[1] * ncols + lax.broadcasted_iota(jnp.int32, (width, ncols), 1)
        for s in range(steps):
            rows = pl.ds(s * width, width)
            pltpu.make_async_copy(stack_ref.at[0], held.at[rows], sems.at[s]).wait()
            masked = jnp.where(columns >= offset_ref[s], held[rows, :], 0.0)
            held[rows, :] = masked
            high, low = halves(masked)
            high_ref[rows, :] = high
            low_ref[rows, :] = low
        for at in column_blocks(ncols):
            high_t_ref[at, :], low_t_ref[at, :] = halves(held[:, at].T)
        gram = dot_t(held[...], held[...])
        gram_ref[...] = jnp.zeros_like(gram_ref)
        first = 0
        for s in range(1, steps):
            gram_ref[:, first:first + s * width] = gram[s * width:(s + 1) * width, :s * width]
            first += s * width

    return pl.pallas_call(
        kernel,
        out_shape=[
            jax.ShapeDtypeStruct((height, ncols), jnp.bfloat16),
            jax.ShapeDtypeStruct((height, ncols), jnp.bfloat16),
            jax.ShapeDtypeStruct((ncols, height), jnp.bfloat16),
            jax.ShapeDtypeStruct((ncols, height), jnp.bfloat16),
            jax.ShapeDtypeStruct((width, packed_width(steps, width)), jnp.float32),
        ],
        in_specs=[SMEM, SMEM, SMEM, ANY] + [ANY] * (2 * turns * splits),
        out_specs=[VMEM] * 5,
        scratch_shapes=[pltpu.VMEM((height, ncols), jnp.float32), pltpu.SemaphoreType.DMA((steps,))],
        compiler_params=params(limit=SMALL_LIMIT),
        cost_estimate=cost(12 * height * height * ncols, 8 * height * ncols),
        name="assemble",
    )(here, place, offsets, stack, *[p for turn in evens for p in turn], *[p for turn in odds for p in turn])


def merge(cross, factors, vecs):
    steps, width, _ = factors.shape
    height, ncols = vecs[0].shape

    def kernel(*refs):
        cross_refs, (factor_ref, v_high, v_low, p_ref, total, m_ref) = refs[:-6], refs[-6:]
        total[...] = sum([ref[...] for ref in cross_refs[1:]], cross_refs[0][...])
        first = 0
        for k in range(steps):
            own = lax.broadcasted_iota(jnp.int32, (width, height), 0) + k * width
            rest = (own == lax.broadcasted_iota(jnp.int32, (width, height), 1)).astype(jnp.float32)
            if k:
                rest = rest - dot(total[:, first:first + k * width], m_ref[:k * width, :])
                first += k * width
            m_ref[k * width:(k + 1) * width, :] = dot(factor_ref[k], rest)
        product = dot3(halves(m_ref[...].T), (v_high[...], v_low[...]), ((1,), (0,)))
        high, low = halves(product)
        for i, half in enumerate((high, high, low)):
            p_ref[i * height:(i + 1) * height, :] = half

    return pl.pallas_call(
        kernel,
        out_shape=jax.ShapeDtypeStruct((3 * height, ncols), jnp.bfloat16),
        out_specs=VMEM,
        in_specs=[VMEM] * (len(cross) + 3),
        scratch_shapes=[pltpu.VMEM(cross[0].shape, jnp.float32), pltpu.VMEM((height, height), jnp.float32)],
        compiler_params=params(),
        cost_estimate=cost(6 * height * height * ncols, 8 * height * ncols),
        name="merge",
    )(*cross, factors, *vecs)


def fold(w):
    half = w.shape[0] // 2
    return jnp.concatenate([w[:half], w[half:]], axis=1)


def unfold(w):
    height = w.shape[1] // 2
    return jnp.concatenate([w[:, :height], w[:, height:]], axis=0)


def column_blocks(ncols):
    cols = COLUMNS if ncols % COLUMNS == 0 else ncols
    return [pl.ds(start, cols) for start in range(0, ncols, cols)]


def inner_products(here, x, vecs_t):
    lead, rows, ncols = x.shape
    height = vecs_t[0].shape[1]
    half = lead * rows // 2
    cuts = [0, lead // 4, lead] if lead % 4 == 0 else [0, lead]

    def kernel(here_ref, x_ref, high_ref, low_ref, mine_ref, theirs_ref, held, total, sems):
        copies = [pltpu.make_async_copy(x_ref.at[i], held.at[i], sems.at[i]) for i in range(lead)]
        for copy in copies:
            copy.start()
        for start, end in zip(cuts[:-1], cuts[1:]):
            for copy in copies[start:end]:
                copy.wait()
            block = held[start:end].reshape((end - start) * rows, ncols)
            total[start * rows:end * rows, :] = dot3(halves(block), (high_ref[...], low_ref[...]), ((1,), (0,)))
        core = lax.rem(here_ref[1], 2)
        mine_ref[...] = fold(total[pl.ds(pl.multiple_of(core * half, 8), half), :])
        theirs_ref[...] = fold(total[pl.ds(pl.multiple_of((1 - core) * half, 8), half), :])

    return pl.pallas_call(
        kernel,
        out_shape=[jax.ShapeDtypeStruct((half // 2, 2 * height), jnp.float32)] * 2 + [pltpu.VMEM(x.shape, jnp.float32)],
        in_specs=[SMEM, ANY, VMEM, VMEM],
        out_specs=[VMEM] * 3,
        scratch_shapes=[pltpu.VMEM((lead * rows, height), jnp.float32), pltpu.SemaphoreType.DMA((lead,))],
        compiler_params=params(),
        cost_estimate=cost(6 * lead * rows * ncols * height, 4 * lead * rows * ncols),
        name="inner_products",
    )(here, in_hbm(x), *vecs_t)


def update(here, x, mine, theirs, changes):
    lead, rows, ncols = x.shape
    height = changes.shape[0] // 3
    half = lead * rows // 2
    blocks = column_blocks(ncols)
    depth = min(2, len(blocks))

    def kernel(here_ref, mine_ref, theirs_ref, x_ref, p_ref, out_ref, w_ref, held, sems):
        core = lax.rem(here_ref[1], 2)
        w_ref[pl.ds(pl.multiple_of(core * half, 8), half), :] = unfold(mine_ref[...])
        w_ref[pl.ds(pl.multiple_of((1 - core) * half, 8), half), :] = unfold(theirs_ref[...])
        high, low = halves(w_ref[...])
        w = jnp.concatenate([high, low, high], axis=1)
        copies = [pltpu.make_async_copy(held.at[i % depth], out_ref.at[:, :, at], sems.at[i]) for i, at in enumerate(blocks)]
        for i, at in enumerate(blocks):
            change = lax.dot_general(w, p_ref[:, at], (((1,), (0,)), ((), ())), preferred_element_type=jnp.float32)
            if i >= depth:
                copies[i - depth].wait()
            held[i % depth] = x_ref[:, :, at] - change.reshape(lead, rows, at.size)
            copies[i].start()
        for copy in copies[-depth:]:
            copy.wait()

    return pl.pallas_call(
        kernel,
        out_shape=jax.ShapeDtypeStruct(x.shape, jnp.float32),
        in_specs=[SMEM] + [VMEM] * 4,
        out_specs=ANY,
        scratch_shapes=[
            pltpu.VMEM((lead * rows, height), jnp.float32),
            pltpu.VMEM((depth, lead, rows, blocks[0].size), jnp.float32),
            pltpu.SemaphoreType.DMA((len(blocks),)),
        ],
        compiler_params=params(),
        cost_estimate=cost(6 * lead * rows * ncols * height, 8 * lead * rows * ncols),
        name="update",
    )(here, mine, theirs, x, changes)


def swap(array, k, size):
    return lax.ppermute(array, "wide", [(i, i ^ k) for i in range(size)])


def spread(pair, size):
    return [pair] + [swap(pair, k, size) for k in range(2, size, 2)]


def body(n_row, n_wide, eigvec_t, householder, wy_factor, block_place, offsets):
    rows, order = eigvec_t.shape
    steps, width, _ = wy_factor.shape
    slots = householder.shape[0]
    ncols = order // n_wide
    here = jnp.stack([lax.axis_index("row"), lax.axis_index("wide")]).astype(jnp.int32)

    turns = max(z + min(steps - 1, slots * (n_row - 1 - z)) for z in range(n_row - 1))
    cols = ncols // SPLITS
    streams = [([], []) for _ in range(SPLITS)]

    def exchange(array, odd):
        pairs = []
        for z in range(n_row):
            mate = ((z + odd) ^ 1) - odd
            for w in range(n_wide):
                target = mate * n_wide + w if 0 <= mate < n_row else z * n_wide + (w ^ 1)
                pairs.append((z * n_wide + w, target))
        return lax.ppermute(array, ("row", "wide"), pairs)

    whole = rows % 8 == 0
    if whole:
        piece = pack(eigvec_t, n_wide)
        x = lax.all_to_all(piece, "wide", split_axis=0, concat_axis=0, tiled=True)
        tokens = [piece]
    else:
        x = lax.all_to_all(eigvec_t, "wide", split_axis=1, concat_axis=0, tiled=True)[None]
        tokens = []
    for turn in range(turns):
        for part in range(SPLITS):
            evens, odds = streams[part]
            to_even, to_odd = feed(after(here, *tokens), block_place, householder, evens, odds, n_row, part, cols)
            tokens = [to_odd]
            streams[part] = (evens + [exchange(to_even, 0)], odds + [exchange(to_odd, 1)])
    evens = list(zip(*[stream[0] for stream in streams]))
    odds = list(zip(*[stream[1] for stream in streams]))
    high, low, high_t, low_t, gram = assemble(here, block_place, offsets, householder, evens, odds, n_row)
    cross = spread(gram + swap(gram, 1, n_wide), n_wide)
    changes = merge(cross, wy_factor, (high, low))

    mine, theirs, x = inner_products(after(here, *cross), x, (high_t, low_t))
    mine = functools.reduce(jnp.add, spread(mine + swap(theirs, 1, n_wide), n_wide))
    return update(here, x, mine, swap(mine, 1, n_wide), changes).reshape(n_wide * rows, ncols)


def solution(mesh):
    return jax.shard_map(
        functools.partial(body, mesh.shape["row"], mesh.shape["wide"]),
        mesh=mesh,
        in_specs=(P(("row", "wide"), None), P("row", None, "wide"), P(), P(), P()),
        out_specs=P("row", "wide"),
        check_vma=False,
    )
```

```python
import functools

import jax
import jax.numpy as jnp
from jax import lax
from jax.experimental import pallas as pl
from jax.experimental.pallas import tpu as pltpu
from jax.sharding import PartitionSpec as P

HIGHEST = lax.Precision.HIGHEST
SMALL_LIMIT = 44 * 1024 * 1024
VMEM_LIMIT = 40 * 1024 * 1024
LARGE_LIMIT = 58 * 1024 * 1024
COLUMNS = 512
SPLITS = 2


def dot_t(a, b):
    return lax.dot_general(a, b, (((1,), (1,)), ((), ())), precision=HIGHEST, preferred_element_type=jnp.float32)


def dot(a, b):
    return lax.dot_general(a, b, (((1,), (0,)), ((), ())), precision=HIGHEST, preferred_element_type=jnp.float32)


def halves(x):
    high = x.astype(jnp.bfloat16)
    return high, (x - high.astype(jnp.float32)).astype(jnp.bfloat16)


def dot3(a, b, dims):
    rows = a[0].shape[0]
    both = lax.dot_general(jnp.concatenate(a, axis=0), b[0], (dims, ((), ())), preferred_element_type=jnp.float32)
    last = lax.dot_general(a[0], b[1], (dims, ((), ())), preferred_element_type=jnp.float32)
    return both[:rows] + (both[rows:] + last)


def after(x, *tokens):
    return lax.optimization_barrier((x, *tokens))[0]


def params(limit=VMEM_LIMIT):
    return pltpu.CompilerParams(vmem_limit_bytes=limit)


def cost(flops, nbytes):
    return pl.CostEstimate(flops=flops, bytes_accessed=nbytes, transcendentals=0)


SMEM = pl.BlockSpec(memory_space=pltpu.SMEM)
ANY = pl.BlockSpec(memory_space=pl.ANY)
VMEM = pl.BlockSpec(memory_space=pltpu.VMEM)


def in_hbm(x):
    return pltpu.with_memory_space_constraint(x, pltpu.HBM)


def pack(x, n_wide):
    rows, order = x.shape
    ncols = order // n_wide
    step = 16 if rows % 16 == 0 else rows
    n_copies = n_wide * rows // step

    def kernel(x_ref, out_ref, held, in_sems, out_sems):
        into, out_of = [], []
        for first in range(0, rows, step):
            for k in range(n_wide):
                i, at = len(into), pl.ds(first, step)
                source = x_ref.at[at, pl.ds(k * ncols, ncols)]
                into.append(pltpu.make_async_copy(source, held.at[k, at], in_sems.at[i]))
                out_of.append(pltpu.make_async_copy(held.at[k, at], out_ref.at[k, at], out_sems.at[i]))
        for copy in into:
            copy.start()
        for came, goes in zip(into, out_of):
            came.wait()
            goes.start()
        for copy in out_of:
            copy.wait()

    return pl.pallas_call(
        kernel,
        out_shape=jax.ShapeDtypeStruct((n_wide, rows, ncols), jnp.float32),
        in_specs=[ANY],
        out_specs=ANY,
        scratch_shapes=[
            pltpu.VMEM((n_wide, rows, ncols), jnp.float32),
            pltpu.SemaphoreType.DMA((n_copies,)),
            pltpu.SemaphoreType.DMA((n_copies,)),
        ],
        compiler_params=params(limit=LARGE_LIMIT),
        cost_estimate=cost(0, 8 * rows * order),
        name="pack",
    )(in_hbm(x))


def plan(place_ref, slots, n_rows):
    places = [place_ref[s] for s in range(place_ref.shape[0])]
    roots = [lax.div(p, slots) for p in places]
    slot = [lax.rem(p, slots) for p in places]
    ranks = [sum([(roots[i] == roots[s]).astype(jnp.int32) for i in range(s)], jnp.int32(0)) for s in range(len(places))]
    counts = [sum([(r == i).astype(jnp.int32) for r in roots], jnp.int32(0)) for i in range(n_rows)]
    return roots, slot, ranks, counts


def feed(here, place, stack, evens, odds, n_rows, part, cols):
    slots, width, _ = stack.shape
    turn = len(evens)

    def kernel(here_ref, place_ref, stack_ref, *refs):
        arrived, (out_even, out_odd, sems) = refs[:-3], refs[-3:]
        roots, slot, ranks, _ = plan(place_ref, slots, n_rows)
        me = here_ref[0]
        mine = [r == me for r in roots]
        count = sum([m.astype(jnp.int32) for m in mine], jnp.int32(0))
        own = sum([jnp.where(m & (k == turn), s, 0) for m, k, s in zip(mine, ranks, slot)], jnp.int32(0))
        older = turn - jnp.maximum(count, 1)
        stored = stack_ref.at[own, :, pl.ds(part * cols, cols)]
        for side, out in ((0, out_even), (1, out_odd)):
            @pl.when((older < 0) | (count > turn))
            def _():
                pltpu.make_async_copy(stored, out, sems.at[side]).start()

            for i in range(turn):
                @pl.when((older == i) & (count <= turn))
                def _():
                    pltpu.make_async_copy(arrived[(1 - side) * turn + i], out, sems.at[side]).start()
        for side, out in ((0, out_even), (1, out_odd)):
            pltpu.make_async_copy(stored, out, sems.at[side]).wait()

    return pl.pallas_call(
        kernel,
        out_shape=[jax.ShapeDtypeStruct((width, cols), jnp.float32)] * 2,
        in_specs=[SMEM, SMEM, ANY] + [ANY] * (2 * turn),
        out_specs=[VMEM] * 2,
        scratch_shapes=[pltpu.SemaphoreType.DMA((2,))],
        compiler_params=params(limit=SMALL_LIMIT),
        cost_estimate=cost(0, 16 * width * cols),
        name="feed",
    )(here, place, stack, *evens, *odds)


def packed_width(steps, width):
    return -(-(width * steps * (steps - 1) // 2) // 128) * 128


def assemble(here, place, offsets, stack, evens, odds, n_rows):
    slots, width, ncols = stack.shape
    steps = place.shape[0]
    height = steps * width
    turns, splits = len(evens), len(evens[0])
    cols = ncols // splits

    def kernel(here_ref, place_ref, offset_ref, stack_ref, *refs):
        arrived, (high_ref, low_ref, high_t_ref, low_t_ref, gram_ref, held, sems) = refs[:-7], refs[-7:]
        even, odd = arrived[:turns * splits], arrived[turns * splits:]
        roots, slot, ranks, counts = plan(place_ref, slots, n_rows)
        me = here_ref[0]
        me_odd = lax.rem(me, 2) == 1
        for s in range(steps):
            root = roots[s]
            low, high = jnp.minimum(root, me), jnp.maximum(root, me)
            between = [jnp.where((i > low) & (i < high), jnp.maximum(counts[i], 1), 0) for i in range(n_rows)]
            turn = sum(between, ranks[s])
            target = held.at[pl.ds(s * width, width)]
            below, above = root < me, root > me

            @pl.when(root == me)
            def _():
                pltpu.make_async_copy(stack_ref.at[slot[s]], target, sems.at[s]).start()

            for side, came in (((below & me_odd) | (above & ~me_odd), even), ((below & ~me_odd) | (above & me_odd), odd)):
                for i in range(turns):
                    @pl.when(side & (turn == i))
                    def _():
                        for p in range(splits):
                            piece = held.at[pl.ds(s * width, width), pl.ds(p * cols, cols)]
                            pltpu.make_async_copy(came[i * splits + p], piece, sems.at[s]).start()
        columns = here_ref[1] * ncols + lax.broadcasted_iota(jnp.int32, (width, ncols), 1)
        for s in range(steps):
            rows = pl.ds(s * width, width)
            pltpu.make_async_copy(stack_ref.at[0], held.at[rows], sems.at[s]).wait()
            masked = jnp.where(columns >= offset_ref[s], held[rows, :], 0.0)
            held[rows, :] = masked
            high, low = halves(masked)
            high_ref[rows, :] = high
            low_ref[rows, :] = low
        for at in column_blocks(ncols):
            high_t_ref[at, :], low_t_ref[at, :] = halves(held[:, at].T)
        gram = dot_t(held[...], held[...])
        gram_ref[...] = jnp.zeros_like(gram_ref)
        first = 0
        for s in range(1, steps):
            gram_ref[:, first:first + s * width] = gram[s * width:(s + 1) * width, :s * width]
            first += s * width

    return pl.pallas_call(
        kernel,
        out_shape=[
            pltpu.HBM((height, ncols), jnp.bfloat16),
            pltpu.HBM((height, ncols), jnp.bfloat16),
            pltpu.HBM((ncols, height), jnp.bfloat16),
            pltpu.HBM((ncols, height), jnp.bfloat16),
            jax.ShapeDtypeStruct((width, packed_width(steps, width)), jnp.float32),
        ],
        in_specs=[SMEM, SMEM, SMEM, ANY] + [ANY] * (2 * turns * splits),
        out_specs=[VMEM] * 5,
        scratch_shapes=[pltpu.VMEM((height, ncols), jnp.float32), pltpu.SemaphoreType.DMA((steps,))],
        compiler_params=params(limit=SMALL_LIMIT),
        cost_estimate=cost(12 * height * height * ncols, 8 * height * ncols),
        name="assemble",
    )(here, place, offsets, stack, *[p for turn in evens for p in turn], *[p for turn in odds for p in turn])


def merge(cross, factors, vecs):
    steps, width, _ = factors.shape
    height, ncols = vecs[0].shape

    def kernel(*refs):
        cross_refs, (factor_ref, v_high, v_low, p_ref, total, m_ref) = refs[:-6], refs[-6:]
        total[...] = sum([ref[...] for ref in cross_refs[1:]], cross_refs[0][...])
        first = 0
        for k in range(steps):
            own = lax.broadcasted_iota(jnp.int32, (width, height), 0) + k * width
            rest = (own == lax.broadcasted_iota(jnp.int32, (width, height), 1)).astype(jnp.float32)
            if k:
                rest = rest - dot(total[:, first:first + k * width], m_ref[:k * width, :])
                first += k * width
            m_ref[k * width:(k + 1) * width, :] = dot(factor_ref[k], rest)
        product = dot3(halves(m_ref[...].T), (v_high[...], v_low[...]), ((1,), (0,)))
        high, low = halves(product)
        for i, half in enumerate((high, high, low)):
            p_ref[i * height:(i + 1) * height, :] = half

    return pl.pallas_call(
        kernel,
        out_shape=jax.ShapeDtypeStruct((3 * height, ncols), jnp.bfloat16),
        out_specs=VMEM,
        in_specs=[VMEM] * (len(cross) + 3),
        scratch_shapes=[pltpu.VMEM(cross[0].shape, jnp.float32), pltpu.VMEM((height, height), jnp.float32)],
        compiler_params=params(),
        cost_estimate=cost(6 * height * height * ncols, 8 * height * ncols),
        name="merge",
    )(*cross, factors, *vecs)


def fold(w):
    half = w.shape[0] // 2
    return jnp.concatenate([w[:half], w[half:]], axis=1)


def unfold(w):
    height = w.shape[1] // 2
    return jnp.concatenate([w[:, :height], w[:, height:]], axis=0)


def column_blocks(ncols):
    cols = COLUMNS if ncols % COLUMNS == 0 else ncols
    return [pl.ds(start, cols) for start in range(0, ncols, cols)]


def inner_products(here, x, vecs_t):
    lead, rows, ncols = x.shape
    height = vecs_t[0].shape[1]
    half = lead * rows // 2
    cuts = [0, lead // 4, lead] if lead % 4 == 0 else [0, lead]

    def kernel(here_ref, x_ref, high_hbm, low_hbm, mine_ref, theirs_ref, held, high_ref, low_ref, total, sems):
        vecs = [pltpu.make_async_copy(high_hbm, high_ref, sems.at[lead]), pltpu.make_async_copy(low_hbm, low_ref, sems.at[lead + 1])]
        copies = [pltpu.make_async_copy(x_ref.at[i], held.at[i], sems.at[i]) for i in range(lead)]
        vecs[0].start()
        for copy in copies[:cuts[1]]:
            copy.start()
        vecs[1].start()
        for copy in copies[cuts[1]:]:
            copy.start()
        for start, end in zip(cuts[:-1], cuts[1:]):
            for copy in copies[start:end]:
                copy.wait()
            if start == 0:
                for copy in vecs:
                    copy.wait()
            block = held[start:end].reshape((end - start) * rows, ncols)
            total[start * rows:end * rows, :] = dot3(halves(block), (high_ref[...], low_ref[...]), ((1,), (0,)))
        core = lax.rem(here_ref[1], 2)
        mine_ref[...] = fold(total[pl.ds(pl.multiple_of(core * half, 8), half), :])
        theirs_ref[...] = fold(total[pl.ds(pl.multiple_of((1 - core) * half, 8), half), :])

    return pl.pallas_call(
        kernel,
        out_shape=[jax.ShapeDtypeStruct((half // 2, 2 * height), jnp.float32)] * 2 + [pltpu.VMEM(x.shape, jnp.float32)],
        in_specs=[SMEM, ANY, ANY, ANY],
        out_specs=[VMEM] * 3,
        scratch_shapes=[
            pltpu.VMEM((ncols, height), jnp.bfloat16),
            pltpu.VMEM((ncols, height), jnp.bfloat16),
            pltpu.VMEM((lead * rows, height), jnp.float32),
            pltpu.SemaphoreType.DMA((lead + 2,)),
        ],
        compiler_params=params(),
        cost_estimate=cost(6 * lead * rows * ncols * height, 4 * lead * rows * ncols),
        name="inner_products",
    )(here, in_hbm(x), *[in_hbm(v) for v in vecs_t])


def update(here, x, mine, theirs, changes):
    lead, rows, ncols = x.shape
    height = changes.shape[0] // 3
    half = lead * rows // 2
    blocks = column_blocks(ncols)
    depth = min(2, len(blocks))

    def kernel(here_ref, mine_ref, theirs_ref, x_ref, p_ref, out_ref, w_ref, held, sems):
        core = lax.rem(here_ref[1], 2)
        w_ref[pl.ds(pl.multiple_of(core * half, 8), half), :] = unfold(mine_ref[...])
        w_ref[pl.ds(pl.multiple_of((1 - core) * half, 8), half), :] = unfold(theirs_ref[...])
        high, low = halves(w_ref[...])
        w = jnp.concatenate([high, low, high], axis=1)
        copies = [pltpu.make_async_copy(held.at[i % depth], out_ref.at[:, :, at], sems.at[i]) for i, at in enumerate(blocks)]
        for i, at in enumerate(blocks):
            change = lax.dot_general(w, p_ref[:, at], (((1,), (0,)), ((), ())), preferred_element_type=jnp.float32)
            if i >= depth:
                copies[i - depth].wait()
            held[i % depth] = x_ref[:, :, at] - change.reshape(lead, rows, at.size)
            copies[i].start()
        for copy in copies[-depth:]:
            copy.wait()

    return pl.pallas_call(
        kernel,
        out_shape=jax.ShapeDtypeStruct(x.shape, jnp.float32),
        in_specs=[SMEM] + [VMEM] * 4,
        out_specs=ANY,
        scratch_shapes=[
            pltpu.VMEM((lead * rows, height), jnp.float32),
            pltpu.VMEM((depth, lead, rows, blocks[0].size), jnp.float32),
            pltpu.SemaphoreType.DMA((len(blocks),)),
        ],
        compiler_params=params(),
        cost_estimate=cost(6 * lead * rows * ncols * height, 8 * lead * rows * ncols),
        name="update",
    )(here, mine, theirs, x, changes)


def swap(array, k, size):
    return lax.ppermute(array, "wide", [(i, i ^ k) for i in range(size)])


def spread(pair, size):
    return [pair] + [swap(pair, k, size) for k in range(2, size, 2)]


def body(n_row, n_wide, eigvec_t, householder, wy_factor, block_place, offsets):
    rows, order = eigvec_t.shape
    steps, width, _ = wy_factor.shape
    slots = householder.shape[0]
    ncols = order // n_wide
    here = jnp.stack([lax.axis_index("row"), lax.axis_index("wide")]).astype(jnp.int32)

    turns = max(z + min(steps - 1, slots * (n_row - 1 - z)) for z in range(n_row - 1))
    cols = ncols // SPLITS
    streams = [([], []) for _ in range(SPLITS)]

    def exchange(array, odd):
        pairs = []
        for z in range(n_row):
            mate = ((z + odd) ^ 1) - odd
            for w in range(n_wide):
                target = mate * n_wide + w if 0 <= mate < n_row else z * n_wide + (w ^ 1)
                pairs.append((z * n_wide + w, target))
        return lax.ppermute(array, ("row", "wide"), pairs)

    whole = rows % 8 == 0
    if whole:
        piece = pack(eigvec_t, n_wide)
        x = lax.all_to_all(piece, "wide", split_axis=0, concat_axis=0, tiled=True)
        tokens = [piece]
    else:
        x = lax.all_to_all(eigvec_t, "wide", split_axis=1, concat_axis=0, tiled=True)[None]
        tokens = []
    for turn in range(turns):
        for part in range(SPLITS):
            evens, odds = streams[part]
            to_even, to_odd = feed(after(here, *tokens), block_place, householder, evens, odds, n_row, part, cols)
            tokens = [to_odd]
            streams[part] = (evens + [exchange(to_even, 0)], odds + [exchange(to_odd, 1)])
    evens = list(zip(*[stream[0] for stream in streams]))
    odds = list(zip(*[stream[1] for stream in streams]))
    high, low, high_t, low_t, gram = assemble(here, block_place, offsets, householder, evens, odds, n_row)
    cross = spread(gram + swap(gram, 1, n_wide), n_wide)
    changes = merge(cross, wy_factor, (high, low))

    mine, theirs, x = inner_products(after(here, cross[0]), x, (high_t, low_t))
    sums = spread(mine + swap(theirs, 1, n_wide), n_wide)
    sums[0] = after(sums[0], changes)
    mine = functools.reduce(jnp.add, sums)
    return update(here, x, mine, swap(mine, 1, n_wide), changes).reshape(n_wide * rows, ncols)


def solution(mesh):
    return jax.shard_map(
        functools.partial(body, mesh.shape["row"], mesh.shape["wide"]),
        mesh=mesh,
        in_specs=(P(("row", "wide"), None), P("row", None, "wide"), P(), P(), P()),
        out_specs=P("row", "wide"),
        check_vma=False,
    )
```

```python
import functools

import jax
import jax.numpy as jnp
from jax import lax
from jax.experimental import pallas as pl
from jax.experimental.pallas import tpu as pltpu
from jax.sharding import PartitionSpec as P

HIGHEST = lax.Precision.HIGHEST
SMALL_LIMIT = 44 * 1024 * 1024
VMEM_LIMIT = 40 * 1024 * 1024
LARGE_LIMIT = 58 * 1024 * 1024
COLUMNS = 512
SPLITS = 2


def dot_t(a, b):
    return lax.dot_general(a, b, (((1,), (1,)), ((), ())), precision=HIGHEST, preferred_element_type=jnp.float32)


def dot(a, b):
    return lax.dot_general(a, b, (((1,), (0,)), ((), ())), precision=HIGHEST, preferred_element_type=jnp.float32)


def halves(x):
    high = x.astype(jnp.bfloat16)
    return high, (x - high.astype(jnp.float32)).astype(jnp.bfloat16)


def dot3(a, b, dims):
    rows = a[0].shape[0]
    both = lax.dot_general(jnp.concatenate(a, axis=0), b[0], (dims, ((), ())), preferred_element_type=jnp.float32)
    last = lax.dot_general(a[0], b[1], (dims, ((), ())), preferred_element_type=jnp.float32)
    return both[:rows] + (both[rows:] + last)


def after(x, *tokens):
    return lax.optimization_barrier((x, *tokens))[0]


def params(limit=VMEM_LIMIT):
    return pltpu.CompilerParams(vmem_limit_bytes=limit)


def cost(flops, nbytes):
    return pl.CostEstimate(flops=flops, bytes_accessed=nbytes, transcendentals=0)


SMEM = pl.BlockSpec(memory_space=pltpu.SMEM)
ANY = pl.BlockSpec(memory_space=pl.ANY)
VMEM = pl.BlockSpec(memory_space=pltpu.VMEM)


def in_hbm(x):
    return pltpu.with_memory_space_constraint(x, pltpu.HBM)


def pack(x, n_wide):
    rows, order = x.shape
    ncols = order // n_wide
    step = 16 if rows % 16 == 0 else rows
    n_copies = n_wide * rows // step

    def kernel(x_ref, out_ref, held, in_sems, out_sems):
        into, out_of = [], []
        for first in range(0, rows, step):
            for k in range(n_wide):
                i, at = len(into), pl.ds(first, step)
                source = x_ref.at[at, pl.ds(k * ncols, ncols)]
                into.append(pltpu.make_async_copy(source, held.at[k, at], in_sems.at[i]))
                out_of.append(pltpu.make_async_copy(held.at[k, at], out_ref.at[k, at], out_sems.at[i]))
        for copy in into:
            copy.start()
        for came, goes in zip(into, out_of):
            came.wait()
            goes.start()
        for copy in out_of:
            copy.wait()

    return pl.pallas_call(
        kernel,
        out_shape=jax.ShapeDtypeStruct((n_wide, rows, ncols), jnp.float32),
        in_specs=[ANY],
        out_specs=ANY,
        scratch_shapes=[
            pltpu.VMEM((n_wide, rows, ncols), jnp.float32),
            pltpu.SemaphoreType.DMA((n_copies,)),
            pltpu.SemaphoreType.DMA((n_copies,)),
        ],
        compiler_params=params(limit=LARGE_LIMIT),
        cost_estimate=cost(0, 8 * rows * order),
        name="pack",
    )(in_hbm(x))


def plan(place_ref, slots, n_rows):
    places = [place_ref[s] for s in range(place_ref.shape[0])]
    roots = [lax.div(p, slots) for p in places]
    slot = [lax.rem(p, slots) for p in places]
    ranks = [sum([(roots[i] == roots[s]).astype(jnp.int32) for i in range(s)], jnp.int32(0)) for s in range(len(places))]
    counts = [sum([(r == i).astype(jnp.int32) for r in roots], jnp.int32(0)) for i in range(n_rows)]
    return roots, slot, ranks, counts


def feed(here, place, stack, evens, odds, n_rows, part, cols):
    slots, width, _ = stack.shape
    turn = len(evens)

    def kernel(here_ref, place_ref, stack_ref, *refs):
        arrived, (out_even, out_odd, sems) = refs[:-3], refs[-3:]
        roots, slot, ranks, _ = plan(place_ref, slots, n_rows)
        me = here_ref[0]
        mine = [r == me for r in roots]
        count = sum([m.astype(jnp.int32) for m in mine], jnp.int32(0))
        own = sum([jnp.where(m & (k == turn), s, 0) for m, k, s in zip(mine, ranks, slot)], jnp.int32(0))
        older = turn - jnp.maximum(count, 1)
        stored = stack_ref.at[own, :, pl.ds(part * cols, cols)]
        for side, out in ((0, out_even), (1, out_odd)):
            @pl.when((older < 0) | (count > turn))
            def _():
                pltpu.make_async_copy(stored, out, sems.at[side]).start()

            for i in range(turn):
                @pl.when((older == i) & (count <= turn))
                def _():
                    pltpu.make_async_copy(arrived[(1 - side) * turn + i], out, sems.at[side]).start()
        for side, out in ((0, out_even), (1, out_odd)):
            pltpu.make_async_copy(stored, out, sems.at[side]).wait()

    return pl.pallas_call(
        kernel,
        out_shape=[jax.ShapeDtypeStruct((width, cols), jnp.float32)] * 2,
        in_specs=[SMEM, SMEM, ANY] + [ANY] * (2 * turn),
        out_specs=[VMEM] * 2,
        scratch_shapes=[pltpu.SemaphoreType.DMA((2,))],
        compiler_params=params(limit=SMALL_LIMIT),
        cost_estimate=cost(0, 16 * width * cols),
        name="feed",
    )(here, place, stack, *evens, *odds)


def packed_width(steps, width):
    return -(-(width * steps * (steps - 1) // 2) // 128) * 128


def assemble(here, place, offsets, stack, evens, odds, n_rows):
    slots, width, ncols = stack.shape
    steps = place.shape[0]
    height = steps * width
    turns, splits = len(evens), len(evens[0])
    cols = ncols // splits

    def kernel(here_ref, place_ref, offset_ref, stack_ref, *refs):
        arrived, (high_ref, low_ref, high_t_ref, low_t_ref, gram_ref, held, sems) = refs[:-7], refs[-7:]
        even, odd = arrived[:turns * splits], arrived[turns * splits:]
        roots, slot, ranks, counts = plan(place_ref, slots, n_rows)
        me = here_ref[0]
        me_odd = lax.rem(me, 2) == 1
        for s in range(steps):
            root = roots[s]
            low, high = jnp.minimum(root, me), jnp.maximum(root, me)
            between = [jnp.where((i > low) & (i < high), jnp.maximum(counts[i], 1), 0) for i in range(n_rows)]
            turn = sum(between, ranks[s])
            target = held.at[pl.ds(s * width, width)]
            below, above = root < me, root > me

            @pl.when(root == me)
            def _():
                pltpu.make_async_copy(stack_ref.at[slot[s]], target, sems.at[s]).start()

            for side, came in (((below & me_odd) | (above & ~me_odd), even), ((below & ~me_odd) | (above & me_odd), odd)):
                for i in range(turns):
                    @pl.when(side & (turn == i))
                    def _():
                        for p in range(splits):
                            piece = held.at[pl.ds(s * width, width), pl.ds(p * cols, cols)]
                            pltpu.make_async_copy(came[i * splits + p], piece, sems.at[s]).start()
        columns = here_ref[1] * ncols + lax.broadcasted_iota(jnp.int32, (width, ncols), 1)
        for s in range(steps):
            rows = pl.ds(s * width, width)
            pltpu.make_async_copy(stack_ref.at[0], held.at[rows], sems.at[s]).wait()
            masked = jnp.where(columns >= offset_ref[s], held[rows, :], 0.0)
            held[rows, :] = masked
            high, low = halves(masked)
            high_ref[rows, :] = high
            low_ref[rows, :] = low
        for at in column_blocks(ncols):
            high_t_ref[at, :], low_t_ref[at, :] = halves(held[:, at].T)
        gram = dot_t(held[...], held[...])
        gram_ref[...] = jnp.zeros_like(gram_ref)
        first = 0
        for s in range(1, steps):
            gram_ref[:, first:first + s * width] = gram[s * width:(s + 1) * width, :s * width]
            first += s * width

    return pl.pallas_call(
        kernel,
        out_shape=[
            pltpu.HBM((height, ncols), jnp.bfloat16),
            pltpu.HBM((height, ncols), jnp.bfloat16),
            pltpu.HBM((ncols, height), jnp.bfloat16),
            pltpu.HBM((ncols, height), jnp.bfloat16),
            jax.ShapeDtypeStruct((width, packed_width(steps, width)), jnp.float32),
        ],
        in_specs=[SMEM, SMEM, SMEM, ANY] + [ANY] * (2 * turns * splits),
        out_specs=[VMEM] * 5,
        scratch_shapes=[pltpu.VMEM((height, ncols), jnp.float32), pltpu.SemaphoreType.DMA((steps,))],
        compiler_params=params(limit=SMALL_LIMIT),
        cost_estimate=cost(12 * height * height * ncols, 8 * height * ncols),
        name="assemble",
    )(here, place, offsets, stack, *[p for turn in evens for p in turn], *[p for turn in odds for p in turn])


def merge(cross, factors, vecs):
    steps, width, _ = factors.shape
    height, ncols = vecs[0].shape

    def kernel(*refs):
        cross_refs, (factor_ref, v_high, v_low, p_ref, total, m_ref) = refs[:-6], refs[-6:]
        total[...] = sum([ref[...] for ref in cross_refs[1:]], cross_refs[0][...])
        first = 0
        for k in range(steps):
            own = lax.broadcasted_iota(jnp.int32, (width, height), 0) + k * width
            rest = (own == lax.broadcasted_iota(jnp.int32, (width, height), 1)).astype(jnp.float32)
            if k:
                rest = rest - dot(total[:, first:first + k * width], m_ref[:k * width, :])
                first += k * width
            m_ref[k * width:(k + 1) * width, :] = dot(factor_ref[k], rest)
        product = dot3(halves(m_ref[...].T), (v_high[...], v_low[...]), ((1,), (0,)))
        high, low = halves(product)
        for i, half in enumerate((high, high, low)):
            p_ref[i * height:(i + 1) * height, :] = half

    return pl.pallas_call(
        kernel,
        out_shape=jax.ShapeDtypeStruct((3 * height, ncols), jnp.bfloat16),
        out_specs=VMEM,
        in_specs=[VMEM] * (len(cross) + 3),
        scratch_shapes=[pltpu.VMEM(cross[0].shape, jnp.float32), pltpu.VMEM((height, height), jnp.float32)],
        compiler_params=params(),
        cost_estimate=cost(6 * height * height * ncols, 8 * height * ncols),
        name="merge",
    )(*cross, factors, *vecs)


def fold(w):
    half = w.shape[0] // 2
    return jnp.concatenate([w[:half], w[half:]], axis=1)


def unfold(w):
    height = w.shape[1] // 2
    return jnp.concatenate([w[:, :height], w[:, height:]], axis=0)


def column_blocks(ncols):
    cols = COLUMNS if ncols % COLUMNS == 0 else ncols
    return [pl.ds(start, cols) for start in range(0, ncols, cols)]


def inner_products(here, x, vecs_t):
    lead, rows, ncols = x.shape
    height = vecs_t[0].shape[1]
    half = lead * rows // 2
    blocks = column_blocks(ncols)

    def kernel(here_ref, x_ref, high_hbm, low_hbm, mine_ref, theirs_ref, held, high_ref, low_ref, total, sems):
        copies = []
        for i, at in enumerate(blocks):
            copies.append([
                pltpu.make_async_copy(high_hbm.at[at], high_ref.at[at], sems.at[i, 0]),
                pltpu.make_async_copy(low_hbm.at[at], low_ref.at[at], sems.at[i, 1]),
                pltpu.make_async_copy(x_ref.at[:, :, at], held.at[:, :, at], sems.at[i, 2]),
            ])
        for block in copies:
            for copy in block:
                copy.start()
        for i, at in enumerate(blocks):
            for copy in copies[i]:
                copy.wait()
            block = held[:, :, at].reshape(lead * rows, at.size)
            part = dot3(halves(block), (high_ref[at, :], low_ref[at, :]), ((1,), (0,)))
            total[...] = part if i == 0 else total[...] + part
        core = lax.rem(here_ref[1], 2)
        mine_ref[...] = fold(total[pl.ds(pl.multiple_of(core * half, 8), half), :])
        theirs_ref[...] = fold(total[pl.ds(pl.multiple_of((1 - core) * half, 8), half), :])

    return pl.pallas_call(
        kernel,
        out_shape=[jax.ShapeDtypeStruct((half // 2, 2 * height), jnp.float32)] * 2 + [pltpu.VMEM(x.shape, jnp.float32)],
        in_specs=[SMEM, ANY, ANY, ANY],
        out_specs=[VMEM] * 3,
        scratch_shapes=[
            pltpu.VMEM((ncols, height), jnp.bfloat16),
            pltpu.VMEM((ncols, height), jnp.bfloat16),
            pltpu.VMEM((lead * rows, height), jnp.float32),
            pltpu.SemaphoreType.DMA((len(blocks), 3)),
        ],
        compiler_params=params(),
        cost_estimate=cost(6 * lead * rows * ncols * height, 4 * lead * rows * ncols),
        name="inner_products",
    )(here, in_hbm(x), *[in_hbm(v) for v in vecs_t])


def update(here, x, mine, theirs, changes):
    lead, rows, ncols = x.shape
    height = changes.shape[0] // 3
    half = lead * rows // 2
    blocks = column_blocks(ncols)
    depth = min(2, len(blocks))

    def kernel(here_ref, mine_ref, theirs_ref, x_ref, p_ref, out_ref, w_ref, held, sems):
        core = lax.rem(here_ref[1], 2)
        w_ref[pl.ds(pl.multiple_of(core * half, 8), half), :] = unfold(mine_ref[...])
        w_ref[pl.ds(pl.multiple_of((1 - core) * half, 8), half), :] = unfold(theirs_ref[...])
        high, low = halves(w_ref[...])
        w = jnp.concatenate([high, low, high], axis=1)
        copies = [pltpu.make_async_copy(held.at[i % depth], out_ref.at[:, :, at], sems.at[i]) for i, at in enumerate(blocks)]
        for i, at in enumerate(blocks):
            change = lax.dot_general(w, p_ref[:, at], (((1,), (0,)), ((), ())), preferred_element_type=jnp.float32)
            if i >= depth:
                copies[i - depth].wait()
            held[i % depth] = x_ref[:, :, at] - change.reshape(lead, rows, at.size)
            copies[i].start()
        for copy in copies[-depth:]:
            copy.wait()

    return pl.pallas_call(
        kernel,
        out_shape=jax.ShapeDtypeStruct(x.shape, jnp.float32),
        in_specs=[SMEM] + [VMEM] * 4,
        out_specs=ANY,
        scratch_shapes=[
            pltpu.VMEM((lead * rows, height), jnp.float32),
            pltpu.VMEM((depth, lead, rows, blocks[0].size), jnp.float32),
            pltpu.SemaphoreType.DMA((len(blocks),)),
        ],
        compiler_params=params(),
        cost_estimate=cost(6 * lead * rows * ncols * height, 8 * lead * rows * ncols),
        name="update",
    )(here, mine, theirs, x, changes)


def swap(array, k, size):
    return lax.ppermute(array, "wide", [(i, i ^ k) for i in range(size)])


def spread(pair, size):
    return [pair] + [swap(pair, k, size) for k in range(2, size, 2)]


def chips_sum(pair, size, token):
    shifts = [k for k in (1 << i for i in range(1, size.bit_length())) if k < size]
    half = pair.shape[0] // 2
    upper, lower = pair[:half], pair[half:]
    for i, (first, second) in enumerate(zip(shifts, reversed(shifts))):
        come_upper, come_lower = swap(upper, first, size), swap(lower, second, size)
        if i == len(shifts) - 1:
            upper = after(upper, token)
        upper, lower = upper + come_upper, lower + come_lower
    return jnp.concatenate([upper, lower], axis=0)


def body(n_row, n_wide, eigvec_t, householder, wy_factor, block_place, offsets):
    rows, order = eigvec_t.shape
    steps, width, _ = wy_factor.shape
    slots = householder.shape[0]
    ncols = order // n_wide
    here = jnp.stack([lax.axis_index("row"), lax.axis_index("wide")]).astype(jnp.int32)

    turns = max(z + min(steps - 1, slots * (n_row - 1 - z)) for z in range(n_row - 1))
    cols = ncols // SPLITS
    streams = [([], []) for _ in range(SPLITS)]

    def exchange(array, odd):
        pairs = []
        for z in range(n_row):
            mate = ((z + odd) ^ 1) - odd
            for w in range(n_wide):
                target = mate * n_wide + w if 0 <= mate < n_row else z * n_wide + (w ^ 1)
                pairs.append((z * n_wide + w, target))
        return lax.ppermute(array, ("row", "wide"), pairs)

    whole = rows % 8 == 0
    if whole:
        piece = pack(eigvec_t, n_wide)
        x = lax.all_to_all(piece, "wide", split_axis=0, concat_axis=0, tiled=True)
        tokens = [piece]
    else:
        x = lax.all_to_all(eigvec_t, "wide", split_axis=1, concat_axis=0, tiled=True)[None]
        tokens = []
    for turn in range(turns):
        for part in range(SPLITS):
            evens, odds = streams[part]
            to_even, to_odd = feed(after(here, *tokens), block_place, householder, evens, odds, n_row, part, cols)
            tokens = [to_odd]
            streams[part] = (evens + [exchange(to_even, 0)], odds + [exchange(to_odd, 1)])
    evens = list(zip(*[stream[0] for stream in streams]))
    odds = list(zip(*[stream[1] for stream in streams]))
    high, low, high_t, low_t, gram = assemble(here, block_place, offsets, householder, evens, odds, n_row)
    cross = functools.reduce(jnp.add, spread(gram + swap(gram, 1, n_wide), n_wide))
    changes = merge([cross], wy_factor, (high, low))

    mine, theirs, x = inner_products(after(here, cross), x, (high_t, low_t))
    mine = chips_sum(mine + swap(theirs, 1, n_wide), n_wide, changes)
    return update(here, x, mine, swap(mine, 1, n_wide), changes).reshape(n_wide * rows, ncols)


def solution(mesh):
    return jax.shard_map(
        functools.partial(body, mesh.shape["row"], mesh.shape["wide"]),
        mesh=mesh,
        in_specs=(P(("row", "wide"), None), P("row", None, "wide"), P(), P(), P()),
        out_specs=P("row", "wide"),
        check_vma=False,
    )
```

```python
import functools

import jax
import jax.numpy as jnp
from jax import lax
from jax.experimental import pallas as pl
from jax.experimental.pallas import tpu as pltpu
from jax.sharding import PartitionSpec as P

HIGHEST = lax.Precision.HIGHEST
SMALL_LIMIT = 44 * 1024 * 1024
VMEM_LIMIT = 40 * 1024 * 1024
LARGE_LIMIT = 58 * 1024 * 1024
COLUMNS = 512
QUEUES = 2
SPLITS = 2


def dot_t(a, b):
    return lax.dot_general(a, b, (((1,), (1,)), ((), ())), precision=HIGHEST, preferred_element_type=jnp.float32)


def dot(a, b):
    return lax.dot_general(a, b, (((1,), (0,)), ((), ())), precision=HIGHEST, preferred_element_type=jnp.float32)


def halves(x):
    high = x.astype(jnp.bfloat16)
    return high, (x - high.astype(jnp.float32)).astype(jnp.bfloat16)


def dot3(a, b, dims):
    rows = a[0].shape[0]
    both = lax.dot_general(jnp.concatenate(a, axis=0), b[0], (dims, ((), ())), preferred_element_type=jnp.float32)
    last = lax.dot_general(a[0], b[1], (dims, ((), ())), preferred_element_type=jnp.float32)
    return both[:rows] + (both[rows:] + last)


def after(x, *tokens):
    return lax.optimization_barrier((x, *tokens))[0]


def params(limit=VMEM_LIMIT):
    return pltpu.CompilerParams(vmem_limit_bytes=limit)


def cost(flops, nbytes):
    return pl.CostEstimate(flops=flops, bytes_accessed=nbytes, transcendentals=0)


SMEM = pl.BlockSpec(memory_space=pltpu.SMEM)
ANY = pl.BlockSpec(memory_space=pl.ANY)
VMEM = pl.BlockSpec(memory_space=pltpu.VMEM)


def in_hbm(x):
    return pltpu.with_memory_space_constraint(x, pltpu.HBM)


def pack(x, n_wide):
    rows, order = x.shape
    ncols = order // n_wide
    step = 16 if rows % 16 == 0 else rows
    n_copies = n_wide * rows // step

    def kernel(x_ref, out_ref, held, in_sems, out_sems):
        into, out_of = [], []
        for first in range(0, rows, step):
            for k in range(n_wide):
                i, at = len(into), pl.ds(first, step)
                source = x_ref.at[at, pl.ds(k * ncols, ncols)]
                into.append(pltpu.make_async_copy(source, held.at[k, at], in_sems.at[i]))
                out_of.append(pltpu.make_async_copy(held.at[k, at], out_ref.at[k, at], out_sems.at[i]))
        for i, copy in enumerate(into):
            copy.start(priority=i % QUEUES)
        for i, (came, goes) in enumerate(zip(into, out_of)):
            came.wait()
            goes.start(priority=i % QUEUES)
        for copy in out_of:
            copy.wait()

    return pl.pallas_call(
        kernel,
        out_shape=jax.ShapeDtypeStruct((n_wide, rows, ncols), jnp.float32),
        in_specs=[ANY],
        out_specs=ANY,
        scratch_shapes=[
            pltpu.VMEM((n_wide, rows, ncols), jnp.float32),
            pltpu.SemaphoreType.DMA((n_copies,)),
            pltpu.SemaphoreType.DMA((n_copies,)),
        ],
        compiler_params=params(limit=LARGE_LIMIT),
        cost_estimate=cost(0, 8 * rows * order),
        name="pack",
    )(in_hbm(x))


def plan(place_ref, slots, n_rows):
    places = [place_ref[s] for s in range(place_ref.shape[0])]
    roots = [lax.div(p, slots) for p in places]
    slot = [lax.rem(p, slots) for p in places]
    ranks = [sum([(roots[i] == roots[s]).astype(jnp.int32) for i in range(s)], jnp.int32(0)) for s in range(len(places))]
    counts = [sum([(r == i).astype(jnp.int32) for r in roots], jnp.int32(0)) for i in range(n_rows)]
    return roots, slot, ranks, counts


def feed(here, place, stack, evens, odds, n_rows, part, cols):
    slots, width, _ = stack.shape
    turn = len(evens)

    def kernel(here_ref, place_ref, stack_ref, *refs):
        arrived, (out_even, out_odd, sems) = refs[:-3], refs[-3:]
        roots, slot, ranks, _ = plan(place_ref, slots, n_rows)
        me = here_ref[0]
        mine = [r == me for r in roots]
        count = sum([m.astype(jnp.int32) for m in mine], jnp.int32(0))
        own = sum([jnp.where(m & (k == turn), s, 0) for m, k, s in zip(mine, ranks, slot)], jnp.int32(0))
        older = turn - jnp.maximum(count, 1)
        stored = stack_ref.at[own, :, pl.ds(part * cols, cols)]
        for side, out in ((0, out_even), (1, out_odd)):
            @pl.when((older < 0) | (count > turn))
            def _():
                pltpu.make_async_copy(stored, out, sems.at[side]).start()

            for i in range(turn):
                @pl.when((older == i) & (count <= turn))
                def _():
                    pltpu.make_async_copy(arrived[(1 - side) * turn + i], out, sems.at[side]).start()
        for side, out in ((0, out_even), (1, out_odd)):
            pltpu.make_async_copy(stored, out, sems.at[side]).wait()

    return pl.pallas_call(
        kernel,
        out_shape=[jax.ShapeDtypeStruct((width, cols), jnp.float32)] * 2,
        in_specs=[SMEM, SMEM, ANY] + [ANY] * (2 * turn),
        out_specs=[VMEM] * 2,
        scratch_shapes=[pltpu.SemaphoreType.DMA((2,))],
        compiler_params=params(limit=SMALL_LIMIT),
        cost_estimate=cost(0, 16 * width * cols),
        name="feed",
    )(here, place, stack, *evens, *odds)


def packed_width(steps, width):
    return -(-(width * steps * (steps - 1) // 2) // 128) * 128


def assemble(here, place, offsets, stack, evens, odds, n_rows):
    slots, width, ncols = stack.shape
    steps = place.shape[0]
    height = steps * width
    turns, splits = len(evens), len(evens[0])
    cols = ncols // splits

    def kernel(here_ref, place_ref, offset_ref, stack_ref, *refs):
        arrived, (high_ref, low_ref, both_t_ref, gram_ref, held, sems) = refs[:-6], refs[-6:]
        even, odd = arrived[:turns * splits], arrived[turns * splits:]
        roots, slot, ranks, counts = plan(place_ref, slots, n_rows)
        me = here_ref[0]
        me_odd = lax.rem(me, 2) == 1
        for s in range(steps):
            root = roots[s]
            low, high = jnp.minimum(root, me), jnp.maximum(root, me)
            between = [jnp.where((i > low) & (i < high), jnp.maximum(counts[i], 1), 0) for i in range(n_rows)]
            turn = sum(between, ranks[s])
            target = held.at[pl.ds(s * width, width)]
            below, above = root < me, root > me

            @pl.when(root == me)
            def _():
                pltpu.make_async_copy(stack_ref.at[slot[s]], target, sems.at[s]).start()

            for side, came in (((below & me_odd) | (above & ~me_odd), even), ((below & ~me_odd) | (above & me_odd), odd)):
                for i in range(turns):
                    @pl.when(side & (turn == i))
                    def _():
                        for p in range(splits):
                            piece = held.at[pl.ds(s * width, width), pl.ds(p * cols, cols)]
                            pltpu.make_async_copy(came[i * splits + p], piece, sems.at[s]).start()
        columns = here_ref[1] * ncols + lax.broadcasted_iota(jnp.int32, (width, ncols), 1)
        for s in range(steps):
            rows = pl.ds(s * width, width)
            pltpu.make_async_copy(stack_ref.at[0], held.at[rows], sems.at[s]).wait()
            masked = jnp.where(columns >= offset_ref[s], held[rows, :], 0.0)
            held[rows, :] = masked
            high, low = halves(masked)
            high_ref[rows, :] = high
            low_ref[rows, :] = low
        for at in column_blocks(ncols):
            high, low = halves(held[:, at].T)
            both_t_ref[at, :] = jnp.concatenate([high, low], axis=1)
        gram = dot_t(held[...], held[...])
        gram_ref[...] = jnp.zeros_like(gram_ref)
        first = 0
        for s in range(1, steps):
            gram_ref[:, first:first + s * width] = gram[s * width:(s + 1) * width, :s * width]
            first += s * width

    return pl.pallas_call(
        kernel,
        out_shape=[
            pltpu.HBM((height, ncols), jnp.bfloat16),
            pltpu.HBM((height, ncols), jnp.bfloat16),
            pltpu.HBM((ncols, 2 * height), jnp.bfloat16),
            jax.ShapeDtypeStruct((width, packed_width(steps, width)), jnp.float32),
        ],
        in_specs=[SMEM, SMEM, SMEM, ANY] + [ANY] * (2 * turns * splits),
        out_specs=[VMEM] * 4,
        scratch_shapes=[pltpu.VMEM((height, ncols), jnp.float32), pltpu.SemaphoreType.DMA((steps,))],
        compiler_params=params(limit=SMALL_LIMIT),
        cost_estimate=cost(12 * height * height * ncols, 8 * height * ncols),
        name="assemble",
    )(here, place, offsets, stack, *[p for turn in evens for p in turn], *[p for turn in odds for p in turn])


def merge(cross, factors, vecs):
    steps, width, _ = factors.shape
    height, ncols = vecs[0].shape

    def kernel(*refs):
        cross_refs, (factor_ref, v_high, v_low, p_ref, total, m_ref) = refs[:-6], refs[-6:]
        total[...] = sum([ref[...] for ref in cross_refs[1:]], cross_refs[0][...])
        first = 0
        for k in range(steps):
            own = lax.broadcasted_iota(jnp.int32, (width, height), 0) + k * width
            rest = (own == lax.broadcasted_iota(jnp.int32, (width, height), 1)).astype(jnp.float32)
            if k:
                rest = rest - dot(total[:, first:first + k * width], m_ref[:k * width, :])
                first += k * width
            m_ref[k * width:(k + 1) * width, :] = dot(factor_ref[k], rest)
        product = dot3(halves(m_ref[...].T), (v_high[...], v_low[...]), ((1,), (0,)))
        high, low = halves(product)
        for i, half in enumerate((high, high, low)):
            p_ref[i * height:(i + 1) * height, :] = half

    return pl.pallas_call(
        kernel,
        out_shape=jax.ShapeDtypeStruct((3 * height, ncols), jnp.bfloat16),
        out_specs=VMEM,
        in_specs=[VMEM] * (len(cross) + 3),
        scratch_shapes=[pltpu.VMEM(cross[0].shape, jnp.float32), pltpu.VMEM((height, height), jnp.float32)],
        compiler_params=params(),
        cost_estimate=cost(6 * height * height * ncols, 8 * height * ncols),
        name="merge",
    )(*cross, factors, *vecs)


def fold(w):
    half = w.shape[0] // 2
    return jnp.concatenate([w[:half], w[half:]], axis=1)


def unfold(w):
    height = w.shape[1] // 2
    return jnp.concatenate([w[:, :height], w[:, height:]], axis=0)


def column_blocks(ncols):
    cols = COLUMNS if ncols % COLUMNS == 0 else ncols
    return [pl.ds(start, cols) for start in range(0, ncols, cols)]


def inner_products(here, x, vecs_t):
    lead, rows, ncols = x.shape
    height = vecs_t.shape[1] // 2
    half = lead * rows // 2
    blocks = column_blocks(ncols)
    lanes = min(-(-height // 128) * 128, 2 * height)

    def kernel(here_ref, x_ref, vecs_hbm, mine_ref, theirs_ref, held, vecs_ref, by_high, by_low, total, sems):
        copies = []
        for i, at in enumerate(blocks):
            copies.append((
                pltpu.make_async_copy(vecs_hbm.at[at], vecs_ref.at[at], sems.at[i, 0]),
                pltpu.make_async_copy(x_ref.at[:lead // 2, :, at], held.at[:lead // 2, :, at], sems.at[i, 1]),
                pltpu.make_async_copy(x_ref.at[lead // 2:, :, at], held.at[lead // 2:, :, at], sems.at[i, 2]),
            )[:3 if lead > 1 else 1])
            if lead == 1:
                copies[i] += (pltpu.make_async_copy(x_ref.at[:, :, at], held.at[:, :, at], sems.at[i, 1]),)
        for i, copy in enumerate(copy for block in copies for copy in block):
            copy.start(priority=i % QUEUES)
        for i, at in enumerate(blocks):
            for copy in copies[i]:
                copy.wait()
            high, low = halves(held[:, :, at].reshape(lead * rows, at.size))
            one = jnp.dot(high, vecs_ref[at, :], preferred_element_type=jnp.float32)
            two = jnp.dot(low, vecs_ref[at, :lanes], preferred_element_type=jnp.float32)
            by_high[...] = one if i == 0 else by_high[...] + one
            by_low[...] = two if i == 0 else by_low[...] + two
        total[...] = by_high[:, :height] + (by_high[:, height:] + by_low[:, :height])
        core = lax.rem(here_ref[1], 2)
        mine_ref[...] = fold(total[pl.ds(pl.multiple_of(core * half, 8), half), :])
        theirs_ref[...] = fold(total[pl.ds(pl.multiple_of((1 - core) * half, 8), half), :])

    return pl.pallas_call(
        kernel,
        out_shape=[jax.ShapeDtypeStruct((half // 2, 2 * height), jnp.float32)] * 2 + [pltpu.VMEM(x.shape, jnp.float32)],
        in_specs=[SMEM, ANY, ANY],
        out_specs=[VMEM] * 3,
        scratch_shapes=[
            pltpu.VMEM(vecs_t.shape, jnp.bfloat16),
            pltpu.VMEM((lead * rows, 2 * height), jnp.float32),
            pltpu.VMEM((lead * rows, lanes), jnp.float32),
            pltpu.VMEM((lead * rows, height), jnp.float32),
            pltpu.SemaphoreType.DMA((len(blocks), 3)),
        ],
        compiler_params=params(),
        cost_estimate=cost(6 * lead * rows * ncols * height, 4 * lead * rows * ncols),
        name="inner_products",
    )(here, in_hbm(x), in_hbm(vecs_t))


def update(here, x, mine, theirs, changes):
    lead, rows, ncols = x.shape
    height = changes.shape[0] // 3
    half = lead * rows // 2
    blocks = column_blocks(ncols)
    depth = min(4, len(blocks))

    def kernel(here_ref, mine_ref, theirs_ref, x_ref, p_ref, out_ref, w_ref, held, sems):
        core = lax.rem(here_ref[1], 2)
        w_ref[pl.ds(pl.multiple_of(core * half, 8), half), :] = unfold(mine_ref[...])
        w_ref[pl.ds(pl.multiple_of((1 - core) * half, 8), half), :] = unfold(theirs_ref[...])
        high, low = halves(w_ref[...])
        w = jnp.concatenate([high, low, high], axis=1)
        copies = [pltpu.make_async_copy(held.at[i % depth], out_ref.at[:, :, at], sems.at[i]) for i, at in enumerate(blocks)]
        for i, at in enumerate(blocks):
            change = lax.dot_general(w, p_ref[:, at], (((1,), (0,)), ((), ())), preferred_element_type=jnp.float32)
            if i >= depth:
                copies[i - depth].wait()
            held[i % depth] = x_ref[:, :, at] - change.reshape(lead, rows, at.size)
            copies[i].start(priority=i % QUEUES)
        for copy in copies[-depth:]:
            copy.wait()

    return pl.pallas_call(
        kernel,
        out_shape=jax.ShapeDtypeStruct(x.shape, jnp.float32),
        in_specs=[SMEM] + [VMEM] * 4,
        out_specs=ANY,
        scratch_shapes=[
            pltpu.VMEM((lead * rows, height), jnp.float32),
            pltpu.VMEM((depth, lead, rows, blocks[0].size), jnp.float32),
            pltpu.SemaphoreType.DMA((len(blocks),)),
        ],
        compiler_params=params(),
        cost_estimate=cost(6 * lead * rows * ncols * height, 8 * lead * rows * ncols),
        name="update",
    )(here, mine, theirs, x, changes)


def swap(array, k, size):
    return lax.ppermute(array, "wide", [(i, i ^ k) for i in range(size)])


def spread(pair, size):
    return [pair] + [swap(pair, k, size) for k in range(2, size, 2)]


def chips_sum(pair, size, token):
    shifts = [k for k in (1 << i for i in range(1, size.bit_length())) if k < size]
    half = pair.shape[0] // 2
    upper, lower = pair[:half], pair[half:]
    for i, (first, second) in enumerate(zip(shifts, reversed(shifts))):
        come_upper, come_lower = swap(upper, first, size), swap(lower, second, size)
        if i == len(shifts) - 1:
            upper = after(upper, token)
        upper, lower = upper + come_upper, lower + come_lower
    return jnp.concatenate([upper, lower], axis=0)


def body(n_row, n_wide, eigvec_t, householder, wy_factor, block_place, offsets):
    rows, order = eigvec_t.shape
    steps, width, _ = wy_factor.shape
    slots = householder.shape[0]
    ncols = order // n_wide
    here = jnp.stack([lax.axis_index("row"), lax.axis_index("wide")]).astype(jnp.int32)

    turns = max(z + min(steps - 1, slots * (n_row - 1 - z)) for z in range(n_row - 1))
    cols = ncols // SPLITS
    streams = [([], []) for _ in range(SPLITS)]

    def exchange(array, odd):
        pairs = []
        for z in range(n_row):
            mate = ((z + odd) ^ 1) - odd
            for w in range(n_wide):
                target = mate * n_wide + w if 0 <= mate < n_row else z * n_wide + (w ^ 1)
                pairs.append((z * n_wide + w, target))
        return lax.ppermute(array, ("row", "wide"), pairs)

    whole = rows % 8 == 0
    if whole:
        piece = pack(eigvec_t, n_wide)
        x = lax.all_to_all(piece, "wide", split_axis=0, concat_axis=0, tiled=True)
        tokens = [piece]
    else:
        x = lax.all_to_all(eigvec_t, "wide", split_axis=1, concat_axis=0, tiled=True)[None]
        tokens = []
    for turn in range(turns):
        for part in range(SPLITS):
            evens, odds = streams[part]
            to_even, to_odd = feed(after(here, *tokens), block_place, householder, evens, odds, n_row, part, cols)
            tokens = [to_odd]
            streams[part] = (evens + [exchange(to_even, 0)], odds + [exchange(to_odd, 1)])
    evens = list(zip(*[stream[0] for stream in streams]))
    odds = list(zip(*[stream[1] for stream in streams]))
    high, low, both_t, gram = assemble(here, block_place, offsets, householder, evens, odds, n_row)
    cross = functools.reduce(jnp.add, spread(gram + swap(gram, 1, n_wide), n_wide))
    changes = merge([cross], wy_factor, (high, low))

    mine, theirs, x = inner_products(after(here, cross), x, both_t)
    mine = chips_sum(mine + swap(theirs, 1, n_wide), n_wide, changes)
    return update(here, x, mine, swap(mine, 1, n_wide), changes).reshape(n_wide * rows, ncols)


def solution(mesh):
    return jax.shard_map(
        functools.partial(body, mesh.shape["row"], mesh.shape["wide"]),
        mesh=mesh,
        in_specs=(P(("row", "wide"), None), P("row", None, "wide"), P(), P(), P()),
        out_specs=P("row", "wide"),
        check_vma=False,
    )
```

```python
import functools

import jax
import jax.numpy as jnp
from jax import lax
from jax.experimental import pallas as pl
from jax.experimental.pallas import tpu as pltpu
from jax.sharding import PartitionSpec as P

HIGHEST = lax.Precision.HIGHEST
SMALL_LIMIT = 44 * 1024 * 1024
VMEM_LIMIT = 40 * 1024 * 1024
LARGE_LIMIT = 58 * 1024 * 1024
COLUMNS = 512
QUEUES = 2
SPLITS = 2


def dot_t(a, b):
    return lax.dot_general(a, b, (((1,), (1,)), ((), ())), precision=HIGHEST, preferred_element_type=jnp.float32)


def dot(a, b):
    return lax.dot_general(a, b, (((1,), (0,)), ((), ())), precision=HIGHEST, preferred_element_type=jnp.float32)


def halves(x):
    high = x.astype(jnp.bfloat16)
    return high, (x - high.astype(jnp.float32)).astype(jnp.bfloat16)


def dot3(a, b, dims):
    rows = a[0].shape[0]
    both = lax.dot_general(jnp.concatenate(a, axis=0), b[0], (dims, ((), ())), preferred_element_type=jnp.float32)
    last = lax.dot_general(a[0], b[1], (dims, ((), ())), preferred_element_type=jnp.float32)
    return both[:rows] + (both[rows:] + last)


def after(x, *tokens):
    return lax.optimization_barrier((x, *tokens))[0]


def params(limit=VMEM_LIMIT):
    return pltpu.CompilerParams(vmem_limit_bytes=limit)


def cost(flops, nbytes):
    return pl.CostEstimate(flops=flops, bytes_accessed=nbytes, transcendentals=0)


SMEM = pl.BlockSpec(memory_space=pltpu.SMEM)
ANY = pl.BlockSpec(memory_space=pl.ANY)
VMEM = pl.BlockSpec(memory_space=pltpu.VMEM)


def in_hbm(x):
    return pltpu.with_memory_space_constraint(x, pltpu.HBM)


def pack(x, n_wide):
    rows, order = x.shape
    ncols = order // n_wide
    step = 16 if rows % 16 == 0 else rows
    n_copies = n_wide * rows // step

    def kernel(x_ref, out_ref, held, in_sems, out_sems):
        into, out_of = [], []
        for first in range(0, rows, step):
            for k in range(n_wide):
                i, at = len(into), pl.ds(first, step)
                source = x_ref.at[at, pl.ds(k * ncols, ncols)]
                into.append(pltpu.make_async_copy(source, held.at[k, at], in_sems.at[i]))
                out_of.append(pltpu.make_async_copy(held.at[k, at], out_ref.at[k, at], out_sems.at[i]))
        for i, copy in enumerate(into):
            copy.start(priority=i % QUEUES)
        for i, (came, goes) in enumerate(zip(into, out_of)):
            came.wait()
            goes.start(priority=i % QUEUES)
        for copy in out_of:
            copy.wait()

    return pl.pallas_call(
        kernel,
        out_shape=jax.ShapeDtypeStruct((n_wide, rows, ncols), jnp.float32),
        in_specs=[ANY],
        out_specs=ANY,
        scratch_shapes=[
            pltpu.VMEM((n_wide, rows, ncols), jnp.float32),
            pltpu.SemaphoreType.DMA((n_copies,)),
            pltpu.SemaphoreType.DMA((n_copies,)),
        ],
        compiler_params=params(limit=LARGE_LIMIT),
        cost_estimate=cost(0, 8 * rows * order),
        name="pack",
    )(in_hbm(x))


def plan(place_ref, slots, n_rows):
    places = [place_ref[s] for s in range(place_ref.shape[0])]
    roots = [lax.div(p, slots) for p in places]
    slot = [lax.rem(p, slots) for p in places]
    ranks = [sum([(roots[i] == roots[s]).astype(jnp.int32) for i in range(s)], jnp.int32(0)) for s in range(len(places))]
    counts = [sum([(r == i).astype(jnp.int32) for r in roots], jnp.int32(0)) for i in range(n_rows)]
    return roots, slot, ranks, counts


def feed(here, place, stack, evens, odds, n_rows, part, cols):
    slots, width, _ = stack.shape
    turn = len(evens)

    def kernel(here_ref, place_ref, stack_ref, *refs):
        arrived, (out_even, out_odd, sems) = refs[:-3], refs[-3:]
        roots, slot, ranks, _ = plan(place_ref, slots, n_rows)
        me = here_ref[0]
        mine = [r == me for r in roots]
        count = sum([m.astype(jnp.int32) for m in mine], jnp.int32(0))
        own = sum([jnp.where(m & (k == turn), s, 0) for m, k, s in zip(mine, ranks, slot)], jnp.int32(0))
        older = turn - jnp.maximum(count, 1)
        stored = stack_ref.at[own, :, pl.ds(part * cols, cols)]
        for side, out in ((0, out_even), (1, out_odd)):
            @pl.when((older < 0) | (count > turn))
            def _():
                pltpu.make_async_copy(stored, out, sems.at[side]).start()

            for i in range(turn):
                @pl.when((older == i) & (count <= turn))
                def _():
                    pltpu.make_async_copy(arrived[(1 - side) * turn + i], out, sems.at[side]).start()
        for side, out in ((0, out_even), (1, out_odd)):
            pltpu.make_async_copy(stored, out, sems.at[side]).wait()

    return pl.pallas_call(
        kernel,
        out_shape=[jax.ShapeDtypeStruct((width, cols), jnp.float32)] * 2,
        in_specs=[SMEM, SMEM, ANY] + [ANY] * (2 * turn),
        out_specs=[VMEM] * 2,
        scratch_shapes=[pltpu.SemaphoreType.DMA((2,))],
        compiler_params=params(limit=SMALL_LIMIT),
        cost_estimate=cost(0, 16 * width * cols),
        name="feed",
    )(here, place, stack, *evens, *odds)


def packed_width(steps, width):
    return -(-(width * steps * (steps - 1) // 2) // 128) * 128


def assemble(here, place, offsets, stack, evens, odds, n_rows):
    slots, width, ncols = stack.shape
    steps = place.shape[0]
    height = steps * width
    turns, splits = len(evens), len(evens[0])
    cols = ncols // splits

    def kernel(here_ref, place_ref, offset_ref, stack_ref, *refs):
        arrived, (high_ref, low_ref, both_t_ref, gram_ref, held, sems) = refs[:-6], refs[-6:]
        even, odd = arrived[:turns * splits], arrived[turns * splits:]
        roots, slot, ranks, counts = plan(place_ref, slots, n_rows)
        me = here_ref[0]
        me_odd = lax.rem(me, 2) == 1
        for s in range(steps):
            root = roots[s]
            low, high = jnp.minimum(root, me), jnp.maximum(root, me)
            between = [jnp.where((i > low) & (i < high), jnp.maximum(counts[i], 1), 0) for i in range(n_rows)]
            turn = sum(between, ranks[s])
            target = held.at[pl.ds(s * width, width)]
            below, above = root < me, root > me

            @pl.when(root == me)
            def _():
                pltpu.make_async_copy(stack_ref.at[slot[s]], target, sems.at[s]).start()

            for side, came in (((below & me_odd) | (above & ~me_odd), even), ((below & ~me_odd) | (above & me_odd), odd)):
                for i in range(turns):
                    @pl.when(side & (turn == i))
                    def _():
                        for p in range(splits):
                            piece = held.at[pl.ds(s * width, width), pl.ds(p * cols, cols)]
                            pltpu.make_async_copy(came[i * splits + p], piece, sems.at[s]).start()
        columns = here_ref[1] * ncols + lax.broadcasted_iota(jnp.int32, (width, ncols), 1)
        for s in range(steps):
            rows = pl.ds(s * width, width)
            pltpu.make_async_copy(stack_ref.at[0], held.at[rows], sems.at[s]).wait()
            masked = jnp.where(columns >= offset_ref[s], held[rows, :], 0.0)
            held[rows, :] = masked
            high, low = halves(masked)
            high_ref[rows, :] = high
            low_ref[rows, :] = low
        for at in column_blocks(ncols):
            high, low = halves(held[:, at].T)
            both_t_ref[at, :] = jnp.concatenate([high, low], axis=1)
        gram = dot_t(held[...], held[...])
        gram_ref[...] = jnp.zeros_like(gram_ref)
        first = 0
        for s in range(1, steps):
            gram_ref[:, first:first + s * width] = gram[s * width:(s + 1) * width, :s * width]
            first += s * width

    return pl.pallas_call(
        kernel,
        out_shape=[
            pltpu.HBM((height, ncols), jnp.bfloat16),
            pltpu.HBM((height, ncols), jnp.bfloat16),
            pltpu.HBM((ncols, 2 * height), jnp.bfloat16),
            jax.ShapeDtypeStruct((width, packed_width(steps, width)), jnp.float32),
        ],
        in_specs=[SMEM, SMEM, SMEM, ANY] + [ANY] * (2 * turns * splits),
        out_specs=[VMEM] * 4,
        scratch_shapes=[pltpu.VMEM((height, ncols), jnp.float32), pltpu.SemaphoreType.DMA((steps,))],
        compiler_params=params(limit=SMALL_LIMIT),
        cost_estimate=cost(12 * height * height * ncols, 8 * height * ncols),
        name="assemble",
    )(here, place, offsets, stack, *[p for turn in evens for p in turn], *[p for turn in odds for p in turn])


def merge(cross, factors, vecs):
    steps, width, _ = factors.shape
    height, ncols = vecs[0].shape

    def kernel(*refs):
        cross_refs, (factor_ref, v_high, v_low, p_ref, total, m_ref) = refs[:-6], refs[-6:]
        total[...] = sum([ref[...] for ref in cross_refs[1:]], cross_refs[0][...])
        first = 0
        for k in range(steps):
            own = lax.broadcasted_iota(jnp.int32, (width, height), 0) + k * width
            rest = (own == lax.broadcasted_iota(jnp.int32, (width, height), 1)).astype(jnp.float32)
            if k:
                rest = rest - dot(total[:, first:first + k * width], m_ref[:k * width, :])
                first += k * width
            m_ref[k * width:(k + 1) * width, :] = dot(factor_ref[k], rest)
        product = dot3(halves(m_ref[...].T), (v_high[...], v_low[...]), ((1,), (0,)))
        high, low = halves(product)
        for i, half in enumerate((high, high, low)):
            p_ref[i * height:(i + 1) * height, :] = half

    return pl.pallas_call(
        kernel,
        out_shape=jax.ShapeDtypeStruct((3 * height, ncols), jnp.bfloat16),
        out_specs=VMEM,
        in_specs=[VMEM] * (len(cross) + 3),
        scratch_shapes=[pltpu.VMEM(cross[0].shape, jnp.float32), pltpu.VMEM((height, height), jnp.float32)],
        compiler_params=params(),
        cost_estimate=cost(6 * height * height * ncols, 8 * height * ncols),
        name="merge",
    )(*cross, factors, *vecs)


def fold(w):
    half = w.shape[0] // 2
    return jnp.concatenate([w[:half], w[half:]], axis=1)


def unfold(w):
    height = w.shape[1] // 2
    return jnp.concatenate([w[:, :height], w[:, height:]], axis=0)


def column_blocks(ncols):
    cols = COLUMNS if ncols % COLUMNS == 0 else ncols
    return [pl.ds(start, cols) for start in range(0, ncols, cols)]


def inner_products(here, x, vecs_t):
    lead, rows, ncols = x.shape
    height = vecs_t.shape[1] // 2
    half = lead * rows // 2
    blocks = column_blocks(ncols)
    lanes = min(-(-height // 128) * 128, 2 * height)
    parts = [pl.ds(0, lead // 2), pl.ds(lead // 2, lead // 2)] if lead % 2 == 0 else [pl.ds(0, lead)]

    def kernel(here_ref, x_ref, vecs_ref, mine_ref, theirs_ref, held, by_high, by_low, total, sems):
        copies = [
            [
                pltpu.make_async_copy(x_ref.at[part, :, at], held.at[part, :, at], sems.at[i, j])
                for j, part in enumerate(parts)
            ]
            for i, at in enumerate(blocks)
        ]
        for i, copy in enumerate(copy for block in copies for copy in block):
            copy.start(priority=i % QUEUES)
        for i, at in enumerate(blocks):
            for copy in copies[i]:
                copy.wait()
            high, low = halves(held[:, :, at].reshape(lead * rows, at.size))
            one = jnp.dot(high, vecs_ref[at, :], preferred_element_type=jnp.float32)
            two = jnp.dot(low, vecs_ref[at, :lanes], preferred_element_type=jnp.float32)
            by_high[...] = one if i == 0 else by_high[...] + one
            by_low[...] = two if i == 0 else by_low[...] + two
        total[...] = by_high[:, :height] + (by_high[:, height:] + by_low[:, :height])
        core = lax.rem(here_ref[1], 2)
        mine_ref[...] = fold(total[pl.ds(pl.multiple_of(core * half, 8), half), :])
        theirs_ref[...] = fold(total[pl.ds(pl.multiple_of((1 - core) * half, 8), half), :])

    return pl.pallas_call(
        kernel,
        out_shape=[jax.ShapeDtypeStruct((half // 2, 2 * height), jnp.float32)] * 2 + [pltpu.VMEM(x.shape, jnp.float32)],
        in_specs=[SMEM, ANY, VMEM],
        out_specs=[VMEM] * 3,
        scratch_shapes=[
            pltpu.VMEM((lead * rows, 2 * height), jnp.float32),
            pltpu.VMEM((lead * rows, lanes), jnp.float32),
            pltpu.VMEM((lead * rows, height), jnp.float32),
            pltpu.SemaphoreType.DMA((len(blocks), len(parts))),
        ],
        compiler_params=params(),
        cost_estimate=cost(6 * lead * rows * ncols * height, 4 * lead * rows * ncols),
        name="inner_products",
    )(here, in_hbm(x), vecs_t)


def update(here, x, mine, theirs, changes):
    lead, rows, ncols = x.shape
    height = changes.shape[0] // 3
    half = lead * rows // 2
    blocks = column_blocks(ncols)
    depth = min(4, len(blocks))

    def kernel(here_ref, mine_ref, theirs_ref, x_ref, p_ref, out_ref, w_ref, held, sems):
        core = lax.rem(here_ref[1], 2)
        w_ref[pl.ds(pl.multiple_of(core * half, 8), half), :] = unfold(mine_ref[...])
        w_ref[pl.ds(pl.multiple_of((1 - core) * half, 8), half), :] = unfold(theirs_ref[...])
        high, low = halves(w_ref[...])
        w = jnp.concatenate([high, low, high], axis=1)
        copies = [pltpu.make_async_copy(held.at[i % depth], out_ref.at[:, :, at], sems.at[i]) for i, at in enumerate(blocks)]
        for i, at in enumerate(blocks):
            change = lax.dot_general(w, p_ref[:, at], (((1,), (0,)), ((), ())), preferred_element_type=jnp.float32)
            if i >= depth:
                copies[i - depth].wait()
            held[i % depth] = x_ref[:, :, at] - change.reshape(lead, rows, at.size)
            copies[i].start(priority=i % QUEUES)
        for copy in copies[-depth:]:
            copy.wait()

    return pl.pallas_call(
        kernel,
        out_shape=jax.ShapeDtypeStruct(x.shape, jnp.float32),
        in_specs=[SMEM] + [VMEM] * 4,
        out_specs=ANY,
        scratch_shapes=[
            pltpu.VMEM((lead * rows, height), jnp.float32),
            pltpu.VMEM((depth, lead, rows, blocks[0].size), jnp.float32),
            pltpu.SemaphoreType.DMA((len(blocks),)),
        ],
        compiler_params=params(),
        cost_estimate=cost(6 * lead * rows * ncols * height, 8 * lead * rows * ncols),
        name="update",
    )(here, mine, theirs, x, changes)


def swap(array, k, size):
    return lax.ppermute(array, "wide", [(i, i ^ k) for i in range(size)])


def spread(pair, size):
    return [pair] + [swap(pair, k, size) for k in range(2, size, 2)]


def chips_sum(pair, size, token):
    shifts = [k for k in (1 << i for i in range(1, size.bit_length())) if k < size]
    half = pair.shape[0] // 2
    upper, lower = pair[:half], pair[half:]
    for i, (first, second) in enumerate(zip(shifts, reversed(shifts))):
        come_upper, come_lower = swap(upper, first, size), swap(lower, second, size)
        if i == 0:
            upper = after(upper, token)
        upper, lower = upper + come_upper, lower + come_lower
    return jnp.concatenate([upper, lower], axis=0)


def body(n_row, n_wide, eigvec_t, householder, wy_factor, block_place, offsets):
    rows, order = eigvec_t.shape
    steps, width, _ = wy_factor.shape
    slots = householder.shape[0]
    ncols = order // n_wide
    here = jnp.stack([lax.axis_index("row"), lax.axis_index("wide")]).astype(jnp.int32)

    turns = max(z + min(steps - 1, slots * (n_row - 1 - z)) for z in range(n_row - 1))
    cols = ncols // SPLITS
    streams = [([], []) for _ in range(SPLITS)]

    def exchange(array, odd):
        pairs = []
        for z in range(n_row):
            mate = ((z + odd) ^ 1) - odd
            for w in range(n_wide):
                target = mate * n_wide + w if 0 <= mate < n_row else z * n_wide + (w ^ 1)
                pairs.append((z * n_wide + w, target))
        return lax.ppermute(array, ("row", "wide"), pairs)

    whole = rows % 8 == 0
    if whole:
        piece = pack(eigvec_t, n_wide)
        x = lax.all_to_all(piece, "wide", split_axis=0, concat_axis=0, tiled=True)
        tokens = [piece]
    else:
        x = lax.all_to_all(eigvec_t, "wide", split_axis=1, concat_axis=0, tiled=True)[None]
        tokens = []
    for turn in range(turns):
        for part in range(SPLITS):
            evens, odds = streams[part]
            to_even, to_odd = feed(after(here, *tokens), block_place, householder, evens, odds, n_row, part, cols)
            tokens = [to_odd]
            streams[part] = (evens + [exchange(to_even, 0)], odds + [exchange(to_odd, 1)])
    evens = list(zip(*[stream[0] for stream in streams]))
    odds = list(zip(*[stream[1] for stream in streams]))
    high, low, both_t, gram = assemble(here, block_place, offsets, householder, evens, odds, n_row)
    cross = spread(gram + swap(gram, 1, n_wide), n_wide)
    cross[0] = after(cross[0], x)
    cross = functools.reduce(jnp.add, cross)
    changes = merge([cross], wy_factor, (high, low))

    mine, theirs, x = inner_products(after(here, cross), x, both_t)
    mine = chips_sum(mine + swap(theirs, 1, n_wide), n_wide, changes)
    return update(here, x, mine, swap(mine, 1, n_wide), changes).reshape(n_wide * rows, ncols)


def solution(mesh):
    return jax.shard_map(
        functools.partial(body, mesh.shape["row"], mesh.shape["wide"]),
        mesh=mesh,
        in_specs=(P(("row", "wide"), None), P("row", None, "wide"), P(), P(), P()),
        out_specs=P("row", "wide"),
        check_vma=False,
    )
```

```python
import functools

import jax
import jax.numpy as jnp
from jax import lax
from jax.experimental import pallas as pl
from jax.experimental.pallas import tpu as pltpu
from jax.sharding import PartitionSpec as P

HIGHEST = lax.Precision.HIGHEST
SMALL_LIMIT = 44 * 1024 * 1024
VMEM_LIMIT = 40 * 1024 * 1024
LARGE_LIMIT = 58 * 1024 * 1024
COLUMNS = 512
QUEUES = 2
SPLITS = 2


def dot_t(a, b):
    return lax.dot_general(a, b, (((1,), (1,)), ((), ())), precision=HIGHEST, preferred_element_type=jnp.float32)


def dot(a, b):
    return lax.dot_general(a, b, (((1,), (0,)), ((), ())), precision=HIGHEST, preferred_element_type=jnp.float32)


def halves(x):
    high = x.astype(jnp.bfloat16)
    return high, (x - high.astype(jnp.float32)).astype(jnp.bfloat16)


def dot3(a, b, dims):
    rows = a[0].shape[0]
    both = lax.dot_general(jnp.concatenate(a, axis=0), b[0], (dims, ((), ())), preferred_element_type=jnp.float32)
    last = lax.dot_general(a[0], b[1], (dims, ((), ())), preferred_element_type=jnp.float32)
    return both[:rows] + (both[rows:] + last)


def after(x, *tokens):
    return lax.optimization_barrier((x, *tokens))[0]


def params(limit=VMEM_LIMIT):
    return pltpu.CompilerParams(vmem_limit_bytes=limit)


def cost(flops, nbytes):
    return pl.CostEstimate(flops=flops, bytes_accessed=nbytes, transcendentals=0)


SMEM = pl.BlockSpec(memory_space=pltpu.SMEM)
ANY = pl.BlockSpec(memory_space=pl.ANY)
VMEM = pl.BlockSpec(memory_space=pltpu.VMEM)


def in_hbm(x):
    return pltpu.with_memory_space_constraint(x, pltpu.HBM)


def pack(x, n_wide):
    rows, order = x.shape
    ncols = order // n_wide
    step = 16 if rows % 16 == 0 else rows
    n_copies = n_wide * rows // step

    def kernel(x_ref, out_ref, held, in_sems, out_sems):
        into, out_of = [], []
        for first in range(0, rows, step):
            for k in range(n_wide):
                i, at = len(into), pl.ds(first, step)
                source = x_ref.at[at, pl.ds(k * ncols, ncols)]
                into.append(pltpu.make_async_copy(source, held.at[k, at], in_sems.at[i]))
                out_of.append(pltpu.make_async_copy(held.at[k, at], out_ref.at[k, at], out_sems.at[i]))
        for i, copy in enumerate(into):
            copy.start(priority=i % QUEUES)
        for i, (came, goes) in enumerate(zip(into, out_of)):
            came.wait()
            goes.start(priority=i % QUEUES)
        for copy in out_of:
            copy.wait()

    return pl.pallas_call(
        kernel,
        out_shape=jax.ShapeDtypeStruct((n_wide, rows, ncols), jnp.float32),
        in_specs=[ANY],
        out_specs=ANY,
        scratch_shapes=[
            pltpu.VMEM((n_wide, rows, ncols), jnp.float32),
            pltpu.SemaphoreType.DMA((n_copies,)),
            pltpu.SemaphoreType.DMA((n_copies,)),
        ],
        compiler_params=params(limit=LARGE_LIMIT),
        cost_estimate=cost(0, 8 * rows * order),
        name="pack",
    )(in_hbm(x))


def plan(place_ref, slots, n_rows):
    places = [place_ref[s] for s in range(place_ref.shape[0])]
    roots = [lax.div(p, slots) for p in places]
    slot = [lax.rem(p, slots) for p in places]
    ranks = [sum([(roots[i] == roots[s]).astype(jnp.int32) for i in range(s)], jnp.int32(0)) for s in range(len(places))]
    counts = [sum([(r == i).astype(jnp.int32) for r in roots], jnp.int32(0)) for i in range(n_rows)]
    return roots, slot, ranks, counts


def feed(here, place, stack, evens, odds, n_rows, part, cols):
    slots, width, _ = stack.shape
    turn = len(evens)

    def kernel(here_ref, place_ref, stack_ref, *refs):
        arrived, (out_even, out_odd, sems) = refs[:-3], refs[-3:]
        roots, slot, ranks, _ = plan(place_ref, slots, n_rows)
        me = here_ref[0]
        mine = [r == me for r in roots]
        count = sum([m.astype(jnp.int32) for m in mine], jnp.int32(0))
        own = sum([jnp.where(m & (k == turn), s, 0) for m, k, s in zip(mine, ranks, slot)], jnp.int32(0))
        older = turn - jnp.maximum(count, 1)
        stored = stack_ref.at[own, :, pl.ds(part * cols, cols)]
        for side, out in ((0, out_even), (1, out_odd)):
            @pl.when((older < 0) | (count > turn))
            def _():
                pltpu.make_async_copy(stored, out, sems.at[side]).start()

            for i in range(turn):
                @pl.when((older == i) & (count <= turn))
                def _():
                    pltpu.make_async_copy(arrived[(1 - side) * turn + i], out, sems.at[side]).start()
        for side, out in ((0, out_even), (1, out_odd)):
            pltpu.make_async_copy(stored, out, sems.at[side]).wait()

    return pl.pallas_call(
        kernel,
        out_shape=[jax.ShapeDtypeStruct((width, cols), jnp.float32)] * 2,
        in_specs=[SMEM, SMEM, ANY] + [ANY] * (2 * turn),
        out_specs=[VMEM] * 2,
        scratch_shapes=[pltpu.SemaphoreType.DMA((2,))],
        compiler_params=params(limit=SMALL_LIMIT),
        cost_estimate=cost(0, 16 * width * cols),
        name="feed",
    )(here, place, stack, *evens, *odds)


def packed_width(steps, width):
    return -(-(width * steps * (steps - 1) // 2) // 128) * 128


def assemble(here, place, offsets, stack, evens, odds, n_rows):
    slots, width, ncols = stack.shape
    steps = place.shape[0]
    height = steps * width
    turns, splits = len(evens), len(evens[0])
    cols = ncols // splits

    def kernel(here_ref, place_ref, offset_ref, stack_ref, *refs):
        arrived, (high_ref, low_ref, both_t_ref, gram_ref, held, sems) = refs[:-6], refs[-6:]
        even, odd = arrived[:turns * splits], arrived[turns * splits:]
        roots, slot, ranks, counts = plan(place_ref, slots, n_rows)
        me = here_ref[0]
        me_odd = lax.rem(me, 2) == 1
        for s in range(steps):
            root = roots[s]
            low, high = jnp.minimum(root, me), jnp.maximum(root, me)
            between = [jnp.where((i > low) & (i < high), jnp.maximum(counts[i], 1), 0) for i in range(n_rows)]
            turn = sum(between, ranks[s])
            target = held.at[pl.ds(s * width, width)]
            below, above = root < me, root > me

            @pl.when(root == me)
            def _():
                pltpu.make_async_copy(stack_ref.at[slot[s]], target, sems.at[s]).start()

            for side, came in (((below & me_odd) | (above & ~me_odd), even), ((below & ~me_odd) | (above & me_odd), odd)):
                for i in range(turns):
                    @pl.when(side & (turn == i))
                    def _():
                        for p in range(splits):
                            piece = held.at[pl.ds(s * width, width), pl.ds(p * cols, cols)]
                            pltpu.make_async_copy(came[i * splits + p], piece, sems.at[s]).start()
        columns = here_ref[1] * ncols + lax.broadcasted_iota(jnp.int32, (width, ncols), 1)
        for s in range(steps):
            rows = pl.ds(s * width, width)
            pltpu.make_async_copy(stack_ref.at[0], held.at[rows], sems.at[s]).wait()
            masked = jnp.where(columns >= offset_ref[s], held[rows, :], 0.0)
            held[rows, :] = masked
            high, low = halves(masked)
            high_ref[rows, :] = high
            low_ref[rows, :] = low
        for at in column_blocks(ncols):
            high, low = halves(held[:, at].T)
            both_t_ref[at, :] = jnp.concatenate([high, low], axis=1)
        gram = dot_t(held[...], held[...])
        gram_ref[...] = jnp.zeros_like(gram_ref)
        first = 0
        for s in range(1, steps):
            gram_ref[:, first:first + s * width] = gram[s * width:(s + 1) * width, :s * width]
            first += s * width

    return pl.pallas_call(
        kernel,
        out_shape=[
            pltpu.HBM((height, ncols), jnp.bfloat16),
            pltpu.HBM((height, ncols), jnp.bfloat16),
            pltpu.HBM((ncols, 2 * height), jnp.bfloat16),
            jax.ShapeDtypeStruct((width, packed_width(steps, width)), jnp.float32),
        ],
        in_specs=[SMEM, SMEM, SMEM, ANY] + [ANY] * (2 * turns * splits),
        out_specs=[VMEM] * 4,
        scratch_shapes=[pltpu.VMEM((height, ncols), jnp.float32), pltpu.SemaphoreType.DMA((steps,))],
        compiler_params=params(limit=SMALL_LIMIT),
        cost_estimate=cost(12 * height * height * ncols, 8 * height * ncols),
        name="assemble",
    )(here, place, offsets, stack, *[p for turn in evens for p in turn], *[p for turn in odds for p in turn])


def merge(cross, factors, vecs):
    steps, width, _ = factors.shape
    height, ncols = vecs[0].shape

    def kernel(*refs):
        cross_refs, (factor_ref, v_high, v_low, p_ref, total, m_ref) = refs[:-6], refs[-6:]
        total[...] = sum([ref[...] for ref in cross_refs[1:]], cross_refs[0][...])
        first = 0
        for k in range(steps):
            own = lax.broadcasted_iota(jnp.int32, (width, height), 0) + k * width
            rest = (own == lax.broadcasted_iota(jnp.int32, (width, height), 1)).astype(jnp.float32)
            if k:
                rest = rest - dot(total[:, first:first + k * width], m_ref[:k * width, :])
                first += k * width
            m_ref[k * width:(k + 1) * width, :] = dot(factor_ref[k], rest)
        product = dot3(halves(m_ref[...].T), (v_high[...], v_low[...]), ((1,), (0,)))
        high, low = halves(product)
        for i, half in enumerate((high, high, low)):
            p_ref[i * height:(i + 1) * height, :] = half

    return pl.pallas_call(
        kernel,
        out_shape=jax.ShapeDtypeStruct((3 * height, ncols), jnp.bfloat16),
        out_specs=VMEM,
        in_specs=[VMEM] * (len(cross) + 3),
        scratch_shapes=[pltpu.VMEM(cross[0].shape, jnp.float32), pltpu.VMEM((height, height), jnp.float32)],
        compiler_params=params(),
        cost_estimate=cost(6 * height * height * ncols, 8 * height * ncols),
        name="merge",
    )(*cross, factors, *vecs)


def fold(w):
    half = w.shape[0] // 2
    return jnp.concatenate([w[:half], w[half:]], axis=1)


def unfold(w):
    height = w.shape[1] // 2
    return jnp.concatenate([w[:, :height], w[:, height:]], axis=0)


def column_blocks(ncols):
    cols = COLUMNS if ncols % COLUMNS == 0 else ncols
    return [pl.ds(start, cols) for start in range(0, ncols, cols)]


def inner_products(here, x, vecs_t):
    lead, rows, ncols = x.shape
    height = vecs_t.shape[1] // 2
    half = lead * rows // 2
    lanes = min(-(-height // 128) * 128, 2 * height)
    cuts = sorted({0, lead // 4, lead * 5 // 8, lead})

    def kernel(here_ref, x_ref, vecs_ref, mine_ref, theirs_ref, held, total, sems):
        copies = [pltpu.make_async_copy(x_ref.at[i], held.at[i], sems.at[i]) for i in range(lead)]
        for i, copy in enumerate(copies):
            copy.start(priority=i % QUEUES)
        for start, end in zip(cuts[:-1], cuts[1:]):
            for copy in copies[start:end]:
                copy.wait()
            high, low = halves(held[start:end].reshape((end - start) * rows, ncols))
            by_high = jnp.dot(high, vecs_ref[...], preferred_element_type=jnp.float32)
            by_low = jnp.dot(low, vecs_ref[:, :lanes], preferred_element_type=jnp.float32)
            total[start * rows:end * rows, :] = by_high[:, :height] + (by_high[:, height:] + by_low[:, :height])
        core = lax.rem(here_ref[1], 2)
        mine_ref[...] = fold(total[pl.ds(pl.multiple_of(core * half, 8), half), :])
        theirs_ref[...] = fold(total[pl.ds(pl.multiple_of((1 - core) * half, 8), half), :])

    return pl.pallas_call(
        kernel,
        out_shape=[jax.ShapeDtypeStruct((half // 2, 2 * height), jnp.float32)] * 2 + [pltpu.VMEM(x.shape, jnp.float32)],
        in_specs=[SMEM, ANY, VMEM],
        out_specs=[VMEM] * 3,
        scratch_shapes=[
            pltpu.VMEM((lead * rows, height), jnp.float32),
            pltpu.SemaphoreType.DMA((lead,)),
        ],
        compiler_params=params(),
        cost_estimate=cost(6 * lead * rows * ncols * height, 4 * lead * rows * ncols),
        name="inner_products",
    )(here, in_hbm(x), vecs_t)


def update(here, x, mine, theirs, changes):
    lead, rows, ncols = x.shape
    height = changes.shape[0] // 3
    half = lead * rows // 2
    blocks = column_blocks(ncols)
    depth = min(4, len(blocks))

    def kernel(here_ref, mine_ref, theirs_ref, x_ref, p_ref, out_ref, w_ref, held, sems):
        core = lax.rem(here_ref[1], 2)
        w_ref[pl.ds(pl.multiple_of(core * half, 8), half), :] = unfold(mine_ref[...])
        w_ref[pl.ds(pl.multiple_of((1 - core) * half, 8), half), :] = unfold(theirs_ref[...])
        high, low = halves(w_ref[...])
        w = jnp.concatenate([high, low, high], axis=1)
        copies = [pltpu.make_async_copy(held.at[i % depth], out_ref.at[:, :, at], sems.at[i]) for i, at in enumerate(blocks)]
        for i, at in enumerate(blocks):
            change = lax.dot_general(w, p_ref[:, at], (((1,), (0,)), ((), ())), preferred_element_type=jnp.float32)
            if i >= depth:
                copies[i - depth].wait()
            held[i % depth] = x_ref[:, :, at] - change.reshape(lead, rows, at.size)
            copies[i].start(priority=i % QUEUES)
        for copy in copies[-depth:]:
            copy.wait()

    return pl.pallas_call(
        kernel,
        out_shape=jax.ShapeDtypeStruct(x.shape, jnp.float32),
        in_specs=[SMEM] + [VMEM] * 4,
        out_specs=ANY,
        scratch_shapes=[
            pltpu.VMEM((lead * rows, height), jnp.float32),
            pltpu.VMEM((depth, lead, rows, blocks[0].size), jnp.float32),
            pltpu.SemaphoreType.DMA((len(blocks),)),
        ],
        compiler_params=params(),
        cost_estimate=cost(6 * lead * rows * ncols * height, 8 * lead * rows * ncols),
        name="update",
    )(here, mine, theirs, x, changes)


def swap(array, k, size):
    return lax.ppermute(array, "wide", [(i, i ^ k) for i in range(size)])


def spread(pair, size):
    return [pair] + [swap(pair, k, size) for k in range(2, size, 2)]


def chips_sum(pair, size, token):
    shifts = [k for k in (1 << i for i in range(1, size.bit_length())) if k < size]
    half = pair.shape[0] // 2
    upper, lower = pair[:half], pair[half:]
    for i, (first, second) in enumerate(zip(shifts, reversed(shifts))):
        come_upper, come_lower = swap(upper, first, size), swap(lower, second, size)
        if i == 0:
            upper, lower, _ = lax.optimization_barrier((upper, lower, token))
        upper, lower = upper + come_upper, lower + come_lower
    return jnp.concatenate([upper, lower], axis=0)


def body(n_row, n_wide, eigvec_t, householder, wy_factor, block_place, offsets):
    rows, order = eigvec_t.shape
    steps, width, _ = wy_factor.shape
    slots = householder.shape[0]
    ncols = order // n_wide
    here = jnp.stack([lax.axis_index("row"), lax.axis_index("wide")]).astype(jnp.int32)

    turns = max(z + min(steps - 1, slots * (n_row - 1 - z)) for z in range(n_row - 1))
    cols = ncols // SPLITS
    streams = [([], []) for _ in range(SPLITS)]

    def exchange(array, odd):
        pairs = []
        for z in range(n_row):
            mate = ((z + odd) ^ 1) - odd
            for w in range(n_wide):
                target = mate * n_wide + w if 0 <= mate < n_row else z * n_wide + (w ^ 1)
                pairs.append((z * n_wide + w, target))
        return lax.ppermute(array, ("row", "wide"), pairs)

    whole = rows % 8 == 0
    if whole:
        piece = pack(eigvec_t, n_wide)
        x = lax.all_to_all(piece, "wide", split_axis=0, concat_axis=0, tiled=True)
        tokens = [piece]
    else:
        x = lax.all_to_all(eigvec_t, "wide", split_axis=1, concat_axis=0, tiled=True)[None]
        tokens = []
    for turn in range(turns):
        for part in range(SPLITS):
            evens, odds = streams[part]
            to_even, to_odd = feed(after(here, *tokens), block_place, householder, evens, odds, n_row, part, cols)
            tokens = [to_odd]
            streams[part] = (evens + [exchange(to_even, 0)], odds + [exchange(to_odd, 1)])
    evens = list(zip(*[stream[0] for stream in streams]))
    odds = list(zip(*[stream[1] for stream in streams]))
    high, low, both_t, gram = assemble(here, block_place, offsets, householder, evens, odds, n_row)
    cross = spread(gram + swap(gram, 1, n_wide), n_wide)
    cross[0] = after(cross[0], x)
    cross = functools.reduce(jnp.add, cross)
    changes = merge([cross], wy_factor, (high, low))

    mine, theirs, x = inner_products(after(here, cross), x, both_t)
    mine = chips_sum(mine + swap(theirs, 1, n_wide), n_wide, changes)
    return update(here, x, mine, swap(mine, 1, n_wide), changes).reshape(n_wide * rows, ncols)


def solution(mesh):
    return jax.shard_map(
        functools.partial(body, mesh.shape["row"], mesh.shape["wide"]),
        mesh=mesh,
        in_specs=(P(("row", "wide"), None), P("row", None, "wide"), P(), P(), P()),
        out_specs=P("row", "wide"),
        check_vma=False,
    )
```

```python
import functools

import jax
import jax.numpy as jnp
from jax import lax
from jax.experimental import pallas as pl
from jax.experimental.pallas import tpu as pltpu
from jax.sharding import PartitionSpec as P

HIGHEST = lax.Precision.HIGHEST
SMALL_LIMIT = 44 * 1024 * 1024
VMEM_LIMIT = 40 * 1024 * 1024
LARGE_LIMIT = 58 * 1024 * 1024
COLUMNS = 512
QUEUES = 2
SPLITS = 2


def dot_t(a, b):
    return lax.dot_general(a, b, (((1,), (1,)), ((), ())), precision=HIGHEST, preferred_element_type=jnp.float32)


def dot(a, b):
    return lax.dot_general(a, b, (((1,), (0,)), ((), ())), precision=HIGHEST, preferred_element_type=jnp.float32)


def halves(x):
    high = x.astype(jnp.bfloat16)
    return high, (x - high.astype(jnp.float32)).astype(jnp.bfloat16)


def dot3(a, b, dims):
    rows = a[0].shape[0]
    both = lax.dot_general(jnp.concatenate(a, axis=0), b[0], (dims, ((), ())), preferred_element_type=jnp.float32)
    last = lax.dot_general(a[0], b[1], (dims, ((), ())), preferred_element_type=jnp.float32)
    return both[:rows] + (both[rows:] + last)


def after(x, *tokens):
    return lax.optimization_barrier((x, *tokens))[0]


def params(limit=VMEM_LIMIT):
    return pltpu.CompilerParams(vmem_limit_bytes=limit)


def cost(flops, nbytes):
    return pl.CostEstimate(flops=flops, bytes_accessed=nbytes, transcendentals=0)


SMEM = pl.BlockSpec(memory_space=pltpu.SMEM)
ANY = pl.BlockSpec(memory_space=pl.ANY)
VMEM = pl.BlockSpec(memory_space=pltpu.VMEM)


def in_hbm(x):
    return pltpu.with_memory_space_constraint(x, pltpu.HBM)


def pack(x, n_wide):
    rows, order = x.shape
    ncols = order // n_wide
    step = 16 if rows % 16 == 0 else rows
    n_copies = n_wide * rows // step

    def kernel(x_ref, out_ref, held, in_sems, out_sems):
        into, out_of = [], []
        for first in range(0, rows, step):
            for k in range(n_wide):
                i, at = len(into), pl.ds(first, step)
                source = x_ref.at[at, pl.ds(k * ncols, ncols)]
                into.append(pltpu.make_async_copy(source, held.at[k, at], in_sems.at[i]))
                out_of.append(pltpu.make_async_copy(held.at[k, at], out_ref.at[k, at], out_sems.at[i]))
        for i, copy in enumerate(into):
            copy.start(priority=i % QUEUES)
        for i, (came, goes) in enumerate(zip(into, out_of)):
            came.wait()
            goes.start(priority=i % QUEUES)
        for copy in out_of:
            copy.wait()

    return pl.pallas_call(
        kernel,
        out_shape=jax.ShapeDtypeStruct((n_wide, rows, ncols), jnp.float32),
        in_specs=[ANY],
        out_specs=ANY,
        scratch_shapes=[
            pltpu.VMEM((n_wide, rows, ncols), jnp.float32),
            pltpu.SemaphoreType.DMA((n_copies,)),
            pltpu.SemaphoreType.DMA((n_copies,)),
        ],
        compiler_params=params(limit=LARGE_LIMIT),
        cost_estimate=cost(0, 8 * rows * order),
        name="pack",
    )(in_hbm(x))


def plan(place_ref, slots, n_rows):
    places = [place_ref[s] for s in range(place_ref.shape[0])]
    roots = [lax.div(p, slots) for p in places]
    slot = [lax.rem(p, slots) for p in places]
    ranks = [sum([(roots[i] == roots[s]).astype(jnp.int32) for i in range(s)], jnp.int32(0)) for s in range(len(places))]
    counts = [sum([(r == i).astype(jnp.int32) for r in roots], jnp.int32(0)) for i in range(n_rows)]
    return roots, slot, ranks, counts


def feed(here, place, stack, evens, odds, n_rows, part, cols):
    slots, width, _ = stack.shape
    turn = len(evens)

    def kernel(here_ref, place_ref, stack_ref, *refs):
        arrived, (out_even, out_odd, sems) = refs[:-3], refs[-3:]
        roots, slot, ranks, _ = plan(place_ref, slots, n_rows)
        me = here_ref[0]
        mine = [r == me for r in roots]
        count = sum([m.astype(jnp.int32) for m in mine], jnp.int32(0))
        own = sum([jnp.where(m & (k == turn), s, 0) for m, k, s in zip(mine, ranks, slot)], jnp.int32(0))
        older = turn - jnp.maximum(count, 1)
        stored = stack_ref.at[own, :, pl.ds(part * cols, cols)]
        for side, out in ((0, out_even), (1, out_odd)):
            @pl.when((older < 0) | (count > turn))
            def _():
                pltpu.make_async_copy(stored, out, sems.at[side]).start()

            for i in range(turn):
                @pl.when((older == i) & (count <= turn))
                def _():
                    pltpu.make_async_copy(arrived[(1 - side) * turn + i], out, sems.at[side]).start()
        for side, out in ((0, out_even), (1, out_odd)):
            pltpu.make_async_copy(stored, out, sems.at[side]).wait()

    return pl.pallas_call(
        kernel,
        out_shape=[jax.ShapeDtypeStruct((width, cols), jnp.float32)] * 2,
        in_specs=[SMEM, SMEM, ANY] + [ANY] * (2 * turn),
        out_specs=[VMEM] * 2,
        scratch_shapes=[pltpu.SemaphoreType.DMA((2,))],
        compiler_params=params(limit=SMALL_LIMIT),
        cost_estimate=cost(0, 16 * width * cols),
        name="feed",
    )(here, place, stack, *evens, *odds)


def packed_width(steps, width):
    return -(-(width * steps * (steps - 1) // 2) // 128) * 128


def assemble(here, place, offsets, stack, evens, odds, n_rows):
    slots, width, ncols = stack.shape
    steps = place.shape[0]
    height = steps * width
    turns, splits = len(evens), len(evens[0])
    cols = ncols // splits

    def kernel(here_ref, place_ref, offset_ref, stack_ref, *refs):
        arrived, (high_ref, low_ref, both_t_ref, gram_ref, held, sems) = refs[:-6], refs[-6:]
        even, odd = arrived[:turns * splits], arrived[turns * splits:]
        roots, slot, ranks, counts = plan(place_ref, slots, n_rows)
        me = here_ref[0]
        me_odd = lax.rem(me, 2) == 1
        for s in range(steps):
            root = roots[s]
            low, high = jnp.minimum(root, me), jnp.maximum(root, me)
            between = [jnp.where((i > low) & (i < high), jnp.maximum(counts[i], 1), 0) for i in range(n_rows)]
            turn = sum(between, ranks[s])
            target = held.at[pl.ds(s * width, width)]
            below, above = root < me, root > me

            @pl.when(root == me)
            def _():
                pltpu.make_async_copy(stack_ref.at[slot[s]], target, sems.at[s]).start()

            for side, came in (((below & me_odd) | (above & ~me_odd), even), ((below & ~me_odd) | (above & me_odd), odd)):
                for i in range(turns):
                    @pl.when(side & (turn == i))
                    def _():
                        for p in range(splits):
                            piece = held.at[pl.ds(s * width, width), pl.ds(p * cols, cols)]
                            pltpu.make_async_copy(came[i * splits + p], piece, sems.at[s]).start()
        columns = here_ref[1] * ncols + lax.broadcasted_iota(jnp.int32, (width, ncols), 1)
        for s in range(steps):
            rows = pl.ds(s * width, width)
            pltpu.make_async_copy(stack_ref.at[0], held.at[rows], sems.at[s]).wait()
            masked = jnp.where(columns >= offset_ref[s], held[rows, :], 0.0)
            held[rows, :] = masked
            high, low = halves(masked)
            high_ref[rows, :] = high
            low_ref[rows, :] = low
        for at in column_blocks(ncols):
            high, low = halves(held[:, at].T)
            both_t_ref[at, :] = jnp.concatenate([high, low], axis=1)
        gram = dot_t(held[...], held[...])
        gram_ref[...] = jnp.zeros_like(gram_ref)
        first = 0
        for s in range(1, steps):
            gram_ref[:, first:first + s * width] = gram[s * width:(s + 1) * width, :s * width]
            first += s * width

    return pl.pallas_call(
        kernel,
        out_shape=[
            pltpu.HBM((height, ncols), jnp.bfloat16),
            pltpu.HBM((height, ncols), jnp.bfloat16),
            pltpu.HBM((ncols, 2 * height), jnp.bfloat16),
            jax.ShapeDtypeStruct((width, packed_width(steps, width)), jnp.float32),
        ],
        in_specs=[SMEM, SMEM, SMEM, ANY] + [ANY] * (2 * turns * splits),
        out_specs=[VMEM] * 4,
        scratch_shapes=[pltpu.VMEM((height, ncols), jnp.float32), pltpu.SemaphoreType.DMA((steps,))],
        compiler_params=params(limit=SMALL_LIMIT),
        cost_estimate=cost(12 * height * height * ncols, 8 * height * ncols),
        name="assemble",
    )(here, place, offsets, stack, *[p for turn in evens for p in turn], *[p for turn in odds for p in turn])


def merge(cross, factors, vecs):
    steps, width, _ = factors.shape
    height, ncols = vecs[0].shape

    def kernel(*refs):
        cross_refs, (factor_ref, v_high, v_low, p_ref, total, m_ref) = refs[:-6], refs[-6:]
        total[...] = sum([ref[...] for ref in cross_refs[1:]], cross_refs[0][...])
        first = 0
        for k in range(steps):
            own = lax.broadcasted_iota(jnp.int32, (width, height), 0) + k * width
            rest = (own == lax.broadcasted_iota(jnp.int32, (width, height), 1)).astype(jnp.float32)
            if k:
                rest = rest - dot(total[:, first:first + k * width], m_ref[:k * width, :])
                first += k * width
            m_ref[k * width:(k + 1) * width, :] = dot(factor_ref[k], rest)
        product = dot3(halves(m_ref[...].T), (v_high[...], v_low[...]), ((1,), (0,)))
        high, low = halves(product)
        for i, half in enumerate((high, high, low)):
            p_ref[i * height:(i + 1) * height, :] = half

    return pl.pallas_call(
        kernel,
        out_shape=jax.ShapeDtypeStruct((3 * height, ncols), jnp.bfloat16),
        out_specs=VMEM,
        in_specs=[VMEM] * (len(cross) + 3),
        scratch_shapes=[pltpu.VMEM(cross[0].shape, jnp.float32), pltpu.VMEM((height, height), jnp.float32)],
        compiler_params=params(),
        cost_estimate=cost(6 * height * height * ncols, 8 * height * ncols),
        name="merge",
    )(*cross, factors, *vecs)


def fold(w):
    half = w.shape[0] // 2
    return jnp.concatenate([w[:half], w[half:]], axis=1)


def unfold(w):
    height = w.shape[1] // 2
    return jnp.concatenate([w[:, :height], w[:, height:]], axis=0)


def column_blocks(ncols):
    cols = COLUMNS if ncols % COLUMNS == 0 else ncols
    return [pl.ds(start, cols) for start in range(0, ncols, cols)]


def lift(x):
    rows = x.shape[0]
    step = rows // 4 if rows % 64 == 0 else rows

    def kernel(x_ref, out_ref, sems):
        copies = [
            pltpu.make_async_copy(x_ref.at[pl.ds(start, step)], out_ref.at[pl.ds(start, step)], sems.at[i])
            for i, start in enumerate(range(0, rows, step))
        ]
        for i, copy in enumerate(copies):
            copy.start(priority=i % QUEUES)
        for copy in copies:
            copy.wait()

    return pl.pallas_call(
        kernel,
        out_shape=pltpu.VMEM(x.shape, x.dtype),
        in_specs=[ANY],
        out_specs=VMEM,
        scratch_shapes=[pltpu.SemaphoreType.DMA((rows // step,))],
        compiler_params=params(),
        cost_estimate=cost(0, 2 * x.size),
        name="lift",
    )(in_hbm(x))


def inner_products(here, x, vecs_t):
    rows, ncols = x.shape
    height = vecs_t.shape[1] // 2
    half = rows // 2
    lanes = min(-(-height // 128) * 128, 2 * height)
    step = rows // 8 if rows % 64 == 0 else rows
    n_copies = rows // step
    cuts = sorted({0, n_copies // 4, n_copies * 5 // 8, n_copies})

    def kernel(here_ref, x_ref, vecs_ref, mine_ref, theirs_ref, held, total, sems):
        copies = []
        for i in range(n_copies):
            at = pl.ds(i * step, step)
            copies.append(pltpu.make_async_copy(x_ref.at[at], held.at[at], sems.at[i]))
        for i, copy in enumerate(copies):
            copy.start(priority=i % QUEUES)
        for start, end in zip(cuts[:-1], cuts[1:]):
            for copy in copies[start:end]:
                copy.wait()
            at = pl.ds(start * step, (end - start) * step)
            high, low = halves(held[at, :])
            by_high = jnp.dot(high, vecs_ref[...], preferred_element_type=jnp.float32)
            by_low = jnp.dot(low, vecs_ref[:, :lanes], preferred_element_type=jnp.float32)
            total[at, :] = by_high[:, :height] + (by_high[:, height:] + by_low[:, :height])
        core = lax.rem(here_ref[1], 2)
        mine_ref[...] = fold(total[pl.ds(pl.multiple_of(core * half, 8), half), :])
        theirs_ref[...] = fold(total[pl.ds(pl.multiple_of((1 - core) * half, 8), half), :])

    return pl.pallas_call(
        kernel,
        out_shape=[jax.ShapeDtypeStruct((half // 2, 2 * height), jnp.float32)] * 2 + [pltpu.VMEM(x.shape, jnp.float32)],
        in_specs=[SMEM, ANY, VMEM],
        out_specs=[VMEM] * 3,
        scratch_shapes=[pltpu.VMEM((rows, height), jnp.float32), pltpu.SemaphoreType.DMA((n_copies,))],
        compiler_params=params(),
        cost_estimate=cost(6 * rows * ncols * height, 4 * rows * ncols),
        name="inner_products",
    )(here, in_hbm(x), vecs_t)


def update(here, x, sums, changes, out, other):
    rows, ncols = x.shape
    half = rows // 2
    blocks = column_blocks(ncols)
    depth = min(4, len(blocks))

    def kernel(here_ref, sum_ref, x_ref, p_ref, *refs):
        out_ref, held, sems = refs[-3:]
        core = lax.rem(here_ref[1], 2)
        mine = pl.ds(pl.multiple_of((1 - core if other else core) * half, 8), half)
        high, low = halves(unfold(sum_ref[...]))
        w = jnp.concatenate([high, low, high], axis=1)
        copies = [pltpu.make_async_copy(held.at[i % depth], out_ref.at[mine, at], sems.at[i]) for i, at in enumerate(blocks)]
        for i, at in enumerate(blocks):
            change = jnp.dot(w, p_ref[:, at], preferred_element_type=jnp.float32)
            if i >= depth:
                copies[i - depth].wait()
            held[i % depth] = x_ref[mine, at] - change
            copies[i].start(priority=i % QUEUES)
        for copy in copies[-depth:]:
            copy.wait()

    operands = [here, sums, x, changes]
    in_specs = [SMEM] + [VMEM] * 3
    aliases = {}
    if out is not None:
        aliases = {len(operands): 0}
        operands.append(out)
        in_specs.append(ANY)
    return pl.pallas_call(
        kernel,
        out_shape=jax.ShapeDtypeStruct(x.shape, jnp.float32),
        in_specs=in_specs,
        out_specs=ANY,
        scratch_shapes=[
            pltpu.VMEM((depth, half, blocks[0].size), jnp.float32),
            pltpu.SemaphoreType.DMA((len(blocks),)),
        ],
        input_output_aliases=aliases,
        compiler_params=params(),
        cost_estimate=cost(3 * rows * ncols * changes.shape[0], 4 * rows * ncols),
        name="update",
    )(*operands)


def swap(array, k, size):
    return lax.ppermute(array, "wide", [(i, i ^ k) for i in range(size)])


def spread(pair, size):
    return [pair] + [swap(pair, k, size) for k in range(2, size, 2)]


def chips_sum(pair, size, token):
    shifts = [k for k in (1 << i for i in range(1, size.bit_length())) if k < size]
    half = pair.shape[0] // 2
    upper, lower = pair[:half], pair[half:]
    for i, (first, second) in enumerate(zip(shifts, reversed(shifts))):
        come_upper, come_lower = swap(upper, first, size), swap(lower, second, size)
        if i == 0:
            upper, lower, _ = lax.optimization_barrier((upper, lower, token))
        upper, lower = upper + come_upper, lower + come_lower
    return jnp.concatenate([upper, lower], axis=0)


def body(n_row, n_wide, eigvec_t, householder, wy_factor, block_place, offsets):
    rows, order = eigvec_t.shape
    steps, width, _ = wy_factor.shape
    slots = householder.shape[0]
    ncols = order // n_wide
    here = jnp.stack([lax.axis_index("row"), lax.axis_index("wide")]).astype(jnp.int32)

    turns = max(z + min(steps - 1, slots * (n_row - 1 - z)) for z in range(n_row - 1))
    cols = ncols // SPLITS
    streams = [([], []) for _ in range(SPLITS)]

    def exchange(array, odd):
        pairs = []
        for z in range(n_row):
            mate = ((z + odd) ^ 1) - odd
            for w in range(n_wide):
                target = mate * n_wide + w if 0 <= mate < n_row else z * n_wide + (w ^ 1)
                pairs.append((z * n_wide + w, target))
        return lax.ppermute(array, ("row", "wide"), pairs)

    whole = rows % 8 == 0
    if whole:
        piece = pack(eigvec_t, n_wide)
        x = lax.all_to_all(piece, "wide", split_axis=0, concat_axis=0, tiled=True)
        tokens = [piece]
    else:
        x = lax.all_to_all(eigvec_t, "wide", split_axis=1, concat_axis=0, tiled=True)[None]
        tokens = []
    for turn in range(turns):
        for part in range(SPLITS):
            evens, odds = streams[part]
            to_even, to_odd = feed(after(here, *tokens), block_place, householder, evens, odds, n_row, part, cols)
            tokens = [to_odd]
            streams[part] = (evens + [exchange(to_even, 0)], odds + [exchange(to_odd, 1)])
    evens = list(zip(*[stream[0] for stream in streams]))
    odds = list(zip(*[stream[1] for stream in streams]))
    high, low, both_t, gram = assemble(here, block_place, offsets, householder, evens, odds, n_row)
    cross = spread(gram + swap(gram, 1, n_wide), n_wide)
    x = x.reshape(n_wide * rows, ncols)
    both_t = lift(after(both_t, x))
    cross[0] = after(cross[0], both_t)
    cross = functools.reduce(jnp.add, cross)
    changes = merge([cross], wy_factor, (high, low))

    mine, theirs, x = inner_products(after(here, cross), x, both_t)
    mine = chips_sum(mine + swap(theirs, 1, n_wide), n_wide, changes)
    theirs = swap(mine, 1, n_wide)
    out = update(here, x, mine, changes, None, False)
    return update(here, x, theirs, changes, out, True)


def solution(mesh):
    return jax.shard_map(
        functools.partial(body, mesh.shape["row"], mesh.shape["wide"]),
        mesh=mesh,
        in_specs=(P(("row", "wide"), None), P("row", None, "wide"), P(), P(), P()),
        out_specs=P("row", "wide"),
        check_vma=False,
    )
```

```python
import functools

import jax
import jax.numpy as jnp
from jax import lax
from jax.experimental import pallas as pl
from jax.experimental.pallas import tpu as pltpu
from jax.sharding import PartitionSpec as P

HIGHEST = lax.Precision.HIGHEST
SMALL_LIMIT = 44 * 1024 * 1024
VMEM_LIMIT = 40 * 1024 * 1024
LARGE_LIMIT = 58 * 1024 * 1024
COLUMNS = 512
QUEUES = 2
ARRIVED = (4, 0)
SPLITS = 2


def dot_t(a, b):
    return lax.dot_general(a, b, (((1,), (1,)), ((), ())), precision=HIGHEST, preferred_element_type=jnp.float32)


def dot(a, b):
    return lax.dot_general(a, b, (((1,), (0,)), ((), ())), precision=HIGHEST, preferred_element_type=jnp.float32)


def halves(x):
    high = x.astype(jnp.bfloat16)
    return high, (x - high.astype(jnp.float32)).astype(jnp.bfloat16)


def dot3(a, b, dims):
    rows = a[0].shape[0]
    both = lax.dot_general(jnp.concatenate(a, axis=0), b[0], (dims, ((), ())), preferred_element_type=jnp.float32)
    last = lax.dot_general(a[0], b[1], (dims, ((), ())), preferred_element_type=jnp.float32)
    return both[:rows] + (both[rows:] + last)


def after(x, *tokens):
    return lax.optimization_barrier((x, *tokens))[0]


def params(limit=VMEM_LIMIT):
    return pltpu.CompilerParams(vmem_limit_bytes=limit)


def cost(flops, nbytes):
    return pl.CostEstimate(flops=flops, bytes_accessed=nbytes, transcendentals=0)


SMEM = pl.BlockSpec(memory_space=pltpu.SMEM)
ANY = pl.BlockSpec(memory_space=pl.ANY)
VMEM = pl.BlockSpec(memory_space=pltpu.VMEM)


def in_hbm(x):
    return pltpu.with_memory_space_constraint(x, pltpu.HBM)


def pack(x, base, rows, n_wide):
    order = x.shape[1]
    ncols = order // n_wide
    step = 16 if rows % 16 == 0 else rows
    n_copies = n_wide * rows // step

    def kernel(x_ref, out_ref, held, in_sems, out_sems):
        into, out_of = [], []
        for first in range(0, rows, step):
            for k in range(n_wide):
                i, at = len(into), pl.ds(first, step)
                source = x_ref.at[pl.ds(base + first, step), pl.ds(k * ncols, ncols)]
                into.append(pltpu.make_async_copy(source, held.at[k, at], in_sems.at[i]))
                out_of.append(pltpu.make_async_copy(held.at[k, at], out_ref.at[k, at], out_sems.at[i]))
        for i, copy in enumerate(into):
            copy.start(priority=i % QUEUES)
        for i, (came, goes) in enumerate(zip(into, out_of)):
            came.wait()
            goes.start(priority=i % QUEUES)
        for copy in out_of:
            copy.wait()

    return pl.pallas_call(
        kernel,
        out_shape=jax.ShapeDtypeStruct((n_wide, rows, ncols), jnp.float32),
        in_specs=[ANY],
        out_specs=ANY,
        scratch_shapes=[
            pltpu.VMEM((n_wide, rows, ncols), jnp.float32),
            pltpu.SemaphoreType.DMA((n_copies,)),
            pltpu.SemaphoreType.DMA((n_copies,)),
        ],
        compiler_params=params(limit=LARGE_LIMIT),
        cost_estimate=cost(0, 8 * rows * order),
        name="pack",
    )(in_hbm(x))


def plan(place_ref, slots, n_rows):
    places = [place_ref[s] for s in range(place_ref.shape[0])]
    roots = [lax.div(p, slots) for p in places]
    slot = [lax.rem(p, slots) for p in places]
    ranks = [sum([(roots[i] == roots[s]).astype(jnp.int32) for i in range(s)], jnp.int32(0)) for s in range(len(places))]
    counts = [sum([(r == i).astype(jnp.int32) for r in roots], jnp.int32(0)) for i in range(n_rows)]
    return roots, slot, ranks, counts


def feed(here, place, stack, turn, turns, last, store, n_rows, part, cols):
    slots, width, _ = stack.shape

    def kernel(here_ref, place_ref, stack_ref, *refs):
        last_refs, (out_even, out_odd, *store_refs, sems) = refs[:len(last)], refs[len(last) + (store is not None):]
        roots, slot, ranks, _ = plan(place_ref, slots, n_rows)
        me = here_ref[0]
        mine = [r == me for r in roots]
        count = sum([m.astype(jnp.int32) for m in mine], jnp.int32(0))
        own = sum([jnp.where(m & (k == turn), s, 0) for m, k, s in zip(mine, ranks, slot)], jnp.int32(0))
        older = turn - jnp.maximum(count, 1)
        stored = stack_ref.at[own, :, pl.ds(part * cols, cols)]
        for side, out in ((0, out_even), (1, out_odd)):
            @pl.when((older < 0) | (count > turn))
            def _():
                pltpu.make_async_copy(stored, out, sems.at[side]).start()

            for i in range(turn):
                source = last_refs[1 - side] if i == turn - 1 else store_refs[0].at[1 - side, i]

                @pl.when((older == i) & (count <= turn))
                def _():
                    pltpu.make_async_copy(source, out, sems.at[side]).start()
        keeps = [
            pltpu.make_async_copy(ref, store_refs[0].at[side, turn - 1], sems.at[2 + side]) for side, ref in enumerate(last_refs)
        ]
        for keep in keeps:
            keep.start()
        for side, out in ((0, out_even), (1, out_odd)):
            pltpu.make_async_copy(stored, out, sems.at[side]).wait()
        for keep in keeps:
            keep.wait()

    out_shape = [jax.ShapeDtypeStruct((width, cols), jnp.float32)] * 2
    out_specs = [VMEM] * 2
    operands = [here, place, stack, *last]
    aliases = {}
    if turn > 0:
        out_shape.append(pltpu.HBM((2, turns, width, cols), jnp.float32))
        out_specs.append(ANY)
    if store is not None:
        aliases = {len(operands): 2}
        operands.append(store)
    results = pl.pallas_call(
        kernel,
        out_shape=out_shape,
        in_specs=[SMEM, SMEM] + [ANY] * (len(operands) - 2),
        out_specs=out_specs,
        scratch_shapes=[pltpu.SemaphoreType.DMA((4,))],
        input_output_aliases=aliases,
        compiler_params=params(limit=SMALL_LIMIT),
        cost_estimate=cost(0, 16 * width * cols),
        name="feed",
    )(*operands)
    return results[0], results[1], (results[2] if turn > 0 else None)


def packed_width(steps, width):
    return -(-(width * steps * (steps - 1) // 2) // 128) * 128


def assemble(here, place, offsets, stack, stores, lasts, n_rows):
    slots, width, ncols = stack.shape
    steps = place.shape[0]
    height = steps * width
    turns, splits = stores[0].shape[1], len(stores)
    cols = ncols // splits

    def kernel(here_ref, place_ref, offset_ref, stack_ref, *refs):
        arrived, (high_ref, low_ref, both_t_ref, gram_ref, held, sems) = refs[:-6], refs[-6:]
        kept, latest = arrived[:splits], arrived[splits:]
        roots, slot, ranks, counts = plan(place_ref, slots, n_rows)
        me = here_ref[0]
        me_odd = lax.rem(me, 2) == 1
        for s in range(steps):
            root = roots[s]
            low, high = jnp.minimum(root, me), jnp.maximum(root, me)
            between = [jnp.where((i > low) & (i < high), jnp.maximum(counts[i], 1), 0) for i in range(n_rows)]
            turn = sum(between, ranks[s])
            target = held.at[pl.ds(s * width, width)]
            below, above = root < me, root > me

            @pl.when(root == me)
            def _():
                pltpu.make_async_copy(stack_ref.at[slot[s]], target, sems.at[s]).start()

            for side, came in ((0, (below & me_odd) | (above & ~me_odd)), (1, (below & ~me_odd) | (above & me_odd))):
                for i in range(turns):
                    @pl.when(came & (turn == i))
                    def _():
                        for p in range(splits):
                            piece = held.at[pl.ds(s * width, width), pl.ds(p * cols, cols)]
                            source = latest[2 * p + side] if i == turns - 1 else kept[p].at[side, i]
                            pltpu.make_async_copy(source, piece, sems.at[s]).start()
        columns = here_ref[1] * ncols + lax.broadcasted_iota(jnp.int32, (width, ncols), 1)
        for s in range(steps):
            rows = pl.ds(s * width, width)
            pltpu.make_async_copy(stack_ref.at[0], held.at[rows], sems.at[s]).wait()
            masked = jnp.where(columns >= offset_ref[s], held[rows, :], 0.0)
            held[rows, :] = masked
            high, low = halves(masked)
            high_ref[rows, :] = high
            low_ref[rows, :] = low
        for at in column_blocks(ncols):
            high, low = halves(held[:, at].T)
            both_t_ref[at, :] = jnp.concatenate([high, low], axis=1)
        gram = dot_t(held[...], held[...])
        gram_ref[...] = jnp.zeros_like(gram_ref)
        first = 0
        for s in range(1, steps):
            gram_ref[:, first:first + s * width] = gram[s * width:(s + 1) * width, :s * width]
            first += s * width

    return pl.pallas_call(
        kernel,
        out_shape=[
            pltpu.HBM((height, ncols), jnp.bfloat16),
            pltpu.HBM((height, ncols), jnp.bfloat16),
            pltpu.HBM((ncols, 2 * height), jnp.bfloat16),
            jax.ShapeDtypeStruct((width, packed_width(steps, width)), jnp.float32),
        ],
        in_specs=[SMEM, SMEM, SMEM, ANY] + [ANY] * (3 * splits),
        out_specs=[VMEM] * 4,
        scratch_shapes=[pltpu.VMEM((height, ncols), jnp.float32), pltpu.SemaphoreType.DMA((steps,))],
        compiler_params=params(limit=SMALL_LIMIT),
        cost_estimate=cost(12 * height * height * ncols, 8 * height * ncols),
        name="assemble",
    )(here, place, offsets, stack, *[in_hbm(store) for store in stores], *[array for last in lasts for array in last])


def merge(cross, factors, vecs):
    steps, width, _ = factors.shape
    height, ncols = vecs[0].shape

    def kernel(*refs):
        cross_refs, (factor_ref, v_high, v_low, p_ref, total, m_ref) = refs[:-6], refs[-6:]
        total[...] = sum([ref[...] for ref in cross_refs[1:]], cross_refs[0][...])
        first = 0
        for k in range(steps):
            own = lax.broadcasted_iota(jnp.int32, (width, height), 0) + k * width
            rest = (own == lax.broadcasted_iota(jnp.int32, (width, height), 1)).astype(jnp.float32)
            if k:
                rest = rest - dot(total[:, first:first + k * width], m_ref[:k * width, :])
                first += k * width
            m_ref[k * width:(k + 1) * width, :] = dot(factor_ref[k], rest)
        product = dot3(halves(m_ref[...].T), (v_high[...], v_low[...]), ((1,), (0,)))
        high, low = halves(product)
        for i, half in enumerate((high, high, low)):
            p_ref[i * height:(i + 1) * height, :] = half

    return pl.pallas_call(
        kernel,
        out_shape=jax.ShapeDtypeStruct((3 * height, ncols), jnp.bfloat16),
        out_specs=VMEM,
        in_specs=[VMEM] * (len(cross) + 3),
        scratch_shapes=[pltpu.VMEM(cross[0].shape, jnp.float32), pltpu.VMEM((height, height), jnp.float32)],
        compiler_params=params(),
        cost_estimate=cost(6 * height * height * ncols, 8 * height * ncols),
        name="merge",
    )(*cross, factors, *vecs)


def fold(w):
    half = w.shape[0] // 2
    return jnp.concatenate([w[:half], w[half:]], axis=1)


def unfold(w):
    height = w.shape[1] // 2
    return jnp.concatenate([w[:, :height], w[:, height:]], axis=0)


def column_blocks(ncols):
    cols = COLUMNS if ncols % COLUMNS == 0 else ncols
    return [pl.ds(start, cols) for start in range(0, ncols, cols)]


def lift(x):
    rows = x.shape[0]
    step = rows // 4 if rows % 64 == 0 else rows

    def kernel(x_ref, out_ref, sems):
        copies = [
            pltpu.make_async_copy(x_ref.at[pl.ds(start, step)], out_ref.at[pl.ds(start, step)], sems.at[i])
            for i, start in enumerate(range(0, rows, step))
        ]
        for i, copy in enumerate(copies):
            copy.start(priority=i % QUEUES)
        for copy in copies:
            copy.wait()

    return pl.pallas_call(
        kernel,
        out_shape=pltpu.VMEM(x.shape, x.dtype),
        in_specs=[ANY],
        out_specs=VMEM,
        scratch_shapes=[pltpu.SemaphoreType.DMA((rows // step,))],
        compiler_params=params(),
        cost_estimate=cost(0, 2 * x.size),
        name="lift",
    )(in_hbm(x))


def inner_products(here, x, vecs_t, hold):
    rows, ncols = x.shape
    height = vecs_t.shape[1] // 2
    half = rows // 2
    lanes = min(-(-height // 128) * 128, 2 * height)
    step = rows // 8 if rows % 64 == 0 else rows
    n_copies = rows // step
    cuts = sorted({0, n_copies // 4, n_copies * 5 // 8, n_copies})

    def kernel(here_ref, x_ref, vecs_ref, mine_ref, theirs_ref, held, total, sems):
        copies = []
        for i in range(n_copies):
            at = pl.ds(i * step, step)
            copies.append(pltpu.make_async_copy(x_ref.at[at], held.at[at], sems.at[i]))
        for i, copy in enumerate(copies):
            copy.start(priority=i % QUEUES)
        for start, end in zip(cuts[:-1], cuts[1:]):
            for copy in copies[start:end]:
                copy.wait()
            at = pl.ds(start * step, (end - start) * step)
            high, low = halves(held[at, :])
            by_high = jnp.dot(high, vecs_ref[...], preferred_element_type=jnp.float32)
            by_low = jnp.dot(low, vecs_ref[:, :lanes], preferred_element_type=jnp.float32)
            total[at, :] = by_high[:, :height] + (by_high[:, height:] + by_low[:, :height])
        core = lax.rem(here_ref[1], 2)
        mine_ref[...] = fold(total[pl.ds(pl.multiple_of(core * half, 8), half), :])
        theirs_ref[...] = fold(total[pl.ds(pl.multiple_of((1 - core) * half, 8), half), :])

    return pl.pallas_call(
        kernel,
        out_shape=[jax.ShapeDtypeStruct((half // 2, 2 * height), jnp.float32)] * 2
        + [pltpu.VMEM(x.shape, jnp.float32)] * hold,
        in_specs=[SMEM, ANY, VMEM],
        out_specs=[VMEM] * (2 + hold),
        scratch_shapes=[pltpu.VMEM(x.shape, jnp.float32)] * (1 - hold)
        + [pltpu.VMEM((rows, height), jnp.float32), pltpu.SemaphoreType.DMA((n_copies,))],
        compiler_params=params(),
        cost_estimate=cost(6 * rows * ncols * height, 4 * rows * ncols),
        name="inner_products",
    )(here, in_hbm(x), vecs_t)


def update(here, early, late, mine, theirs, changes):
    chunks = early + [late]
    lead, rows, ncols = late.shape
    height = changes.shape[0] // 3
    size = lead * rows
    half = size // 2
    blocks = column_blocks(ncols)
    depth = min(4, len(blocks))

    def kernel(here_ref, mine_ref, theirs_ref, p_ref, *refs):
        x_refs, (out_ref, w_ref, fetched, held, in_sems, out_sems) = refs[:len(chunks)], refs[len(chunks):]
        fetches = [
            [pltpu.make_async_copy(x_refs[c].at[:, :, at], fetched.at[c, :, :, at], in_sems.at[c, i]) for c in range(len(early))]
            for i, at in enumerate(blocks)
        ]
        for fetch in fetches:
            for copy in fetch:
                copy.start(priority=1)
        core = lax.rem(here_ref[1], 2)
        for c in range(len(chunks)):
            folded = slice(c * half // 2, (c + 1) * half // 2)
            w_ref[pl.ds(pl.multiple_of(c * size + core * half, 8), half), :] = unfold(mine_ref[folded, :])
            w_ref[pl.ds(pl.multiple_of(c * size + (1 - core) * half, 8), half), :] = unfold(theirs_ref[folded, :])
        high, low = halves(w_ref[...])
        w = jnp.concatenate([high, low, high], axis=1)
        stores = [
            [
                pltpu.make_async_copy(held.at[i % depth, c], out_ref.at[:, pl.ds(c * rows, rows), at], out_sems.at[c, i])
                for c in range(len(chunks))
            ]
            for i, at in enumerate(blocks)
        ]
        for i, at in enumerate(blocks):
            change = jnp.dot(w, p_ref[:, at], preferred_element_type=jnp.float32)
            for copy in fetches[i] + (stores[i - depth] if i >= depth else []):
                copy.wait()
            for c in range(len(chunks)):
                x = x_refs[c][:, :, at] if c == len(early) else fetched[c, :, :, at]
                held[i % depth, c] = x - change[c * size:(c + 1) * size].reshape(lead, rows, at.size)
                stores[i][c].start(priority=0)
        for store in stores[-depth:]:
            for copy in store:
                copy.wait()

    return pl.pallas_call(
        kernel,
        out_shape=jax.ShapeDtypeStruct((lead, len(chunks) * rows, ncols), jnp.float32),
        in_specs=[SMEM] + [VMEM] * 3 + [ANY] * len(early) + [VMEM],
        out_specs=ANY,
        scratch_shapes=[
            pltpu.VMEM((len(chunks) * size, height), jnp.float32),
            pltpu.VMEM((max(len(early), 1), lead, rows, ncols), jnp.float32),
            pltpu.VMEM((depth, len(chunks), lead, rows, blocks[0].size), jnp.float32),
            pltpu.SemaphoreType.DMA((max(len(early), 1), len(blocks))),
            pltpu.SemaphoreType.DMA((len(chunks), len(blocks))),
        ],
        compiler_params=params(),
        cost_estimate=cost(6 * len(chunks) * size * ncols * height, 8 * len(chunks) * size * ncols),
        name="update",
    )(here, mine, theirs, changes, *[in_hbm(x) for x in early], late)


def swap(array, k, size):
    return lax.ppermute(array, "wide", [(i, i ^ k) for i in range(size)])


def spread(pair, size):
    return [pair] + [swap(pair, k, size) for k in range(2, size, 2)]


def chips_sum(upper, lower, size, token):
    shifts = [k for k in (1 << i for i in range(1, size.bit_length())) if k < size]
    for i, (first, second) in enumerate(zip(shifts, reversed(shifts))):
        come_upper, come_lower = swap(upper, first, size), swap(lower, second, size)
        if i == 0:
            upper, lower, _ = lax.optimization_barrier((upper, lower, token))
        upper, lower = upper + come_upper, lower + come_lower
    return jnp.concatenate([upper, lower], axis=0)


def body(n_row, n_wide, eigvec_t, householder, wy_factor, block_place, offsets):
    rows, order = eigvec_t.shape
    steps, width, _ = wy_factor.shape
    slots = householder.shape[0]
    ncols = order // n_wide
    here = jnp.stack([lax.axis_index("row"), lax.axis_index("wide")]).astype(jnp.int32)

    turns = max(z + min(steps - 1, slots * (n_row - 1 - z)) for z in range(n_row - 1))
    cols = ncols // SPLITS
    streams = [((), None)] * SPLITS

    def exchange(array, odd):
        pairs = []
        for z in range(n_row):
            mate = ((z + odd) ^ 1) - odd
            for w in range(n_wide):
                target = mate * n_wide + w if 0 <= mate < n_row else z * n_wide + (w ^ 1)
                pairs.append((z * n_wide + w, target))
        return lax.ppermute(array, ("row", "wide"), pairs)

    chunks = 2 if rows % 16 == 0 else 1
    size = rows // chunks
    if chunks > 1:
        pieces = [pack(eigvec_t, i * size, size, n_wide) for i in range(chunks)]
        parts = [lax.all_to_all(pieces[0], "wide", split_axis=0, concat_axis=0, tiled=True)]
        tokens = [pieces[0]]
    else:
        parts = [lax.all_to_all(eigvec_t, "wide", split_axis=1, concat_axis=0, tiled=True)[None]]
        tokens = []
    for turn in range(turns):
        for part in range(SPLITS):
            last, store = streams[part]
            to_even, to_odd, store = feed(
                after(here, *tokens), block_place, householder, turn, turns, last, store, n_row, part, cols
            )
            tokens = [to_odd]
            streams[part] = ((exchange(to_even, 0), exchange(to_odd, 1)), store)
            if chunks > 1 and (turn, part) == (0, 1):
                tokens.append(pieces[1])
            if chunks > 1 and (turn, part) == ARRIVED:
                piece = after(pieces[1], parts[0], to_odd)
                parts.append(lax.all_to_all(piece, "wide", split_axis=0, concat_axis=0, tiled=True))
                tokens.append(piece)
    stores, lasts = [store for _, store in streams], [last for last, _ in streams]
    high, low, both_t, gram = assemble(here, block_place, offsets, householder, stores, lasts, n_row)
    cross = spread(gram + swap(gram, 1, n_wide), n_wide)

    def flat(x):
        return x.reshape(-1, ncols)

    pairs = []
    for x in parts[:-1]:
        mine, theirs = inner_products(here, flat(x), lift(both_t), 0)
        pairs.append(mine + swap(theirs, 1, n_wide))
    late_t = lift(after(both_t, parts[-1], *pairs))
    cross[0] = after(cross[0], late_t)
    cross = functools.reduce(jnp.add, cross)
    changes = merge([cross], wy_factor, (high, low))
    mine, theirs, late = inner_products(after(here, cross), flat(parts[-1]), late_t, 1)
    pairs.append(mine + swap(theirs, 1, n_wide))
    if chunks == 1:
        middle = pairs[0].shape[0] // 2
        pairs = [pairs[0][:middle], pairs[0][middle:]]
    mine = chips_sum(pairs[0], pairs[1], n_wide, changes)
    theirs = swap(mine, 1, n_wide)
    out = update(here, parts[:-1], late.reshape(parts[-1].shape), mine, theirs, changes)
    return out.reshape(n_wide * rows, ncols)


def solution(mesh):
    return jax.shard_map(
        functools.partial(body, mesh.shape["row"], mesh.shape["wide"]),
        mesh=mesh,
        in_specs=(P(("row", "wide"), None), P("row", None, "wide"), P(), P(), P()),
        out_specs=P("row", "wide"),
        check_vma=False,
    )
```

```python
import functools

import jax
import jax.numpy as jnp
from jax import lax
from jax.experimental import pallas as pl
from jax.experimental.pallas import tpu as pltpu
from jax.sharding import PartitionSpec as P

HIGHEST = lax.Precision.HIGHEST
SMALL_LIMIT = 44 * 1024 * 1024
VMEM_LIMIT = 40 * 1024 * 1024
LARGE_LIMIT = 58 * 1024 * 1024
COLUMNS = 512
QUEUES = 2
SPLITS = 2


def dot_t(a, b):
    return lax.dot_general(a, b, (((1,), (1,)), ((), ())), precision=HIGHEST, preferred_element_type=jnp.float32)


def dot(a, b):
    return lax.dot_general(a, b, (((1,), (0,)), ((), ())), precision=HIGHEST, preferred_element_type=jnp.float32)


def halves(x):
    high = x.astype(jnp.bfloat16)
    return high, (x - high.astype(jnp.float32)).astype(jnp.bfloat16)


def dot3(a, b, dims):
    rows = a[0].shape[0]
    both = lax.dot_general(jnp.concatenate(a, axis=0), b[0], (dims, ((), ())), preferred_element_type=jnp.float32)
    last = lax.dot_general(a[0], b[1], (dims, ((), ())), preferred_element_type=jnp.float32)
    return both[:rows] + (both[rows:] + last)


def after(x, *tokens):
    return lax.optimization_barrier((x, *tokens))[0]


def params(limit=VMEM_LIMIT):
    return pltpu.CompilerParams(vmem_limit_bytes=limit)


def cost(flops, nbytes):
    return pl.CostEstimate(flops=flops, bytes_accessed=nbytes, transcendentals=0)


SMEM = pl.BlockSpec(memory_space=pltpu.SMEM)
ANY = pl.BlockSpec(memory_space=pl.ANY)
VMEM = pl.BlockSpec(memory_space=pltpu.VMEM)


def in_hbm(x):
    return pltpu.with_memory_space_constraint(x, pltpu.HBM)


def pack(x, n_wide):
    rows, order = x.shape
    ncols = order // n_wide
    step = 16 if rows % 16 == 0 else rows
    n_copies = n_wide * rows // step

    def kernel(x_ref, out_ref, held, in_sems, out_sems):
        into, out_of = [], []
        for first in range(0, rows, step):
            for k in range(n_wide):
                i, at = len(into), pl.ds(first, step)
                source = x_ref.at[at, pl.ds(k * ncols, ncols)]
                into.append(pltpu.make_async_copy(source, held.at[k, at], in_sems.at[i]))
                out_of.append(pltpu.make_async_copy(held.at[k, at], out_ref.at[k, at], out_sems.at[i]))
        for i, copy in enumerate(into):
            copy.start(priority=i % QUEUES)
        for i, (came, goes) in enumerate(zip(into, out_of)):
            came.wait()
            goes.start(priority=i % QUEUES)
        for copy in out_of:
            copy.wait()

    return pl.pallas_call(
        kernel,
        out_shape=jax.ShapeDtypeStruct((n_wide, rows, ncols), jnp.float32),
        in_specs=[ANY],
        out_specs=ANY,
        scratch_shapes=[
            pltpu.VMEM((n_wide, rows, ncols), jnp.float32),
            pltpu.SemaphoreType.DMA((n_copies,)),
            pltpu.SemaphoreType.DMA((n_copies,)),
        ],
        compiler_params=params(limit=LARGE_LIMIT),
        cost_estimate=cost(0, 8 * rows * order),
        name="pack",
    )(in_hbm(x))


def plan(place_ref, slots, n_rows):
    places = [place_ref[s] for s in range(place_ref.shape[0])]
    roots = [lax.div(p, slots) for p in places]
    slot = [lax.rem(p, slots) for p in places]
    ranks = [sum([(roots[i] == roots[s]).astype(jnp.int32) for i in range(s)], jnp.int32(0)) for s in range(len(places))]
    counts = [sum([(r == i).astype(jnp.int32) for r in roots], jnp.int32(0)) for i in range(n_rows)]
    return roots, slot, ranks, counts


def feed(here, place, stack, evens, odds, n_rows, part, cols):
    slots, width, _ = stack.shape
    turn = len(evens)

    def kernel(here_ref, place_ref, stack_ref, *refs):
        arrived, (out_even, out_odd, sems) = refs[:-3], refs[-3:]
        roots, slot, ranks, _ = plan(place_ref, slots, n_rows)
        me = here_ref[0]
        mine = [r == me for r in roots]
        count = sum([m.astype(jnp.int32) for m in mine], jnp.int32(0))
        own = sum([jnp.where(m & (k == turn), s, 0) for m, k, s in zip(mine, ranks, slot)], jnp.int32(0))
        older = turn - jnp.maximum(count, 1)
        stored = stack_ref.at[own, :, pl.ds(part * cols, cols)]
        for side, out in ((0, out_even), (1, out_odd)):
            @pl.when((older < 0) | (count > turn))
            def _():
                pltpu.make_async_copy(stored, out, sems.at[side]).start()

            for i in range(turn):
                @pl.when((older == i) & (count <= turn))
                def _():
                    pltpu.make_async_copy(arrived[(1 - side) * turn + i], out, sems.at[side]).start()
        for side, out in ((0, out_even), (1, out_odd)):
            pltpu.make_async_copy(stored, out, sems.at[side]).wait()

    return pl.pallas_call(
        kernel,
        out_shape=[jax.ShapeDtypeStruct((width, cols), jnp.float32)] * 2,
        in_specs=[SMEM, SMEM, ANY] + [ANY] * (2 * turn),
        out_specs=[VMEM] * 2,
        scratch_shapes=[pltpu.SemaphoreType.DMA((2,))],
        compiler_params=params(limit=SMALL_LIMIT),
        cost_estimate=cost(0, 16 * width * cols),
        name="feed",
    )(here, place, stack, *evens, *odds)


def packed_width(steps, width):
    return -(-(width * steps * (steps - 1) // 2) // 128) * 128


def assemble(here, place, offsets, stack, evens, odds, n_rows):
    slots, width, ncols = stack.shape
    steps = place.shape[0]
    height = steps * width
    turns, splits = len(evens), len(evens[0])
    cols = ncols // splits

    def kernel(here_ref, place_ref, offset_ref, stack_ref, *refs):
        arrived, (high_ref, low_ref, high_t_ref, low_t_ref, gram_ref, held, sems) = refs[:-7], refs[-7:]
        even, odd = arrived[:turns * splits], arrived[turns * splits:]
        roots, slot, ranks, counts = plan(place_ref, slots, n_rows)
        me = here_ref[0]
        me_odd = lax.rem(me, 2) == 1
        for s in range(steps):
            root = roots[s]
            low, high = jnp.minimum(root, me), jnp.maximum(root, me)
            between = [jnp.where((i > low) & (i < high), jnp.maximum(counts[i], 1), 0) for i in range(n_rows)]
            turn = sum(between, ranks[s])
            target = held.at[pl.ds(s * width, width)]
            below, above = root < me, root > me

            @pl.when(root == me)
            def _():
                pltpu.make_async_copy(stack_ref.at[slot[s]], target, sems.at[s]).start()

            for side, came in (((below & me_odd) | (above & ~me_odd), even), ((below & ~me_odd) | (above & me_odd), odd)):
                for i in range(turns):
                    @pl.when(side & (turn == i))
                    def _():
                        for p in range(splits):
                            piece = held.at[pl.ds(s * width, width), pl.ds(p * cols, cols)]
                            pltpu.make_async_copy(came[i * splits + p], piece, sems.at[s]).start()
        columns = here_ref[1] * ncols + lax.broadcasted_iota(jnp.int32, (width, ncols), 1)
        for s in range(steps):
            rows = pl.ds(s * width, width)
            pltpu.make_async_copy(stack_ref.at[0], held.at[rows], sems.at[s]).wait()
            masked = jnp.where(columns >= offset_ref[s], held[rows, :], 0.0)
            held[rows, :] = masked
            high, low = halves(masked)
            high_ref[rows, :] = high
            low_ref[rows, :] = low
        for at in column_blocks(ncols):
            high_t_ref[at, :], low_t_ref[at, :] = halves(held[:, at].T)
        gram = dot_t(held[...], held[...])
        gram_ref[...] = jnp.zeros_like(gram_ref)
        first = 0
        for s in range(1, steps):
            gram_ref[:, first:first + s * width] = gram[s * width:(s + 1) * width, :s * width]
            first += s * width

    return pl.pallas_call(
        kernel,
        out_shape=[
            pltpu.HBM((height, ncols), jnp.bfloat16),
            pltpu.HBM((height, ncols), jnp.bfloat16),
            pltpu.HBM((ncols, height), jnp.bfloat16),
            pltpu.HBM((ncols, height), jnp.bfloat16),
            jax.ShapeDtypeStruct((width, packed_width(steps, width)), jnp.float32),
        ],
        in_specs=[SMEM, SMEM, SMEM, ANY] + [ANY] * (2 * turns * splits),
        out_specs=[VMEM] * 5,
        scratch_shapes=[pltpu.VMEM((height, ncols), jnp.float32), pltpu.SemaphoreType.DMA((steps,))],
        compiler_params=params(limit=SMALL_LIMIT),
        cost_estimate=cost(12 * height * height * ncols, 8 * height * ncols),
        name="assemble",
    )(here, place, offsets, stack, *[p for turn in evens for p in turn], *[p for turn in odds for p in turn])


def merge(cross, factors, vecs):
    steps, width, _ = factors.shape
    height, ncols = vecs[0].shape

    def kernel(*refs):
        cross_refs, (factor_ref, v_high, v_low, p_ref, total, m_ref) = refs[:-6], refs[-6:]
        total[...] = sum([ref[...] for ref in cross_refs[1:]], cross_refs[0][...])
        first = 0
        for k in range(steps):
            own = lax.broadcasted_iota(jnp.int32, (width, height), 0) + k * width
            rest = (own == lax.broadcasted_iota(jnp.int32, (width, height), 1)).astype(jnp.float32)
            if k:
                rest = rest - dot(total[:, first:first + k * width], m_ref[:k * width, :])
                first += k * width
            m_ref[k * width:(k + 1) * width, :] = dot(factor_ref[k], rest)
        product = dot3(halves(m_ref[...].T), (v_high[...], v_low[...]), ((1,), (0,)))
        high, low = halves(product)
        for i, half in enumerate((high, high, low)):
            p_ref[i * height:(i + 1) * height, :] = half

    return pl.pallas_call(
        kernel,
        out_shape=jax.ShapeDtypeStruct((3 * height, ncols), jnp.bfloat16),
        out_specs=VMEM,
        in_specs=[VMEM] * (len(cross) + 3),
        scratch_shapes=[pltpu.VMEM(cross[0].shape, jnp.float32), pltpu.VMEM((height, height), jnp.float32)],
        compiler_params=params(),
        cost_estimate=cost(6 * height * height * ncols, 8 * height * ncols),
        name="merge",
    )(*cross, factors, *vecs)


def fold(w):
    half = w.shape[0] // 2
    return jnp.concatenate([w[:half], w[half:]], axis=1)


def unfold(w):
    height = w.shape[1] // 2
    return jnp.concatenate([w[:, :height], w[:, height:]], axis=0)


def column_blocks(ncols):
    cols = COLUMNS if ncols % COLUMNS == 0 else ncols
    return [pl.ds(start, cols) for start in range(0, ncols, cols)]


def lift(arrays):
    n, rows = len(arrays), arrays[0].shape[0]
    step = rows // 4 if rows % 64 == 0 else rows

    def kernel(*refs):
        sems = refs[-1]
        copies = []
        for source, out in zip(refs[:n], refs[n:2 * n]):
            for start in range(0, rows, step):
                at = pl.ds(start, step)
                copies.append(pltpu.make_async_copy(source.at[at], out.at[at], sems.at[len(copies)]))
        for i, copy in enumerate(copies):
            copy.start(priority=i % QUEUES)
        for copy in copies:
            copy.wait()

    return pl.pallas_call(
        kernel,
        out_shape=[pltpu.VMEM(x.shape, x.dtype) for x in arrays],
        in_specs=[ANY] * n,
        out_specs=[VMEM] * n,
        scratch_shapes=[pltpu.SemaphoreType.DMA((n * rows // step,))],
        compiler_params=params(),
        cost_estimate=cost(0, 2 * n * arrays[0].size),
        name="lift",
    )(*[in_hbm(x) for x in arrays])


def inner_products(here, x, vecs_t):
    rows, ncols = x.shape
    height = vecs_t[0].shape[1]
    half = rows // 2
    step = rows // 8 if rows % 64 == 0 else rows
    n_copies = rows // step
    cuts = sorted({0, n_copies // 4, n_copies})

    def kernel(here_ref, x_ref, high_ref, low_ref, mine_ref, theirs_ref, held, total, sems):
        copies = []
        for i in range(n_copies):
            at = pl.ds(i * step, step)
            copies.append(pltpu.make_async_copy(x_ref.at[at], held.at[at], sems.at[i]))
        for i, copy in enumerate(copies):
            copy.start(priority=i % QUEUES)
        for start, end in zip(cuts[:-1], cuts[1:]):
            for copy in copies[start:end]:
                copy.wait()
            at = pl.ds(start * step, (end - start) * step)
            total[at, :] = dot3(halves(held[at, :]), (high_ref[...], low_ref[...]), ((1,), (0,)))
        core = lax.rem(here_ref[1], 2)
        mine_ref[...] = fold(total[pl.ds(pl.multiple_of(core * half, 8), half), :])
        theirs_ref[...] = fold(total[pl.ds(pl.multiple_of((1 - core) * half, 8), half), :])

    return pl.pallas_call(
        kernel,
        out_shape=[jax.ShapeDtypeStruct((half // 2, 2 * height), jnp.float32)] * 2 + [pltpu.VMEM(x.shape, jnp.float32)],
        in_specs=[SMEM, ANY, VMEM, VMEM],
        out_specs=[VMEM] * 3,
        scratch_shapes=[pltpu.VMEM((rows, height), jnp.float32), pltpu.SemaphoreType.DMA((n_copies,))],
        compiler_params=params(),
        cost_estimate=cost(6 * rows * ncols * height, 4 * rows * ncols),
        name="inner_products",
    )(here, in_hbm(x), *vecs_t)


def update(here, x, mine, theirs, changes):
    rows, ncols = x.shape
    height = changes.shape[0] // 3
    half = rows // 2
    blocks = column_blocks(ncols)
    depth = min(4, len(blocks))

    def kernel(here_ref, mine_ref, theirs_ref, x_ref, p_ref, out_ref, w_ref, held, sems):
        core = lax.rem(here_ref[1], 2)
        w_ref[pl.ds(pl.multiple_of(core * half, 8), half), :] = unfold(mine_ref[...])
        w_ref[pl.ds(pl.multiple_of((1 - core) * half, 8), half), :] = unfold(theirs_ref[...])
        high, low = halves(w_ref[...])
        w = jnp.concatenate([high, low, high], axis=1)
        copies = [pltpu.make_async_copy(held.at[i % depth], out_ref.at[:, at], sems.at[i]) for i, at in enumerate(blocks)]
        for i, at in enumerate(blocks):
            change = lax.dot_general(w, p_ref[:, at], (((1,), (0,)), ((), ())), preferred_element_type=jnp.float32)
            if i >= depth:
                copies[i - depth].wait()
            held[i % depth] = x_ref[:, at] - change
            copies[i].start(priority=i % QUEUES)
        for copy in copies[-depth:]:
            copy.wait()

    return pl.pallas_call(
        kernel,
        out_shape=jax.ShapeDtypeStruct(x.shape, jnp.float32),
        in_specs=[SMEM] + [VMEM] * 4,
        out_specs=ANY,
        scratch_shapes=[
            pltpu.VMEM((rows, height), jnp.float32),
            pltpu.VMEM((depth, rows, blocks[0].size), jnp.float32),
            pltpu.SemaphoreType.DMA((len(blocks),)),
        ],
        compiler_params=params(),
        cost_estimate=cost(6 * rows * ncols * height, 8 * rows * ncols),
        name="update",
    )(here, mine, theirs, x, changes)


def swap(array, k, size):
    return lax.ppermute(array, "wide", [(i, i ^ k) for i in range(size)])


def spread(pair, size):
    return [pair] + [swap(pair, k, size) for k in range(2, size, 2)]


def chips_sum(pair, size, token):
    shifts = [k for k in (1 << i for i in range(1, size.bit_length())) if k < size]
    half = pair.shape[0] // 2
    upper, lower = pair[:half], pair[half:]
    for i, (first, second) in enumerate(zip(shifts, reversed(shifts))):
        come_upper, come_lower = swap(upper, first, size), swap(lower, second, size)
        if i == 0:
            upper, lower, _ = lax.optimization_barrier((upper, lower, token))
        upper, lower = upper + come_upper, lower + come_lower
    return jnp.concatenate([upper, lower], axis=0)


def body(n_row, n_wide, eigvec_t, householder, wy_factor, block_place, offsets):
    rows, order = eigvec_t.shape
    steps, width, _ = wy_factor.shape
    slots = householder.shape[0]
    ncols = order // n_wide
    here = jnp.stack([lax.axis_index("row"), lax.axis_index("wide")]).astype(jnp.int32)

    turns = max(z + min(steps - 1, slots * (n_row - 1 - z)) for z in range(n_row - 1))
    cols = ncols // SPLITS
    streams = [([], []) for _ in range(SPLITS)]

    def exchange(array, odd):
        pairs = []
        for z in range(n_row):
            mate = ((z + odd) ^ 1) - odd
            for w in range(n_wide):
                target = mate * n_wide + w if 0 <= mate < n_row else z * n_wide + (w ^ 1)
                pairs.append((z * n_wide + w, target))
        return lax.ppermute(array, ("row", "wide"), pairs)

    whole = rows % 8 == 0
    if whole:
        piece = pack(eigvec_t, n_wide)
        x = lax.all_to_all(piece, "wide", split_axis=0, concat_axis=0, tiled=True)
        tokens = [piece]
    else:
        x = lax.all_to_all(eigvec_t, "wide", split_axis=1, concat_axis=0, tiled=True)[None]
        tokens = []
    for turn in range(turns):
        for part in range(SPLITS):
            evens, odds = streams[part]
            to_even, to_odd = feed(after(here, *tokens), block_place, householder, evens, odds, n_row, part, cols)
            tokens = [to_odd]
            streams[part] = (evens + [exchange(to_even, 0)], odds + [exchange(to_odd, 1)])
    evens = list(zip(*[stream[0] for stream in streams]))
    odds = list(zip(*[stream[1] for stream in streams]))
    high, low, high_t, low_t, gram = assemble(here, block_place, offsets, householder, evens, odds, n_row)
    x = x.reshape(n_wide * rows, ncols)
    vecs_t = lift([high_t, low_t])
    cross = functools.reduce(jnp.add, spread(after(gram + swap(gram, 1, n_wide), *vecs_t), n_wide))
    changes = merge([cross], wy_factor, (high, low))

    mine, theirs, x = inner_products(here, x, vecs_t)
    mine = chips_sum(mine + swap(after(theirs, cross), 1, n_wide), n_wide, changes)
    return update(here, x, mine, swap(mine, 1, n_wide), changes)


def solution(mesh):
    return jax.shard_map(
        functools.partial(body, mesh.shape["row"], mesh.shape["wide"]),
        mesh=mesh,
        in_specs=(P(("row", "wide"), None), P("row", None, "wide"), P(), P(), P()),
        out_specs=P("row", "wide"),
        check_vma=False,
    )
```

```python
import functools

import jax
import jax.numpy as jnp
from jax import lax
from jax.experimental import pallas as pl
from jax.experimental.pallas import tpu as pltpu
from jax.sharding import PartitionSpec as P

HIGHEST = lax.Precision.HIGHEST
SMALL_LIMIT = 44 * 1024 * 1024
VMEM_LIMIT = 40 * 1024 * 1024
LARGE_LIMIT = 58 * 1024 * 1024
COLUMNS = 512
QUEUES = 2
SPLITS = 2


def dot_t(a, b):
    return lax.dot_general(a, b, (((1,), (1,)), ((), ())), precision=HIGHEST, preferred_element_type=jnp.float32)


def dot(a, b):
    return lax.dot_general(a, b, (((1,), (0,)), ((), ())), precision=HIGHEST, preferred_element_type=jnp.float32)


def halves(x):
    high = x.astype(jnp.bfloat16)
    return high, (x - high.astype(jnp.float32)).astype(jnp.bfloat16)


def dot3(a, b, dims):
    rows = a[0].shape[0]
    both = lax.dot_general(jnp.concatenate(a, axis=0), b[0], (dims, ((), ())), preferred_element_type=jnp.float32)
    last = lax.dot_general(a[0], b[1], (dims, ((), ())), preferred_element_type=jnp.float32)
    return both[:rows] + (both[rows:] + last)


def after(x, *tokens):
    return lax.optimization_barrier((x, *tokens))[0]


def params(limit=VMEM_LIMIT):
    return pltpu.CompilerParams(vmem_limit_bytes=limit)


def cost(flops, nbytes):
    return pl.CostEstimate(flops=flops, bytes_accessed=nbytes, transcendentals=0)


SMEM = pl.BlockSpec(memory_space=pltpu.SMEM)
ANY = pl.BlockSpec(memory_space=pl.ANY)
VMEM = pl.BlockSpec(memory_space=pltpu.VMEM)


def in_hbm(x):
    return pltpu.with_memory_space_constraint(x, pltpu.HBM)


def pack(x, n_wide):
    rows, order = x.shape
    ncols = order // n_wide
    step = 16 if rows % 16 == 0 else rows
    n_copies = n_wide * rows // step

    def kernel(x_ref, out_ref, held, in_sems, out_sems):
        into, out_of = [], []
        for first in range(0, rows, step):
            for k in range(n_wide):
                i, at = len(into), pl.ds(first, step)
                source = x_ref.at[at, pl.ds(k * ncols, ncols)]
                into.append(pltpu.make_async_copy(source, held.at[k, at], in_sems.at[i]))
                out_of.append(pltpu.make_async_copy(held.at[k, at], out_ref.at[k, at], out_sems.at[i]))
        for copy in into:
            copy.start()
        for came, goes in zip(into, out_of):
            came.wait()
            goes.start(priority=1)
        for copy in out_of:
            copy.wait()

    return pl.pallas_call(
        kernel,
        out_shape=jax.ShapeDtypeStruct((n_wide, rows, ncols), jnp.float32),
        in_specs=[ANY],
        out_specs=ANY,
        scratch_shapes=[
            pltpu.VMEM((n_wide, rows, ncols), jnp.float32),
            pltpu.SemaphoreType.DMA((n_copies,)),
            pltpu.SemaphoreType.DMA((n_copies,)),
        ],
        compiler_params=params(limit=LARGE_LIMIT),
        cost_estimate=cost(0, 8 * rows * order),
        name="pack",
    )(in_hbm(x))


def plan(place_ref, slots, n_rows):
    places = [place_ref[s] for s in range(place_ref.shape[0])]
    roots = [lax.div(p, slots) for p in places]
    slot = [lax.rem(p, slots) for p in places]
    ranks = [sum([(roots[i] == roots[s]).astype(jnp.int32) for i in range(s)], jnp.int32(0)) for s in range(len(places))]
    counts = [sum([(r == i).astype(jnp.int32) for r in roots], jnp.int32(0)) for i in range(n_rows)]
    return roots, slot, ranks, counts


def feed(here, place, stack, evens, odds, n_rows, part, cols):
    slots, width, _ = stack.shape
    turn = len(evens)

    def kernel(here_ref, place_ref, stack_ref, *refs):
        arrived, (out_even, out_odd, sems) = refs[:-3], refs[-3:]
        roots, slot, ranks, _ = plan(place_ref, slots, n_rows)
        me = here_ref[0]
        mine = [r == me for r in roots]
        count = sum([m.astype(jnp.int32) for m in mine], jnp.int32(0))
        own = sum([jnp.where(m & (k == turn), s, 0) for m, k, s in zip(mine, ranks, slot)], jnp.int32(0))
        older = turn - jnp.maximum(count, 1)
        stored = stack_ref.at[own, :, pl.ds(part * cols, cols)]
        for side, out in ((0, out_even), (1, out_odd)):
            @pl.when((older < 0) | (count > turn))
            def _():
                pltpu.make_async_copy(stored, out, sems.at[side]).start()

            for i in range(turn):
                @pl.when((older == i) & (count <= turn))
                def _():
                    pltpu.make_async_copy(arrived[(1 - side) * turn + i], out, sems.at[side]).start()
        for side, out in ((0, out_even), (1, out_odd)):
            pltpu.make_async_copy(stored, out, sems.at[side]).wait()

    return pl.pallas_call(
        kernel,
        out_shape=[jax.ShapeDtypeStruct((width, cols), jnp.float32)] * 2,
        in_specs=[SMEM, SMEM, ANY] + [ANY] * (2 * turn),
        out_specs=[VMEM] * 2,
        scratch_shapes=[pltpu.SemaphoreType.DMA((2,))],
        compiler_params=params(limit=SMALL_LIMIT),
        cost_estimate=cost(0, 16 * width * cols),
        name="feed",
    )(here, place, stack, *evens, *odds)


def packed_width(steps, width):
    return -(-(width * steps * (steps - 1) // 2) // 128) * 128


def assemble(here, place, offsets, stack, evens, odds, n_rows):
    slots, width, ncols = stack.shape
    steps = place.shape[0]
    height = steps * width
    turns, splits = len(evens), len(evens[0])
    cols = ncols // splits

    def kernel(here_ref, place_ref, offset_ref, stack_ref, *refs):
        arrived, (high_ref, low_ref, high_t_ref, low_t_ref, gram_ref, held, sems) = refs[:-7], refs[-7:]
        even, odd = arrived[:turns * splits], arrived[turns * splits:]
        roots, slot, ranks, counts = plan(place_ref, slots, n_rows)
        me = here_ref[0]
        me_odd = lax.rem(me, 2) == 1
        for s in range(steps):
            root = roots[s]
            low, high = jnp.minimum(root, me), jnp.maximum(root, me)
            between = [jnp.where((i > low) & (i < high), jnp.maximum(counts[i], 1), 0) for i in range(n_rows)]
            turn = sum(between, ranks[s])
            target = held.at[pl.ds(s * width, width)]
            below, above = root < me, root > me

            @pl.when(root == me)
            def _():
                pltpu.make_async_copy(stack_ref.at[slot[s]], target, sems.at[s]).start()

            for side, came in (((below & me_odd) | (above & ~me_odd), even), ((below & ~me_odd) | (above & me_odd), odd)):
                for i in range(turns):
                    @pl.when(side & (turn == i))
                    def _():
                        for p in range(splits):
                            piece = held.at[pl.ds(s * width, width), pl.ds(p * cols, cols)]
                            pltpu.make_async_copy(came[i * splits + p], piece, sems.at[s]).start()
        columns = here_ref[1] * ncols + lax.broadcasted_iota(jnp.int32, (width, ncols), 1)
        for s in range(steps):
            rows = pl.ds(s * width, width)
            pltpu.make_async_copy(stack_ref.at[0], held.at[rows], sems.at[s]).wait()
            masked = jnp.where(columns >= offset_ref[s], held[rows, :], 0.0)
            held[rows, :] = masked
            high, low = halves(masked)
            high_ref[rows, :] = high
            low_ref[rows, :] = low
        for at in column_blocks(ncols):
            high_t_ref[at, :], low_t_ref[at, :] = halves(held[:, at].T)
        gram = dot_t(held[...], held[...])
        gram_ref[...] = jnp.zeros_like(gram_ref)
        first = 0
        for s in range(1, steps):
            gram_ref[:, first:first + s * width] = gram[s * width:(s + 1) * width, :s * width]
            first += s * width

    return pl.pallas_call(
        kernel,
        out_shape=[
            pltpu.HBM((height, ncols), jnp.bfloat16),
            pltpu.HBM((height, ncols), jnp.bfloat16),
            pltpu.HBM((ncols, height), jnp.bfloat16),
            pltpu.HBM((ncols, height), jnp.bfloat16),
            jax.ShapeDtypeStruct((width, packed_width(steps, width)), jnp.float32),
        ],
        in_specs=[SMEM, SMEM, SMEM, ANY] + [ANY] * (2 * turns * splits),
        out_specs=[VMEM] * 5,
        scratch_shapes=[pltpu.VMEM((height, ncols), jnp.float32), pltpu.SemaphoreType.DMA((steps,))],
        compiler_params=params(limit=SMALL_LIMIT),
        cost_estimate=cost(12 * height * height * ncols, 8 * height * ncols),
        name="assemble",
    )(here, place, offsets, stack, *[p for turn in evens for p in turn], *[p for turn in odds for p in turn])


def merge(cross, factors, vecs):
    steps, width, _ = factors.shape
    height, ncols = vecs[0].shape

    def kernel(*refs):
        cross_refs, (factor_ref, v_high, v_low, p_ref, total, m_ref) = refs[:-6], refs[-6:]
        total[...] = sum([ref[...] for ref in cross_refs[1:]], cross_refs[0][...])
        first = 0
        for k in range(steps):
            own = lax.broadcasted_iota(jnp.int32, (width, height), 0) + k * width
            rest = (own == lax.broadcasted_iota(jnp.int32, (width, height), 1)).astype(jnp.float32)
            if k:
                rest = rest - dot(total[:, first:first + k * width], m_ref[:k * width, :])
                first += k * width
            m_ref[k * width:(k + 1) * width, :] = dot(factor_ref[k], rest)
        product = dot3(halves(m_ref[...].T), (v_high[...], v_low[...]), ((1,), (0,)))
        high, low = halves(product)
        for i, half in enumerate((high, high, low)):
            p_ref[i * height:(i + 1) * height, :] = half

    return pl.pallas_call(
        kernel,
        out_shape=jax.ShapeDtypeStruct((3 * height, ncols), jnp.bfloat16),
        out_specs=VMEM,
        in_specs=[VMEM] * (len(cross) + 3),
        scratch_shapes=[pltpu.VMEM(cross[0].shape, jnp.float32), pltpu.VMEM((height, height), jnp.float32)],
        compiler_params=params(),
        cost_estimate=cost(6 * height * height * ncols, 8 * height * ncols),
        name="merge",
    )(*cross, factors, *vecs)


def fold(w):
    half = w.shape[0] // 2
    return jnp.concatenate([w[:half], w[half:]], axis=1)


def unfold(w):
    height = w.shape[1] // 2
    return jnp.concatenate([w[:, :height], w[:, height:]], axis=0)


def column_blocks(ncols):
    cols = COLUMNS if ncols % COLUMNS == 0 else ncols
    return [pl.ds(start, cols) for start in range(0, ncols, cols)]


def lift(arrays):
    n, rows = len(arrays), arrays[0].shape[0]
    step = rows // 4 if rows % 64 == 0 else rows

    def kernel(*refs):
        sems = refs[-1]
        copies = []
        for source, out in zip(refs[:n], refs[n:2 * n]):
            for start in range(0, rows, step):
                at = pl.ds(start, step)
                copies.append(pltpu.make_async_copy(source.at[at], out.at[at], sems.at[len(copies)]))
        for i, copy in enumerate(copies):
            copy.start(priority=i % QUEUES)
        for copy in copies:
            copy.wait()

    return pl.pallas_call(
        kernel,
        out_shape=[pltpu.VMEM(x.shape, x.dtype) for x in arrays],
        in_specs=[ANY] * n,
        out_specs=[VMEM] * n,
        scratch_shapes=[pltpu.SemaphoreType.DMA((n * rows // step,))],
        compiler_params=params(),
        cost_estimate=cost(0, 2 * n * arrays[0].size),
        name="lift",
    )(*[in_hbm(x) for x in arrays])


def inner_products(here, x, vecs_t):
    rows, ncols = x.shape
    height = vecs_t[0].shape[1]
    half = rows // 2
    step = rows // 8 if rows % 64 == 0 else rows
    n_copies = rows // step
    cuts = sorted({0, n_copies // 4, n_copies})

    def kernel(here_ref, x_ref, high_ref, low_ref, mine_ref, theirs_ref, held, total, sems):
        copies = []
        for i in range(n_copies):
            at = pl.ds(i * step, step)
            copies.append(pltpu.make_async_copy(x_ref.at[at], held.at[at], sems.at[i]))
        for copy in copies:
            copy.start()
        for start, end in zip(cuts[:-1], cuts[1:]):
            for copy in copies[start:end]:
                copy.wait()
            at = pl.ds(start * step, (end - start) * step)
            total[at, :] = dot3(halves(held[at, :]), (high_ref[...], low_ref[...]), ((1,), (0,)))
        core = lax.rem(here_ref[1], 2)
        mine_ref[...] = fold(total[pl.ds(pl.multiple_of(core * half, 8), half), :])
        theirs_ref[...] = fold(total[pl.ds(pl.multiple_of((1 - core) * half, 8), half), :])

    return pl.pallas_call(
        kernel,
        out_shape=[jax.ShapeDtypeStruct((half // 2, 2 * height), jnp.float32)] * 2 + [pltpu.VMEM(x.shape, jnp.float32)],
        in_specs=[SMEM, ANY, VMEM, VMEM],
        out_specs=[VMEM] * 3,
        scratch_shapes=[pltpu.VMEM((rows, height), jnp.float32), pltpu.SemaphoreType.DMA((n_copies,))],
        compiler_params=params(),
        cost_estimate=cost(6 * rows * ncols * height, 4 * rows * ncols),
        name="inner_products",
    )(here, in_hbm(x), *vecs_t)


def update(here, x, mine, theirs, changes):
    rows, ncols = x.shape
    height = changes.shape[0] // 3
    half = rows // 2
    blocks = column_blocks(ncols)
    depth = min(4, len(blocks))

    def kernel(here_ref, mine_ref, theirs_ref, x_ref, p_ref, out_ref, w_ref, held, sems):
        core = lax.rem(here_ref[1], 2)
        w_ref[pl.ds(pl.multiple_of(core * half, 8), half), :] = unfold(mine_ref[...])
        w_ref[pl.ds(pl.multiple_of((1 - core) * half, 8), half), :] = unfold(theirs_ref[...])
        high, low = halves(w_ref[...])
        w = jnp.concatenate([high, low, high], axis=1)
        copies = [pltpu.make_async_copy(held.at[i % depth], out_ref.at[:, at], sems.at[i]) for i, at in enumerate(blocks)]
        for i, at in enumerate(blocks):
            change = lax.dot_general(w, p_ref[:, at], (((1,), (0,)), ((), ())), preferred_element_type=jnp.float32)
            if i >= depth:
                copies[i - depth].wait()
            held[i % depth] = x_ref[:, at] - change
            copies[i].start(priority=i % QUEUES)
        for copy in copies[-depth:]:
            copy.wait()

    return pl.pallas_call(
        kernel,
        out_shape=jax.ShapeDtypeStruct(x.shape, jnp.float32),
        in_specs=[SMEM] + [VMEM] * 4,
        out_specs=ANY,
        scratch_shapes=[
            pltpu.VMEM((rows, height), jnp.float32),
            pltpu.VMEM((depth, rows, blocks[0].size), jnp.float32),
            pltpu.SemaphoreType.DMA((len(blocks),)),
        ],
        compiler_params=params(),
        cost_estimate=cost(6 * rows * ncols * height, 8 * rows * ncols),
        name="update",
    )(here, mine, theirs, x, changes)


def swap(array, k, size):
    return lax.ppermute(array, "wide", [(i, i ^ k) for i in range(size)])


def spread(pair, size):
    return [pair] + [swap(pair, k, size) for k in range(2, size, 2)]


def chips_sum(pair, size, token):
    shifts = [k for k in (1 << i for i in range(1, size.bit_length())) if k < size]
    half = pair.shape[0] // 2
    upper, lower = pair[:half], pair[half:]
    for i, (first, second) in enumerate(zip(shifts, reversed(shifts))):
        come_upper, come_lower = swap(upper, first, size), swap(lower, second, size)
        if i == 0:
            upper, lower, _ = lax.optimization_barrier((upper, lower, token))
        upper, lower = upper + come_upper, lower + come_lower
    return jnp.concatenate([upper, lower], axis=0)


def body(n_row, n_wide, eigvec_t, householder, wy_factor, block_place, offsets):
    rows, order = eigvec_t.shape
    steps, width, _ = wy_factor.shape
    slots = householder.shape[0]
    ncols = order // n_wide
    here = jnp.stack([lax.axis_index("row"), lax.axis_index("wide")]).astype(jnp.int32)

    turns = max(z + min(steps - 1, slots * (n_row - 1 - z)) for z in range(n_row - 1))
    cols = ncols // SPLITS
    streams = [([], []) for _ in range(SPLITS)]

    def exchange(array, odd):
        pairs = []
        for z in range(n_row):
            mate = ((z + odd) ^ 1) - odd
            for w in range(n_wide):
                target = mate * n_wide + w if 0 <= mate < n_row else z * n_wide + (w ^ 1)
                pairs.append((z * n_wide + w, target))
        return lax.ppermute(array, ("row", "wide"), pairs)

    whole = rows % 8 == 0
    if whole:
        piece = pack(eigvec_t, n_wide)
        x = lax.all_to_all(piece, "wide", split_axis=0, concat_axis=0, tiled=True)
        tokens = [piece]
    else:
        x = lax.all_to_all(eigvec_t, "wide", split_axis=1, concat_axis=0, tiled=True)[None]
        tokens = []
    for turn in range(turns):
        for part in range(SPLITS):
            evens, odds = streams[part]
            to_even, to_odd = feed(after(here, *tokens), block_place, householder, evens, odds, n_row, part, cols)
            tokens = [to_odd]
            streams[part] = (evens + [exchange(to_even, 0)], odds + [exchange(to_odd, 1)])
    evens = list(zip(*[stream[0] for stream in streams]))
    odds = list(zip(*[stream[1] for stream in streams]))
    high, low, high_t, low_t, gram = assemble(here, block_place, offsets, householder, evens, odds, n_row)
    x = x.reshape(n_wide * rows, ncols)
    vecs_t = lift([after(high_t, x), low_t])
    cross = spread(gram + swap(gram, 1, n_wide), n_wide)
    cross[0] = after(cross[0], *vecs_t)
    cross = functools.reduce(jnp.add, cross)
    changes = merge([cross], wy_factor, (high, low))

    mine, theirs, x = inner_products(after(here, cross), x, vecs_t)
    mine = chips_sum(mine + swap(theirs, 1, n_wide), n_wide, changes)
    return update(here, x, mine, swap(mine, 1, n_wide), changes)


def solution(mesh):
    return jax.shard_map(
        functools.partial(body, mesh.shape["row"], mesh.shape["wide"]),
        mesh=mesh,
        in_specs=(P(("row", "wide"), None), P("row", None, "wide"), P(), P(), P()),
        out_specs=P("row", "wide"),
        check_vma=False,
    )
```

```python
import functools

import jax
import jax.numpy as jnp
from jax import lax
from jax.experimental import pallas as pl
from jax.experimental.pallas import tpu as pltpu
from jax.sharding import PartitionSpec as P

HIGHEST = lax.Precision.HIGHEST
SMALL_LIMIT = 44 * 1024 * 1024
VMEM_LIMIT = 40 * 1024 * 1024
LARGE_LIMIT = 58 * 1024 * 1024
COLUMNS = 512
QUEUES = 2
SPLITS = 2


def dot_t(a, b):
    return lax.dot_general(a, b, (((1,), (1,)), ((), ())), precision=HIGHEST, preferred_element_type=jnp.float32)


def dot(a, b):
    return lax.dot_general(a, b, (((1,), (0,)), ((), ())), precision=HIGHEST, preferred_element_type=jnp.float32)


def halves(x):
    high = x.astype(jnp.bfloat16)
    return high, (x - high.astype(jnp.float32)).astype(jnp.bfloat16)


def dot3(a, b, dims):
    rows = a[0].shape[0]
    both = lax.dot_general(jnp.concatenate(a, axis=0), b[0], (dims, ((), ())), preferred_element_type=jnp.float32)
    last = lax.dot_general(a[0], b[1], (dims, ((), ())), preferred_element_type=jnp.float32)
    return both[:rows] + (both[rows:] + last)


def after(x, *tokens):
    return lax.optimization_barrier((x, *tokens))[0]


def params(limit=VMEM_LIMIT):
    return pltpu.CompilerParams(vmem_limit_bytes=limit)


def cost(flops, nbytes):
    return pl.CostEstimate(flops=flops, bytes_accessed=nbytes, transcendentals=0)


SMEM = pl.BlockSpec(memory_space=pltpu.SMEM)
ANY = pl.BlockSpec(memory_space=pl.ANY)
VMEM = pl.BlockSpec(memory_space=pltpu.VMEM)


def in_hbm(x):
    return pltpu.with_memory_space_constraint(x, pltpu.HBM)


def pack(x, n_wide):
    rows, order = x.shape
    ncols = order // n_wide
    step = 16 if rows % 16 == 0 else rows
    n_copies = n_wide * rows // step

    def kernel(x_ref, out_ref, held, in_sems, out_sems):
        into, out_of = [], []
        for first in range(0, rows, step):
            for k in range(n_wide):
                i, at = len(into), pl.ds(first, step)
                source = x_ref.at[at, pl.ds(k * ncols, ncols)]
                into.append(pltpu.make_async_copy(source, held.at[k, at], in_sems.at[i]))
                out_of.append(pltpu.make_async_copy(held.at[k, at], out_ref.at[k, at], out_sems.at[i]))
        for i, copy in enumerate(into):
            copy.start(priority=i % QUEUES)
        for i, (came, goes) in enumerate(zip(into, out_of)):
            came.wait()
            goes.start(priority=i % QUEUES)
        for copy in out_of:
            copy.wait()

    return pl.pallas_call(
        kernel,
        out_shape=jax.ShapeDtypeStruct((n_wide, rows, ncols), jnp.float32),
        in_specs=[ANY],
        out_specs=ANY,
        scratch_shapes=[
            pltpu.VMEM((n_wide, rows, ncols), jnp.float32),
            pltpu.SemaphoreType.DMA((n_copies,)),
            pltpu.SemaphoreType.DMA((n_copies,)),
        ],
        compiler_params=params(limit=LARGE_LIMIT),
        cost_estimate=cost(0, 8 * rows * order),
        name="pack",
    )(in_hbm(x))


def plan(place_ref, slots, n_rows):
    places = [place_ref[s] for s in range(place_ref.shape[0])]
    roots = [lax.div(p, slots) for p in places]
    slot = [lax.rem(p, slots) for p in places]
    ranks = [sum([(roots[i] == roots[s]).astype(jnp.int32) for i in range(s)], jnp.int32(0)) for s in range(len(places))]
    counts = [sum([(r == i).astype(jnp.int32) for r in roots], jnp.int32(0)) for i in range(n_rows)]
    return roots, slot, ranks, counts


def feed(here, place, stack, evens, odds, n_rows, part, cols):
    slots, width, _ = stack.shape
    turn = len(evens)

    def kernel(here_ref, place_ref, stack_ref, *refs):
        arrived, (out_even, out_odd, sems) = refs[:-3], refs[-3:]
        roots, slot, ranks, _ = plan(place_ref, slots, n_rows)
        me = here_ref[0]
        mine = [r == me for r in roots]
        count = sum([m.astype(jnp.int32) for m in mine], jnp.int32(0))
        own = sum([jnp.where(m & (k == turn), s, 0) for m, k, s in zip(mine, ranks, slot)], jnp.int32(0))
        older = turn - jnp.maximum(count, 1)
        stored = stack_ref.at[own, :, pl.ds(part * cols, cols)]
        for side, out in ((0, out_even), (1, out_odd)):
            @pl.when((older < 0) | (count > turn))
            def _():
                pltpu.make_async_copy(stored, out, sems.at[side]).start()

            for i in range(turn):
                @pl.when((older == i) & (count <= turn))
                def _():
                    pltpu.make_async_copy(arrived[(1 - side) * turn + i], out, sems.at[side]).start()
        for side, out in ((0, out_even), (1, out_odd)):
            pltpu.make_async_copy(stored, out, sems.at[side]).wait()

    return pl.pallas_call(
        kernel,
        out_shape=[jax.ShapeDtypeStruct((width, cols), jnp.float32)] * 2,
        in_specs=[SMEM, SMEM, ANY] + [ANY] * (2 * turn),
        out_specs=[VMEM] * 2,
        scratch_shapes=[pltpu.SemaphoreType.DMA((2,))],
        compiler_params=params(limit=SMALL_LIMIT),
        cost_estimate=cost(0, 16 * width * cols),
        name="feed",
    )(here, place, stack, *evens, *odds)


def packed_width(steps, width):
    return -(-(width * steps * (steps - 1) // 2) // 128) * 128


def assemble(here, place, offsets, stack, evens, odds, n_rows):
    slots, width, ncols = stack.shape
    steps = place.shape[0]
    height = steps * width
    turns, splits = len(evens), len(evens[0])
    cols = ncols // splits

    def kernel(here_ref, place_ref, offset_ref, stack_ref, *refs):
        arrived, (high_ref, low_ref, high_t_ref, low_t_ref, gram_ref, held, sems) = refs[:-7], refs[-7:]
        even, odd = arrived[:turns * splits], arrived[turns * splits:]
        roots, slot, ranks, counts = plan(place_ref, slots, n_rows)
        me = here_ref[0]
        me_odd = lax.rem(me, 2) == 1
        for s in range(steps):
            root = roots[s]
            low, high = jnp.minimum(root, me), jnp.maximum(root, me)
            between = [jnp.where((i > low) & (i < high), jnp.maximum(counts[i], 1), 0) for i in range(n_rows)]
            turn = sum(between, ranks[s])
            target = held.at[pl.ds(s * width, width)]
            below, above = root < me, root > me

            @pl.when(root == me)
            def _():
                pltpu.make_async_copy(stack_ref.at[slot[s]], target, sems.at[s]).start()

            for side, came in (((below & me_odd) | (above & ~me_odd), even), ((below & ~me_odd) | (above & me_odd), odd)):
                for i in range(turns):
                    @pl.when(side & (turn == i))
                    def _():
                        for p in range(splits):
                            piece = held.at[pl.ds(s * width, width), pl.ds(p * cols, cols)]
                            pltpu.make_async_copy(came[i * splits + p], piece, sems.at[s]).start()
        columns = here_ref[1] * ncols + lax.broadcasted_iota(jnp.int32, (width, ncols), 1)
        for s in range(steps):
            rows = pl.ds(s * width, width)
            pltpu.make_async_copy(stack_ref.at[0], held.at[rows], sems.at[s]).wait()
            masked = jnp.where(columns >= offset_ref[s], held[rows, :], 0.0)
            held[rows, :] = masked
            high, low = halves(masked)
            high_ref[rows, :] = high
            low_ref[rows, :] = low
        for at in column_blocks(ncols):
            high_t_ref[at, :], low_t_ref[at, :] = halves(held[:, at].T)
        gram = dot_t(held[...], held[...])
        gram_ref[...] = jnp.zeros_like(gram_ref)
        first = 0
        for s in range(1, steps):
            gram_ref[:, first:first + s * width] = gram[s * width:(s + 1) * width, :s * width]
            first += s * width

    return pl.pallas_call(
        kernel,
        out_shape=[
            pltpu.HBM((height, ncols), jnp.bfloat16),
            pltpu.HBM((height, ncols), jnp.bfloat16),
            pltpu.HBM((ncols, height), jnp.bfloat16),
            pltpu.HBM((ncols, height), jnp.bfloat16),
            jax.ShapeDtypeStruct((width, packed_width(steps, width)), jnp.float32),
        ],
        in_specs=[SMEM, SMEM, SMEM, ANY] + [ANY] * (2 * turns * splits),
        out_specs=[VMEM] * 5,
        scratch_shapes=[pltpu.VMEM((height, ncols), jnp.float32), pltpu.SemaphoreType.DMA((steps,))],
        compiler_params=params(limit=SMALL_LIMIT),
        cost_estimate=cost(12 * height * height * ncols, 8 * height * ncols),
        name="assemble",
    )(here, place, offsets, stack, *[p for turn in evens for p in turn], *[p for turn in odds for p in turn])


def merge(cross, factors, vecs):
    steps, width, _ = factors.shape
    height, ncols = vecs[0].shape

    def kernel(*refs):
        cross_refs, (factor_ref, v_high, v_low, p_ref, total, m_ref) = refs[:-6], refs[-6:]
        total[...] = sum([ref[...] for ref in cross_refs[1:]], cross_refs[0][...])
        first = 0
        for k in range(steps):
            own = lax.broadcasted_iota(jnp.int32, (width, height), 0) + k * width
            rest = (own == lax.broadcasted_iota(jnp.int32, (width, height), 1)).astype(jnp.float32)
            if k:
                rest = rest - dot(total[:, first:first + k * width], m_ref[:k * width, :])
                first += k * width
            m_ref[k * width:(k + 1) * width, :] = dot(factor_ref[k], rest)
        product = dot3(halves(m_ref[...].T), (v_high[...], v_low[...]), ((1,), (0,)))
        high, low = halves(product)
        for i, half in enumerate((high, high, low)):
            p_ref[i * height:(i + 1) * height, :] = half

    return pl.pallas_call(
        kernel,
        out_shape=jax.ShapeDtypeStruct((3 * height, ncols), jnp.bfloat16),
        out_specs=VMEM,
        in_specs=[VMEM] * (len(cross) + 3),
        scratch_shapes=[pltpu.VMEM(cross[0].shape, jnp.float32), pltpu.VMEM((height, height), jnp.float32)],
        compiler_params=params(),
        cost_estimate=cost(6 * height * height * ncols, 8 * height * ncols),
        name="merge",
    )(*cross, factors, *vecs)


def fold(w):
    half = w.shape[0] // 2
    return jnp.concatenate([w[:half], w[half:]], axis=1)


def unfold(w):
    height = w.shape[1] // 2
    return jnp.concatenate([w[:, :height], w[:, height:]], axis=0)


def column_blocks(ncols):
    cols = COLUMNS if ncols % COLUMNS == 0 else ncols
    return [pl.ds(start, cols) for start in range(0, ncols, cols)]


def lift(arrays):
    n, rows = len(arrays), arrays[0].shape[0]
    step = rows // 4 if rows % 64 == 0 else rows

    def kernel(*refs):
        sems = refs[-1]
        copies = []
        for source, out in zip(refs[:n], refs[n:2 * n]):
            for start in range(0, rows, step):
                at = pl.ds(start, step)
                copies.append(pltpu.make_async_copy(source.at[at], out.at[at], sems.at[len(copies)]))
        for i, copy in enumerate(copies):
            copy.start(priority=i % QUEUES)
        for copy in copies:
            copy.wait()

    return pl.pallas_call(
        kernel,
        out_shape=[pltpu.VMEM(x.shape, x.dtype) for x in arrays],
        in_specs=[ANY] * n,
        out_specs=[VMEM] * n,
        scratch_shapes=[pltpu.SemaphoreType.DMA((n * rows // step,))],
        compiler_params=params(),
        cost_estimate=cost(0, 2 * n * arrays[0].size),
        name="lift",
    )(*[in_hbm(x) for x in arrays])


def inner_products(here, x, vecs_t):
    rows, ncols = x.shape
    height = vecs_t[0].shape[1]
    half = rows // 2
    step = rows // 8 if rows % 64 == 0 else rows
    n_copies = rows // step
    cuts = sorted({0, n_copies * 3 // 8, n_copies})

    def kernel(here_ref, x_ref, high_ref, low_ref, mine_ref, theirs_ref, held, total, sems):
        copies = []
        for i in range(n_copies):
            at = pl.ds(i * step, step)
            copies.append(pltpu.make_async_copy(x_ref.at[at], held.at[at], sems.at[i]))
        for copy in copies:
            copy.start()
        for start, end in zip(cuts[:-1], cuts[1:]):
            for copy in copies[start:end]:
                copy.wait()
            at = pl.ds(start * step, (end - start) * step)
            total[at, :] = dot3(halves(held[at, :]), (high_ref[...], low_ref[...]), ((1,), (0,)))
        core = lax.rem(here_ref[1], 2)
        mine_ref[...] = fold(total[pl.ds(pl.multiple_of(core * half, 8), half), :])
        theirs_ref[...] = fold(total[pl.ds(pl.multiple_of((1 - core) * half, 8), half), :])

    return pl.pallas_call(
        kernel,
        out_shape=[jax.ShapeDtypeStruct((half // 2, 2 * height), jnp.float32)] * 2 + [pltpu.VMEM(x.shape, jnp.float32)],
        in_specs=[SMEM, ANY, VMEM, VMEM],
        out_specs=[VMEM] * 3,
        scratch_shapes=[pltpu.VMEM((rows, height), jnp.float32), pltpu.SemaphoreType.DMA((n_copies,))],
        compiler_params=params(),
        cost_estimate=cost(6 * rows * ncols * height, 4 * rows * ncols),
        name="inner_products",
    )(here, in_hbm(x), *vecs_t)


def update(here, x, mine, theirs, changes):
    rows, ncols = x.shape
    height = changes.shape[0] // 3
    half = rows // 2
    blocks = column_blocks(ncols)
    depth = min(4, len(blocks))

    def kernel(here_ref, mine_ref, theirs_ref, x_ref, p_ref, out_ref, w_ref, held, sems):
        core = lax.rem(here_ref[1], 2)
        w_ref[pl.ds(pl.multiple_of(core * half, 8), half), :] = unfold(mine_ref[...])
        w_ref[pl.ds(pl.multiple_of((1 - core) * half, 8), half), :] = unfold(theirs_ref[...])
        high, low = halves(w_ref[...])
        w = jnp.concatenate([high, low, high], axis=1)
        copies = [pltpu.make_async_copy(held.at[i % depth], out_ref.at[:, at], sems.at[i]) for i, at in enumerate(blocks)]
        for i, at in enumerate(blocks):
            change = lax.dot_general(w, p_ref[:, at], (((1,), (0,)), ((), ())), preferred_element_type=jnp.float32)
            if i >= depth:
                copies[i - depth].wait()
            held[i % depth] = x_ref[:, at] - change
            copies[i].start(priority=i % QUEUES)
        for copy in copies[-depth:]:
            copy.wait()

    return pl.pallas_call(
        kernel,
        out_shape=jax.ShapeDtypeStruct(x.shape, jnp.float32),
        in_specs=[SMEM] + [VMEM] * 4,
        out_specs=ANY,
        scratch_shapes=[
            pltpu.VMEM((rows, height), jnp.float32),
            pltpu.VMEM((depth, rows, blocks[0].size), jnp.float32),
            pltpu.SemaphoreType.DMA((len(blocks),)),
        ],
        compiler_params=params(),
        cost_estimate=cost(6 * rows * ncols * height, 8 * rows * ncols),
        name="update",
    )(here, mine, theirs, x, changes)


def swap(array, k, size):
    return lax.ppermute(array, "wide", [(i, i ^ k) for i in range(size)])


def spread(pair, size):
    return [pair] + [swap(pair, k, size) for k in range(2, size, 2)]


def chips_sum(pair, size, token):
    shifts = [k for k in (1 << i for i in range(1, size.bit_length())) if k < size]
    half = pair.shape[0] // 2
    upper, lower = pair[:half], pair[half:]
    for i, (first, second) in enumerate(zip(shifts, reversed(shifts))):
        come_upper, come_lower = swap(upper, first, size), swap(lower, second, size)
        if i == 0:
            upper, lower, _ = lax.optimization_barrier((upper, lower, token))
        upper, lower = upper + come_upper, lower + come_lower
    return jnp.concatenate([upper, lower], axis=0)


def body(n_row, n_wide, eigvec_t, householder, wy_factor, block_place, offsets):
    rows, order = eigvec_t.shape
    steps, width, _ = wy_factor.shape
    slots = householder.shape[0]
    ncols = order // n_wide
    here = jnp.stack([lax.axis_index("row"), lax.axis_index("wide")]).astype(jnp.int32)

    turns = max(z + min(steps - 1, slots * (n_row - 1 - z)) for z in range(n_row - 1))
    cols = ncols // SPLITS
    streams = [([], []) for _ in range(SPLITS)]

    def exchange(array, odd):
        pairs = []
        for z in range(n_row):
            mate = ((z + odd) ^ 1) - odd
            for w in range(n_wide):
                target = mate * n_wide + w if 0 <= mate < n_row else z * n_wide + (w ^ 1)
                pairs.append((z * n_wide + w, target))
        return lax.ppermute(array, ("row", "wide"), pairs)

    whole = rows % 8 == 0
    if whole:
        piece = pack(eigvec_t, n_wide)
        x = lax.all_to_all(piece, "wide", split_axis=0, concat_axis=0, tiled=True)
        tokens = [piece]
    else:
        x = lax.all_to_all(eigvec_t, "wide", split_axis=1, concat_axis=0, tiled=True)[None]
        tokens = []
    for turn in range(turns):
        for part in range(SPLITS):
            evens, odds = streams[part]
            to_even, to_odd = feed(after(here, *tokens), block_place, householder, evens, odds, n_row, part, cols)
            tokens = [to_odd]
            streams[part] = (evens + [exchange(to_even, 0)], odds + [exchange(to_odd, 1)])
    evens = list(zip(*[stream[0] for stream in streams]))
    odds = list(zip(*[stream[1] for stream in streams]))
    high, low, high_t, low_t, gram = assemble(here, block_place, offsets, householder, evens, odds, n_row)
    x = x.reshape(n_wide * rows, ncols)
    vecs_t = lift([after(high_t, x), low_t])
    cross = spread(gram + swap(gram, 1, n_wide), n_wide)
    cross[0] = after(cross[0], *vecs_t)
    cross = functools.reduce(jnp.add, cross)
    changes = merge([cross], wy_factor, (high, low))

    mine, theirs, x = inner_products(after(here, cross), x, vecs_t)
    mine = chips_sum(mine + swap(theirs, 1, n_wide), n_wide, changes)
    return update(here, x, mine, swap(mine, 1, n_wide), changes)


def solution(mesh):
    return jax.shard_map(
        functools.partial(body, mesh.shape["row"], mesh.shape["wide"]),
        mesh=mesh,
        in_specs=(P(("row", "wide"), None), P("row", None, "wide"), P(), P(), P()),
        out_specs=P("row", "wide"),
        check_vma=False,
    )
```

```python
import functools

import jax
import jax.numpy as jnp
from jax import lax
from jax.experimental import pallas as pl
from jax.experimental.pallas import tpu as pltpu
from jax.sharding import PartitionSpec as P

HIGHEST = lax.Precision.HIGHEST
SMALL_LIMIT = 44 * 1024 * 1024
VMEM_LIMIT = 40 * 1024 * 1024
LARGE_LIMIT = 58 * 1024 * 1024
COLUMNS = 512
QUEUES = 2
SPLITS = 2


def dot_t(a, b):
    return lax.dot_general(a, b, (((1,), (1,)), ((), ())), precision=HIGHEST, preferred_element_type=jnp.float32)


def dot(a, b):
    return lax.dot_general(a, b, (((1,), (0,)), ((), ())), precision=HIGHEST, preferred_element_type=jnp.float32)


def halves(x):
    high = x.astype(jnp.bfloat16)
    return high, (x - high.astype(jnp.float32)).astype(jnp.bfloat16)


def dot3(a, b, dims):
    rows = a[0].shape[0]
    both = lax.dot_general(jnp.concatenate(a, axis=0), b[0], (dims, ((), ())), preferred_element_type=jnp.float32)
    last = lax.dot_general(a[0], b[1], (dims, ((), ())), preferred_element_type=jnp.float32)
    return both[:rows] + (both[rows:] + last)


def after(x, *tokens):
    return lax.optimization_barrier((x, *tokens))[0]


def params(limit=VMEM_LIMIT):
    return pltpu.CompilerParams(vmem_limit_bytes=limit)


def cost(flops, nbytes):
    return pl.CostEstimate(flops=flops, bytes_accessed=nbytes, transcendentals=0)


SMEM = pl.BlockSpec(memory_space=pltpu.SMEM)
ANY = pl.BlockSpec(memory_space=pl.ANY)
VMEM = pl.BlockSpec(memory_space=pltpu.VMEM)


def in_hbm(x):
    return pltpu.with_memory_space_constraint(x, pltpu.HBM)


def pack(x, n_wide):
    rows, order = x.shape
    ncols = order // n_wide
    step = 16 if rows % 16 == 0 else rows
    n_copies = n_wide * rows // step

    def kernel(x_ref, out_ref, held, in_sems, out_sems):
        into, out_of = [], []
        for first in range(0, rows, step):
            for k in range(n_wide):
                i, at = len(into), pl.ds(first, step)
                source = x_ref.at[at, pl.ds(k * ncols, ncols)]
                into.append(pltpu.make_async_copy(source, held.at[k, at], in_sems.at[i]))
                out_of.append(pltpu.make_async_copy(held.at[k, at], out_ref.at[k, at], out_sems.at[i]))
        for i, copy in enumerate(into):
            copy.start(priority=i % QUEUES)
        for i, (came, goes) in enumerate(zip(into, out_of)):
            came.wait()
            goes.start(priority=i % QUEUES)
        for copy in out_of:
            copy.wait()

    return pl.pallas_call(
        kernel,
        out_shape=jax.ShapeDtypeStruct((n_wide, rows, ncols), jnp.float32),
        in_specs=[ANY],
        out_specs=ANY,
        scratch_shapes=[
            pltpu.VMEM((n_wide, rows, ncols), jnp.float32),
            pltpu.SemaphoreType.DMA((n_copies,)),
            pltpu.SemaphoreType.DMA((n_copies,)),
        ],
        compiler_params=params(limit=LARGE_LIMIT),
        cost_estimate=cost(0, 8 * rows * order),
        name="pack",
    )(in_hbm(x))


def plan(place_ref, slots, n_rows):
    places = [place_ref[s] for s in range(place_ref.shape[0])]
    roots = [lax.div(p, slots) for p in places]
    slot = [lax.rem(p, slots) for p in places]
    ranks = [sum([(roots[i] == roots[s]).astype(jnp.int32) for i in range(s)], jnp.int32(0)) for s in range(len(places))]
    counts = [sum([(r == i).astype(jnp.int32) for r in roots], jnp.int32(0)) for i in range(n_rows)]
    return roots, slot, ranks, counts


def feed(here, place, stack, evens, odds, n_rows, part, cols):
    slots, width, _ = stack.shape
    turn = len(evens)

    def kernel(here_ref, place_ref, stack_ref, *refs):
        arrived, (out_even, out_odd, sems) = refs[:-3], refs[-3:]
        roots, slot, ranks, _ = plan(place_ref, slots, n_rows)
        me = here_ref[0]
        mine = [r == me for r in roots]
        count = sum([m.astype(jnp.int32) for m in mine], jnp.int32(0))
        own = sum([jnp.where(m & (k == turn), s, 0) for m, k, s in zip(mine, ranks, slot)], jnp.int32(0))
        older = turn - jnp.maximum(count, 1)
        stored = stack_ref.at[own, :, pl.ds(part * cols, cols)]
        for side, out in ((0, out_even), (1, out_odd)):
            @pl.when((older < 0) | (count > turn))
            def _():
                pltpu.make_async_copy(stored, out, sems.at[side]).start()

            for i in range(turn):
                @pl.when((older == i) & (count <= turn))
                def _():
                    pltpu.make_async_copy(arrived[(1 - side) * turn + i], out, sems.at[side]).start()
        for side, out in ((0, out_even), (1, out_odd)):
            pltpu.make_async_copy(stored, out, sems.at[side]).wait()

    return pl.pallas_call(
        kernel,
        out_shape=[jax.ShapeDtypeStruct((width, cols), jnp.float32)] * 2,
        in_specs=[SMEM, SMEM, ANY] + [ANY] * (2 * turn),
        out_specs=[VMEM] * 2,
        scratch_shapes=[pltpu.SemaphoreType.DMA((2,))],
        compiler_params=params(limit=SMALL_LIMIT),
        cost_estimate=cost(0, 16 * width * cols),
        name="feed",
    )(here, place, stack, *evens, *odds)


def packed_width(steps, width):
    return -(-(width * steps * (steps - 1) // 2) // 128) * 128


def assemble(here, place, offsets, stack, evens, odds, n_rows):
    slots, width, ncols = stack.shape
    steps = place.shape[0]
    height = steps * width
    turns, splits = len(evens), len(evens[0])
    cols = ncols // splits

    def kernel(here_ref, place_ref, offset_ref, stack_ref, *refs):
        arrived, (high_ref, low_ref, high_t_ref, low_t_ref, gram_ref, held, sems) = refs[:-7], refs[-7:]
        even, odd = arrived[:turns * splits], arrived[turns * splits:]
        roots, slot, ranks, counts = plan(place_ref, slots, n_rows)
        me = here_ref[0]
        me_odd = lax.rem(me, 2) == 1
        for s in range(steps):
            root = roots[s]
            low, high = jnp.minimum(root, me), jnp.maximum(root, me)
            between = [jnp.where((i > low) & (i < high), jnp.maximum(counts[i], 1), 0) for i in range(n_rows)]
            turn = sum(between, ranks[s])
            target = held.at[pl.ds(s * width, width)]
            below, above = root < me, root > me

            @pl.when(root == me)
            def _():
                pltpu.make_async_copy(stack_ref.at[slot[s]], target, sems.at[s]).start()

            for side, came in (((below & me_odd) | (above & ~me_odd), even), ((below & ~me_odd) | (above & me_odd), odd)):
                for i in range(turns):
                    @pl.when(side & (turn == i))
                    def _():
                        for p in range(splits):
                            piece = held.at[pl.ds(s * width, width), pl.ds(p * cols, cols)]
                            pltpu.make_async_copy(came[i * splits + p], piece, sems.at[s]).start()
        columns = here_ref[1] * ncols + lax.broadcasted_iota(jnp.int32, (width, ncols), 1)
        for s in range(steps):
            rows = pl.ds(s * width, width)
            pltpu.make_async_copy(stack_ref.at[0], held.at[rows], sems.at[s]).wait()
            masked = jnp.where(columns >= offset_ref[s], held[rows, :], 0.0)
            held[rows, :] = masked
            high, low = halves(masked)
            high_ref[rows, :] = high
            low_ref[rows, :] = low
        for at in column_blocks(ncols):
            high_t_ref[at, :], low_t_ref[at, :] = halves(held[:, at].T)
        gram = dot_t(held[...], held[...])
        gram_ref[...] = jnp.zeros_like(gram_ref)
        first = 0
        for s in range(1, steps):
            gram_ref[:, first:first + s * width] = gram[s * width:(s + 1) * width, :s * width]
            first += s * width

    return pl.pallas_call(
        kernel,
        out_shape=[
            pltpu.HBM((height, ncols), jnp.bfloat16),
            pltpu.HBM((height, ncols), jnp.bfloat16),
            pltpu.HBM((ncols, height), jnp.bfloat16),
            pltpu.HBM((ncols, height), jnp.bfloat16),
            jax.ShapeDtypeStruct((width, packed_width(steps, width)), jnp.float32),
        ],
        in_specs=[SMEM, SMEM, SMEM, ANY] + [ANY] * (2 * turns * splits),
        out_specs=[VMEM] * 5,
        scratch_shapes=[pltpu.VMEM((height, ncols), jnp.float32), pltpu.SemaphoreType.DMA((steps,))],
        compiler_params=params(limit=SMALL_LIMIT),
        cost_estimate=cost(12 * height * height * ncols, 8 * height * ncols),
        name="assemble",
    )(here, place, offsets, stack, *[p for turn in evens for p in turn], *[p for turn in odds for p in turn])


def merge(cross, factors, vecs):
    steps, width, _ = factors.shape
    height, ncols = vecs[0].shape

    def kernel(*refs):
        cross_refs, (factor_ref, v_high, v_low, p_ref, total, m_ref) = refs[:-6], refs[-6:]
        total[...] = sum([ref[...] for ref in cross_refs[1:]], cross_refs[0][...])
        first = 0
        for k in range(steps):
            own = lax.broadcasted_iota(jnp.int32, (width, height), 0) + k * width
            rest = (own == lax.broadcasted_iota(jnp.int32, (width, height), 1)).astype(jnp.float32)
            if k:
                rest = rest - dot(total[:, first:first + k * width], m_ref[:k * width, :])
                first += k * width
            m_ref[k * width:(k + 1) * width, :] = dot(factor_ref[k], rest)
        product = dot3(halves(m_ref[...].T), (v_high[...], v_low[...]), ((1,), (0,)))
        high, low = halves(product)
        for i, half in enumerate((high, high, low)):
            p_ref[i * height:(i + 1) * height, :] = half

    return pl.pallas_call(
        kernel,
        out_shape=jax.ShapeDtypeStruct((3 * height, ncols), jnp.bfloat16),
        out_specs=VMEM,
        in_specs=[VMEM] * (len(cross) + 3),
        scratch_shapes=[pltpu.VMEM(cross[0].shape, jnp.float32), pltpu.VMEM((height, height), jnp.float32)],
        compiler_params=params(),
        cost_estimate=cost(6 * height * height * ncols, 8 * height * ncols),
        name="merge",
    )(*cross, factors, *vecs)


def fold(w):
    half = w.shape[0] // 2
    return jnp.concatenate([w[:half], w[half:]], axis=1)


def unfold(w):
    height = w.shape[1] // 2
    return jnp.concatenate([w[:, :height], w[:, height:]], axis=0)


def column_blocks(ncols):
    cols = COLUMNS if ncols % COLUMNS == 0 else ncols
    return [pl.ds(start, cols) for start in range(0, ncols, cols)]


def lift(arrays):
    n, rows = len(arrays), arrays[0].shape[0]
    step = rows // 4 if rows % 64 == 0 else rows

    def kernel(*refs):
        sems = refs[-1]
        copies = []
        for source, out in zip(refs[:n], refs[n:2 * n]):
            for start in range(0, rows, step):
                at = pl.ds(start, step)
                copies.append(pltpu.make_async_copy(source.at[at], out.at[at], sems.at[len(copies)]))
        for i, copy in enumerate(copies):
            copy.start(priority=i % QUEUES)
        for copy in copies:
            copy.wait()

    return pl.pallas_call(
        kernel,
        out_shape=[pltpu.VMEM(x.shape, x.dtype) for x in arrays],
        in_specs=[ANY] * n,
        out_specs=[VMEM] * n,
        scratch_shapes=[pltpu.SemaphoreType.DMA((n * rows // step,))],
        compiler_params=params(),
        cost_estimate=cost(0, 2 * n * arrays[0].size),
        name="lift",
    )(*[in_hbm(x) for x in arrays])


def inner_products(here, x, vecs_t):
    rows, ncols = x.shape
    height = vecs_t[0].shape[1]
    half = rows // 2
    step = rows // 8 if rows % 64 == 0 else rows
    n_copies = rows // step
    cuts = sorted({0, n_copies // 2, n_copies})

    def kernel(here_ref, x_ref, high_ref, low_ref, mine_ref, theirs_ref, held, total, sems):
        copies = []
        for i in range(n_copies):
            at = pl.ds(i * step, step)
            copies.append(pltpu.make_async_copy(x_ref.at[at], held.at[at], sems.at[i]))
        for copy in copies:
            copy.start()
        for start, end in zip(cuts[:-1], cuts[1:]):
            for copy in copies[start:end]:
                copy.wait()
            at = pl.ds(start * step, (end - start) * step)
            total[at, :] = dot3(halves(held[at, :]), (high_ref[...], low_ref[...]), ((1,), (0,)))
        core = lax.rem(here_ref[1], 2)
        mine_ref[...] = fold(total[pl.ds(pl.multiple_of(core * half, 8), half), :])
        theirs_ref[...] = fold(total[pl.ds(pl.multiple_of((1 - core) * half, 8), half), :])

    return pl.pallas_call(
        kernel,
        out_shape=[jax.ShapeDtypeStruct((half // 2, 2 * height), jnp.float32)] * 2 + [pltpu.VMEM(x.shape, jnp.float32)],
        in_specs=[SMEM, ANY, VMEM, VMEM],
        out_specs=[VMEM] * 3,
        scratch_shapes=[pltpu.VMEM((rows, height), jnp.float32), pltpu.SemaphoreType.DMA((n_copies,))],
        compiler_params=params(),
        cost_estimate=cost(6 * rows * ncols * height, 4 * rows * ncols),
        name="inner_products",
    )(here, in_hbm(x), *vecs_t)


def update(here, x, mine, theirs, changes):
    rows, ncols = x.shape
    height = changes.shape[0] // 3
    half = rows // 2
    blocks = column_blocks(ncols)
    depth = min(4, len(blocks))

    def kernel(here_ref, mine_ref, theirs_ref, x_ref, p_ref, out_ref, w_ref, held, sems):
        core = lax.rem(here_ref[1], 2)
        w_ref[pl.ds(pl.multiple_of(core * half, 8), half), :] = unfold(mine_ref[...])
        w_ref[pl.ds(pl.multiple_of((1 - core) * half, 8), half), :] = unfold(theirs_ref[...])
        high, low = halves(w_ref[...])
        w = jnp.concatenate([high, low, high], axis=1)
        copies = [pltpu.make_async_copy(held.at[i % depth], out_ref.at[:, at], sems.at[i]) for i, at in enumerate(blocks)]
        for i, at in enumerate(blocks):
            change = lax.dot_general(w, p_ref[:, at], (((1,), (0,)), ((), ())), preferred_element_type=jnp.float32)
            if i >= depth:
                copies[i - depth].wait()
            held[i % depth] = x_ref[:, at] - change
            copies[i].start(priority=i % QUEUES)
        for copy in copies[-depth:]:
            copy.wait()

    return pl.pallas_call(
        kernel,
        out_shape=jax.ShapeDtypeStruct(x.shape, jnp.float32),
        in_specs=[SMEM] + [VMEM] * 4,
        out_specs=ANY,
        scratch_shapes=[
            pltpu.VMEM((rows, height), jnp.float32),
            pltpu.VMEM((depth, rows, blocks[0].size), jnp.float32),
            pltpu.SemaphoreType.DMA((len(blocks),)),
        ],
        compiler_params=params(),
        cost_estimate=cost(6 * rows * ncols * height, 8 * rows * ncols),
        name="update",
    )(here, mine, theirs, x, changes)


def swap(array, k, size):
    return lax.ppermute(array, "wide", [(i, i ^ k) for i in range(size)])


def spread(pair, size):
    return [pair] + [swap(pair, k, size) for k in range(2, size, 2)]


def chips_sum(pair, size, token):
    shifts = [k for k in (1 << i for i in range(1, size.bit_length())) if k < size]
    half = pair.shape[0] // 2
    upper, lower = pair[:half], pair[half:]
    for i, (first, second) in enumerate(zip(shifts, reversed(shifts))):
        come_upper, come_lower = swap(upper, first, size), swap(lower, second, size)
        if i == 0:
            upper, lower, _ = lax.optimization_barrier((upper, lower, token))
        upper, lower = upper + come_upper, lower + come_lower
    return jnp.concatenate([upper, lower], axis=0)


def body(n_row, n_wide, eigvec_t, householder, wy_factor, block_place, offsets):
    rows, order = eigvec_t.shape
    steps, width, _ = wy_factor.shape
    slots = householder.shape[0]
    ncols = order // n_wide
    here = jnp.stack([lax.axis_index("row"), lax.axis_index("wide")]).astype(jnp.int32)

    turns = max(z + min(steps - 1, slots * (n_row - 1 - z)) for z in range(n_row - 1))
    cols = ncols // SPLITS
    streams = [([], []) for _ in range(SPLITS)]

    def exchange(array, odd):
        pairs = []
        for z in range(n_row):
            mate = ((z + odd) ^ 1) - odd
            for w in range(n_wide):
                target = mate * n_wide + w if 0 <= mate < n_row else z * n_wide + (w ^ 1)
                pairs.append((z * n_wide + w, target))
        return lax.ppermute(array, ("row", "wide"), pairs)

    whole = rows % 8 == 0
    if whole:
        piece = pack(eigvec_t, n_wide)
        x = lax.all_to_all(piece, "wide", split_axis=0, concat_axis=0, tiled=True)
        tokens = [piece]
    else:
        x = lax.all_to_all(eigvec_t, "wide", split_axis=1, concat_axis=0, tiled=True)[None]
        tokens = []
    for turn in range(turns):
        for part in range(SPLITS):
            evens, odds = streams[part]
            to_even, to_odd = feed(after(here, *tokens), block_place, householder, evens, odds, n_row, part, cols)
            tokens = [to_odd]
            streams[part] = (evens + [exchange(to_even, 0)], odds + [exchange(to_odd, 1)])
    evens = list(zip(*[stream[0] for stream in streams]))
    odds = list(zip(*[stream[1] for stream in streams]))
    high, low, high_t, low_t, gram = assemble(here, block_place, offsets, householder, evens, odds, n_row)
    x = x.reshape(n_wide * rows, ncols)
    vecs_t = lift([after(high_t, x), low_t])
    cross = spread(gram + swap(gram, 1, n_wide), n_wide)
    cross[0] = after(cross[0], *vecs_t)
    cross = functools.reduce(jnp.add, cross)
    changes = merge([cross], wy_factor, (high, low))

    mine, theirs, x = inner_products(after(here, cross), x, vecs_t)
    mine = chips_sum(mine + swap(theirs, 1, n_wide), n_wide, changes)
    return update(here, x, mine, swap(mine, 1, n_wide), changes)


def solution(mesh):
    return jax.shard_map(
        functools.partial(body, mesh.shape["row"], mesh.shape["wide"]),
        mesh=mesh,
        in_specs=(P(("row", "wide"), None), P("row", None, "wide"), P(), P(), P()),
        out_specs=P("row", "wide"),
        check_vma=False,
    )
```

```python
import functools

import jax
import jax.numpy as jnp
from jax import lax
from jax.experimental import pallas as pl
from jax.experimental.pallas import tpu as pltpu
from jax.sharding import PartitionSpec as P

HIGHEST = lax.Precision.HIGHEST
SMALL_LIMIT = 44 * 1024 * 1024
VMEM_LIMIT = 40 * 1024 * 1024
LARGE_LIMIT = 58 * 1024 * 1024
COLUMNS = 512
QUEUES = 2
SPLITS = 2


def dot_t(a, b):
    return lax.dot_general(a, b, (((1,), (1,)), ((), ())), precision=HIGHEST, preferred_element_type=jnp.float32)


def dot(a, b):
    return lax.dot_general(a, b, (((1,), (0,)), ((), ())), precision=HIGHEST, preferred_element_type=jnp.float32)


def halves(x):
    high = x.astype(jnp.bfloat16)
    return high, (x - high.astype(jnp.float32)).astype(jnp.bfloat16)


def dot3(a, b, dims):
    rows = a[0].shape[0]
    both = lax.dot_general(jnp.concatenate(a, axis=0), b[0], (dims, ((), ())), preferred_element_type=jnp.float32)
    last = lax.dot_general(a[0], b[1], (dims, ((), ())), preferred_element_type=jnp.float32)
    return both[:rows] + (both[rows:] + last)


def after(x, *tokens):
    return lax.optimization_barrier((x, *tokens))[0]


def params(limit=VMEM_LIMIT):
    return pltpu.CompilerParams(vmem_limit_bytes=limit)


def cost(flops, nbytes):
    return pl.CostEstimate(flops=flops, bytes_accessed=nbytes, transcendentals=0)


SMEM = pl.BlockSpec(memory_space=pltpu.SMEM)
ANY = pl.BlockSpec(memory_space=pl.ANY)
VMEM = pl.BlockSpec(memory_space=pltpu.VMEM)


def in_hbm(x):
    return pltpu.with_memory_space_constraint(x, pltpu.HBM)


def pack(x, n_wide):
    rows, order = x.shape
    ncols = order // n_wide
    step = 16 if rows % 16 == 0 else rows
    n_copies = n_wide * rows // step

    def kernel(x_ref, out_ref, held, in_sems, out_sems):
        into, out_of = [], []
        for first in range(0, rows, step):
            for k in range(n_wide):
                i, at = len(into), pl.ds(first, step)
                source = x_ref.at[at, pl.ds(k * ncols, ncols)]
                into.append(pltpu.make_async_copy(source, held.at[k, at], in_sems.at[i]))
                out_of.append(pltpu.make_async_copy(held.at[k, at], out_ref.at[k, at], out_sems.at[i]))
        for i, copy in enumerate(into):
            copy.start(priority=i % QUEUES)
        for i, (came, goes) in enumerate(zip(into, out_of)):
            came.wait()
            goes.start(priority=i % QUEUES)
        for copy in out_of:
            copy.wait()

    return pl.pallas_call(
        kernel,
        out_shape=jax.ShapeDtypeStruct((n_wide, rows, ncols), jnp.float32),
        in_specs=[ANY],
        out_specs=ANY,
        scratch_shapes=[
            pltpu.VMEM((n_wide, rows, ncols), jnp.float32),
            pltpu.SemaphoreType.DMA((n_copies,)),
            pltpu.SemaphoreType.DMA((n_copies,)),
        ],
        compiler_params=params(limit=LARGE_LIMIT),
        cost_estimate=cost(0, 8 * rows * order),
        name="pack",
    )(in_hbm(x))


def plan(place_ref, slots, n_rows):
    places = [place_ref[s] for s in range(place_ref.shape[0])]
    roots = [lax.div(p, slots) for p in places]
    slot = [lax.rem(p, slots) for p in places]
    ranks = [sum([(roots[i] == roots[s]).astype(jnp.int32) for i in range(s)], jnp.int32(0)) for s in range(len(places))]
    counts = [sum([(r == i).astype(jnp.int32) for r in roots], jnp.int32(0)) for i in range(n_rows)]
    return roots, slot, ranks, counts


def feed(here, place, stack, evens, odds, n_rows, part, cols):
    slots, width, _ = stack.shape
    turn = len(evens)

    def kernel(here_ref, place_ref, stack_ref, *refs):
        arrived, (out_even, out_odd, sems) = refs[:-3], refs[-3:]
        roots, slot, ranks, _ = plan(place_ref, slots, n_rows)
        me = here_ref[0]
        mine = [r == me for r in roots]
        count = sum([m.astype(jnp.int32) for m in mine], jnp.int32(0))
        own = sum([jnp.where(m & (k == turn), s, 0) for m, k, s in zip(mine, ranks, slot)], jnp.int32(0))
        older = turn - jnp.maximum(count, 1)
        stored = stack_ref.at[own, :, pl.ds(part * cols, cols)]
        for side, out in ((0, out_even), (1, out_odd)):
            @pl.when((older < 0) | (count > turn))
            def _():
                pltpu.make_async_copy(stored, out, sems.at[side]).start()

            for i in range(turn):
                @pl.when((older == i) & (count <= turn))
                def _():
                    pltpu.make_async_copy(arrived[(1 - side) * turn + i], out, sems.at[side]).start()
        for side, out in ((0, out_even), (1, out_odd)):
            pltpu.make_async_copy(stored, out, sems.at[side]).wait()

    return pl.pallas_call(
        kernel,
        out_shape=[jax.ShapeDtypeStruct((width, cols), jnp.float32)] * 2,
        in_specs=[SMEM, SMEM, ANY] + [ANY] * (2 * turn),
        out_specs=[VMEM] * 2,
        scratch_shapes=[pltpu.SemaphoreType.DMA((2,))],
        compiler_params=params(limit=SMALL_LIMIT),
        cost_estimate=cost(0, 16 * width * cols),
        name="feed",
    )(here, place, stack, *evens, *odds)


def packed_width(steps, width):
    return -(-(width * steps * (steps - 1) // 2) // 128) * 128


def assemble(here, place, offsets, stack, evens, odds, n_rows):
    slots, width, ncols = stack.shape
    steps = place.shape[0]
    height = steps * width
    turns, splits = len(evens), len(evens[0])
    cols = ncols // splits

    def kernel(here_ref, place_ref, offset_ref, stack_ref, *refs):
        arrived, (high_ref, low_ref, high_t_ref, low_t_ref, gram_ref, held, sems) = refs[:-7], refs[-7:]
        even, odd = arrived[:turns * splits], arrived[turns * splits:]
        roots, slot, ranks, counts = plan(place_ref, slots, n_rows)
        me = here_ref[0]
        me_odd = lax.rem(me, 2) == 1
        for s in range(steps):
            root = roots[s]
            low, high = jnp.minimum(root, me), jnp.maximum(root, me)
            between = [jnp.where((i > low) & (i < high), jnp.maximum(counts[i], 1), 0) for i in range(n_rows)]
            turn = sum(between, ranks[s])
            target = held.at[pl.ds(s * width, width)]
            below, above = root < me, root > me

            @pl.when(root == me)
            def _():
                pltpu.make_async_copy(stack_ref.at[slot[s]], target, sems.at[s]).start()

            for side, came in (((below & me_odd) | (above & ~me_odd), even), ((below & ~me_odd) | (above & me_odd), odd)):
                for i in range(turns):
                    @pl.when(side & (turn == i))
                    def _():
                        for p in range(splits):
                            piece = held.at[pl.ds(s * width, width), pl.ds(p * cols, cols)]
                            pltpu.make_async_copy(came[i * splits + p], piece, sems.at[s]).start()
        columns = here_ref[1] * ncols + lax.broadcasted_iota(jnp.int32, (width, ncols), 1)
        for s in range(steps):
            rows = pl.ds(s * width, width)
            pltpu.make_async_copy(stack_ref.at[0], held.at[rows], sems.at[s]).wait()
            masked = jnp.where(columns >= offset_ref[s], held[rows, :], 0.0)
            held[rows, :] = masked
            high, low = halves(masked)
            high_ref[rows, :] = high
            low_ref[rows, :] = low
        for at in column_blocks(ncols):
            high_t_ref[at, :], low_t_ref[at, :] = halves(held[:, at].T)
        gram = dot_t(held[...], held[...])
        gram_ref[...] = jnp.zeros_like(gram_ref)
        first = 0
        for s in range(1, steps):
            gram_ref[:, first:first + s * width] = gram[s * width:(s + 1) * width, :s * width]
            first += s * width

    return pl.pallas_call(
        kernel,
        out_shape=[
            pltpu.HBM((height, ncols), jnp.bfloat16),
            pltpu.HBM((height, ncols), jnp.bfloat16),
            pltpu.HBM((ncols, height), jnp.bfloat16),
            pltpu.HBM((ncols, height), jnp.bfloat16),
            jax.ShapeDtypeStruct((width, packed_width(steps, width)), jnp.float32),
        ],
        in_specs=[SMEM, SMEM, SMEM, ANY] + [ANY] * (2 * turns * splits),
        out_specs=[VMEM] * 5,
        scratch_shapes=[pltpu.VMEM((height, ncols), jnp.float32), pltpu.SemaphoreType.DMA((steps,))],
        compiler_params=params(limit=SMALL_LIMIT),
        cost_estimate=cost(12 * height * height * ncols, 8 * height * ncols),
        name="assemble",
    )(here, place, offsets, stack, *[p for turn in evens for p in turn], *[p for turn in odds for p in turn])


def merge(cross, factors, vecs):
    steps, width, _ = factors.shape
    height, ncols = vecs[0].shape

    def kernel(*refs):
        cross_refs, (factor_ref, v_high, v_low, p_ref, total, m_ref) = refs[:-6], refs[-6:]
        total[...] = sum([ref[...] for ref in cross_refs[1:]], cross_refs[0][...])
        first = 0
        for k in range(steps):
            own = lax.broadcasted_iota(jnp.int32, (width, height), 0) + k * width
            rest = (own == lax.broadcasted_iota(jnp.int32, (width, height), 1)).astype(jnp.float32)
            if k:
                rest = rest - dot(total[:, first:first + k * width], m_ref[:k * width, :])
                first += k * width
            m_ref[k * width:(k + 1) * width, :] = dot(factor_ref[k], rest)
        product = dot3(halves(m_ref[...].T), (v_high[...], v_low[...]), ((1,), (0,)))
        high, low = halves(product)
        for i, half in enumerate((high, high, low)):
            p_ref[i * height:(i + 1) * height, :] = half

    return pl.pallas_call(
        kernel,
        out_shape=jax.ShapeDtypeStruct((3 * height, ncols), jnp.bfloat16),
        out_specs=VMEM,
        in_specs=[VMEM] * (len(cross) + 3),
        scratch_shapes=[pltpu.VMEM(cross[0].shape, jnp.float32), pltpu.VMEM((height, height), jnp.float32)],
        compiler_params=params(),
        cost_estimate=cost(6 * height * height * ncols, 8 * height * ncols),
        name="merge",
    )(*cross, factors, *vecs)


def fold(w):
    half = w.shape[0] // 2
    return jnp.concatenate([w[:half], w[half:]], axis=1)


def unfold(w):
    height = w.shape[1] // 2
    return jnp.concatenate([w[:, :height], w[:, height:]], axis=0)


def column_blocks(ncols):
    cols = COLUMNS if ncols % COLUMNS == 0 else ncols
    return [pl.ds(start, cols) for start in range(0, ncols, cols)]


def lift(arrays):
    n, rows = len(arrays), arrays[0].shape[0]
    step = rows // 4 if rows % 64 == 0 else rows

    def kernel(*refs):
        sems = refs[-1]
        copies = []
        for source, out in zip(refs[:n], refs[n:2 * n]):
            for start in range(0, rows, step):
                at = pl.ds(start, step)
                copies.append(pltpu.make_async_copy(source.at[at], out.at[at], sems.at[len(copies)]))
        for i, copy in enumerate(copies):
            copy.start(priority=i % QUEUES)
        for copy in copies:
            copy.wait()

    return pl.pallas_call(
        kernel,
        out_shape=[pltpu.VMEM(x.shape, x.dtype) for x in arrays],
        in_specs=[ANY] * n,
        out_specs=[VMEM] * n,
        scratch_shapes=[pltpu.SemaphoreType.DMA((n * rows // step,))],
        compiler_params=params(),
        cost_estimate=cost(0, 2 * n * arrays[0].size),
        name="lift",
    )(*[in_hbm(x) for x in arrays])


def inner_products(here, x, vecs_t):
    rows, ncols = x.shape
    height = vecs_t[0].shape[1]
    half = rows // 2
    step = rows // 8 if rows % 64 == 0 else rows
    n_copies = rows // step
    cuts = sorted({0, n_copies // 8, n_copies})

    def kernel(here_ref, x_ref, high_ref, low_ref, mine_ref, theirs_ref, held, total, sems):
        copies = []
        for i in range(n_copies):
            at = pl.ds(i * step, step)
            copies.append(pltpu.make_async_copy(x_ref.at[at], held.at[at], sems.at[i]))
        for copy in copies:
            copy.start()
        for start, end in zip(cuts[:-1], cuts[1:]):
            for copy in copies[start:end]:
                copy.wait()
            at = pl.ds(start * step, (end - start) * step)
            total[at, :] = dot3(halves(held[at, :]), (high_ref[...], low_ref[...]), ((1,), (0,)))
        core = lax.rem(here_ref[1], 2)
        mine_ref[...] = fold(total[pl.ds(pl.multiple_of(core * half, 8), half), :])
        theirs_ref[...] = fold(total[pl.ds(pl.multiple_of((1 - core) * half, 8), half), :])

    return pl.pallas_call(
        kernel,
        out_shape=[jax.ShapeDtypeStruct((half // 2, 2 * height), jnp.float32)] * 2 + [pltpu.VMEM(x.shape, jnp.float32)],
        in_specs=[SMEM, ANY, VMEM, VMEM],
        out_specs=[VMEM] * 3,
        scratch_shapes=[pltpu.VMEM((rows, height), jnp.float32), pltpu.SemaphoreType.DMA((n_copies,))],
        compiler_params=params(),
        cost_estimate=cost(6 * rows * ncols * height, 4 * rows * ncols),
        name="inner_products",
    )(here, in_hbm(x), *vecs_t)


def update(here, x, mine, theirs, changes):
    rows, ncols = x.shape
    height = changes.shape[0] // 3
    half = rows // 2
    blocks = column_blocks(ncols)
    depth = min(4, len(blocks))

    def kernel(here_ref, mine_ref, theirs_ref, x_ref, p_ref, out_ref, w_ref, held, sems):
        core = lax.rem(here_ref[1], 2)
        w_ref[pl.ds(pl.multiple_of(core * half, 8), half), :] = unfold(mine_ref[...])
        w_ref[pl.ds(pl.multiple_of((1 - core) * half, 8), half), :] = unfold(theirs_ref[...])
        high, low = halves(w_ref[...])
        w = jnp.concatenate([high, low, high], axis=1)
        copies = [pltpu.make_async_copy(held.at[i % depth], out_ref.at[:, at], sems.at[i]) for i, at in enumerate(blocks)]
        for i, at in enumerate(blocks):
            change = lax.dot_general(w, p_ref[:, at], (((1,), (0,)), ((), ())), preferred_element_type=jnp.float32)
            if i >= depth:
                copies[i - depth].wait()
            held[i % depth] = x_ref[:, at] - change
            copies[i].start(priority=i % QUEUES)
        for copy in copies[-depth:]:
            copy.wait()

    return pl.pallas_call(
        kernel,
        out_shape=jax.ShapeDtypeStruct(x.shape, jnp.float32),
        in_specs=[SMEM] + [VMEM] * 4,
        out_specs=ANY,
        scratch_shapes=[
            pltpu.VMEM((rows, height), jnp.float32),
            pltpu.VMEM((depth, rows, blocks[0].size), jnp.float32),
            pltpu.SemaphoreType.DMA((len(blocks),)),
        ],
        compiler_params=params(),
        cost_estimate=cost(6 * rows * ncols * height, 8 * rows * ncols),
        name="update",
    )(here, mine, theirs, x, changes)


def swap(array, k, size):
    return lax.ppermute(array, "wide", [(i, i ^ k) for i in range(size)])


def spread(pair, size):
    return [pair] + [swap(pair, k, size) for k in range(2, size, 2)]


def chips_sum(pair, size, token):
    shifts = [k for k in (1 << i for i in range(1, size.bit_length())) if k < size]
    half = pair.shape[0] // 2
    upper, lower = pair[:half], pair[half:]
    for i, (first, second) in enumerate(zip(shifts, reversed(shifts))):
        come_upper, come_lower = swap(upper, first, size), swap(lower, second, size)
        if i == 0:
            upper, lower, _ = lax.optimization_barrier((upper, lower, token))
        upper, lower = upper + come_upper, lower + come_lower
    return jnp.concatenate([upper, lower], axis=0)


def body(n_row, n_wide, eigvec_t, householder, wy_factor, block_place, offsets):
    rows, order = eigvec_t.shape
    steps, width, _ = wy_factor.shape
    slots = householder.shape[0]
    ncols = order // n_wide
    here = jnp.stack([lax.axis_index("row"), lax.axis_index("wide")]).astype(jnp.int32)

    turns = max(z + min(steps - 1, slots * (n_row - 1 - z)) for z in range(n_row - 1))
    cols = ncols // SPLITS
    streams = [([], []) for _ in range(SPLITS)]

    def exchange(array, odd):
        pairs = []
        for z in range(n_row):
            mate = ((z + odd) ^ 1) - odd
            for w in range(n_wide):
                target = mate * n_wide + w if 0 <= mate < n_row else z * n_wide + (w ^ 1)
                pairs.append((z * n_wide + w, target))
        return lax.ppermute(array, ("row", "wide"), pairs)

    whole = rows % 8 == 0
    if whole:
        piece = pack(eigvec_t, n_wide)
        x = lax.all_to_all(piece, "wide", split_axis=0, concat_axis=0, tiled=True)
        tokens = [piece]
    else:
        x = lax.all_to_all(eigvec_t, "wide", split_axis=1, concat_axis=0, tiled=True)[None]
        tokens = []
    for turn in range(turns):
        for part in range(SPLITS):
            evens, odds = streams[part]
            to_even, to_odd = feed(after(here, *tokens), block_place, householder, evens, odds, n_row, part, cols)
            tokens = [to_odd]
            streams[part] = (evens + [exchange(to_even, 0)], odds + [exchange(to_odd, 1)])
    evens = list(zip(*[stream[0] for stream in streams]))
    odds = list(zip(*[stream[1] for stream in streams]))
    high, low, high_t, low_t, gram = assemble(here, block_place, offsets, householder, evens, odds, n_row)
    x = x.reshape(n_wide * rows, ncols)
    vecs_t = lift([after(high_t, x), low_t])
    cross = spread(gram + swap(gram, 1, n_wide), n_wide)
    cross[0] = after(cross[0], *vecs_t)
    cross = functools.reduce(jnp.add, cross)
    changes = merge([cross], wy_factor, (high, low))

    mine, theirs, x = inner_products(after(here, cross), x, vecs_t)
    mine = chips_sum(mine + swap(theirs, 1, n_wide), n_wide, changes)
    return update(here, x, mine, swap(mine, 1, n_wide), changes)


def solution(mesh):
    return jax.shard_map(
        functools.partial(body, mesh.shape["row"], mesh.shape["wide"]),
        mesh=mesh,
        in_specs=(P(("row", "wide"), None), P("row", None, "wide"), P(), P(), P()),
        out_specs=P("row", "wide"),
        check_vma=False,
    )
```
